32 devices in a mesh: dp: 8 (over z, x), mp: 4 (over y, core).
Axes of the slice: x: 2, y: 2, z: 4, core: 2. Of those that a mesh axis runs over, the one named last changes fastest.
Arguments:
- tokens: bfloat16 [4096, 768], P('dp'), may hold values from -6 to 6
- time_embed: bfloat16 [32, 768], P('dp'), may hold values from -6 to 6
- segment_ids: int32 [32, 128], P('dp'), may hold values from 0 to 15, never falling along the last dimension, each value on 1 to 64 neighbouring positions
- norm1_gain: float32 [768], replicated, may hold values from 0.5 to 2
- norm1_bias: float32 [768], replicated, may hold values from -3 to 3
- qkv_weight: bfloat16 [3, 768, 768], P(None, None, 'mp'), may hold values from -0.21875 to 0.21875
- qv_bias: float32 [2, 768], P(None, 'mp'), may hold values from -3 to 3
- out_weight: bfloat16 [768, 768], P('mp'), may hold values from -0.875 to 0.875
- out_bias: float32 [768], replicated, may hold values from -3 to 3
- norm2_gain: float32 [768], replicated, may hold values from 0.5 to 2
- norm2_bias: float32 [768], replicated, may hold values from -3 to 3
- up_weight: bfloat16 [768, 3072], P(None, 'mp'), may hold values from -0.21875 to 0.21875
- up_bias: float32 [3072], P('mp'), may hold values from -3 to 3
- down_weight: bfloat16 [3072, 768], P('mp'), may hold values from -0.109375 to 0.109375
- down_bias: float32 [768], replicated, may hold values from -3 to 3
- cotangent: bfloat16 [4096, 768], P('dp'), may hold values from -6 to 6
Outputs:
- output: bfloat16 [4096, 768], P('dp')
- input_grad: bfloat16 [4096, 768], P('dp')
- time_grad: float32 [32, 768], P('dp')
- norm1_gain_grad: float32 [768], replicated
- norm1_bias_grad: float32 [768], replicated
- qkv_grad: float32 [3, 768, 768], P(None, None, 'mp')
- qv_bias_grad: float32 [2, 768], P(None, 'mp')
- out_weight_grad: float32 [768, 768], P('mp')
- out_bias_grad: float32 [768], replicated
- norm2_gain_grad: float32 [768], replicated
- norm2_bias_grad: float32 [768], replicated
- up_grad: float32 [768, 3072], P(None, 'mp')
- up_bias_grad: float32 [3072], P('mp')
- down_grad: float32 [3072, 768], P('mp')
- down_bias_grad: float32 [768], replicated
The draws below stay inside these ranges and needn't reach their ends.
Inputs may be any that keep to these rules, and one draw needn't show every extreme that they name: `segment_ids`: within each packed row the ids never fall, each sentence has 1 to 64 positions, and some sentence of each row has exactly 64.
All inputs are finite; a program needn't handle non-finite values.
Results may differ from the reference program's by a relative error of at most 0.0093.
Values sent between devices are 32-bit elements; how exact they have to be, the bound alone decides.
A program may use at most 128 MiB of HBM per device.

```python
import math
import jax
import jax.numpy as jnp
import numpy as np
from jax import lax

H = 12
HD = 64
D = 768
FF = 3072
SEQ = 128
ROWS = 32
TOKENS = 4096


def levels(own_key, extent, cuts, smallest, largest):
    def one(position, parts):
        steps = jax.random.uniform(jax.random.fold_in(jax.random.fold_in(own_key, 6), position), (parts,), jnp.float32, smallest / len(cuts), largest / len(cuts))
        return jnp.repeat(jnp.exp(steps), extent[position] // parts).reshape((-1,) + (1,) * (len(extent) - position - 1))

    level = one(*cuts[0])
    for cut in cuts[1:]:
        level = level * one(*cut)
    return level


def profile(amount, total, limit, skew):
    portions = [(1 << 20) // math.isqrt(rank ** skew) + 1 for rank in range(2, amount + 1)]
    surplus, holding = total - limit - (amount - 1), [1] * (amount - 1)
    while surplus > 0:
        movable = [i for i in range(amount - 1) if holding[i] < limit]
        whole, remaining = sum([portions[i] for i in movable]), surplus
        for i in movable:
            addition = min(limit - holding[i], max(1, remaining * portions[i] // whole), surplus)
            holding[i] = holding[i] + addition
            surplus = surplus - addition
    return np.array([limit] + holding)


def ragged(key, count, total, limit, skew):
    if count == 2:
        one = jax.random.randint(key, (), max(1, total - limit), min(limit, total - 1) + 1)
        return jnp.stack([one, total - one])
    tallies = jnp.asarray(profile(count, total, limit, skew), jnp.int32)
    twos = (count - 1) // 2
    donor, receiver = tallies[1:1 + 2 * twos:2], tallies[2:2 + 2 * twos:2]
    room = jnp.minimum(donor - 1, limit - receiver)
    passed = jax.random.randint(jax.random.fold_in(key, 1), (twos,), 0, 1 << 20) % (room + 1)
    tallies = tallies.at[1:1 + 2 * twos:2].set(donor - passed).at[2:2 + 2 * twos:2].set(receiver + passed)
    return tallies[jax.random.permutation(jax.random.fold_in(key, 2), count)]


def scatter_about(rng, shape, scale, bound, cuts=(), kind=jnp.bfloat16):
    values = scale * jax.random.normal(rng, shape, jnp.float32)
    if cuts:
        values = values * levels(rng, shape, cuts, -0.22, 0.18)
    return jnp.clip(values, -bound, bound).astype(kind)


def setup_inputs(seed: int = 0) -> dict:
    keys = jax.random.split(jax.random.key(seed), 17)
    return {
        "tokens": scatter_about(keys[0], (TOKENS, D), 1.0, 6.0, ((0, 8),)),
        "time_embed": scatter_about(keys[1], (ROWS, D), 1.0, 6.0, ((0, 8),)),
        "segment_ids": jax.vmap(lambda own: jnp.searchsorted(jnp.cumsum(ragged(own, SEQ // 8, SEQ, SEQ // 2, 0)), jnp.arange(SEQ), side="right"))(jax.random.split(keys[2], ROWS)).reshape((ROWS, SEQ)).astype(jnp.int32),
        "norm1_gain": jnp.clip(jnp.exp(jax.random.uniform(keys[3], (D,), jnp.float32, math.log(0.5), math.log(2.0))), 0.5, 2.0),
        "norm1_bias": scatter_about(keys[4], (D,), 0.5, 3.0, (), jnp.float32),
        "qkv_weight": scatter_about(keys[5], (3, D, D), D ** -0.5, 0.21875, ((2, 4),)),
        "qv_bias": scatter_about(keys[6], (2, D), 0.5, 3.0, ((1, 4),), jnp.float32),
        "out_weight": scatter_about(keys[7], (D, D), (D // 16) ** -0.5, 0.875, ((0, 4),)),
        "out_bias": scatter_about(keys[8], (D,), 0.5, 3.0, (), jnp.float32),
        "norm2_gain": jnp.clip(jnp.exp(jax.random.uniform(keys[9], (D,), jnp.float32, math.log(0.5), math.log(2.0))), 0.5, 2.0),
        "norm2_bias": scatter_about(keys[10], (D,), 0.5, 3.0, (), jnp.float32),
        "up_weight": scatter_about(keys[11], (D, FF), D ** -0.5, 0.21875, ((1, 4),)),
        "up_bias": scatter_about(keys[12], (FF,), 0.5, 3.0, ((0, 4),), jnp.float32),
        "down_weight": scatter_about(keys[13], (FF, D), FF ** -0.5, 0.109375, ((0, 4),)),
        "down_bias": scatter_about(keys[14], (D,), 0.5, 3.0, (), jnp.float32),
        "cotangent": scatter_about(keys[15], (TOKENS, D), 1.0, 6.0, ((0, 8),)),
    }


precise = lax.Precision.HIGHEST

@jax.custom_vjp
def low(v):
    return lax.optimization_barrier(v.astype(jnp.bfloat16)).astype(jnp.float32)

@jax.custom_vjp
def low_back(v):
    return v

def low_keep(v):
    return (low(v), None)

def low_pass(kept, grad):
    return (grad,)

def back_keep(v):
    return (v, None)

def back_low(kept, grad):
    return (low(grad),)
low.defvjp(low_keep, low_pass)
low_back.defvjp(back_keep, back_low)

def both_round(inputs):
    return low(low_back(inputs))

def layer_norm(inputs, norm_gain, norm_shift):
    centred = inputs - lax.optimization_barrier(jnp.mean(inputs, -1, keepdims=True))
    spread = lax.optimization_barrier(jnp.mean(centred * centred, -1, keepdims=True))
    return centred * lax.rsqrt(spread + 1e-05) * norm_gain + norm_shift

def attend_row(pieces):
    queries_row, keys_row, values_row, labels_row = pieces
    scores = low_back(jnp.einsum('qhd,khd->hqk', queries_row, keys_row, precision=precise) * HD ** (-0.5))
    same_doc = (labels_row[:, None] == labels_row[None, :])[None]
    scores = jnp.where(same_doc, scores, -1e+30)
    row_max = lax.optimization_barrier(jnp.max(scores, -1, keepdims=True))
    weights = jnp.exp(scores - row_max)
    weights_low = low(weights / lax.optimization_barrier(jnp.sum(weights, -1, keepdims=True)))
    return jnp.einsum('hqk,khd->qhd', weights_low, values_row, precision=precise)

def denoiser_layer(segment_ids, tokens, time_embed, norm1_gain, norm1_bias, qkv_weight, qv_bias, out_weight, out_bias, norm2_gain, norm2_bias, up_weight, up_bias, down_weight, down_bias):
    row_count = time_embed.shape[0]
    start = (tokens.reshape(row_count, SEQ, D) + time_embed[:, None, :]).reshape(-1, D)
    entry = low(layer_norm(start, norm1_gain, norm1_bias))
    queries = both_round(jnp.dot(entry, qkv_weight[0], precision=precise) + qv_bias[0])
    keys_all = both_round(jnp.dot(entry, qkv_weight[1], precision=precise))
    values_all = both_round(jnp.dot(entry, qkv_weight[2], precision=precise) + qv_bias[1])
    split_shape = (row_count, SEQ, H, HD)
    mixed = lax.map(jax.checkpoint(attend_row), (queries.reshape(split_shape), keys_all.reshape(split_shape), values_all.reshape(split_shape), segment_ids))
    mixed = both_round(mixed.reshape(-1, D))
    branch = low_back(jnp.dot(mixed, out_weight, precision=precise) + out_bias)
    middle = start + branch
    entry2 = low(layer_norm(middle, norm2_gain, norm2_bias))
    hidden_pre = low_back(jnp.dot(entry2, up_weight, precision=precise) + up_bias)
    act_low = low(jax.nn.gelu(hidden_pre, approximate=False))
    return middle + jnp.dot(act_low, down_weight, precision=precise) + down_bias

def reference(tokens, time_embed, segment_ids, norm1_gain, norm1_bias, qkv_weight, qv_bias, out_weight, out_bias, norm2_gain, norm2_bias, up_weight, up_bias, down_weight, down_bias, cotangent):
    floats = [array.astype(jnp.float32) for array in (tokens, time_embed, norm1_gain, norm1_bias, qkv_weight, qv_bias, out_weight, out_bias, norm2_gain, norm2_bias, up_weight, up_bias, down_weight, down_bias)]

    def forward(*values):
        return denoiser_layer(segment_ids, *values)
    result, pullback = jax.vjp(forward, *floats)
    grads = pullback(cotangent.astype(jnp.float32))
    return (result.astype(jnp.bfloat16), grads[0].astype(jnp.bfloat16), grads[1], grads[2], grads[3], grads[4], grads[5], grads[6], grads[7], grads[8], grads[9], grads[10], grads[11], grads[12], grads[13])
```

```python
import functools

import jax
import jax.numpy as jnp
from jax import lax
from jax.experimental import pallas as pl
from jax.experimental.pallas import tpu as pltpu
from jax.sharding import PartitionSpec as P

HD = 64
SUB = 32
CH = 8
MESH = pl.DeviceIdType.MESH
F32 = jnp.float32
BF16 = jnp.bfloat16


def when(cond, fn):
    pl.when(cond)(fn)


def nt(a, b):
    return lax.dot_general(a, b, (((1,), (1,)), ((), ())), preferred_element_type=F32)


def tn(a, b):
    return lax.dot_general(a, b, (((0,), (0,)), ((), ())), preferred_element_type=F32)


def nn(a, b):
    return jnp.dot(a, b, preferred_element_type=F32)


def normed(v):
    centred = v - jnp.mean(v, -1, keepdims=True)
    spread = jnp.mean(centred * centred, -1, keepdims=True)
    scale = lax.rsqrt(spread + 1e-05)
    return centred * scale, scale


def colsum(v):
    return jnp.sum(v, 0, keepdims=True)


def kernel(n_dp, units, names, *refs):
    (tok, tim, seg, n1g, n1b, wqkv, qvb, wout, outb, n2g, n2b, wup, upb, wdn, dnb, cot) = refs[:16]
    out, ig, tg, fa_out, fb_out = refs[16:21]
    R = dict(zip(names, refs[21:]))
    timf, start, entry, q_s, k_s, v_s = (R[s] for s in ("timf", "start", "entry", "q", "k", "v"))
    probs, mixed_s, part, cr, ys, yr = (R[s] for s in ("probs", "mixed", "part", "cr", "ys", "yr"))
    tot, mid, e2, hp, act, gp = (R[s] for s in ("tot", "mid", "e2", "hp", "act", "gp"))
    gact, gmid, gbr, lta, ltb = (R[s] for s in ("gact", "gmid", "gbr", "lta", "ltb"))
    ga, gb, fa, fb = (R[s] for s in ("ga", "gb", "fa", "fb"))

    rows_n, seq = seg.shape
    width = tok.shape[1]
    half = width // 2
    loc = wout.shape[0]
    heads = loc // HD
    ff = wup.shape[1]
    UA, UB = units
    L = n_dp // 2
    D = L // 2
    root = D - 1
    dp = lax.axis_index("dp")
    mp = lax.axis_index("mp")
    core = mp % 2
    x = dp % 2
    z = dp // 2
    to_core = (dp, mp + 1 - 2 * core)
    to_y = (dp, (mp + 2) % 4)
    to_x = (dp + 1 - 2 * x, mp)
    zlo = jnp.maximum(z - 1, 0) * 2 + x
    zhi = jnp.minimum(z + 1, L - 1) * 2 + x

    barrier = pltpu.get_barrier_semaphore()
    for dev in (to_core, to_y, to_x):
        pl.semaphore_signal(barrier, 1, device_id=dev, device_id_type=MESH)
    when(z > 0, lambda: pl.semaphore_signal(barrier, 1, device_id=(zlo, mp), device_id_type=MESH))
    when(z < L - 1, lambda: pl.semaphore_signal(barrier, 1, device_id=(zhi, mp), device_id_type=MESH))

    def sl(r, n=seq):
        return pl.ds(pl.multiple_of(r * n, n), n)

    def sub(r, i):
        return pl.ds(pl.multiple_of(r * seq + i * SUB, SUB), SUB)

    mine = pl.ds(pl.multiple_of(core * half, 128), half)
    other = pl.ds(pl.multiple_of((1 - core) * half, 128), half)

    def remote(src, dst, ssem, rsem, dev):
        return pltpu.make_async_remote_copy(
            src_ref=src, dst_ref=dst, send_sem=ssem, recv_sem=rsem, device_id=dev, device_id_type=MESH
        )

    def core_copy(p, r):
        i = p * rows_n + r
        return remote(part.at[sl(r), other], cr.at[sl(r)], R["cs"].at[i], R["crs"].at[i], to_core)

    def y_copy(p, r):
        i = p * rows_n + r
        return remote(ys.at[sl(r)], yr.at[p % 2, sl(r)], R["yss"].at[i], R["yrs"].at[i], to_y)

    def ag_copy(p, r):
        i = p * rows_n + r
        return remote(tot.at[sl(r), mine], tot.at[sl(r), mine], R["gs"].at[i], R["grs"].at[i], to_core)

    def sum_b(p, r):
        core_copy(p, r).wait()
        ys[sl(r), :] = part[sl(r), mine] + cr[sl(r), :]
        y_copy(p, r).start()

    def sum_c(p, r):
        y_copy(p, r).wait()
        tot[sl(r), mine] = ys[sl(r), :] + yr[p % 2, sl(r), :]
        ag_copy(p, r).start()

    def sum_d(p, r):
        ag_copy(p, r).wait()

    def vec(ref):
        return ref[...]

    small = UA * 4 * CH - 4 * CH

    def small_add(i, v):
        ga[small + i : small + i + 1, :] += v

    lane = lax.broadcasted_iota(jnp.int32, (1, loc), 1)
    masks = [((lane >= h * HD) & (lane < (h + 1) * HD)).astype(F32) for h in range(heads)]

    def by_head(v):
        return jnp.concatenate([v * m.astype(BF16) for m in masks], 0)

    def from_heads(v):
        total = v[:seq] * masks[0]
        for h in range(1, heads):
            total = total + v[h * seq : (h + 1) * seq] * masks[h]
        return total

    def norm1(r):
        @pl.loop(0, seq // SUB)
        def _(i):
            s = sub(r, i)
            v = tok[s, :].astype(F32) + timf[pl.ds(r, 1), :]
            start[s, :] = v
            xhat, _ = normed(v)
            entry[s, :] = (xhat * n1g[...] + n1b[...]).astype(BF16)

    def project(r):
        e = entry[sl(r), :]
        q_s[sl(r), :] = (nn(e, wqkv[0]) + qvb[0:1, :]).astype(BF16)
        k_s[sl(r), :] = nn(e, wqkv[1]).astype(BF16)
        v_s[sl(r), :] = (nn(e, wqkv[2]) + qvb[1:2, :]).astype(BF16)

    def attend(r):
        labels = jnp.broadcast_to(seg[pl.ds(r, 1), :], (seq, seq))
        same = labels == labels.T
        same = jnp.concatenate([same.astype(F32)] * heads, 0) > 0.5
        scores = nt(by_head(q_s[sl(r), :]), k_s[sl(r), :]) * HD ** (-0.5)
        scores = jnp.where(same, scores, -1e30)
        w = jnp.exp(scores - jnp.max(scores, -1, keepdims=True))
        pr = w / jnp.sum(w, -1, keepdims=True)
        probs[sl(r, heads * seq), :] = pr
        mixed = from_heads(nn(pr.astype(BF16), v_s[sl(r), :])).astype(BF16)
        mixed_s[sl(r), :] = mixed
        part[sl(r), :] = nn(mixed, wout[...])
        core_copy(0, r).start()
        lta[ff : ff + loc, sl(r)] = mixed.T

    def grad_act(r):
        c = cot[sl(r), :]
        gact[sl(r), :] = nt(c, wdn[...])
        small_add(0, colsum(c.astype(F32)))

    def feed(r):
        @pl.loop(0, seq // SUB)
        def _(i):
            s = sub(r, i)
            v = start[s, :] + (tot[s, :] + outb[...])
            mid[s, :] = v
            xhat, _ = normed(v)
            e2[s, :] = (xhat * n2g[...] + n2b[...]).astype(BF16)

        hp[...] = nn(e2[sl(r), :], wup[...])

        @pl.loop(0, seq // SUB)
        def _(i):
            s = sub(r, i)
            u = hp[pl.ds(pl.multiple_of(i * SUB, SUB), SUB), :] + upb[...]
            cdf = 0.5 * (1.0 + lax.erf(u * 0.7071067811865476))
            act[s, :] = (u * cdf).astype(BF16)
            slope = cdf + u * (0.3989422804014327 * jnp.exp(-0.5 * u * u))
            g = (gact[s, :] * slope).astype(BF16)
            gp[s, :] = g
            small_add(1, colsum(g.astype(F32)))

        part[sl(r), :] = nt(gp[sl(r), :], wup[...])
        core_copy(1, r).start()
        lta[0:ff, sl(r)] = act[sl(r), :].T
        ltb[0:width, sl(r)] = e2[sl(r), :].T

    def back2(r):
        @pl.loop(0, seq // SUB)
        def _(i):
            s = sub(r, i)
            g = tot[s, :]
            xhat, scale = normed(mid[s, :])
            small_add(2, colsum(g * xhat))
            small_add(3, colsum(g))
            gx = g * n2g[...]
            gm = cot[s, :].astype(F32) + scale * (
                gx - jnp.mean(gx, -1, keepdims=True) - xhat * jnp.mean(gx * xhat, -1, keepdims=True)
            )
            gmid[s, :] = gm
            low = gm.astype(BF16)
            gbr[s, :] = low
            small_add(4, colsum(low.astype(F32)))

        g3 = by_head(nt(gbr[sl(r), :], wout[...]).astype(BF16))
        pr = probs[sl(r, heads * seq), :]
        grad_probs = nt(g3, v_s[sl(r), :])
        inner = jnp.sum(pr * grad_probs, -1, keepdims=True)
        ds = (pr * (grad_probs - inner)).astype(BF16)
        gq = (from_heads(nn(ds, k_s[sl(r), :])) * HD ** (-0.5)).astype(BF16)
        gk = (tn(ds, by_head(q_s[sl(r), :])) * HD ** (-0.5)).astype(BF16)
        gv = tn(pr.astype(BF16), g3).astype(BF16)
        part[sl(r), :] = nt(gq, wqkv[0]) + nt(gk, wqkv[1]) + nt(gv, wqkv[2])
        core_copy(2, r).start()
        lta[ff + loc : ff + 2 * loc, sl(r)] = gq.T
        ltb[width : width + loc, sl(r)] = gk.T
        ltb[width + loc : width + 2 * loc, sl(r)] = gv.T
        ga[small + 7 : small + 8, 0:loc] += colsum(gq.astype(F32))
        ga[small + 7 : small + 8, half : half + loc] += colsum(gv.astype(F32))

    def back1(r):
        tg[pl.ds(r, 1), :] = jnp.zeros((1, width), F32)

        @pl.loop(0, seq // SUB)
        def _(i):
            s = sub(r, i)
            g = tot[s, :]
            xhat, scale = normed(start[s, :])
            small_add(5, colsum(g * xhat))
            small_add(6, colsum(g))
            gy = g * n1g[...]
            gs = gmid[s, :] + scale * (
                gy - jnp.mean(gy, -1, keepdims=True) - xhat * jnp.mean(gy * xhat, -1, keepdims=True)
            )
            ig[s, :] = gs.astype(BF16)
            tg[pl.ds(r, 1), :] += colsum(gs)

    def down(r):
        part[sl(r), :] = nn(act[sl(r), :], wdn[...])
        core_copy(3, r).start()

    def finish(r):
        @pl.loop(0, seq // SUB)
        def _(i):
            s = sub(r, i)
            out[s, :] = (mid[s, :] + (tot[s, :] + dnb[...])).astype(BF16)

    blk = loc

    def weight_grads(j):
        s = pl.ds(pl.multiple_of(j * blk, blk), blk)
        late = ff // blk

        def a_early():
            ga[s, :] = nn(lta[s, :], cot[...])
            gb[s, :] = nn(ltb[s, :], gp[...])

        def a_out():
            ga[s, :] = nn(lta[s, :], gbr[...])

        def a_q():
            ga[s, :] = nn(lta[s, :], entry[...])

        def b_late():
            gb[s, :] = nn(ltb[s, :], entry[...])

        when(j < late, a_early)
        when(j == late, a_out)
        when(j == late + 1, a_q)
        when(j >= late, b_late)

    def ok(u, n):
        return (u >= 0) & (u < n)

    def a_own(u, d):
        return pl.ds(pl.multiple_of(u * 4 * CH + x * 2 * CH + d * CH, CH), CH)

    def a_slot(u):
        return pl.ds(pl.multiple_of(u * CH, CH), CH)

    def b_own(u, d):
        return pl.ds(pl.multiple_of(u * 4 * CH + d * 2 * CH, CH), 2 * CH)

    def b_slot(u):
        return pl.ds(pl.multiple_of(u * 2 * CH, CH), 2 * CH)

    def x_first(u):
        src = pl.ds(pl.multiple_of(u * 4 * CH + (1 - x) * 2 * CH, CH), 2 * CH)
        return remote(ga.at[src], R["xrb"].at[b_slot(u)], R["xs"].at[u], R["xr"].at[u], to_x)

    ways = []
    for d in (0, 1):
        w = z if d == 0 else L - 1 - z
        up = (zhi if d == 0 else zlo, mp)
        dn = (zlo if d == 0 else zhi, mp)
        ways.append((d, w, up, dn))

    def streams(kind, d, up, dn):
        if kind == "a":
            g, f, lo, hi, own, slot = ga, fa, R["arl"], R["arh"], a_own, a_slot
            s, lr, hr, bu, bd, br = (R[t] for t in ("ars", "arlr", "arhr", "abu", "abd", "abr"))
        else:
            g, f, lo, hi, own, slot = gb, fb, R["brl"], R["brh"], b_own, b_slot
            s, lr, hr, bu, bd, br = (R[t] for t in ("brs", "brlr", "brhr", "bbu", "bbd", "bbr"))

        def send_up(u):
            return remote(g.at[own(u, d)], lo.at[d, slot(u)], s.at[d, u], lr.at[d, u], up)

        def send_dn(u):
            return remote(g.at[own(u, d)], hi.at[d, slot(u)], s.at[d, u], hr.at[d, u], dn)

        def bcast_up(u):
            return remote(f.at[own(u, d)], f.at[own(u, d)], bu.at[d, u], br.at[d, u], up)

        def bcast_dn(u):
            return remote(f.at[own(u, d)], f.at[own(u, d)], bd.at[d, u], br.at[d, u], dn)

        return g, f, lo, hi, own, slot, send_up, send_dn, bcast_up, bcast_dn

    def x_last(u, d):
        s = a_own(u, d)
        return remote(fa.at[s], fa.at[s], R["xgs"].at[d, u], R["xgr"].at[d, u], to_x)

    def x_last_in(u, d):
        s = pl.ds(pl.multiple_of(u * 4 * CH + (1 - x) * 2 * CH + d * CH, CH), CH)
        return remote(fa.at[s], fa.at[s], R["xgs"].at[d, u], R["xgr"].at[d, u], to_x)

    def b_x(u, d):
        return remote(gb.at[b_own(u, d)], R["bxb"].at[d, b_slot(u)], R["bxs"].at[d, u], R["bxr"].at[d, u], to_x)

    def reduce_step(kind, d, w, up, dn, u):
        g, f, lo, hi, own, slot, send_up, send_dn, bcast_up, bcast_dn = streams(kind, d, up, dn)

        def from_low():
            send_up(u).wait_recv()
            g[own(u, d), :] += lo[d, slot(u), :]

        def from_high():
            send_dn(u).wait_recv()
            g[own(u, d), :] += hi[d, slot(u), :]

        when((w > 0) & (w <= root), from_low)
        when((w < L - 1) & (w >= root), from_high)
        when(w < root, lambda: send_up(u).start())
        when(w > root, lambda: send_dn(u).start())

    def root_step(kind, d, w, up, dn, u):
        g, f, lo, hi, own, slot, send_up, send_dn, bcast_up, bcast_dn = streams(kind, d, up, dn)
        if kind == "a":
            f[own(u, d), :] = g[own(u, d), :]
        else:
            b_x(u, d).wait_recv()
            f[own(u, d), :] = g[own(u, d), :] + R["bxb"][d, slot(u), :]
        bcast_up(u).start()
        when(w > 0, lambda: bcast_dn(u).start())
        if kind == "a":
            x_last(u, d).start()

    def spread_step(kind, d, w, up, dn, u):
        g, f, lo, hi, own, slot, send_up, send_dn, bcast_up, bcast_dn = streams(kind, d, up, dn)
        bcast_up(u).wait_recv()
        when((w > root) & (w < L - 1), lambda: bcast_up(u).start())
        when((w < root) & (w > 0), lambda: bcast_dn(u).start())
        if kind == "a":
            x_last(u, d).start()

    def dp_tick(t):
        when(t < UA, lambda: x_first(t).start())

        def x_add():
            u = t - 1
            x_first(u).wait_recv()
            s = pl.ds(pl.multiple_of(u * 4 * CH + x * 2 * CH, CH), 2 * CH)
            ga[s, :] += R["xrb"][b_slot(u), :]

        when(ok(t - 1, UA), x_add)
        for kind, n, first, gap in (("b", UB, 0, 1), ("a", UA, 1, 0)):
            for d, w, up, dn in ways:
                far = jnp.where(w <= root, w + 1, L - 1 - w)
                dist = jnp.abs(w - root)
                u = t - first - far
                when(ok(u, n), functools.partial(reduce_step, kind, d, w, up, dn, u))
                if kind == "b":
                    when(ok(u, n) & (w == root), lambda u=u, d=d: b_x(u, d).start())
                v = t - first - D - gap
                when(ok(v, n) & (w == root), functools.partial(root_step, kind, d, w, up, dn, v))
                v = t - first - D - gap - dist
                when(ok(v, n) & (w != root), functools.partial(spread_step, kind, d, w, up, dn, v))

    def dp_drain():
        @pl.loop(0, UA)
        def _(u):
            x_first(u).wait_send()
            for d, w, up, dn in ways:
                x_last(u, d).wait_send()
                x_last_in(u, d).wait_recv()

        for kind, n in (("a", UA), ("b", UB)):

            @pl.loop(0, n)
            def _(u):
                for d, w, up, dn in ways:
                    fs = streams(kind, d, up, dn)
                    when(w != root, lambda: fs[6](u).wait_send())
                    when((w >= root) & (w < L - 1), lambda: fs[8](u).wait_send())
                    when((w <= root) & (w > 0), lambda: fs[9](u).wait_send())
                    if kind == "b":
                        when(w == root, lambda: b_x(u, d).wait_send())

    timf[...] = tim[...].astype(F32)
    ga[small : small + 4 * CH, :] = jnp.zeros((4 * CH, width), F32)
    pl.loop(0, rows_n)(norm1)
    pl.loop(0, rows_n)(project)
    pl.semaphore_wait(barrier, 3 + jnp.minimum(z, 1) + jnp.minimum(L - 1 - z, 1))

    @pl.loop(0, rows_n)
    def _(r):
        attend(r)
        when(r > 0, lambda: sum_b(0, r - 1))

    sum_b(0, rows_n - 1)

    @pl.loop(0, rows_n)
    def _(r):
        grad_act(r)
        sum_c(0, r)
        sum_d(0, r)
        feed(r)
        sum_b(1, r)

    weight_grads(0)

    ticks = max(UA, UB) + 2 * D + 1
    per = blk // (4 * CH)
    blocks = (ff + 2 * loc) // blk

    @pl.loop(0, ticks)
    def _(t):
        dp_tick(t)

        def at(first, step, fn):
            r = (t - first) // step
            when((t >= first) & ((t - first) % step == 0) & (r < rows_n), lambda: fn(r))

        at(0, 2, lambda r: sum_c(1, r))

        def second(r):
            sum_d(1, r)
            back2(r)

        at(1, 2, second)
        at(2, 2, lambda r: sum_b(2, r))
        at(5, 2, lambda r: sum_c(2, r))

        def third(r):
            sum_d(2, r)
            back1(r)

        at(6, 2, third)
        at(9, 2, down)
        at(10, 2, lambda r: sum_b(3, r))
        at(13, 2, lambda r: sum_c(3, r))

        def fourth(r):
            sum_d(3, r)
            finish(r)

        at(14, 2, fourth)
        when((t % per == per - 2) & (t // per + 1 < blocks), lambda: weight_grads(t // per + 1))

    dp_drain()
    copies = [
        pltpu.make_async_copy(fa, fa_out, R["fin"].at[0]),
        pltpu.make_async_copy(fb, fb_out, R["fin"].at[1]),
    ]
    for copy in copies:
        copy.start()
    for copy in copies:
        copy.wait()


def shards(n_dp, *args):
    (tok, tim, seg, n1g, n1b, wqkv, qvb, wout, outb, n2g, n2b, wup, upb, wdn, dnb, cot) = args
    tokens, width = tok.shape
    rows_n, seq = seg.shape
    loc, ff = wout.shape[0], wup.shape[1]
    heads = loc // HD
    half = width // 2
    big = ff + 2 * loc
    UB = big // (4 * CH)
    UA = UB + 1
    vm = pltpu.VMEM
    dma = pltpu.SemaphoreType.DMA
    dp_sem = lambda n: dma((2, n))
    scratch = dict(
        timf=vm((rows_n, width), F32),
        start=vm((tokens, width), F32),
        entry=vm((tokens, width), BF16),
        q=vm((tokens, loc), BF16),
        k=vm((tokens, loc), BF16),
        v=vm((tokens, loc), BF16),
        probs=vm((heads * tokens, seq), F32),
        mixed=vm((tokens, loc), BF16),
        part=vm((tokens, width), F32),
        cr=vm((tokens, half), F32),
        ys=vm((tokens, half), F32),
        yr=vm((2, tokens, half), F32),
        tot=vm((tokens, width), F32),
        mid=vm((tokens, width), F32),
        e2=vm((tokens, width), BF16),
        hp=vm((seq, ff), F32),
        act=vm((tokens, ff), BF16),
        gp=vm((tokens, ff), BF16),
        gact=vm((tokens, ff), F32),
        gmid=vm((tokens, width), F32),
        gbr=vm((tokens, width), BF16),
        lta=vm((big, tokens), BF16),
        ltb=vm((big, tokens), BF16),
        ga=vm((UA * 4 * CH, width), F32),
        gb=vm((UB * 4 * CH, width), F32),
        fa=vm((UA * 4 * CH, width), F32),
        fb=vm((UB * 4 * CH, width), F32),
        xrb=vm((UA * 2 * CH, width), F32),
        arl=vm((2, UA * CH, width), F32),
        arh=vm((2, UA * CH, width), F32),
        brl=vm((2, UB * 2 * CH, width), F32),
        brh=vm((2, UB * 2 * CH, width), F32),
        bxb=vm((2, UB * 2 * CH, width), F32),
        **{s: dma((4 * rows_n,)) for s in ("cs", "crs", "yss", "yrs", "gs", "grs")},
        fin=dma((2,)),
        **{s: dma((UA,)) for s in ("xs", "xr")},
        **{s: dp_sem(UA) for s in ("ars", "arlr", "arhr", "abu", "abd", "abr", "xgs", "xgr")},
        **{s: dp_sem(UB) for s in ("brs", "brlr", "brhr", "bxs", "bxr", "bbu", "bbd", "bbr")},
    )
    row = lambda v: v.reshape(1, -1)
    any_spec = pl.BlockSpec(memory_space=pl.ANY)
    vm_spec = pl.BlockSpec(memory_space=pltpu.VMEM)
    out, ig, tg, fa, fb = pl.pallas_call(
        functools.partial(kernel, n_dp, (UA, UB), tuple(scratch)),
        out_shape=(
            jax.ShapeDtypeStruct((tokens, width), BF16),
            jax.ShapeDtypeStruct((tokens, width), BF16),
            jax.ShapeDtypeStruct((rows_n, width), F32),
            jax.ShapeDtypeStruct((UA * 4 * CH, width), F32),
            jax.ShapeDtypeStruct((UB * 4 * CH, width), F32),
        ),
        in_specs=[vm_spec] * 16,
        out_specs=(vm_spec, vm_spec, vm_spec, any_spec, any_spec),
        scratch_shapes=list(scratch.values()),
        compiler_params=pltpu.CompilerParams(
            collective_id=0, has_side_effects=True, vmem_limit_bytes=63 * 2**20
        ),
        cost_estimate=pl.CostEstimate(flops=6 * 10**9, bytes_accessed=20 * 10**6, transcendentals=0),
    )(
        tok, tim, seg, row(n1g), row(n1b), wqkv, qvb, wout, row(outb), row(n2g), row(n2b), wup, row(upb), wdn,
        row(dnb), cot,
    )
    sm = fa[big : big + 8]
    qkv_grad = jnp.stack([fa[ff + loc : big].T, fb[width : width + loc].T, fb[width + loc :].T])
    return (
        out,
        ig,
        tg,
        sm[5],
        sm[6],
        qkv_grad,
        jnp.stack([sm[7, :loc], sm[7, half : half + loc]]),
        fa[ff : ff + loc],
        sm[4],
        sm[2],
        sm[3],
        fb[:width],
        sm[1],
        fa[:ff],
        sm[0],
    )


def solution(mesh):
    placed = (
        P("dp", None),
        P("dp", None),
        P("dp", None),
        P(),
        P(),
        P(None, None, "mp"),
        P(None, "mp"),
        P("mp", None),
        P(),
        P(),
        P(),
        P(None, "mp"),
        P("mp"),
        P("mp", None),
        P(),
        P("dp", None),
    )
    return jax.shard_map(
        functools.partial(shards, mesh.shape["dp"]),
        mesh=mesh,
        in_specs=placed,
        out_specs=(
            P("dp", None),
            P("dp", None),
            P("dp", None),
            P(),
            P(),
            P(None, None, "mp"),
            P(None, "mp"),
            P("mp", None),
            P(),
            P(),
            P(),
            P(None, "mp"),
            P("mp"),
            P("mp", None),
            P(),
        ),
        check_vma=False,
    )
```

```python
import functools

import jax
import jax.numpy as jnp
from jax import lax
from jax.experimental import pallas as pl
from jax.experimental.pallas import tpu as pltpu
from jax.sharding import PartitionSpec as P

HD = 64
SUB = 32
CH = 8
SENDS = 3
MESH = pl.DeviceIdType.MESH
F32 = jnp.float32
BF16 = jnp.bfloat16


def when(cond, fn):
    pl.when(cond)(fn)


def nt(a, b):
    return lax.dot_general(a, b, (((1,), (1,)), ((), ())), preferred_element_type=F32)


def tn(a, b):
    return lax.dot_general(a, b, (((0,), (0,)), ((), ())), preferred_element_type=F32)


def nn(a, b):
    return jnp.dot(a, b, preferred_element_type=F32)


def normed(v):
    centred = v - jnp.mean(v, -1, keepdims=True)
    spread = jnp.mean(centred * centred, -1, keepdims=True)
    scale = lax.rsqrt(spread + 1e-05)
    return centred * scale, scale


def colsum(v):
    return jnp.sum(v, 0, keepdims=True)


def kernel(n_dp, units, names, *refs):
    (tok, tim, seg, _, _, wqkv, qvb, wout, _, _, _, wup, _, wdn, _, cot) = refs[:16]
    out, ig, tg, fa_out, fb_out = refs[16:21]
    R = dict(zip(names, refs[21:]))
    flat = [refs[i] for i in (3, 4, 8, 9, 10, 12, 14)]
    n1g, n1b, outb, n2g, n2b, upb, dnb = (R["vecs"].at[pl.ds(i, 1)] for i in range(7))
    timf, start, entry, q_s, k_s, v_s = (R[s] for s in ("timf", "start", "entry", "q", "k", "v"))
    probs, mixed_s, part, cr, ys, yr = (R[s] for s in ("probs", "mixed", "part", "cr", "ys", "yr"))
    tot, mid, e2, hp, act, gp = (R[s] for s in ("tot", "mid", "e2", "hp", "act", "gp"))
    gact, gmid, gbr, lta, ltb = (R[s] for s in ("gact", "gmid", "gbr", "lta", "ltb"))
    ga, gb, fa, fb = (R[s] for s in ("ga", "gb", "fa", "fb"))

    rows_n, seq = seg.shape
    width = tok.shape[1]
    half = width // 2
    loc = wout.shape[0]
    heads = loc // HD
    ff = wup.shape[1]
    UA, UB = units
    L = n_dp // 2
    D = L // 2
    root = D - 1
    dp = lax.axis_index("dp")
    mp = lax.axis_index("mp")
    core = mp % 2
    x = dp % 2
    z = dp // 2
    to_core = (dp, mp + 1 - 2 * core)
    to_y = (dp, (mp + 2) % 4)
    to_x = (dp + 1 - 2 * x, mp)
    zlo = jnp.maximum(z - 1, 0) * 2 + x
    zhi = jnp.minimum(z + 1, L - 1) * 2 + x

    barrier = pltpu.get_barrier_semaphore()
    for dev in (to_core, to_y, to_x):
        pl.semaphore_signal(barrier, 1, device_id=dev, device_id_type=MESH)
    when(z > 0, lambda: pl.semaphore_signal(barrier, 1, device_id=(zlo, mp), device_id_type=MESH))
    when(z < L - 1, lambda: pl.semaphore_signal(barrier, 1, device_id=(zhi, mp), device_id_type=MESH))

    def sl(r, n=seq):
        return pl.ds(pl.multiple_of(r * n, n), n)

    def sub(r, i):
        return pl.ds(pl.multiple_of(r * seq + i * SUB, SUB), SUB)

    mine = pl.ds(pl.multiple_of(core * half, 128), half)
    other = pl.ds(pl.multiple_of((1 - core) * half, 128), half)

    def remote(src, dst, ssem, rsem, dev):
        return pltpu.make_async_remote_copy(
            src_ref=src, dst_ref=dst, send_sem=ssem, recv_sem=rsem, device_id=dev, device_id_type=MESH
        )

    def core_copy(p, r):
        return remote(part.at[sl(r), other], cr.at[sl(r)], R["cs"].at[r], R["crs"].at[r], to_core)

    def y_copy(p, r):
        return remote(ys.at[sl(r)], yr.at[p % 2, sl(r)], R["yss"].at[r], R["yrs"].at[p % 2, r], to_y)

    def ag_copy(p, r):
        return remote(tot.at[sl(r), mine], tot.at[sl(r), mine], R["gs"].at[r], R["grs"].at[r], to_core)

    def sum_b(p, r):
        core_copy(p, r).wait()
        ys[sl(r), :] = part[sl(r), mine] + cr[sl(r), :]
        y_copy(p, r).start()

    def sum_c(p, r):
        y_copy(p, r).wait()
        tot[sl(r), mine] = ys[sl(r), :] + yr[p % 2, sl(r), :]
        ag_copy(p, r).start()

    def sum_d(p, r):
        ag_copy(p, r).wait()

    def vec(ref):
        return ref[...]

    small = UA * 4 * CH - 4 * CH

    def small_add(i, v):
        ga[small + i : small + i + 1, :] += v

    lane = lax.broadcasted_iota(jnp.int32, (1, loc), 1)
    masks = [((lane >= h * HD) & (lane < (h + 1) * HD)).astype(F32) for h in range(heads)]

    def by_head(v):
        return jnp.concatenate([v * m.astype(BF16) for m in masks], 0)

    def from_heads(v):
        total = v[:seq] * masks[0]
        for h in range(1, heads):
            total = total + v[h * seq : (h + 1) * seq] * masks[h]
        return total

    def norm1(r):
        @pl.loop(0, seq // SUB)
        def _(i):
            s = sub(r, i)
            v = tok[s, :].astype(F32) + timf[pl.ds(r, 1), :]
            start[s, :] = v
            xhat, _ = normed(v)
            entry[s, :] = (xhat * n1g[...] + n1b[...]).astype(BF16)

    def project(r):
        e = entry[sl(r), :]
        q_s[sl(r), :] = (nt(e, wqkv[0]) + qvb[0:1, :]).astype(BF16)
        k_s[sl(r), :] = nt(e, wqkv[1]).astype(BF16)
        v_s[sl(r), :] = (nt(e, wqkv[2]) + qvb[1:2, :]).astype(BF16)

    def attend(r):
        labels = jnp.broadcast_to(seg[pl.ds(r, 1), :], (seq, seq))
        same = labels == labels.T
        same = jnp.concatenate([same.astype(F32)] * heads, 0) > 0.5
        scores = nt(by_head(q_s[sl(r), :]), k_s[sl(r), :]) * HD ** (-0.5)
        scores = jnp.where(same, scores, -1e30)
        w = jnp.exp(scores - jnp.max(scores, -1, keepdims=True))
        pr = w / jnp.sum(w, -1, keepdims=True)
        probs[sl(r, heads * seq), :] = pr
        mixed = from_heads(nn(pr.astype(BF16), v_s[sl(r), :])).astype(BF16)
        mixed_s[sl(r), :] = mixed
        part[sl(r), :] = nn(mixed, wout[...])
        core_copy(0, r).start()
        lta[ff : ff + loc, sl(r)] = mixed.T

    def grad_act(r):
        c = cot[sl(r), :]
        gact[sl(r), :] = nt(c, wdn[...])
        small_add(0, colsum(c.astype(F32)))

    def feed(r):
        @pl.loop(0, seq // SUB)
        def _(i):
            s = sub(r, i)
            v = start[s, :] + (tot[s, :] + outb[...])
            mid[s, :] = v
            xhat, _ = normed(v)
            e2[s, :] = (xhat * n2g[...] + n2b[...]).astype(BF16)

        hp[...] = nn(e2[sl(r), :], wup[...])

        @pl.loop(0, seq // SUB)
        def _(i):
            s = sub(r, i)
            u = hp[pl.ds(pl.multiple_of(i * SUB, SUB), SUB), :] + upb[...]
            cdf = 0.5 * (1.0 + lax.erf(u * 0.7071067811865476))
            act[s, :] = (u * cdf).astype(BF16)
            slope = cdf + u * (0.3989422804014327 * jnp.exp(-0.5 * u * u))
            g = (gact[s, :] * slope).astype(BF16)
            gp[s, :] = g
            small_add(1, colsum(g.astype(F32)))

        part[sl(r), :] = nt(gp[sl(r), :], wup[...])
        core_copy(1, r).start()
        lta[0:ff, sl(r)] = act[sl(r), :].T
        ltb[0:width, sl(r)] = e2[sl(r), :].T

    def back2(r):
        @pl.loop(0, seq // SUB)
        def _(i):
            s = sub(r, i)
            g = tot[s, :]
            xhat, scale = normed(mid[s, :])
            small_add(2, colsum(g * xhat))
            small_add(3, colsum(g))
            gx = g * n2g[...]
            gm = cot[s, :].astype(F32) + scale * (
                gx - jnp.mean(gx, -1, keepdims=True) - xhat * jnp.mean(gx * xhat, -1, keepdims=True)
            )
            gmid[s, :] = gm
            low = gm.astype(BF16)
            gbr[s, :] = low
            small_add(4, colsum(low.astype(F32)))

        g3 = by_head(nt(gbr[sl(r), :], wout[...]).astype(BF16))
        pr = probs[sl(r, heads * seq), :]
        grad_probs = nt(g3, v_s[sl(r), :])
        inner = jnp.sum(pr * grad_probs, -1, keepdims=True)
        ds = (pr * (grad_probs - inner)).astype(BF16)
        gq = (from_heads(nn(ds, k_s[sl(r), :])) * HD ** (-0.5)).astype(BF16)
        gk = (tn(ds, by_head(q_s[sl(r), :])) * HD ** (-0.5)).astype(BF16)
        gv = tn(pr.astype(BF16), g3).astype(BF16)
        part[sl(r), :] = nn(gq, wqkv[0]) + nn(gk, wqkv[1]) + nn(gv, wqkv[2])
        core_copy(2, r).start()
        lta[ff + loc : ff + 2 * loc, sl(r)] = gq.T
        ltb[width : width + loc, sl(r)] = gk.T
        ltb[width + loc : width + 2 * loc, sl(r)] = gv.T
        ga[small + 7 : small + 8, 0:loc] += colsum(gq.astype(F32))
        ga[small + 7 : small + 8, half : half + loc] += colsum(gv.astype(F32))

    def back1(r):
        tg[pl.ds(r, 1), :] = jnp.zeros((1, width), F32)

        @pl.loop(0, seq // SUB)
        def _(i):
            s = sub(r, i)
            g = tot[s, :]
            xhat, scale = normed(start[s, :])
            small_add(5, colsum(g * xhat))
            small_add(6, colsum(g))
            gy = g * n1g[...]
            gs = gmid[s, :] + scale * (
                gy - jnp.mean(gy, -1, keepdims=True) - xhat * jnp.mean(gy * xhat, -1, keepdims=True)
            )
            ig[s, :] = gs.astype(BF16)
            tg[pl.ds(r, 1), :] += colsum(gs)

    def down(r):
        part[sl(r), :] = nn(act[sl(r), :], wdn[...])
        core_copy(3, r).start()

    def finish(r):
        @pl.loop(0, seq // SUB)
        def _(i):
            s = sub(r, i)
            out[s, :] = (mid[s, :] + (tot[s, :] + dnb[...])).astype(BF16)

    blk = loc

    def weight_grads(j):
        s = pl.ds(pl.multiple_of(j * blk, blk), blk)
        late = ff // blk

        def a_early():
            ga[s, :] = nn(lta[s, :], cot[...])
            gb[s, :] = nn(ltb[s, :], gp[...])

        def a_out():
            ga[s, :] = nn(lta[s, :], gbr[...])

        def a_q():
            ga[s, :] = nn(lta[s, :], entry[...])

        def b_late():
            gb[s, :] = nn(ltb[s, :], entry[...])

        when(j < late, a_early)
        when(j == late, a_out)
        when(j == late + 1, a_q)
        when(j >= late, b_late)

    def ok(u, n):
        return (u >= 0) & (u < n)

    def a_own(u, d):
        return pl.ds(pl.multiple_of(u * 4 * CH + x * 2 * CH + d * CH, CH), CH)

    W = R["xr"].shape[0]

    def a_slot(u):
        return pl.ds(pl.multiple_of(u % W * CH, CH), CH)

    def b_own(u, d):
        return pl.ds(pl.multiple_of(u * 4 * CH + d * 2 * CH, CH), 2 * CH)

    def b_slot(u):
        return pl.ds(pl.multiple_of(u % W * 2 * CH, CH), 2 * CH)

    def go(copy, u):
        when(u >= SENDS, lambda: copy(u - SENDS).wait_send())
        copy(u).start()

    def end(copy, n):
        for u in range(n - min(SENDS, n), n):
            copy(u).wait_send()

    def x_first(u):
        src = pl.ds(pl.multiple_of(u * 4 * CH + (1 - x) * 2 * CH, CH), 2 * CH)
        return remote(ga.at[src], R["xrb"].at[b_slot(u)], R["xs"].at[u % SENDS], R["xr"].at[u % W], to_x)

    ways = []
    for d in (0, 1):
        w = z if d == 0 else L - 1 - z
        up = (zhi if d == 0 else zlo, mp)
        dn = (zlo if d == 0 else zhi, mp)
        ways.append((d, w, up, dn))

    def streams(kind, d, up, dn):
        if kind == "a":
            g, f, lo, hi, own, slot = ga, fa, R["arl"], R["arh"], a_own, a_slot
            s, rr, bu, bd, br = (R[t] for t in ("ars", "arr", "abu", "abd", "abr"))
        else:
            g, f, lo, hi, own, slot = gb, fb, R["brl"], R["brh"], b_own, b_slot
            s, rr, bu, bd, br = (R[t] for t in ("brs", "brr", "bbu", "bbd", "bbr"))

        def send_up(u):
            return remote(g.at[own(u, d)], lo.at[d, slot(u)], s.at[d, u % SENDS], rr.at[d, u % W], up)

        def send_up_root(u):
            return remote(g.at[own(u, d)], lo.at[d, slot(u)], s.at[d, u % SENDS], br.at[d, u % W], up)

        def send_dn(u):
            return remote(g.at[own(u, d)], hi.at[d, slot(u)], s.at[d, u % SENDS], rr.at[d, u % W], dn)

        def bcast_up(u):
            return remote(f.at[own(u, d)], f.at[own(u, d)], bu.at[d, u % SENDS], br.at[d, u % W], up)

        def bcast_dn(u):
            return remote(f.at[own(u, d)], f.at[own(u, d)], bd.at[d, u % SENDS], br.at[d, u % W], dn)

        return g, f, lo, hi, own, slot, send_up, send_up_root, send_dn, bcast_up, bcast_dn

    def x_last(u, d):
        s = a_own(u, d)
        return remote(fa.at[s], fa.at[s], R["xgs"].at[d, u % SENDS], R["xgr"].at[d, u % W], to_x)

    def b_x(u, d):
        return remote(
            gb.at[b_own(u, d)], R["bxb"].at[d, b_slot(u)], R["bxs"].at[d, u % SENDS], R["bxr"].at[d, u % W], to_x
        )

    def reduce_step(kind, d, w, up, dn, u):
        g, f, lo, hi, own, slot, send_up, send_up_root, send_dn, bcast_up, bcast_dn = streams(kind, d, up, dn)

        def from_low():
            when(w < root, lambda: send_up(u).wait_recv())
            when(w == root, lambda: send_up_root(u).wait_recv())
            g[own(u, d), :] += lo[d, slot(u), :]

        def from_high():
            send_dn(u).wait_recv()
            g[own(u, d), :] += hi[d, slot(u), :]

        when((w > 0) & (w <= root), from_low)
        when((w < L - 1) & (w >= root), from_high)
        when(w < root - 1, lambda: go(send_up, u))
        when(w == root - 1, lambda: go(send_up_root, u))
        when(w > root, lambda: go(send_dn, u))

    def root_step(kind, d, w, up, dn, u):
        g, f, lo, hi, own, slot, send_up, send_up_root, send_dn, bcast_up, bcast_dn = streams(kind, d, up, dn)
        if kind == "a":
            f[own(u, d), :] = g[own(u, d), :]
        else:
            b_x(u, d).wait_recv()
            f[own(u, d), :] = g[own(u, d), :] + R["bxb"][d, slot(u), :]
        go(bcast_up, u)
        when(w > 0, lambda: go(bcast_dn, u))
        if kind == "a":
            go(lambda i: x_last(i, d), u)

    def spread_step(kind, d, w, up, dn, u):
        g, f, lo, hi, own, slot, send_up, send_up_root, send_dn, bcast_up, bcast_dn = streams(kind, d, up, dn)
        bcast_up(u).wait_recv()
        when((w > root) & (w < L - 1), lambda: go(bcast_up, u))
        when((w < root) & (w > 0), lambda: go(bcast_dn, u))
        if kind == "a":
            go(lambda i: x_last(i, d), u)

    def dp_tick(t):
        when(t < UA, lambda: go(x_first, t))

        def x_add():
            u = t - 1
            x_first(u).wait_recv()
            s = pl.ds(pl.multiple_of(u * 4 * CH + x * 2 * CH, CH), 2 * CH)
            ga[s, :] += R["xrb"][b_slot(u), :]

        when(ok(t - 1, UA), x_add)
        for kind, n, first, gap in (("b", UB, 0, 1), ("a", UA, 1, 0)):
            for d, w, up, dn in ways:
                far = jnp.where(w <= root, w + 1, L - 1 - w)
                dist = jnp.abs(w - root)
                u = t - first - far
                when(ok(u, n), functools.partial(reduce_step, kind, d, w, up, dn, u))
                if kind == "b":
                    when(ok(u, n) & (w == root), lambda u=u, d=d: go(lambda i: b_x(i, d), u))
                v = t - first - D - gap
                when(ok(v, n) & (w == root), functools.partial(root_step, kind, d, w, up, dn, v))
                v = v - dist
                when(ok(v, n) & (w != root), functools.partial(spread_step, kind, d, w, up, dn, v))
                if kind == "a":
                    v = v - 1
                    when(ok(v, n), lambda v=v, d=d: x_last(v, d).wait_recv())

    def dp_drain():
        end(x_first, UA)
        for kind, n in (("a", UA), ("b", UB)):
            for d, w, up, dn in ways:
                fs = streams(kind, d, up, dn)
                when(w < root - 1, lambda: end(fs[6], n))
                when(w == root - 1, lambda: end(fs[7], n))
                when(w > root, lambda: end(fs[8], n))
                when((w >= root) & (w < L - 1), lambda: end(fs[9], n))
                when((w <= root) & (w > 0), lambda: end(fs[10], n))
                if kind == "a":
                    end(lambda i: x_last(i, d), n)
                else:
                    when(w == root, lambda: end(lambda i: b_x(i, d), n))

    for i, ref in enumerate(flat):
        R["vecs"][i : i + 1, :] = ref[...][None, :]
    timf[...] = tim[...].astype(F32)
    ga[small : small + 4 * CH, :] = jnp.zeros((4 * CH, width), F32)
    pl.loop(0, rows_n)(norm1)
    pl.loop(0, rows_n)(project)
    pl.semaphore_wait(barrier, 3 + jnp.minimum(z, 1) + jnp.minimum(L - 1 - z, 1))

    @pl.loop(0, rows_n)
    def _(r):
        attend(r)
        when(r > 0, lambda: sum_b(0, r - 1))

    sum_b(0, rows_n - 1)

    @pl.loop(0, rows_n)
    def _(r):
        grad_act(r)
        sum_c(0, r)
        sum_d(0, r)
        feed(r)
        sum_b(1, r)

    weight_grads(0)

    ticks = max(UA, UB) + 2 * D + 2
    per = blk // (4 * CH)
    blocks = (ff + 2 * loc) // blk

    @pl.loop(0, ticks)
    def _(t):
        dp_tick(t)

        def at(first, step, fn):
            r = (t - first) // step
            when((t >= first) & ((t - first) % step == 0) & (r < rows_n), lambda: fn(r))

        at(0, 2, lambda r: sum_c(1, r))

        def second(r):
            sum_d(1, r)
            back2(r)

        at(1, 2, second)
        at(2, 2, lambda r: sum_b(2, r))
        at(5, 2, lambda r: sum_c(2, r))

        def third(r):
            sum_d(2, r)
            back1(r)

        at(6, 2, third)
        at(9, 2, down)
        at(10, 2, lambda r: sum_b(3, r))
        at(13, 2, lambda r: sum_c(3, r))

        def fourth(r):
            sum_d(3, r)
            finish(r)

        at(14, 2, fourth)
        when((t % per == per - 2) & (t // per + 1 < blocks), lambda: weight_grads(t // per + 1))

    dp_drain()
    copies = [
        pltpu.make_async_copy(fa, fa_out, R["fin"].at[0]),
        pltpu.make_async_copy(fb, fb_out, R["fin"].at[1]),
    ]
    for copy in copies:
        copy.start()
    for copy in copies:
        copy.wait()


def shards(n_dp, *args):
    (tok, tim, seg, n1g, n1b, wqkv, qvb, wout, outb, n2g, n2b, wup, upb, wdn, dnb, cot) = args
    tokens, width = tok.shape
    rows_n, seq = seg.shape
    loc, ff = wout.shape[0], wup.shape[1]
    heads = loc // HD
    half = width // 2
    big = ff + 2 * loc
    UB = big // (4 * CH)
    UA = UB + 1
    vm = pltpu.VMEM
    dma = pltpu.SemaphoreType.DMA
    W = n_dp // 2 + 4
    scratch = dict(
        vecs=vm((8, width), F32),
        timf=vm((rows_n, width), F32),
        start=vm((tokens, width), F32),
        entry=vm((tokens, width), BF16),
        q=vm((tokens, loc), BF16),
        k=vm((tokens, loc), BF16),
        v=vm((tokens, loc), BF16),
        probs=vm((heads * tokens, seq), F32),
        mixed=vm((tokens, loc), BF16),
        part=vm((tokens, width), F32),
        cr=vm((tokens, half), F32),
        ys=vm((tokens, half), F32),
        yr=vm((2, tokens, half), F32),
        tot=vm((tokens, width), F32),
        mid=vm((tokens, width), F32),
        e2=vm((tokens, width), BF16),
        hp=vm((seq, ff), F32),
        act=vm((tokens, ff), BF16),
        gp=vm((tokens, ff), BF16),
        gact=vm((tokens, ff), F32),
        gmid=vm((tokens, width), F32),
        gbr=vm((tokens, width), BF16),
        lta=vm((big, tokens), BF16),
        ltb=vm((big, tokens), BF16),
        ga=vm((UA * 4 * CH, width), F32),
        gb=vm((UB * 4 * CH, width), F32),
        fa=vm((UA * 4 * CH, width), F32),
        fb=vm((UB * 4 * CH, width), F32),
        xrb=vm((W * 2 * CH, width), F32),
        arl=vm((2, W * CH, width), F32),
        arh=vm((2, W * CH, width), F32),
        brl=vm((2, W * 2 * CH, width), F32),
        brh=vm((2, W * 2 * CH, width), F32),
        bxb=vm((2, W * 2 * CH, width), F32),
        **{s: dma((rows_n,)) for s in ("cs", "crs", "yss", "gs", "grs")},
        yrs=dma((2, rows_n)),
        fin=dma((2,)),
        xs=dma((SENDS,)),
        xr=dma((W,)),
        **{s: dma((2, SENDS)) for s in ("ars", "abu", "abd", "xgs", "brs", "bxs", "bbu", "bbd")},
        **{s: dma((2, W)) for s in ("arr", "abr", "xgr", "brr", "bxr", "bbr")},
    )
    any_spec = pl.BlockSpec(memory_space=pl.ANY)
    vm_spec = pl.BlockSpec(memory_space=pltpu.VMEM)
    out, ig, tg, fa, fb = pl.pallas_call(
        functools.partial(kernel, n_dp, (UA, UB), tuple(scratch)),
        out_shape=(
            jax.ShapeDtypeStruct((tokens, width), BF16),
            jax.ShapeDtypeStruct((tokens, width), BF16),
            jax.ShapeDtypeStruct((rows_n, width), F32),
            jax.ShapeDtypeStruct((UA * 4 * CH, width), F32),
            jax.ShapeDtypeStruct((UB * 4 * CH, width), F32),
        ),
        in_specs=[vm_spec] * 16,
        out_specs=(vm_spec, vm_spec, vm_spec, any_spec, any_spec),
        scratch_shapes=list(scratch.values()),
        compiler_params=pltpu.CompilerParams(
            collective_id=0, has_side_effects=True, vmem_limit_bytes=63 * 2**20
        ),
        cost_estimate=pl.CostEstimate(flops=6 * 10**9, bytes_accessed=20 * 10**6, transcendentals=0),
    )(
        tok, tim, seg, n1g, n1b, wqkv.transpose(0, 2, 1), qvb, wout, outb, n2g, n2b, wup, upb, wdn, dnb, cot
    )
    f32 = lambda *shape: jax.ShapeDtypeStruct(shape, F32)
    moved = (
        jax.ShapeDtypeStruct((tokens, width), BF16),
        jax.ShapeDtypeStruct((tokens, width), BF16),
        f32(rows_n, width),
        f32(3, loc, width),
        f32(loc, width),
        f32(width, ff),
        f32(ff, width),
    )
    results = pl.pallas_call(
        functools.partial(place, big),
        out_shape=moved + (f32(2, loc), f32(ff)) + (f32(width),) * 6,
        in_specs=[any_spec] * 5,
        out_specs=(any_spec,) * 7 + (vm_spec,) * 8,
        scratch_shapes=[
            vm((8, width), F32),
            vm((big, width), F32),
            vm((big, width), F32),
            vm((tokens, width), BF16),
            vm((tokens, width), BF16),
            vm((rows_n, width), F32),
            dma((10,)),
            dma((10,)),
        ],
        compiler_params=pltpu.CompilerParams(vmem_limit_bytes=63 * 2**20),
    )(out, ig, tg, fa, fb)
    out, ig, tg, qkv, outw, up, down, qvb, upb, downb, n2g, n2b, outb, n1g, n1b = results
    return out, ig, tg, n1g, n1b, qkv.transpose(0, 2, 1), qvb, outw, outb, n2g, n2b, up, upb, down, downb


def place(big, *refs):
    out, ig, tg, fa, fb, out_o, ig_o, tg_o, qkv, outw, up, down, qvb, upb, downb = refs[:15]
    n2g, n2b, outb, n1g, n1b, sm, va, vb, vo, vi, vt, sem, sem_o = refs[15:]
    loc, ff = outw.shape[0], down.shape[0]
    half = fa.shape[1] // 2
    width = up.shape[0]
    rows = [pl.ds(0, ff), pl.ds(ff, loc), pl.ds(ff + loc, loc)]
    moves = [
        (fa.at[rows[0]], va.at[rows[0]], down),
        (fb.at[rows[0]], vb.at[rows[0]], up),
        (fa.at[rows[1]], va.at[rows[1]], outw),
        (fa.at[rows[2]], va.at[rows[2]], qkv.at[0]),
        (fb.at[rows[1]], vb.at[rows[1]], qkv.at[1]),
        (fb.at[rows[2]], vb.at[rows[2]], qkv.at[2]),
        (out, vo, out_o),
        (ig, vi, ig_o),
        (tg, vt, tg_o),
    ]
    first = pltpu.make_async_copy(fa.at[pl.ds(big, 8)], sm, sem.at[9])
    first.start()
    loads = [pltpu.make_async_copy(a, v, sem.at[i]) for i, (a, v, b) in enumerate(moves)]
    stores = [pltpu.make_async_copy(v, b, sem_o.at[i]) for i, (a, v, b) in enumerate(moves)]
    for copy in loads:
        copy.start()
    for load, store in zip(loads, stores):
        load.wait()
        store.start()
    first.wait()
    for i, ref in enumerate((downb, upb, n2g, n2b, outb, n1g, n1b)):
        ref[...] = sm[i : i + 1, :].reshape(ref.shape)
    qvb[0:1, :] = sm[7:8, 0:loc]
    qvb[1:2, :] = sm[7:8, half : half + loc]
    for copy in stores:
        copy.wait()


def solution(mesh):
    placed = (
        P("dp", None),
        P("dp", None),
        P("dp", None),
        P(),
        P(),
        P(None, None, "mp"),
        P(None, "mp"),
        P("mp", None),
        P(),
        P(),
        P(),
        P(None, "mp"),
        P("mp"),
        P("mp", None),
        P(),
        P("dp", None),
    )
    return jax.shard_map(
        functools.partial(shards, mesh.shape["dp"]),
        mesh=mesh,
        in_specs=placed,
        out_specs=(
            P("dp", None),
            P("dp", None),
            P("dp", None),
            P(),
            P(),
            P(None, None, "mp"),
            P(None, "mp"),
            P("mp", None),
            P(),
            P(),
            P(),
            P(None, "mp"),
            P("mp"),
            P("mp", None),
            P(),
        ),
        check_vma=False,
    )
```

```python
import functools

import jax
import jax.numpy as jnp
from jax import lax
from jax.experimental import pallas as pl
from jax.experimental.pallas import tpu as pltpu
from jax.sharding import PartitionSpec as P

HD = 64
SUB = 32
CH = 8
SENDS = 4
MESH = pl.DeviceIdType.MESH
F32 = jnp.float32
BF16 = jnp.bfloat16


ARGS = ("tok", "tim", "seg", "n1g", "n1b", "wqkv", "qvb", "wout", "outb", "n2g", "n2b")
ARGS += ("wup", "upb", "wdn", "dnb", "cot")


def hop_ticks(line):
    return 2 if line <= 8 else 1


def when(cond, fn):
    pl.when(cond)(fn)


def nt(a, b):
    return lax.dot_general(a, b, (((1,), (1,)), ((), ())), preferred_element_type=F32)


def tn(a, b):
    return lax.dot_general(a, b, (((0,), (0,)), ((), ())), preferred_element_type=F32)


def nn(a, b):
    return jnp.dot(a, b, preferred_element_type=F32)


def normed(v):
    centred = v - jnp.mean(v, -1, keepdims=True)
    spread = jnp.mean(centred * centred, -1, keepdims=True)
    scale = lax.rsqrt(spread + 1e-05)
    return centred * scale, scale


def colsum(v):
    return jnp.sum(v, 0, keepdims=True)


def kernel(n_dp, units, names, *refs):
    out, ig, tg, f_out = refs[16:20]
    R = dict(zip(names, refs[20:]))
    order = ("tok", "tim", "n1g", "n1b", "wqkv", "qvb", "seg", "wout", "outb", "cot", "wdn")
    order += ("n2g", "n2b", "wup", "upb", "dnb")
    tok, tim, wqkv, qvb, seg, wout, cot, wdn, wup = (
        R[s] for s in ("tok", "tim", "wqkv", "qvb", "seg", "wout", "cot", "wdn", "wup")
    )
    loads = {
        name: pltpu.make_async_copy(refs[ARGS.index(name)], R[name], R["ins"].at[i]) for i, name in enumerate(order)
    }
    n1g, n1b, outb, n2g, n2b, upb, dnb = (R["vecs"].at[pl.ds(i, 1)] for i in range(7))
    timf, start, entry, q_s, k_s, v_s = (R[s] for s in ("timf", "start", "entry", "q", "k", "v"))
    probs, mixed_s, part, cr, ys, yr = (R[s] for s in ("probs", "mixed", "part", "cr", "ys", "yr"))
    tot, mid, e2, hp, act, gp = (R[s] for s in ("tot", "mid", "e2", "hp", "act", "gp"))
    gact, gmid, gbr, lt, g, f = (R[s] for s in ("gact", "gmid", "gbr", "lt", "g", "f"))

    rows_n, seq = seg.shape
    width = tok.shape[1]
    half = width // 2
    loc = wout.shape[0]
    heads = loc // HD
    ff = wup.shape[1]
    UA, UB = units
    L = n_dp // 2
    LAG = hop_ticks(L)
    D = L // 2
    root = D - 1
    dp = lax.axis_index("dp")
    mp = lax.axis_index("mp")
    core = mp % 2
    x = dp % 2
    z = dp // 2
    to_core = (dp, mp + 1 - 2 * core)
    to_y = (dp, (mp + 2) % 4)
    to_x = (dp + 1 - 2 * x, mp)
    zlo = jnp.maximum(z - 1, 0) * 2 + x
    zhi = jnp.minimum(z + 1, L - 1) * 2 + x

    barrier = pltpu.get_barrier_semaphore()
    for dev in (to_core, to_y, to_x):
        pl.semaphore_signal(barrier, 1, device_id=dev, device_id_type=MESH)
    when(z > 0, lambda: pl.semaphore_signal(barrier, 1, device_id=(zlo, mp), device_id_type=MESH))
    when(z < L - 1, lambda: pl.semaphore_signal(barrier, 1, device_id=(zhi, mp), device_id_type=MESH))

    def sl(r, n=seq):
        return pl.ds(pl.multiple_of(r * n, n), n)

    def sub(r, i):
        return pl.ds(pl.multiple_of(r * seq + i * SUB, SUB), SUB)

    mine = pl.ds(pl.multiple_of(core * half, 128), half)
    other = pl.ds(pl.multiple_of((1 - core) * half, 128), half)

    def remote(src, dst, ssem, rsem, dev):
        return pltpu.make_async_remote_copy(
            src_ref=src, dst_ref=dst, send_sem=ssem, recv_sem=rsem, device_id=dev, device_id_type=MESH
        )

    def core_copy(p, r):
        return remote(part.at[sl(r), other], cr.at[sl(r)], R["cs"].at[r], R["crs"].at[r], to_core)

    def y_copy(p, r):
        return remote(ys.at[sl(r)], yr.at[p % 2, sl(r)], R["yss"].at[r], R["yrs"].at[p % 2, r], to_y)

    def ag_copy(p, r):
        return remote(tot.at[sl(r), mine], tot.at[sl(r), mine], R["gs"].at[r], R["grs"].at[r], to_core)

    def sum_b(p, r):
        core_copy(p, r).wait()
        ys[sl(r), :] = part[sl(r), mine] + cr[sl(r), :]
        y_copy(p, r).start()

    def sum_c(p, r):
        y_copy(p, r).wait()
        tot[sl(r), mine] = ys[sl(r), :] + yr[p % 2, sl(r), :]
        ag_copy(p, r).start()

    def sum_d(p, r):
        ag_copy(p, r).wait()

    def vec(ref):
        return ref[...]

    small = 2 * ff + 4 * loc

    def small_add(i, v):
        g[small + i : small + i + 1, :] += v

    lane = lax.broadcasted_iota(jnp.int32, (1, loc), 1)
    masks = [((lane >= h * HD) & (lane < (h + 1) * HD)).astype(F32) for h in range(heads)]

    def by_head(v):
        return jnp.concatenate([v * m.astype(BF16) for m in masks], 0)

    def from_heads(v):
        total = v[:seq] * masks[0]
        for h in range(1, heads):
            total = total + v[h * seq : (h + 1) * seq] * masks[h]
        return total

    def norm1(r):
        @pl.loop(0, seq // SUB)
        def _(i):
            s = sub(r, i)
            v = tok[s, :].astype(F32) + timf[pl.ds(r, 1), :]
            start[s, :] = v
            xhat, _ = normed(v)
            entry[s, :] = (xhat * n1g[...] + n1b[...]).astype(BF16)

    def project(r):
        e = entry[sl(r), :]
        q_s[sl(r), :] = (nt(e, wqkv[0]) + qvb[0:1, :]).astype(BF16)
        k_s[sl(r), :] = nt(e, wqkv[1]).astype(BF16)
        v_s[sl(r), :] = (nt(e, wqkv[2]) + qvb[1:2, :]).astype(BF16)

    def attend(r):
        labels = jnp.broadcast_to(seg[pl.ds(r, 1), :], (seq, seq))
        same = labels == labels.T
        same = jnp.concatenate([same.astype(F32)] * heads, 0) > 0.5
        scores = nt(by_head(q_s[sl(r), :]), k_s[sl(r), :]) * HD ** (-0.5)
        scores = jnp.where(same, scores, -1e30)
        w = jnp.exp(scores - jnp.max(scores, -1, keepdims=True))
        pr = w / jnp.sum(w, -1, keepdims=True)
        probs[sl(r, heads * seq), :] = pr
        mixed = from_heads(nn(pr.astype(BF16), v_s[sl(r), :])).astype(BF16)
        mixed_s[sl(r), :] = mixed
        part[sl(r), :] = nn(mixed, wout[...])

        @pl.when(r == 0)
        def _():
            pl.semaphore_wait(barrier, 3 + jnp.minimum(z, 1) + jnp.minimum(L - 1 - z, 1))

        core_copy(0, r).start()
        lt[2 * ff : 2 * ff + loc, sl(r)] = mixed.T

    def grad_act(r):
        c = cot[sl(r), :]
        gact[sl(r), :] = nt(c, wdn[...])
        small_add(0, colsum(c.astype(F32)))

    def feed(r):
        @pl.loop(0, seq // SUB)
        def _(i):
            s = sub(r, i)
            v = start[s, :] + (tot[s, :] + outb[...])
            mid[s, :] = v
            xhat, _ = normed(v)
            e2[s, :] = (xhat * n2g[...] + n2b[...]).astype(BF16)

        hp[...] = nn(e2[sl(r), :], wup[...])

        @pl.loop(0, seq // SUB)
        def _(i):
            s = sub(r, i)
            u = hp[pl.ds(pl.multiple_of(i * SUB, SUB), SUB), :] + upb[...]
            cdf = 0.5 * (1.0 + lax.erf(u * 0.7071067811865476))
            act[s, :] = (u * cdf).astype(BF16)
            slope = cdf + u * (0.3989422804014327 * jnp.exp(-0.5 * u * u))
            pre = (gact[s, :] * slope).astype(BF16)
            gp[s, :] = pre
            small_add(1, colsum(pre.astype(F32)))

        part[sl(r), :] = nt(gp[sl(r), :], wup[...])
        core_copy(1, r).start()
        lt[0:ff, sl(r)] = act[sl(r), :].T
        lt[ff : 2 * ff, sl(r)] = e2[sl(r), :].T

    def back2(r):
        @pl.loop(0, seq // SUB)
        def _(i):
            s = sub(r, i)
            ge = tot[s, :]
            xhat, scale = normed(mid[s, :])
            small_add(2, colsum(ge * xhat))
            small_add(3, colsum(ge))
            gx = ge * n2g[...]
            gm = cot[s, :].astype(F32) + scale * (
                gx - jnp.mean(gx, -1, keepdims=True) - xhat * jnp.mean(gx * xhat, -1, keepdims=True)
            )
            gmid[s, :] = gm
            low = gm.astype(BF16)
            gbr[s, :] = low
            small_add(4, colsum(low.astype(F32)))

        g3 = by_head(nt(gbr[sl(r), :], wout[...]).astype(BF16))
        pr = probs[sl(r, heads * seq), :]
        grad_probs = nt(g3, v_s[sl(r), :])
        inner = jnp.sum(pr * grad_probs, -1, keepdims=True)
        ds = (pr * (grad_probs - inner)).astype(BF16)
        gq = (from_heads(nn(ds, k_s[sl(r), :])) * HD ** (-0.5)).astype(BF16)
        gk = (tn(ds, by_head(q_s[sl(r), :])) * HD ** (-0.5)).astype(BF16)
        gv = tn(pr.astype(BF16), g3).astype(BF16)
        part[sl(r), :] = nn(gq, wqkv[0]) + nn(gk, wqkv[1]) + nn(gv, wqkv[2])
        core_copy(2, r).start()
        late = 2 * ff + loc
        for i, v in enumerate((gq, gk, gv)):
            lt[late + i * loc : late + (i + 1) * loc, sl(r)] = v.T
        g[small + 7 : small + 8, 0:loc] += colsum(gq.astype(F32))
        g[small + 7 : small + 8, half : half + loc] += colsum(gv.astype(F32))

    def back1(r):
        tg[pl.ds(r, 1), :] = jnp.zeros((1, width), F32)

        @pl.loop(0, seq // SUB)
        def _(i):
            s = sub(r, i)
            ge = tot[s, :]
            xhat, scale = normed(start[s, :])
            small_add(5, colsum(ge * xhat))
            small_add(6, colsum(ge))
            gy = ge * n1g[...]
            gs = gmid[s, :] + scale * (
                gy - jnp.mean(gy, -1, keepdims=True) - xhat * jnp.mean(gy * xhat, -1, keepdims=True)
            )
            ig[s, :] = gs.astype(BF16)
            tg[pl.ds(r, 1), :] += colsum(gs)

    def down(r):
        part[sl(r), :] = nn(act[sl(r), :], wdn[...])
        core_copy(3, r).start()

    def finish(r):
        @pl.loop(0, seq // SUB)
        def _(i):
            s = sub(r, i)
            out[s, :] = (mid[s, :] + (tot[s, :] + dnb[...])).astype(BF16)

    blk = loc

    early = ff // blk

    def weight_grads(j):
        s = pl.ds(pl.multiple_of(j * blk, blk), blk)

        def by(right):
            def fn():
                g[s, :] = nn(lt[s, :], right[...])

            return fn

        when(j < early, by(cot))
        when((j >= early) & (j < 2 * early), by(gp))
        when(j == 2 * early, by(gbr))
        when(j > 2 * early, by(entry))

    def ok(u, n):
        return (u >= 0) & (u < n)

    def go(copy, u, depth):
        when(u >= depth, lambda: copy(u - depth).wait_send())
        copy(u).start()

    def end(copy, n, depth):
        for u in range(n - min(depth, n), n):
            copy(u).wait_send()

    def a_base(u):
        return (u // 3 * 5 + u % 3) * 4 * CH

    def x_slot(u):
        return pl.ds(pl.multiple_of(u % R["xr"].shape[0] * 2 * CH, CH), 2 * CH)

    def x_first(u):
        src = pl.ds(pl.multiple_of(a_base(u) + (1 - x) * 2 * CH, CH), 2 * CH)
        return remote(
            g.at[src], R["xrb"].at[x_slot(u)], R["xs"].at[u % SENDS], R["xr"].at[u % R["xr"].shape[0]], to_x
        )

    class Way:
        def __init__(self, kind, d):
            self.kind, self.d = kind, d
            self.two = kind != "a"
            self.w = z if d == 0 else L - 1 - z
            self.up = (zhi if d == 0 else zlo, mp)
            self.dn = (zlo if d == 0 else zhi, mp)
            self.root = 0 if kind == "c" else D - 1
            self.depth = L - 1 - self.root
            self.n = UB if self.two else UA
            self.first = {"a": LAG, "b": 0, "c": 1}[kind]
            self.stride = 3 if self.two else 1
            self.gap = LAG if self.two else 0
            self.rows = 2 * CH if self.two else CH
            self.lo, self.hi = R[kind + "lo"], R[kind + "hi"]
            self.sems = {t: R[kind + "_" + t] for t in ("s", "r", "u", "d", "t", "xs", "xr")}
            self.flight, self.W = self.sems["s"].shape[1], self.sems["r"].shape[1]

        def unit(self, t, offset):
            rel = t - self.first - offset
            return rel // self.stride, (rel >= 0) & (rel < self.n * self.stride) & (rel % self.stride == 0)

        def own(self, u):
            if self.two:
                base = (u * 5 + (3 if self.kind == "b" else 4)) * 4 * CH
            else:
                base = a_base(u) + x * 2 * CH
            return pl.ds(pl.multiple_of(base + self.d * self.rows, CH), self.rows)

        def slot(self, u):
            return pl.ds(pl.multiple_of(u % self.W * self.rows, CH), self.rows)

        def copy(self, src, dst, ssem, rsem, u, dev):
            return remote(
                src, dst, self.sems[ssem].at[self.d, u % self.flight], self.sems[rsem].at[self.d, u % self.W], dev
            )

        def send_up(self, u):
            return self.copy(g.at[self.own(u)], self.lo.at[self.d, self.slot(u)], "s", "r", u, self.up)

        def send_up_root(self, u):
            return self.copy(g.at[self.own(u)], self.lo.at[self.d, self.slot(u)], "s", "t", u, self.up)

        def send_dn(self, u):
            return self.copy(g.at[self.own(u)], self.hi.at[self.d, self.slot(u)], "s", "r", u, self.dn)

        def total_up(self, u):
            return self.copy(f.at[self.own(u)], f.at[self.own(u)], "u", "t", u, self.up)

        def total_dn(self, u):
            return self.copy(f.at[self.own(u)], f.at[self.own(u)], "d", "t", u, self.dn)

        def x_copy(self, u):
            if self.two:
                return self.copy(g.at[self.own(u)], R[self.kind + "xb"].at[self.d, self.slot(u)], "xs", "xr", u, to_x)
            return self.copy(f.at[self.own(u)], f.at[self.own(u)], "xs", "xr", u, to_x)

        def go(self, copy, u):
            go(copy, u, self.flight)

        def reduce(self, u):
            w, root, own = self.w, self.root, self.own(u)

            def from_low():
                when(w < root, lambda: self.send_up(u).wait_recv())
                when(w == root, lambda: self.send_up_root(u).wait_recv())
                g[own, :] += self.lo[self.d, self.slot(u), :]

            def from_high():
                self.send_dn(u).wait_recv()
                g[own, :] += self.hi[self.d, self.slot(u), :]

            if root > 0:
                when((w > 0) & (w <= root), from_low)
            when((w < L - 1) & (w >= root), from_high)
            if root > 1:
                when(w < root - 1, lambda: self.go(self.send_up, u))
            if root > 0:
                when(w == root - 1, lambda: self.go(self.send_up_root, u))
            when(w > root, lambda: self.go(self.send_dn, u))
            if self.two:
                when(w == root, lambda: self.go(self.x_copy, u))

        def turn(self, u):
            own = self.own(u)
            if self.two:
                self.x_copy(u).wait_recv()
                f[own, :] = g[own, :] + R[self.kind + "xb"][self.d, self.slot(u), :]
            else:
                f[own, :] = g[own, :]
            self.go(self.total_up, u)
            if self.root > 0:
                self.go(self.total_dn, u)
            if not self.two:
                self.go(self.x_copy, u)

        def spread(self, u):
            w, root = self.w, self.root
            self.total_up(u).wait_recv()
            when((w > root) & (w < L - 1), lambda: self.go(self.total_up, u))
            if root > 1:
                when((w < root) & (w > 0), lambda: self.go(self.total_dn, u))
            if not self.two:
                self.go(self.x_copy, u)

        def tick(self, t):
            w, root = self.w, self.root
            dist = jnp.abs(w - root) * LAG
            u, valid = self.unit(t, self.depth * LAG - dist)
            when(valid, lambda: self.reduce(u))
            v, valid_v = self.unit(t, self.depth * LAG + self.gap)
            when(valid_v & (w == root), lambda: self.turn(v))
            q, valid_q = self.unit(t, self.depth * LAG + self.gap + dist)
            when(valid_q & (w != root), lambda: self.spread(q))
            if not self.two:
                e, valid_e = self.unit(t, self.depth * LAG + self.gap + dist + LAG)
                when(valid_e, lambda: self.x_copy(e).wait_recv())

        def drain(self):
            w, root, n, flight = self.w, self.root, self.n, self.flight
            if root > 1:
                when(w < root - 1, lambda: end(self.send_up, n, flight))
            if root > 0:
                when(w == root - 1, lambda: end(self.send_up_root, n, flight))
                when((w <= root) & (w > 0), lambda: end(self.total_dn, n, flight))
            when(w > root, lambda: end(self.send_dn, n, flight))
            when((w >= root) & (w < L - 1), lambda: end(self.total_up, n, flight))
            if self.two:
                when(w == root, lambda: end(self.x_copy, n, flight))
            else:
                end(self.x_copy, n, flight)

    ways = [Way(kind, d) for kind in ("c", "b", "a") for d in (0, 1)]

    def dp_tick(t):
        when(t < UA, lambda: go(x_first, t, SENDS))

        def x_add():
            u = t - LAG
            x_first(u).wait_recv()
            s = pl.ds(pl.multiple_of(a_base(u) + x * 2 * CH, CH), 2 * CH)
            g[s, :] += R["xrb"][x_slot(u), :]

        when(ok(t - LAG, UA), x_add)
        for way in ways:
            way.tick(t)

    def dp_drain():
        end(x_first, UA, SENDS)
        for way in ways:
            way.drain()

    for copy in loads.values():
        copy.start()

    def vector(i, name):
        loads[name].wait()
        R["vecs"][i : i + 1, :] = R[name][...][None, :]

    g[small : small + 4 * CH, :] = jnp.zeros((4 * CH, width), F32)
    for name in ("tok", "tim"):
        loads[name].wait()
    timf[...] = tim[...].astype(F32)
    vector(0, "n1g")
    vector(1, "n1b")

    @pl.loop(0, rows_n)
    def _(r):
        norm1(r)

        @pl.when(r == 0)
        def _():
            for name in ("wqkv", "qvb", "seg", "wout"):
                loads[name].wait()

        project(r)
        attend(r)
        sum_b(0, r)

    for name in ("cot", "wdn", "wup"):
        loads[name].wait()
    for i, name in enumerate(("outb", "n2g", "n2b", "upb", "dnb")):
        vector(2 + i, name)

    @pl.loop(0, rows_n)
    def _(r):
        grad_act(r)
        when(r > 0, lambda: sum_b(1, r - 1))
        sum_c(0, r)
        sum_d(0, r)
        feed(r)

    weight_grads(jnp.int32(0))

    blocks = (2 * ff + 4 * loc) // blk
    per = blk // (4 * CH)
    a_last = LAG * (2 * D + 2)
    c_last = LAG * (2 * L - 1)
    ticks = max(UA + a_last, 3 * UB + c_last)

    def out_copy(j):
        s = pl.ds(j * blk, blk if j < blocks else 4 * CH)
        return pltpu.make_async_copy(f.at[s], f_out.at[s], R["fin"].at[j])

    @pl.loop(0, ticks)
    def _(t):
        dp_tick(t)

        def at(first, step, fn):
            r = (t - first) // step
            when((t >= first) & ((t - first) % step == 0) & (r < rows_n), lambda: fn(r))

        when(t == 0, lambda: sum_b(1, rows_n - 1))
        at(0, 2, lambda r: sum_c(1, r))

        def second(r):
            sum_d(1, r)
            back2(r)

        at(1, 2, second)
        at(2, 2, lambda r: sum_b(2, r))
        at(5, 2, lambda r: sum_c(2, r))

        def third(r):
            sum_d(2, r)
            back1(r)

        at(6, 2, third)
        at(9, 2, down)
        at(10, 2, lambda r: sum_b(3, r))
        at(13, 2, lambda r: sum_c(3, r))

        def fourth(r):
            sum_d(3, r)
            finish(r)

        at(14, 2, fourth)
        when((t % 3 == 1) & (t < 3 * blocks - 2), lambda: weight_grads((t + 2) // 3))
        for j in range(blocks):
            done = (per * (j + 1) - 1) // 5 * 3 + 2 + max(a_last, c_last)
            if done < ticks:
                when(t == done, lambda: out_copy(j).start())

    dp_drain()
    for j in range(blocks + 1):
        if j == blocks or (per * (j + 1) - 1) // 5 * 3 + 2 + max(a_last, c_last) >= ticks:
            out_copy(j).start()
    for j in range(blocks + 1):
        out_copy(j).wait()


def shards(n_dp, *args):
    (tok, tim, seg, n1g, n1b, wqkv, qvb, wout, outb, n2g, n2b, wup, upb, wdn, dnb, cot) = args
    tokens, width = tok.shape
    rows_n, seq = seg.shape
    loc, ff = wout.shape[0], wup.shape[1]
    heads = loc // HD
    half = width // 2
    big = 2 * ff + 4 * loc
    count = big // (4 * CH) + 1
    UB = count // 5
    UA = count - 2 * UB
    L = n_dp // 2
    LAG = hop_ticks(L)
    vm = pltpu.VMEM
    dma = pltpu.SemaphoreType.DMA
    W = LAG * (L + 1) + 2
    WB = LAG * (L + 1) // 3 + 3
    WC = LAG * (2 * L - 1) // 3 + 3
    total = count * 4 * CH
    slots = lambda w, rows: vm((2, w * rows, width), F32)
    flat = lambda n: vm((n,), F32)
    scratch = dict(
        tok=vm((tokens, width), BF16),
        cot=vm((tokens, width), BF16),
        wqkv=vm((3, loc, width), BF16),
        wout=vm((loc, width), BF16),
        wup=vm((width, ff), BF16),
        wdn=vm((ff, width), BF16),
        ins=dma((16,)),
        tim=vm((rows_n, width), BF16),
        seg=vm((rows_n, seq), jnp.int32),
        qvb=vm((2, loc), F32),
        **{s: flat(width) for s in ("n1g", "n1b", "outb", "n2g", "n2b", "dnb")},
        upb=flat(ff),
        vecs=vm((8, width), F32),
        timf=vm((rows_n, width), F32),
        start=vm((tokens, width), F32),
        entry=vm((tokens, width), BF16),
        q=vm((tokens, loc), BF16),
        k=vm((tokens, loc), BF16),
        v=vm((tokens, loc), BF16),
        probs=vm((heads * tokens, seq), F32),
        mixed=vm((tokens, loc), BF16),
        part=vm((tokens, width), F32),
        cr=vm((tokens, half), F32),
        ys=vm((tokens, half), F32),
        yr=vm((2, tokens, half), F32),
        tot=vm((tokens, width), F32),
        mid=vm((tokens, width), F32),
        e2=vm((tokens, width), BF16),
        hp=vm((seq, ff), F32),
        act=vm((tokens, ff), BF16),
        gp=vm((tokens, ff), BF16),
        gact=vm((tokens, ff), F32),
        gmid=vm((tokens, width), F32),
        gbr=vm((tokens, width), BF16),
        lt=vm((big, tokens), BF16),
        g=vm((total, width), F32),
        f=vm((total, width), F32),
        xrb=vm((W * 2 * CH, width), F32),
        alo=slots(W, CH),
        ahi=slots(W, CH),
        blo=slots(WB, 2 * CH),
        bhi=slots(WB, 2 * CH),
        bxb=slots(WB, 2 * CH),
        clo=slots(1, 2 * CH),
        chi=slots(WC, 2 * CH),
        cxb=slots(WC, 2 * CH),
        **{s: dma((rows_n,)) for s in ("cs", "crs", "yss", "gs", "grs")},
        yrs=dma((2, rows_n)),
        fin=dma((big // loc + 1,)),
        xs=dma((SENDS,)),
        xr=dma((W,)),
        **{k + "_" + s: dma((2, SENDS if k == "a" else 2)) for k in "abc" for s in ("s", "u", "d", "xs")},
        **{k + "_" + s: dma((2, w)) for k, w in (("a", W), ("b", WB), ("c", WC)) for s in ("r", "t", "xr")},
    )
    any_spec = pl.BlockSpec(memory_space=pl.ANY)
    vm_spec = pl.BlockSpec(memory_space=pltpu.VMEM)
    out, ig, tg, f = pl.pallas_call(
        functools.partial(kernel, n_dp, (UA, UB), tuple(scratch)),
        out_shape=(
            jax.ShapeDtypeStruct((tokens, width), BF16),
            jax.ShapeDtypeStruct((tokens, width), BF16),
            jax.ShapeDtypeStruct((rows_n, width), F32),
            jax.ShapeDtypeStruct((total, width), F32),
        ),
        in_specs=[any_spec] * 16,
        out_specs=(vm_spec, vm_spec, vm_spec, any_spec),
        scratch_shapes=list(scratch.values()),
        compiler_params=pltpu.CompilerParams(
            collective_id=0, has_side_effects=True, vmem_limit_bytes=63 * 2**20
        ),
        cost_estimate=pl.CostEstimate(flops=6 * 10**9, bytes_accessed=20 * 10**6, transcendentals=0),
    )(
        tok, tim, seg, n1g, n1b, wqkv.transpose(0, 2, 1), qvb, wout, outb, n2g, n2b, wup, upb, wdn, dnb, cot
    )
    f32 = lambda *shape: jax.ShapeDtypeStruct(shape, F32)
    moved = (
        jax.ShapeDtypeStruct((tokens, width), BF16),
        jax.ShapeDtypeStruct((tokens, width), BF16),
        f32(rows_n, width),
        f32(3, loc, width),
        f32(loc, width),
        f32(width, ff),
        f32(ff, width),
    )
    results = pl.pallas_call(
        functools.partial(place, big),
        out_shape=moved + (f32(2, loc), f32(ff)) + (f32(width),) * 6,
        in_specs=[any_spec] * 4,
        out_specs=(any_spec,) * 7 + (vm_spec,) * 8,
        scratch_shapes=[
            vm((8, width), F32),
            vm((big, width), F32),
            vm((tokens, width), BF16),
            vm((tokens, width), BF16),
            vm((rows_n, width), F32),
            dma((10,)),
            dma((10,)),
        ],
        compiler_params=pltpu.CompilerParams(vmem_limit_bytes=63 * 2**20),
    )(out, ig, tg, f)
    out, ig, tg, qkv, outw, up, down, qvb, upb, downb, n2g, n2b, outb, n1g, n1b = results
    return out, ig, tg, n1g, n1b, qkv.transpose(0, 2, 1), qvb, outw, outb, n2g, n2b, up, upb, down, downb


def place(big, *refs):
    out, ig, tg, f, out_o, ig_o, tg_o, qkv, outw, up, down, qvb, upb, downb = refs[:14]
    n2g, n2b, outb, n1g, n1b, sm, buf, vo, vi, vt, sem, sem_o = refs[14:]
    loc, ff = outw.shape[0], down.shape[0]
    half = f.shape[1] // 2
    moves = []
    row = 0
    for n, ref in ((ff, down), (ff, up), (loc, outw), (loc, qkv.at[0]), (loc, qkv.at[1]), (loc, qkv.at[2])):
        s = pl.ds(row, n)
        moves.append((f.at[s], buf.at[s], ref))
        row += n
    moves += [(out, vo, out_o), (ig, vi, ig_o), (tg, vt, tg_o)]
    first = pltpu.make_async_copy(f.at[pl.ds(big, 8)], sm, sem.at[9])
    first.start()
    loads = [pltpu.make_async_copy(a, v, sem.at[i]) for i, (a, v, b) in enumerate(moves)]
    stores = [pltpu.make_async_copy(v, b, sem_o.at[i]) for i, (a, v, b) in enumerate(moves)]
    for copy in loads:
        copy.start()
    for load, store in zip(loads, stores):
        load.wait()
        store.start()
    first.wait()
    for i, ref in enumerate((downb, upb, n2g, n2b, outb, n1g, n1b)):
        ref[...] = sm[i : i + 1, :].reshape(ref.shape)
    qvb[0:1, :] = sm[7:8, 0:loc]
    qvb[1:2, :] = sm[7:8, half : half + loc]
    for copy in stores:
        copy.wait()


def solution(mesh):
    placed = (
        P("dp", None),
        P("dp", None),
        P("dp", None),
        P(),
        P(),
        P(None, None, "mp"),
        P(None, "mp"),
        P("mp", None),
        P(),
        P(),
        P(),
        P(None, "mp"),
        P("mp"),
        P("mp", None),
        P(),
        P("dp", None),
    )
    return jax.shard_map(
        functools.partial(shards, mesh.shape["dp"]),
        mesh=mesh,
        in_specs=placed,
        out_specs=(
            P("dp", None),
            P("dp", None),
            P("dp", None),
            P(),
            P(),
            P(None, None, "mp"),
            P(None, "mp"),
            P("mp", None),
            P(),
            P(),
            P(),
            P(None, "mp"),
            P("mp"),
            P("mp", None),
            P(),
        ),
        check_vma=False,
    )
```

```python
import functools

import jax
import jax.numpy as jnp
from jax import lax
from jax.experimental import pallas as pl
from jax.experimental.pallas import tpu as pltpu
from jax.sharding import PartitionSpec as P

HD = 64
SUB = 128
CH = 8
SENDS = 4
MESH = pl.DeviceIdType.MESH
F32 = jnp.float32
BF16 = jnp.bfloat16


ARGS = ("tok", "tim", "seg", "n1g", "n1b", "wqkv", "qvb", "wout", "outb", "n2g", "n2b")
ARGS += ("wup", "upb", "wdn", "dnb", "cot")


def hop_ticks(line):
    return 2 if line <= 8 else 1


def when(cond, fn):
    pl.when(cond)(fn)


def nt(a, b):
    return lax.dot_general(a, b, (((1,), (1,)), ((), ())), preferred_element_type=F32)


def tn(a, b):
    return lax.dot_general(a, b, (((0,), (0,)), ((), ())), preferred_element_type=F32)


def nn(a, b):
    return jnp.dot(a, b, preferred_element_type=F32)


def normed(v):
    centred = v - jnp.mean(v, -1, keepdims=True)
    spread = jnp.mean(centred * centred, -1, keepdims=True)
    scale = lax.rsqrt(spread + 1e-05)
    return centred * scale, scale


def colsum(v):
    return jnp.sum(v, 0, keepdims=True)


def kernel(n_dp, units, names, *refs):
    out_o, ig_o, tg_o, f_out = refs[16:20]
    R = dict(zip(names, refs[20:]))
    order = ("tok", "tim", "n1g", "n1b", "wqkv", "qvb", "seg", "wout", "outb", "cot", "wdn")
    order += ("n2g", "n2b", "wup", "upb", "dnb")
    tok, tim, wqkv, qvb, seg, wout, cot, wdn, wup = (
        R[s] for s in ("tok", "tim", "wqkv", "qvb", "seg", "wout", "cot", "wdn", "wup")
    )
    loads = {
        name: pltpu.make_async_copy(refs[ARGS.index(name)], R[name], R["ins"].at[i]) for i, name in enumerate(order)
    }
    n1g, n1b, outb, n2g, n2b, upb, dnb = (R["vecs"].at[pl.ds(i, 1)] for i in range(7))
    timf, start, entry, q_s, k_s, v_s = (R[s] for s in ("timf", "start", "entry", "q", "k", "v"))
    probs, mixed_s, part, cr, ys, yr = (R[s] for s in ("probs", "mixed", "part", "cr", "ys", "yr"))
    tot, mid, e2, hp, act, gp = (R[s] for s in ("tot", "mid", "e2", "hp", "act", "gp"))
    out, ig, tg = (R[s] for s in ("out", "ig", "tg"))
    gact, gmid, gbr, lt, g, f = (R[s] for s in ("gact", "gmid", "gbr", "lt", "g", "f"))

    rows_n, seq = seg.shape
    width = tok.shape[1]
    half = width // 2
    loc = wout.shape[0]
    heads = loc // HD
    ff = wup.shape[1]
    UA, UB, UC = units
    L = n_dp // 2
    LAG = hop_ticks(L)
    D = L // 2
    root = D - 1
    dp = lax.axis_index("dp")
    mp = lax.axis_index("mp")
    core = mp % 2
    x = dp % 2
    z = dp // 2
    to_core = (dp, mp + 1 - 2 * core)
    to_y = (dp, (mp + 2) % 4)
    to_x = (dp + 1 - 2 * x, mp)
    zlo = jnp.maximum(z - 1, 0) * 2 + x
    zhi = jnp.minimum(z + 1, L - 1) * 2 + x

    barrier = pltpu.get_barrier_semaphore()
    for dev in (to_core, to_y, to_x):
        pl.semaphore_signal(barrier, 1, device_id=dev, device_id_type=MESH)
    when(z > 0, lambda: pl.semaphore_signal(barrier, 1, device_id=(zlo, mp), device_id_type=MESH))
    when(z < L - 1, lambda: pl.semaphore_signal(barrier, 1, device_id=(zhi, mp), device_id_type=MESH))

    def sl(r, n=seq):
        return pl.ds(pl.multiple_of(r * n, n), n)

    def sub(r, i):
        return pl.ds(pl.multiple_of(r * seq + i * SUB, SUB), SUB)

    mine = pl.ds(pl.multiple_of(core * half, 128), half)
    other = pl.ds(pl.multiple_of((1 - core) * half, 128), half)

    def remote(src, dst, ssem, rsem, dev):
        return pltpu.make_async_remote_copy(
            src_ref=src, dst_ref=dst, send_sem=ssem, recv_sem=rsem, device_id=dev, device_id_type=MESH
        )

    def core_copy(p, r):
        return remote(part.at[sl(r), other], cr.at[sl(r)], R["cs"].at[r], R["crs"].at[r], to_core)

    def y_copy(p, r):
        return remote(ys.at[sl(r)], yr.at[p % 2, sl(r)], R["yss"].at[r], R["yrs"].at[p % 2, r], to_y)

    def ag_copy(p, r):
        return remote(tot.at[sl(r), mine], tot.at[sl(r), mine], R["gs"].at[r], R["grs"].at[r], to_core)

    def sum_b(p, r):
        core_copy(p, r).wait()
        ys[sl(r), :] = part[sl(r), mine] + cr[sl(r), :]
        y_copy(p, r).start()

    def sum_c(p, r):
        y_copy(p, r).wait()
        tot[sl(r), mine] = ys[sl(r), :] + yr[p % 2, sl(r), :]
        ag_copy(p, r).start()

    def sum_d(p, r):
        ag_copy(p, r).wait()

    def vec(ref):
        return ref[...]

    small = 2 * ff + 4 * loc

    def small_add(i, v):
        g[small + i : small + i + 1, :] += v

    lane = lax.broadcasted_iota(jnp.int32, (1, loc), 1)
    masks = [((lane >= h * HD) & (lane < (h + 1) * HD)).astype(F32) for h in range(heads)]

    def by_head(v):
        return jnp.concatenate([v * m.astype(BF16) for m in masks], 0)

    def from_heads(v):
        total = v[:seq] * masks[0]
        for h in range(1, heads):
            total = total + v[h * seq : (h + 1) * seq] * masks[h]
        return total

    def norm1(r):
        @pl.loop(0, seq // SUB)
        def _(i):
            s = sub(r, i)
            v = tok[s, :].astype(F32) + timf[pl.ds(r, 1), :]
            start[s, :] = v
            xhat, _ = normed(v)
            entry[s, :] = (xhat * n1g[...] + n1b[...]).astype(BF16)

    def project(r):
        e = entry[sl(r), :]
        q_s[sl(r), :] = (nt(e, wqkv[0]) + qvb[0:1, :]).astype(BF16)
        k_s[sl(r), :] = nt(e, wqkv[1]).astype(BF16)
        v_s[sl(r), :] = (nt(e, wqkv[2]) + qvb[1:2, :]).astype(BF16)

    def attend(r):
        labels = jnp.broadcast_to(seg[pl.ds(r, 1), :], (seq, seq))
        same = labels == labels.T
        same = jnp.concatenate([same.astype(F32)] * heads, 0) > 0.5
        scores = nt(by_head(q_s[sl(r), :]), k_s[sl(r), :]) * HD ** (-0.5)
        scores = jnp.where(same, scores, -1e30)
        w = jnp.exp(scores - jnp.max(scores, -1, keepdims=True))
        pr = w / jnp.sum(w, -1, keepdims=True)
        probs[sl(r, heads * seq), :] = pr
        mixed = from_heads(nn(pr.astype(BF16), v_s[sl(r), :])).astype(BF16)
        mixed_s[sl(r), :] = mixed
        part[sl(r), :] = nn(mixed, wout[...])

        @pl.when(r == 0)
        def _():
            pl.semaphore_wait(barrier, 3 + jnp.minimum(z, 1) + jnp.minimum(L - 1 - z, 1))

        core_copy(0, r).start()
        lt[2 * ff : 2 * ff + loc, sl(r)] = mixed.T

    def grad_act(r):
        c = cot[sl(r), :]
        gact[sl(r), :] = nt(c, wdn[...])
        small_add(0, colsum(c.astype(F32)))

    def feed(r):
        @pl.loop(0, seq // SUB)
        def _(i):
            s = sub(r, i)
            v = start[s, :] + (tot[s, :] + outb[...])
            mid[s, :] = v
            xhat, _ = normed(v)
            e2[s, :] = (xhat * n2g[...] + n2b[...]).astype(BF16)

        hp[...] = nn(e2[sl(r), :], wup[...])

        @pl.loop(0, seq // SUB)
        def _(i):
            s = sub(r, i)
            u = hp[pl.ds(pl.multiple_of(i * SUB, SUB), SUB), :] + upb[...]
            cdf = 0.5 * (1.0 + lax.erf(u * 0.7071067811865476))
            act[s, :] = (u * cdf).astype(BF16)
            slope = cdf + u * (0.3989422804014327 * jnp.exp(-0.5 * u * u))
            pre = (gact[s, :] * slope).astype(BF16)
            gp[s, :] = pre
            small_add(1, colsum(pre.astype(F32)))

        part[sl(r), :] = nt(gp[sl(r), :], wup[...])
        core_copy(1, r).start()
        lt[0:ff, sl(r)] = act[sl(r), :].T
        lt[ff : 2 * ff, sl(r)] = e2[sl(r), :].T

    def back2(r):
        @pl.loop(0, seq // SUB)
        def _(i):
            s = sub(r, i)
            ge = tot[s, :]
            xhat, scale = normed(mid[s, :])
            small_add(2, colsum(ge * xhat))
            small_add(3, colsum(ge))
            gx = ge * n2g[...]
            gm = cot[s, :].astype(F32) + scale * (
                gx - jnp.mean(gx, -1, keepdims=True) - xhat * jnp.mean(gx * xhat, -1, keepdims=True)
            )
            gmid[s, :] = gm
            low = gm.astype(BF16)
            gbr[s, :] = low
            small_add(4, colsum(low.astype(F32)))

        g3 = by_head(nt(gbr[sl(r), :], wout[...]).astype(BF16))
        pr = probs[sl(r, heads * seq), :]
        grad_probs = nt(g3, v_s[sl(r), :])
        inner = jnp.sum(pr * grad_probs, -1, keepdims=True)
        ds = (pr * (grad_probs - inner)).astype(BF16)
        gq = (from_heads(nn(ds, k_s[sl(r), :])) * HD ** (-0.5)).astype(BF16)
        gk = (tn(ds, by_head(q_s[sl(r), :])) * HD ** (-0.5)).astype(BF16)
        gv = tn(pr.astype(BF16), g3).astype(BF16)
        part[sl(r), :] = nn(gq, wqkv[0]) + nn(gk, wqkv[1]) + nn(gv, wqkv[2])
        core_copy(2, r).start()
        late = 2 * ff + loc
        for i, v in enumerate((gq, gk, gv)):
            lt[late + i * loc : late + (i + 1) * loc, sl(r)] = v.T
        g[small + 7 : small + 8, 0:loc] += colsum(gq.astype(F32))
        g[small + 7 : small + 8, half : half + loc] += colsum(gv.astype(F32))

    def back1(r):
        tg[pl.ds(r, 1), :] = jnp.zeros((1, width), F32)

        @pl.loop(0, seq // SUB)
        def _(i):
            s = sub(r, i)
            ge = tot[s, :]
            xhat, scale = normed(start[s, :])
            small_add(5, colsum(ge * xhat))
            small_add(6, colsum(ge))
            gy = ge * n1g[...]
            gs = gmid[s, :] + scale * (
                gy - jnp.mean(gy, -1, keepdims=True) - xhat * jnp.mean(gy * xhat, -1, keepdims=True)
            )
            ig[s, :] = gs.astype(BF16)
            tg[pl.ds(r, 1), :] += colsum(gs)

    def down(r):
        part[sl(r), :] = nn(act[sl(r), :], wdn[...])
        core_copy(3, r).start()

    def finish(r):
        @pl.loop(0, seq // SUB)
        def _(i):
            s = sub(r, i)
            out[s, :] = (mid[s, :] + (tot[s, :] + dnb[...])).astype(BF16)

    blk = loc

    early = ff // blk

    def weight_grads(j):
        s = pl.ds(pl.multiple_of(j * blk, blk), blk)

        def by(right):
            def fn():
                g[s, :] = nn(lt[s, :], right[...])

            return fn

        when(j < early, by(cot))
        when((j >= early) & (j < 2 * early), by(gp))
        when(j == 2 * early, by(gbr))
        when(j > 2 * early, by(entry))

    def ok(u, n):
        return (u >= 0) & (u < n)

    def go(copy, u, depth):
        when(u >= depth, lambda: copy(u - depth).wait_send())
        copy(u).start()

    def end(copy, n, depth):
        for u in range(n - min(depth, n), n):
            copy(u).wait_send()

    def a_base(u):
        return (u // 3 * 5 + u % 3) * 4 * CH

    def x_slot(u):
        return pl.ds(pl.multiple_of(u % R["xr"].shape[0] * 2 * CH, CH), 2 * CH)

    def x_first(u):
        src = pl.ds(pl.multiple_of(a_base(u) + (1 - x) * 2 * CH, CH), 2 * CH)
        return remote(
            g.at[src], R["xrb"].at[x_slot(u)], R["xs"].at[u % SENDS], R["xr"].at[u % R["xr"].shape[0]], to_x
        )

    class Way:
        def __init__(self, kind, d):
            self.kind, self.d = kind, d
            self.two = kind != "a"
            self.w = z if d == 0 else L - 1 - z
            self.up = (zhi if d == 0 else zlo, mp)
            self.dn = (zlo if d == 0 else zhi, mp)
            self.root = 0 if kind == "c" else D - 1
            self.depth = L - 1 - self.root
            self.n = {"a": UA, "b": UB, "c": UC}[kind]
            self.first = {"a": LAG, "b": 0, "c": 1}[kind]
            self.stride = 3 if self.two else 1
            self.gap = LAG if self.two else 0
            self.rows = 2 * CH if self.two else CH
            self.lo, self.hi = R[kind + "lo"], R[kind + "hi"]
            self.sems = {t: R[kind + "_" + t] for t in ("s", "r", "u", "d", "t", "xs", "xr")}
            self.flight, self.W = self.sems["s"].shape[1], self.sems["r"].shape[1]

        def unit(self, t, offset):
            rel = t - self.first - offset
            return rel // self.stride, (rel >= 0) & (rel < self.n * self.stride) & (rel % self.stride == 0)

        def own(self, u):
            if self.two:
                base = jnp.minimum(u * 5 + (3 if self.kind == "b" else 4), UA + UB + UC - 1) * 4 * CH
            else:
                base = a_base(u) + x * 2 * CH
            return pl.ds(pl.multiple_of(base + self.d * self.rows, CH), self.rows)

        def slot(self, u):
            return pl.ds(pl.multiple_of(u % self.W * self.rows, CH), self.rows)

        def copy(self, src, dst, ssem, rsem, u, dev):
            return remote(
                src, dst, self.sems[ssem].at[self.d, u % self.flight], self.sems[rsem].at[self.d, u % self.W], dev
            )

        def send_up(self, u):
            return self.copy(g.at[self.own(u)], self.lo.at[self.d, self.slot(u)], "s", "r", u, self.up)

        def send_up_root(self, u):
            return self.copy(g.at[self.own(u)], self.lo.at[self.d, self.slot(u)], "s", "t", u, self.up)

        def send_dn(self, u):
            return self.copy(g.at[self.own(u)], self.hi.at[self.d, self.slot(u)], "s", "r", u, self.dn)

        def total_up(self, u):
            return self.copy(f.at[self.own(u)], f.at[self.own(u)], "u", "t", u, self.up)

        def total_dn(self, u):
            return self.copy(f.at[self.own(u)], f.at[self.own(u)], "d", "t", u, self.dn)

        def x_copy(self, u):
            if self.two:
                return self.copy(g.at[self.own(u)], R[self.kind + "xb"].at[self.d, self.slot(u)], "xs", "xr", u, to_x)
            return self.copy(f.at[self.own(u)], f.at[self.own(u)], "xs", "xr", u, to_x)

        def go(self, copy, u):
            go(copy, u, self.flight)

        def reduce(self, u):
            w, root, own = self.w, self.root, self.own(u)

            def from_low():
                when(w < root, lambda: self.send_up(u).wait_recv())
                when(w == root, lambda: self.send_up_root(u).wait_recv())
                g[own, :] += self.lo[self.d, self.slot(u), :]

            def from_high():
                self.send_dn(u).wait_recv()
                g[own, :] += self.hi[self.d, self.slot(u), :]

            if root > 0:
                when((w > 0) & (w <= root), from_low)
            when((w < L - 1) & (w >= root), from_high)
            if root > 1:
                when(w < root - 1, lambda: self.go(self.send_up, u))
            if root > 0:
                when(w == root - 1, lambda: self.go(self.send_up_root, u))
            when(w > root, lambda: self.go(self.send_dn, u))
            if self.two:
                when(w == root, lambda: self.go(self.x_copy, u))

        def turn(self, u):
            own = self.own(u)
            if self.two:
                self.x_copy(u).wait_recv()
                f[own, :] = g[own, :] + R[self.kind + "xb"][self.d, self.slot(u), :]
            else:
                f[own, :] = g[own, :]
            self.go(self.total_up, u)
            if self.root > 0:
                self.go(self.total_dn, u)
            if not self.two:
                self.go(self.x_copy, u)

        def spread(self, u):
            w, root = self.w, self.root
            self.total_up(u).wait_recv()
            when((w > root) & (w < L - 1), lambda: self.go(self.total_up, u))
            if root > 1:
                when((w < root) & (w > 0), lambda: self.go(self.total_dn, u))
            if not self.two:
                self.go(self.x_copy, u)

        def tick(self, t):
            w, root = self.w, self.root
            dist = jnp.abs(w - root) * LAG
            u, valid = self.unit(t, self.depth * LAG - dist)
            when(valid, lambda: self.reduce(u))
            v, valid_v = self.unit(t, self.depth * LAG + self.gap)
            when(valid_v & (w == root), lambda: self.turn(v))
            q, valid_q = self.unit(t, self.depth * LAG + self.gap + dist)
            when(valid_q & (w != root), lambda: self.spread(q))
            if not self.two:
                e, valid_e = self.unit(t, self.depth * LAG + self.gap + dist + LAG)
                when(valid_e, lambda: self.x_copy(e).wait_recv())

        def drain(self):
            w, root, n, flight = self.w, self.root, self.n, self.flight
            if root > 1:
                when(w < root - 1, lambda: end(self.send_up, n, flight))
            if root > 0:
                when(w == root - 1, lambda: end(self.send_up_root, n, flight))
                when((w <= root) & (w > 0), lambda: end(self.total_dn, n, flight))
            when(w > root, lambda: end(self.send_dn, n, flight))
            when((w >= root) & (w < L - 1), lambda: end(self.total_up, n, flight))
            if self.two:
                when(w == root, lambda: end(self.x_copy, n, flight))
            else:
                end(self.x_copy, n, flight)

    ways = [Way(kind, d) for kind in ("c", "b", "a") for d in (0, 1)]

    def dp_tick(t):
        when(t < UA, lambda: go(x_first, t, SENDS))

        def x_add():
            u = t - LAG
            x_first(u).wait_recv()
            s = pl.ds(pl.multiple_of(a_base(u) + x * 2 * CH, CH), 2 * CH)
            g[s, :] += R["xrb"][x_slot(u), :]

        when(ok(t - LAG, UA), x_add)
        for way in ways:
            way.tick(t)

    def dp_drain():
        end(x_first, UA, SENDS)
        for way in ways:
            way.drain()

    for copy in loads.values():
        copy.start()

    def vector(i, name):
        loads[name].wait()
        R["vecs"][i : i + 1, :] = R[name][...][None, :]

    g[small : small + 4 * CH, :] = jnp.zeros((4 * CH, width), F32)
    for name in ("tok", "tim"):
        loads[name].wait()
    timf[...] = tim[...].astype(F32)
    vector(0, "n1g")
    vector(1, "n1b")

    @pl.loop(0, rows_n)
    def _(r):
        norm1(r)

        @pl.when(r == 0)
        def _():
            for name in ("wqkv", "qvb", "seg", "wout"):
                loads[name].wait()

        project(r)
        attend(r)
        sum_b(0, r)

    for name in ("cot", "wdn", "wup"):
        loads[name].wait()
    for i, name in enumerate(("outb", "n2g", "n2b", "upb", "dnb")):
        vector(2 + i, name)

    @pl.loop(0, rows_n)
    def _(r):
        grad_act(r)
        when(r > 0, lambda: sum_b(1, r - 1))
        sum_c(0, r)
        sum_d(0, r)
        feed(r)

    weight_grads(jnp.int32(0))

    blocks = (2 * ff + 4 * loc) // blk
    per = blk // (4 * CH)
    a_last = LAG * (2 * D + 2)
    b_last, c_last = LAG * (L + 1), LAG * (2 * L - 1)
    ticks = max(UA + a_last, 3 * UB - 2 + b_last, 3 * UC - 1 + c_last)

    def out_copy(j):
        s = pl.ds(j * blk, blk if j < blocks else 4 * CH)
        return pltpu.make_async_copy(f.at[s], f_out.at[s], R["fin"].at[j])

    done_copies = [
        pltpu.make_async_copy(a, b, R["fin"].at[blocks + 1 + i])
        for i, (a, b) in enumerate(((ig, ig_o), (tg, tg_o), (out, out_o)))
    ]

    @pl.loop(0, ticks)
    def _(t):
        dp_tick(t)

        def at(first, step, fn):
            r = (t - first) // step
            when((t >= first) & ((t - first) % step == 0) & (r < rows_n), lambda: fn(r))

        when(t == 0, lambda: sum_b(1, rows_n - 1))
        at(2, 3, lambda r: sum_c(1, r))

        def second(r):
            sum_d(1, r)
            back2(r)

        at(3, 3, second)
        at(4, 3, lambda r: sum_b(2, r))
        at(10, 3, lambda r: sum_c(2, r))

        def third(r):
            sum_d(2, r)
            back1(r)

        at(11, 3, third)
        at(12, 3, down)
        at(13, 3, lambda r: sum_b(3, r))
        at(18, 3, lambda r: sum_c(3, r))

        def fourth(r):
            sum_d(3, r)
            finish(r)

        at(19, 3, fourth)

        @pl.when(t == 19 + 3 * rows_n)
        def _():
            for copy in done_copies:
                copy.start()

        when((t % 3 == 1) & (t < 3 * blocks - 2), lambda: weight_grads((t + 2) // 3))
        for j in range(blocks):
            done = (per * (j + 1) - 1) // 5 * 3 + 2 + max(a_last, c_last)
            if done < ticks:
                when(t == done, lambda: out_copy(j).start())

    dp_drain()
    for j in range(blocks + 1):
        if j == blocks or (per * (j + 1) - 1) // 5 * 3 + 2 + max(a_last, c_last) >= ticks:
            out_copy(j).start()
    for copy in done_copies + [out_copy(j) for j in range(blocks + 1)]:
        copy.wait()


def shards(n_dp, *args):
    (tok, tim, seg, n1g, n1b, wqkv, qvb, wout, outb, n2g, n2b, wup, upb, wdn, dnb, cot) = args
    tokens, width = tok.shape
    rows_n, seq = seg.shape
    loc, ff = wout.shape[0], wup.shape[1]
    heads = loc // HD
    half = width // 2
    big = 2 * ff + 4 * loc
    count = big // (4 * CH) + 1
    UC = count // 5
    UB = UC + (count % 5) // 3
    UA = count - UB - UC
    L = n_dp // 2
    LAG = hop_ticks(L)
    vm = pltpu.VMEM
    dma = pltpu.SemaphoreType.DMA
    W = LAG * L + 2
    WX = 2 * LAG + 2
    WB = LAG * (L + 1) // 3 + 2
    WC = LAG * (2 * L - 1) // 3 + 2
    total = count * 4 * CH
    slots = lambda w, rows: vm((2, w * rows, width), F32)
    flat = lambda n: vm((n,), F32)
    scratch = dict(
        tok=vm((tokens, width), BF16),
        cot=vm((tokens, width), BF16),
        wqkv=vm((3, loc, width), BF16),
        wout=vm((loc, width), BF16),
        wup=vm((width, ff), BF16),
        wdn=vm((ff, width), BF16),
        ins=dma((16,)),
        tim=vm((rows_n, width), BF16),
        seg=vm((rows_n, seq), jnp.int32),
        qvb=vm((2, loc), F32),
        **{s: flat(width) for s in ("n1g", "n1b", "outb", "n2g", "n2b", "dnb")},
        upb=flat(ff),
        vecs=vm((8, width), F32),
        timf=vm((rows_n, width), F32),
        start=vm((tokens, width), F32),
        entry=vm((tokens, width), BF16),
        q=vm((tokens, loc), BF16),
        k=vm((tokens, loc), BF16),
        v=vm((tokens, loc), BF16),
        probs=vm((heads * tokens, seq), F32),
        mixed=vm((tokens, loc), BF16),
        part=vm((tokens, width), F32),
        cr=vm((tokens, half), F32),
        ys=vm((tokens, half), F32),
        yr=vm((2, tokens, half), F32),
        tot=vm((tokens, width), F32),
        mid=vm((tokens, width), F32),
        e2=vm((tokens, width), BF16),
        hp=vm((seq, ff), F32),
        act=vm((tokens, ff), BF16),
        gp=vm((tokens, ff), BF16),
        gact=vm((tokens, ff), F32),
        gmid=vm((tokens, width), F32),
        gbr=vm((tokens, width), BF16),
        out=vm((tokens, width), BF16),
        ig=vm((tokens, width), BF16),
        tg=vm((rows_n, width), F32),
        lt=vm((big, tokens), BF16),
        g=vm((total, width), F32),
        f=vm((total, width), F32),
        xrb=vm((WX * 2 * CH, width), F32),
        alo=slots(W, CH),
        ahi=slots(W, CH),
        blo=slots(WB, 2 * CH),
        bhi=slots(WB, 2 * CH),
        bxb=slots(WB, 2 * CH),
        clo=slots(1, 2 * CH),
        chi=slots(WC, 2 * CH),
        cxb=slots(WC, 2 * CH),
        **{s: dma((rows_n,)) for s in ("cs", "crs", "yss", "gs", "grs")},
        yrs=dma((2, rows_n)),
        fin=dma((big // loc + 4,)),
        xs=dma((SENDS,)),
        xr=dma((WX,)),
        **{k + "_" + s: dma((2, SENDS if k == "a" else 2)) for k in "abc" for s in ("s", "u", "d", "xs")},
        **{k + "_" + s: dma((2, w)) for k, w in (("a", W), ("b", WB), ("c", WC)) for s in ("r", "t", "xr")},
    )
    any_spec = pl.BlockSpec(memory_space=pl.ANY)
    vm_spec = pl.BlockSpec(memory_space=pltpu.VMEM)
    out, ig, tg, f = pl.pallas_call(
        functools.partial(kernel, n_dp, (UA, UB, UC), tuple(scratch)),
        out_shape=(
            jax.ShapeDtypeStruct((tokens, width), BF16),
            jax.ShapeDtypeStruct((tokens, width), BF16),
            jax.ShapeDtypeStruct((rows_n, width), F32),
            jax.ShapeDtypeStruct((total, width), F32),
        ),
        in_specs=[any_spec] * 16,
        out_specs=(any_spec,) * 4,
        scratch_shapes=list(scratch.values()),
        compiler_params=pltpu.CompilerParams(
            collective_id=0, has_side_effects=True, vmem_limit_bytes=63 * 2**20
        ),
        cost_estimate=pl.CostEstimate(flops=6 * 10**9, bytes_accessed=20 * 10**6, transcendentals=0),
    )(
        tok, tim, seg, n1g, n1b, wqkv.transpose(0, 2, 1), qvb, wout, outb, n2g, n2b, wup, upb, wdn, dnb, cot
    )
    f32 = lambda *shape: jax.ShapeDtypeStruct(shape, F32)
    moved = (
        jax.ShapeDtypeStruct((tokens, width), BF16),
        jax.ShapeDtypeStruct((tokens, width), BF16),
        f32(rows_n, width),
        f32(3, loc, width),
        f32(loc, width),
        f32(width, ff),
        f32(ff, width),
    )
    results = pl.pallas_call(
        functools.partial(place, big),
        out_shape=moved + (f32(2, loc), f32(ff)) + (f32(width),) * 6,
        in_specs=[any_spec] * 4,
        out_specs=(any_spec,) * 7 + (vm_spec,) * 8,
        scratch_shapes=[
            vm((8, width), F32),
            vm((big, width), F32),
            vm((tokens, width), BF16),
            vm((tokens, width), BF16),
            vm((rows_n, width), F32),
            dma((10,)),
            dma((10,)),
        ],
        compiler_params=pltpu.CompilerParams(vmem_limit_bytes=63 * 2**20),
    )(out, ig, tg, f)
    out, ig, tg, qkv, outw, up, down, qvb, upb, downb, n2g, n2b, outb, n1g, n1b = results
    return out, ig, tg, n1g, n1b, qkv.transpose(0, 2, 1), qvb, outw, outb, n2g, n2b, up, upb, down, downb


def place(big, *refs):
    out, ig, tg, f, out_o, ig_o, tg_o, qkv, outw, up, down, qvb, upb, downb = refs[:14]
    n2g, n2b, outb, n1g, n1b, sm, buf, vo, vi, vt, sem, sem_o = refs[14:]
    loc, ff = outw.shape[0], down.shape[0]
    half = f.shape[1] // 2
    moves = []
    row = 0
    for n, ref in ((ff, down), (ff, up), (loc, outw), (loc, qkv.at[0]), (loc, qkv.at[1]), (loc, qkv.at[2])):
        s = pl.ds(row, n)
        moves.append((f.at[s], buf.at[s], ref))
        row += n
    moves += [(out, vo, out_o), (ig, vi, ig_o), (tg, vt, tg_o)]
    first = pltpu.make_async_copy(f.at[pl.ds(big, 8)], sm, sem.at[9])
    first.start()
    loads = [pltpu.make_async_copy(a, v, sem.at[i]) for i, (a, v, b) in enumerate(moves)]
    stores = [pltpu.make_async_copy(v, b, sem_o.at[i]) for i, (a, v, b) in enumerate(moves)]
    for copy in loads:
        copy.start()
    for load, store in zip(loads, stores):
        load.wait()
        store.start()
    first.wait()
    for i, ref in enumerate((downb, upb, n2g, n2b, outb, n1g, n1b)):
        ref[...] = sm[i : i + 1, :].reshape(ref.shape)
    qvb[0:1, :] = sm[7:8, 0:loc]
    qvb[1:2, :] = sm[7:8, half : half + loc]
    for copy in stores:
        copy.wait()


def solution(mesh):
    placed = (
        P("dp", None),
        P("dp", None),
        P("dp", None),
        P(),
        P(),
        P(None, None, "mp"),
        P(None, "mp"),
        P("mp", None),
        P(),
        P(),
        P(),
        P(None, "mp"),
        P("mp"),
        P("mp", None),
        P(),
        P("dp", None),
    )
    return jax.shard_map(
        functools.partial(shards, mesh.shape["dp"]),
        mesh=mesh,
        in_specs=placed,
        out_specs=(
            P("dp", None),
            P("dp", None),
            P("dp", None),
            P(),
            P(),
            P(None, None, "mp"),
            P(None, "mp"),
            P("mp", None),
            P(),
            P(),
            P(),
            P(None, "mp"),
            P("mp"),
            P("mp", None),
            P(),
        ),
        check_vma=False,
    )
```

```python
import functools

import jax
import jax.numpy as jnp
from jax import lax
from jax.experimental import pallas as pl
from jax.experimental.pallas import tpu as pltpu
from jax.sharding import PartitionSpec as P

HD = 64
SUB = 128
CH = 8
SENDS = 4
MESH = pl.DeviceIdType.MESH
F32 = jnp.float32
BF16 = jnp.bfloat16


ARGS = ("tok", "tim", "seg", "n1g", "n1b", "wqkv", "qvb", "wout", "outb", "n2g", "n2b")
ARGS += ("wup", "upb", "wdn", "dnb", "cot")


def hop_ticks(line):
    return 2 if line <= 8 else 1


def direct_units(line):
    return (2, 0, 1) if line <= 8 else (0, 0, 0)


def when(cond, fn):
    pl.when(cond)(fn)


def nt(a, b):
    return lax.dot_general(a, b, (((1,), (1,)), ((), ())), preferred_element_type=F32)


def tn(a, b):
    return lax.dot_general(a, b, (((0,), (0,)), ((), ())), preferred_element_type=F32)


def nn(a, b):
    return jnp.dot(a, b, preferred_element_type=F32)


def normed(v):
    centred = v - jnp.mean(v, -1, keepdims=True)
    spread = jnp.mean(centred * centred, -1, keepdims=True)
    scale = lax.rsqrt(spread + 1e-05)
    return centred * scale, scale


def colsum(v):
    return jnp.sum(v, 0, keepdims=True)


def kernel(n_dp, units, names, *refs):
    out_o, ig_o, tg_o, f_out = refs[16:20]
    R = dict(zip(names, refs[20:]))
    order = ("tok", "tim", "n1g", "n1b", "wqkv", "qvb", "seg", "wout", "outb", "cot", "wdn")
    order += ("n2g", "n2b", "wup", "upb", "dnb")
    tok, tim, wqkv, qvb, seg, wout, cot, wdn, wup = (
        R[s] for s in ("tok", "tim", "wqkv", "qvb", "seg", "wout", "cot", "wdn", "wup")
    )
    loads = {
        name: pltpu.make_async_copy(refs[ARGS.index(name)], R[name], R["ins"].at[i]) for i, name in enumerate(order)
    }
    n1g, n1b, outb, n2g, n2b, upb, dnb = (R["vecs"].at[pl.ds(i, 1)] for i in range(7))
    timf, start, entry, q_s, k_s, v_s = (R[s] for s in ("timf", "start", "entry", "q", "k", "v"))
    probs, mixed_s, part, cr, ys, yr = (R[s] for s in ("probs", "mixed", "part", "cr", "ys", "yr"))
    tot, mid, e2, hp, act, gp = (R[s] for s in ("tot", "mid", "e2", "hp", "act", "gp"))
    out, ig, tg = (R[s] for s in ("out", "ig", "tg"))
    gact, gmid, gbr, lt, g, f = (R[s] for s in ("gact", "gmid", "gbr", "lt", "g", "f"))

    rows_n, seq = seg.shape
    width = tok.shape[1]
    half = width // 2
    loc = wout.shape[0]
    heads = loc // HD
    ff = wup.shape[1]
    UA, UB, UC = units
    L = n_dp // 2
    LAG = hop_ticks(L)
    DIRECT = direct_units(L)
    D = L // 2
    root = D - 1
    dp = lax.axis_index("dp")
    mp = lax.axis_index("mp")
    core = mp % 2
    x = dp % 2
    z = dp // 2
    to_core = (dp, mp + 1 - 2 * core)
    to_y = (dp, (mp + 2) % 4)
    to_x = (dp + 1 - 2 * x, mp)
    zlo = jnp.maximum(z - 1, 0) * 2 + x
    zhi = jnp.minimum(z + 1, L - 1) * 2 + x

    barrier = pltpu.get_barrier_semaphore()
    for dev in (to_core, to_y, to_x):
        pl.semaphore_signal(barrier, 1, device_id=dev, device_id_type=MESH)
    when(z > 0, lambda: pl.semaphore_signal(barrier, 1, device_id=(zlo, mp), device_id_type=MESH))
    when(z < L - 1, lambda: pl.semaphore_signal(barrier, 1, device_id=(zhi, mp), device_id_type=MESH))
    greeted = 3 + jnp.minimum(z, 1) + jnp.minimum(L - 1 - z, 1)

    def sl(r, n=seq):
        return pl.ds(pl.multiple_of(r * n, n), n)

    def sub(r, i):
        return pl.ds(pl.multiple_of(r * seq + i * SUB, SUB), SUB)

    mine = pl.ds(pl.multiple_of(core * half, 128), half)
    other = pl.ds(pl.multiple_of((1 - core) * half, 128), half)

    def remote(src, dst, ssem, rsem, dev):
        return pltpu.make_async_remote_copy(
            src_ref=src, dst_ref=dst, send_sem=ssem, recv_sem=rsem, device_id=dev, device_id_type=MESH
        )

    def core_copy(p, r):
        return remote(part.at[sl(r), other], cr.at[sl(r)], R["cs"].at[r], R["crs"].at[r], to_core)

    def y_copy(p, r):
        return remote(ys.at[sl(r)], yr.at[p % 2, sl(r)], R["yss"].at[r], R["yrs"].at[p % 2, r], to_y)

    def ag_copy(p, r):
        return remote(tot.at[sl(r), mine], tot.at[sl(r), mine], R["gs"].at[r], R["grs"].at[r], to_core)

    def sum_b(p, r):
        core_copy(p, r).wait()
        ys[sl(r), :] = part[sl(r), mine] + cr[sl(r), :]
        y_copy(p, r).start()

    def sum_c(p, r):
        y_copy(p, r).wait()
        tot[sl(r), mine] = ys[sl(r), :] + yr[p % 2, sl(r), :]
        ag_copy(p, r).start()

    def sum_d(p, r):
        ag_copy(p, r).wait()

    def vec(ref):
        return ref[...]

    small = 2 * ff + 4 * loc

    def small_add(i, v):
        g[small + i : small + i + 1, :] += v

    lane = lax.broadcasted_iota(jnp.int32, (1, loc), 1)
    masks = [((lane >= h * HD) & (lane < (h + 1) * HD)).astype(F32) for h in range(heads)]

    def by_head(v):
        return jnp.concatenate([v * m.astype(BF16) for m in masks], 0)

    def from_heads(v):
        total = v[:seq] * masks[0]
        for h in range(1, heads):
            total = total + v[h * seq : (h + 1) * seq] * masks[h]
        return total

    def norm1(r):
        @pl.loop(0, seq // SUB)
        def _(i):
            s = sub(r, i)
            v = tok[s, :].astype(F32) + timf[pl.ds(r, 1), :]
            start[s, :] = v
            xhat, _ = normed(v)
            entry[s, :] = (xhat * n1g[...] + n1b[...]).astype(BF16)

    def project(r):
        e = entry[sl(r), :]
        q_s[sl(r), :] = (nt(e, wqkv[0]) + qvb[0:1, :]).astype(BF16)
        k_s[sl(r), :] = nt(e, wqkv[1]).astype(BF16)
        v_s[sl(r), :] = (nt(e, wqkv[2]) + qvb[1:2, :]).astype(BF16)

    def attend(r):
        labels = jnp.broadcast_to(seg[pl.ds(r, 1), :], (seq, seq))
        same = labels == labels.T
        same = jnp.concatenate([same.astype(F32)] * heads, 0) > 0.5
        scores = nt(by_head(q_s[sl(r), :]), k_s[sl(r), :]) * HD ** (-0.5)
        scores = jnp.where(same, scores, -1e30)
        w = jnp.exp(scores - jnp.max(scores, -1, keepdims=True))
        pr = w / jnp.sum(w, -1, keepdims=True)
        probs[sl(r, heads * seq), :] = pr
        mixed = from_heads(nn(pr.astype(BF16), v_s[sl(r), :])).astype(BF16)
        mixed_s[sl(r), :] = mixed
        part[sl(r), :] = nn(mixed, wout[...])

        @pl.when(r == 0)
        def _():
            pl.semaphore_wait(barrier, greeted)

        core_copy(0, r).start()
        lt[2 * ff : 2 * ff + loc, sl(r)] = mixed.T

    def grad_act(r):
        c = cot[sl(r), :]
        gact[sl(r), :] = nt(c, wdn[...])
        small_add(0, colsum(c.astype(F32)))

    def feed(r):
        @pl.loop(0, seq // SUB)
        def _(i):
            s = sub(r, i)
            v = start[s, :] + (tot[s, :] + outb[...])
            mid[s, :] = v
            xhat, _ = normed(v)
            e2[s, :] = (xhat * n2g[...] + n2b[...]).astype(BF16)

        hp[...] = nn(e2[sl(r), :], wup[...])

        @pl.loop(0, seq // SUB)
        def _(i):
            s = sub(r, i)
            u = hp[pl.ds(pl.multiple_of(i * SUB, SUB), SUB), :] + upb[...]
            cdf = 0.5 * (1.0 + lax.erf(u * 0.7071067811865476))
            act[s, :] = (u * cdf).astype(BF16)
            slope = cdf + u * (0.3989422804014327 * jnp.exp(-0.5 * u * u))
            pre = (gact[s, :] * slope).astype(BF16)
            gp[s, :] = pre
            small_add(1, colsum(pre.astype(F32)))

        part[sl(r), :] = nt(gp[sl(r), :], wup[...])
        core_copy(1, r).start()
        lt[0:ff, sl(r)] = act[sl(r), :].T
        lt[ff : 2 * ff, sl(r)] = e2[sl(r), :].T

    def back2(r):
        @pl.loop(0, seq // SUB)
        def _(i):
            s = sub(r, i)
            ge = tot[s, :]
            xhat, scale = normed(mid[s, :])
            small_add(2, colsum(ge * xhat))
            small_add(3, colsum(ge))
            gx = ge * n2g[...]
            gm = cot[s, :].astype(F32) + scale * (
                gx - jnp.mean(gx, -1, keepdims=True) - xhat * jnp.mean(gx * xhat, -1, keepdims=True)
            )
            gmid[s, :] = gm
            low = gm.astype(BF16)
            gbr[s, :] = low
            small_add(4, colsum(low.astype(F32)))

        g3 = by_head(nt(gbr[sl(r), :], wout[...]).astype(BF16))
        pr = probs[sl(r, heads * seq), :]
        grad_probs = nt(g3, v_s[sl(r), :])
        inner = jnp.sum(pr * grad_probs, -1, keepdims=True)
        ds = (pr * (grad_probs - inner)).astype(BF16)
        gq = (from_heads(nn(ds, k_s[sl(r), :])) * HD ** (-0.5)).astype(BF16)
        gk = (tn(ds, by_head(q_s[sl(r), :])) * HD ** (-0.5)).astype(BF16)
        gv = tn(pr.astype(BF16), g3).astype(BF16)
        part[sl(r), :] = nn(gq, wqkv[0]) + nn(gk, wqkv[1]) + nn(gv, wqkv[2])
        core_copy(2, r).start()
        late = 2 * ff + loc
        for i, v in enumerate((gq, gk, gv)):
            lt[late + i * loc : late + (i + 1) * loc, sl(r)] = v.T
        g[small + 7 : small + 8, 0:loc] += colsum(gq.astype(F32))
        g[small + 7 : small + 8, half : half + loc] += colsum(gv.astype(F32))

    def back1(r):
        tg[pl.ds(r, 1), :] = jnp.zeros((1, width), F32)

        @pl.loop(0, seq // SUB)
        def _(i):
            s = sub(r, i)
            ge = tot[s, :]
            xhat, scale = normed(start[s, :])
            small_add(5, colsum(ge * xhat))
            small_add(6, colsum(ge))
            gy = ge * n1g[...]
            gs = gmid[s, :] + scale * (
                gy - jnp.mean(gy, -1, keepdims=True) - xhat * jnp.mean(gy * xhat, -1, keepdims=True)
            )
            ig[s, :] = gs.astype(BF16)
            tg[pl.ds(r, 1), :] += colsum(gs)

    def down(r):
        part[sl(r), :] = nn(act[sl(r), :], wdn[...])
        core_copy(3, r).start()

    def finish(r):
        @pl.loop(0, seq // SUB)
        def _(i):
            s = sub(r, i)
            out[s, :] = (mid[s, :] + (tot[s, :] + dnb[...])).astype(BF16)

    blk = loc

    early = ff // blk

    def weight_grads(j):
        s = pl.ds(pl.multiple_of(j * blk, blk), blk)

        def by(right):
            def fn():
                g[s, :] = nn(lt[s, :], right[...])

            return fn

        when(j < early, by(cot))
        when((j >= early) & (j < 2 * early), by(gp))
        when(j == 2 * early, by(gbr))
        when(j > 2 * early, by(entry))

    def ok(u, n):
        return (u >= 0) & (u < n)

    def go(copy, u, depth):
        when(u >= depth, lambda: copy(u - depth).wait_send())
        copy(u).start()

    def end(copy, n, depth):
        for u in range(n - min(depth, n), n):
            copy(u).wait_send()

    def a_base(u):
        return (u // 3 * 5 + u % 3) * 4 * CH

    def x_slot(u):
        return pl.ds(pl.multiple_of(u % R["xr"].shape[0] * 2 * CH, CH), 2 * CH)

    def x_first(u):
        src = pl.ds(pl.multiple_of(a_base(u) + (1 - x) * 2 * CH, CH), 2 * CH)
        return remote(
            g.at[src], R["xrb"].at[x_slot(u)], R["xs"].at[u % SENDS], R["xr"].at[u % R["xr"].shape[0]], to_x
        )

    class Way:
        def __init__(self, kind, d):
            self.kind, self.d = kind, d
            self.two = kind != "a"
            self.w = z if d == 0 else L - 1 - z
            self.up = (zhi if d == 0 else zlo, mp)
            self.dn = (zlo if d == 0 else zhi, mp)
            self.root = 0 if kind == "c" else D - 1
            self.depth = L - 1 - self.root
            self.n = {"a": UA, "b": UB, "c": UC}[kind]
            self.first = {"a": LAG, "b": 0, "c": 1}[kind]
            self.stride = 3 if self.two else 1
            self.gap = LAG if self.two else 0
            self.rows = 2 * CH if self.two else CH
            self.lo, self.hi = R[kind + "lo"], R[kind + "hi"]
            self.sems = {t: R[kind + "_" + t] for t in ("s", "r", "u", "d", "t", "xs", "xr")}
            self.flight, self.W = self.sems["s"].shape[1], self.sems["r"].shape[1]
            self.normal = self.n - DIRECT["abc".index(kind)]

        def column(self, w):
            return ((w if self.d == 0 else L - 1 - w) * 2 + x, mp)

        def straight(self, u, w):
            own = self.own(u)
            ssem, rsem = R[self.kind + "_q"].at[self.d, w], self.sems["t"].at[self.d, u % self.W]
            return remote(f.at[own], f.at[own], ssem, rsem, self.column(w))

        def straight_all(self, u, what):
            for w in range(L):
                if w != self.root:
                    getattr(self.straight(u, w), what)()

        def unit(self, t, offset):
            rel = t - self.first - offset
            return rel // self.stride, (rel >= 0) & (rel < self.n * self.stride) & (rel % self.stride == 0)

        def own(self, u):
            if self.two:
                base = jnp.minimum(u * 5 + (3 if self.kind == "b" else 4), UA + UB + UC - 1) * 4 * CH
            else:
                base = a_base(u) + x * 2 * CH
            return pl.ds(pl.multiple_of(base + self.d * self.rows, CH), self.rows)

        def slot(self, u):
            return pl.ds(pl.multiple_of(u % self.W * self.rows, CH), self.rows)

        def copy(self, src, dst, ssem, rsem, u, dev):
            return remote(
                src, dst, self.sems[ssem].at[self.d, u % self.flight], self.sems[rsem].at[self.d, u % self.W], dev
            )

        def send_up(self, u):
            return self.copy(g.at[self.own(u)], self.lo.at[self.d, self.slot(u)], "s", "r", u, self.up)

        def send_up_root(self, u):
            return self.copy(g.at[self.own(u)], self.lo.at[self.d, self.slot(u)], "s", "t", u, self.up)

        def send_dn(self, u):
            return self.copy(g.at[self.own(u)], self.hi.at[self.d, self.slot(u)], "s", "r", u, self.dn)

        def total_up(self, u):
            return self.copy(f.at[self.own(u)], f.at[self.own(u)], "u", "t", u, self.up)

        def total_dn(self, u):
            return self.copy(f.at[self.own(u)], f.at[self.own(u)], "d", "t", u, self.dn)

        def x_copy(self, u):
            if self.two:
                return self.copy(g.at[self.own(u)], R[self.kind + "xb"].at[self.d, self.slot(u)], "xs", "xr", u, to_x)
            return self.copy(f.at[self.own(u)], f.at[self.own(u)], "xs", "xr", u, to_x)

        def go(self, copy, u):
            go(copy, u, self.flight)

        def reduce(self, u):
            w, root, own = self.w, self.root, self.own(u)

            def from_low():
                when(w < root, lambda: self.send_up(u).wait_recv())
                when(w == root, lambda: self.send_up_root(u).wait_recv())
                g[own, :] += self.lo[self.d, self.slot(u), :]

            def from_high():
                self.send_dn(u).wait_recv()
                g[own, :] += self.hi[self.d, self.slot(u), :]

            if root > 0:
                when((w > 0) & (w <= root), from_low)
            when((w < L - 1) & (w >= root), from_high)
            if root > 1:
                when(w < root - 1, lambda: self.go(self.send_up, u))
            if root > 0:
                when(w == root - 1, lambda: self.go(self.send_up_root, u))
            when(w > root, lambda: self.go(self.send_dn, u))
            if self.two:
                when(w == root, lambda: self.go(self.x_copy, u))

        def turn(self, u):
            own = self.own(u)
            if self.two:
                self.x_copy(u).wait_recv()
                f[own, :] = g[own, :] + R[self.kind + "xb"][self.d, self.slot(u), :]
            else:
                f[own, :] = g[own, :]

            def near():
                self.go(self.total_up, u)
                if self.root > 0:
                    self.go(self.total_dn, u)

            def far():
                when(u > self.normal, lambda: self.straight_all(u - 1, "wait_send"))
                self.straight_all(u, "start")

            if self.normal < self.n:
                when(u < self.normal, near)
                when(u >= self.normal, far)
            else:
                near()
            if not self.two:
                self.go(self.x_copy, u)

        def spread(self, u):
            w, root = self.w, self.root
            self.total_up(u).wait_recv()
            when((w > root) & (w < L - 1), lambda: self.go(self.total_up, u))
            if root > 1:
                when((w < root) & (w > 0), lambda: self.go(self.total_dn, u))
            if not self.two:
                self.go(self.x_copy, u)

        def tick(self, t):
            w, root = self.w, self.root
            dist = jnp.abs(w - root) * LAG
            u, valid = self.unit(t, self.depth * LAG - dist)
            when(valid, lambda: self.reduce(u))
            v, valid_v = self.unit(t, self.depth * LAG + self.gap)
            when(valid_v & (w == root), lambda: self.turn(v))
            after = self.depth * LAG + self.gap
            q, valid_q = self.unit(t, after + dist)
            when(valid_q & (w != root) & (q < self.normal), lambda: self.spread(q))
            if not self.two:
                e, valid_e = self.unit(t, after + dist + LAG)
                when(valid_e & (e < self.normal), lambda: self.x_copy(e).wait_recv())
            if self.normal < self.n:
                h, valid_h = self.unit(t, after + LAG)

                def arrive():
                    self.total_up(h).wait_recv()
                    if not self.two:
                        self.go(self.x_copy, h)

                when(valid_h & (h >= self.normal) & (w != root), arrive)
                if not self.two:
                    i, valid_i = self.unit(t, after + jnp.minimum(dist, LAG) + LAG)
                    when(valid_i & (i >= self.normal), lambda: self.x_copy(i).wait_recv())

        def drain(self):
            w, root, n, flight = self.w, self.root, self.n, self.flight
            if self.normal < n:
                when(w == root, lambda: self.straight_all(n - 1, "wait_send"))
            if root > 1:
                when(w < root - 1, lambda: end(self.send_up, n, flight))
            if root > 0:
                when(w == root - 1, lambda: end(self.send_up_root, n, flight))
                when((w <= root) & (w > 0), lambda: end(self.total_dn, self.normal, flight))
            when(w > root, lambda: end(self.send_dn, n, flight))
            when((w >= root) & (w < L - 1), lambda: end(self.total_up, self.normal, flight))
            if self.two:
                when(w == root, lambda: end(self.x_copy, n, flight))
            else:
                end(self.x_copy, n, flight)

    ways = [Way(kind, d) for kind in ("c", "b", "a") for d in (0, 1)]

    def dp_tick(t):
        when(t < UA, lambda: go(x_first, t, SENDS))

        def x_add():
            u = t - LAG
            x_first(u).wait_recv()
            s = pl.ds(pl.multiple_of(a_base(u) + x * 2 * CH, CH), 2 * CH)
            g[s, :] += R["xrb"][x_slot(u), :]

        when(ok(t - LAG, UA), x_add)
        for way in ways:
            way.tick(t)

    def dp_drain():
        end(x_first, UA, SENDS)
        for way in ways:
            way.drain()

    for copy in loads.values():
        copy.start()

    def vector(i, name):
        loads[name].wait()
        R["vecs"][i : i + 1, :] = R[name][...][None, :]

    g[small : small + 4 * CH, :] = jnp.zeros((4 * CH, width), F32)
    for name in ("tok", "tim"):
        loads[name].wait()
    timf[...] = tim[...].astype(F32)
    vector(0, "n1g")
    vector(1, "n1b")

    @pl.loop(0, rows_n)
    def _(r):
        norm1(r)

        @pl.when(r == 0)
        def _():
            for name in ("wqkv", "qvb", "seg", "wout"):
                loads[name].wait()

        project(r)
        attend(r)
        sum_b(0, r)

    for name in ("cot", "wdn", "wup"):
        loads[name].wait()
    for i, name in enumerate(("outb", "n2g", "n2b", "upb", "dnb")):
        vector(2 + i, name)

    @pl.loop(0, rows_n)
    def _(r):
        grad_act(r)
        when(r > 0, lambda: sum_b(1, r - 1))
        sum_c(0, r)
        sum_d(0, r)
        feed(r)

    weight_grads(jnp.int32(0))

    blocks = (2 * ff + 4 * loc) // blk
    per = blk // (4 * CH)
    a_last = LAG * (2 * D + 2)
    b_last, c_last = LAG * (L + 1), LAG * (2 * L - 1)
    ends = []
    for n, k, stride, first, late, soon in (
        (UA, DIRECT[0], 1, 0, a_last, LAG * (D + 3)),
        (UB, DIRECT[1], 3, 0, b_last, LAG * (D + 2)),
        (UC, DIRECT[2], 3, 1, c_last, LAG * (L + 1)),
    ):
        ends += [first + stride * (n - k - 1) + late, first + stride * (n - 1) + soon if k else 0]
    ticks = max(ends) + 1

    def out_copy(j):
        s = pl.ds(j * blk, blk if j < blocks else 4 * CH)
        return pltpu.make_async_copy(f.at[s], f_out.at[s], R["fin"].at[j])

    done_copies = [
        pltpu.make_async_copy(a, b, R["fin"].at[blocks + 1 + i])
        for i, (a, b) in enumerate(((ig, ig_o), (tg, tg_o), (out, out_o)))
    ]

    @pl.loop(0, ticks)
    def _(t):
        dp_tick(t)

        def at(first, step, fn):
            r = (t - first) // step
            when((t >= first) & ((t - first) % step == 0) & (r < rows_n), lambda: fn(r))

        when(t == 0, lambda: sum_b(1, rows_n - 1))
        at(2, 3, lambda r: sum_c(1, r))

        def second(r):
            sum_d(1, r)
            back2(r)

        at(3, 3, second)
        at(4, 3, lambda r: sum_b(2, r))
        at(10, 3, lambda r: sum_c(2, r))

        def third(r):
            sum_d(2, r)
            back1(r)

        at(11, 3, third)
        at(12, 3, down)
        at(13, 3, lambda r: sum_b(3, r))
        at(18, 3, lambda r: sum_c(3, r))

        def fourth(r):
            sum_d(3, r)
            finish(r)

        at(19, 3, fourth)

        @pl.when(t == 19 + 3 * rows_n)
        def _():
            for copy in done_copies:
                copy.start()

        when((t % 3 == 1) & (t < 3 * blocks - 2), lambda: weight_grads((t + 2) // 3))
        for j in range(blocks):
            done = (per * (j + 1) - 1) // 5 * 3 + 2 + max(a_last, c_last)
            if done < ticks:
                when(t == done, lambda: out_copy(j).start())

    dp_drain()
    for j in range(blocks + 1):
        if j == blocks or (per * (j + 1) - 1) // 5 * 3 + 2 + max(a_last, c_last) >= ticks:
            out_copy(j).start()
    for copy in done_copies + [out_copy(j) for j in range(blocks + 1)]:
        copy.wait()


def shards(n_dp, *args):
    (tok, tim, seg, n1g, n1b, wqkv, qvb, wout, outb, n2g, n2b, wup, upb, wdn, dnb, cot) = args
    tokens, width = tok.shape
    rows_n, seq = seg.shape
    loc, ff = wout.shape[0], wup.shape[1]
    heads = loc // HD
    half = width // 2
    big = 2 * ff + 4 * loc
    count = big // (4 * CH) + 1
    UC = count // 5
    UB = UC + (count % 5) // 3
    UA = count - UB - UC
    L = n_dp // 2
    LAG = hop_ticks(L)
    vm = pltpu.VMEM
    dma = pltpu.SemaphoreType.DMA
    W = LAG * L + 2
    WX = 2 * LAG + 2
    WB = LAG * (L + 1) // 3 + 2
    WC = LAG * (2 * L - 1) // 3 + 2
    total = count * 4 * CH
    slots = lambda w, rows: vm((2, w * rows, width), F32)
    flat = lambda n: vm((n,), F32)
    scratch = dict(
        tok=vm((tokens, width), BF16),
        cot=vm((tokens, width), BF16),
        wqkv=vm((3, loc, width), BF16),
        wout=vm((loc, width), BF16),
        wup=vm((width, ff), BF16),
        wdn=vm((ff, width), BF16),
        ins=dma((16,)),
        tim=vm((rows_n, width), BF16),
        seg=vm((rows_n, seq), jnp.int32),
        qvb=vm((2, loc), F32),
        **{s: flat(width) for s in ("n1g", "n1b", "outb", "n2g", "n2b", "dnb")},
        upb=flat(ff),
        vecs=vm((8, width), F32),
        timf=vm((rows_n, width), F32),
        start=vm((tokens, width), F32),
        entry=vm((tokens, width), BF16),
        q=vm((tokens, loc), BF16),
        k=vm((tokens, loc), BF16),
        v=vm((tokens, loc), BF16),
        probs=vm((heads * tokens, seq), F32),
        mixed=vm((tokens, loc), BF16),
        part=vm((tokens, width), F32),
        cr=vm((tokens, half), F32),
        ys=vm((tokens, half), F32),
        yr=vm((2, tokens, half), F32),
        tot=vm((tokens, width), F32),
        mid=vm((tokens, width), F32),
        e2=vm((tokens, width), BF16),
        hp=vm((seq, ff), F32),
        act=vm((tokens, ff), BF16),
        gp=vm((tokens, ff), BF16),
        gact=vm((tokens, ff), F32),
        gmid=vm((tokens, width), F32),
        gbr=vm((tokens, width), BF16),
        out=vm((tokens, width), BF16),
        ig=vm((tokens, width), BF16),
        tg=vm((rows_n, width), F32),
        lt=vm((big, tokens), BF16),
        g=vm((total, width), F32),
        f=vm((total, width), F32),
        xrb=vm((WX * 2 * CH, width), F32),
        alo=slots(W, CH),
        ahi=slots(W, CH),
        blo=slots(WB, 2 * CH),
        bhi=slots(WB, 2 * CH),
        bxb=slots(WB, 2 * CH),
        clo=slots(1, 2 * CH),
        chi=slots(WC, 2 * CH),
        cxb=slots(WC, 2 * CH),
        **{s: dma((rows_n,)) for s in ("cs", "crs", "yss", "gs", "grs")},
        yrs=dma((2, rows_n)),
        fin=dma((big // loc + 4,)),
        xs=dma((SENDS,)),
        xr=dma((WX,)),
        **{k + "_q": dma((2, L)) for k, n in zip("abc", direct_units(L)) if n},
        **{k + "_" + s: dma((2, SENDS if k == "a" else 2)) for k in "abc" for s in ("s", "u", "d", "xs")},
        **{k + "_" + s: dma((2, w)) for k, w in (("a", W), ("b", WB), ("c", WC)) for s in ("r", "t", "xr")},
    )
    any_spec = pl.BlockSpec(memory_space=pl.ANY)
    vm_spec = pl.BlockSpec(memory_space=pltpu.VMEM)
    out, ig, tg, f = pl.pallas_call(
        functools.partial(kernel, n_dp, (UA, UB, UC), tuple(scratch)),
        out_shape=(
            jax.ShapeDtypeStruct((tokens, width), BF16),
            jax.ShapeDtypeStruct((tokens, width), BF16),
            jax.ShapeDtypeStruct((rows_n, width), F32),
            jax.ShapeDtypeStruct((total, width), F32),
        ),
        in_specs=[any_spec] * 16,
        out_specs=(any_spec,) * 4,
        scratch_shapes=list(scratch.values()),
        compiler_params=pltpu.CompilerParams(
            collective_id=0, has_side_effects=True, vmem_limit_bytes=63 * 2**20
        ),
        cost_estimate=pl.CostEstimate(flops=6 * 10**9, bytes_accessed=20 * 10**6, transcendentals=0),
    )(
        tok, tim, seg, n1g, n1b, wqkv.transpose(0, 2, 1), qvb, wout, outb, n2g, n2b, wup, upb, wdn, dnb, cot
    )
    f32 = lambda *shape: jax.ShapeDtypeStruct(shape, F32)
    moved = (
        jax.ShapeDtypeStruct((tokens, width), BF16),
        jax.ShapeDtypeStruct((tokens, width), BF16),
        f32(rows_n, width),
        f32(3, loc, width),
        f32(loc, width),
        f32(width, ff),
        f32(ff, width),
    )
    results = pl.pallas_call(
        functools.partial(place, big),
        out_shape=moved + (f32(2, loc), f32(ff)) + (f32(width),) * 6,
        in_specs=[any_spec] * 4,
        out_specs=(any_spec,) * 7 + (vm_spec,) * 8,
        scratch_shapes=[
            vm((8, width), F32),
            vm((big, width), F32),
            vm((tokens, width), BF16),
            vm((tokens, width), BF16),
            vm((rows_n, width), F32),
            dma((10,)),
            dma((10,)),
        ],
        compiler_params=pltpu.CompilerParams(vmem_limit_bytes=63 * 2**20),
    )(out, ig, tg, f)
    out, ig, tg, qkv, outw, up, down, qvb, upb, downb, n2g, n2b, outb, n1g, n1b = results
    return out, ig, tg, n1g, n1b, qkv.transpose(0, 2, 1), qvb, outw, outb, n2g, n2b, up, upb, down, downb


def place(big, *refs):
    out, ig, tg, f, out_o, ig_o, tg_o, qkv, outw, up, down, qvb, upb, downb = refs[:14]
    n2g, n2b, outb, n1g, n1b, sm, buf, vo, vi, vt, sem, sem_o = refs[14:]
    loc, ff = outw.shape[0], down.shape[0]
    half = f.shape[1] // 2
    moves = []
    row = 0
    for n, ref in ((ff, down), (ff, up), (loc, outw), (loc, qkv.at[0]), (loc, qkv.at[1]), (loc, qkv.at[2])):
        s = pl.ds(row, n)
        moves.append((f.at[s], buf.at[s], ref))
        row += n
    moves += [(out, vo, out_o), (ig, vi, ig_o), (tg, vt, tg_o)]
    first = pltpu.make_async_copy(f.at[pl.ds(big, 8)], sm, sem.at[9])
    first.start()
    loads = [pltpu.make_async_copy(a, v, sem.at[i]) for i, (a, v, b) in enumerate(moves)]
    stores = [pltpu.make_async_copy(v, b, sem_o.at[i]) for i, (a, v, b) in enumerate(moves)]
    for copy in loads:
        copy.start()
    for load, store in zip(loads, stores):
        load.wait()
        store.start()
    first.wait()
    for i, ref in enumerate((downb, upb, n2g, n2b, outb, n1g, n1b)):
        ref[...] = sm[i : i + 1, :].reshape(ref.shape)
    qvb[0:1, :] = sm[7:8, 0:loc]
    qvb[1:2, :] = sm[7:8, half : half + loc]
    for copy in stores:
        copy.wait()


def solution(mesh):
    placed = (
        P("dp", None),
        P("dp", None),
        P("dp", None),
        P(),
        P(),
        P(None, None, "mp"),
        P(None, "mp"),
        P("mp", None),
        P(),
        P(),
        P(),
        P(None, "mp"),
        P("mp"),
        P("mp", None),
        P(),
        P("dp", None),
    )
    return jax.shard_map(
        functools.partial(shards, mesh.shape["dp"]),
        mesh=mesh,
        in_specs=placed,
        out_specs=(
            P("dp", None),
            P("dp", None),
            P("dp", None),
            P(),
            P(),
            P(None, None, "mp"),
            P(None, "mp"),
            P("mp", None),
            P(),
            P(),
            P(),
            P(None, "mp"),
            P("mp"),
            P("mp", None),
            P(),
        ),
        check_vma=False,
    )
```

```python
import functools

import jax
import jax.numpy as jnp
from jax import lax
from jax.experimental import pallas as pl
from jax.experimental.pallas import tpu as pltpu
from jax.sharding import PartitionSpec as P

HD = 64
SUB = 128
CH = 8
PRE = False
EACH = 4 if PRE else 3
SENDS = 4
MESH = pl.DeviceIdType.MESH
F32 = jnp.float32
BF16 = jnp.bfloat16


ARGS = ("tok", "tim", "seg", "n1g", "n1b", "wqkv", "qvb", "wout", "outb", "n2g", "n2b")
ARGS += ("wup", "upb", "wdn", "dnb", "cot")


def hop_ticks(line):
    return 2 if line <= 8 else 1


def when(cond, fn):
    pl.when(cond)(fn)


def rem(a, n):
    return lax.rem(a, jnp.int32(n))


def div(a, n):
    return lax.div(a, jnp.int32(n))


def two_power(n):
    return 1 << (n - 1).bit_length()


def nt(a, b):
    return lax.dot_general(a, b, (((1,), (1,)), ((), ())), preferred_element_type=F32)


def tn(a, b):
    return lax.dot_general(a, b, (((0,), (0,)), ((), ())), preferred_element_type=F32)


def nn(a, b):
    return jnp.dot(a, b, preferred_element_type=F32)


def normed(v):
    centred = v - jnp.mean(v, -1, keepdims=True)
    spread = jnp.mean(centred * centred, -1, keepdims=True)
    scale = lax.rsqrt(spread + 1e-05)
    return centred * scale, scale


def colsum(v):
    return jnp.sum(v, 0, keepdims=True)


def kernel(n_dp, units, names, *refs):
    out_o, ig_o, tg_o, f_out = refs[16:20]
    R = dict(zip(names, refs[20:]))
    order = ("tok", "tim", "n1g", "n1b", "wqkv", "qvb", "seg", "wout", "outb", "cot", "wdn")
    order += ("n2g", "n2b", "wup", "upb", "dnb")
    tok, tim, wqkv, qvb, seg, wout, cot, wdn, wup = (
        R[s] for s in ("tok", "tim", "wqkv", "qvb", "seg", "wout", "cot", "wdn", "wup")
    )
    loads = {
        name: pltpu.make_async_copy(refs[ARGS.index(name)], R[name], R["ins"].at[i]) for i, name in enumerate(order)
    }
    n1g, n1b, outb, n2g, n2b, upb, dnb = (R["vecs"].at[pl.ds(i, 1)] for i in range(7))
    timf, start, entry, q_s, k_s, v_s = (R[s] for s in ("timf", "start", "entry", "q", "k", "v"))
    probs, mixed_s, part, cr, ys, yr = (R[s] for s in ("probs", "mixed", "part", "cr", "ys", "yr"))
    tot, mid, e2, hp, act, gp = (R[s] for s in ("tot", "mid", "e2", "hp", "act", "gp"))
    out, ig, tg = (R[s] for s in ("out", "ig", "tg"))
    gact, gmid, gbr, lt, g, f = (R[s] for s in ("gact", "gmid", "gbr", "lt", "g", "f"))

    rows_n, seq = seg.shape
    width = tok.shape[1]
    half = width // 2
    loc = wout.shape[0]
    heads = loc // HD
    ff = wup.shape[1]
    UA, UB, UC = units
    L = n_dp // 2
    LAG = hop_ticks(L)
    H = L // 2
    dp = lax.axis_index("dp")
    mp = lax.axis_index("mp")
    core = mp % 2
    x = dp % 2
    z = dp // 2
    to_core = (dp, mp + 1 - 2 * core)
    to_y = (dp, (mp + 2) % 4)
    to_x = (dp + 1 - 2 * x, mp)
    last = jnp.minimum(z, L - 1 - z)
    side = div(z, H)
    cross = jnp.where(last == H - 1, 1, 0)
    to_in = ((z + 1 - 2 * side) * 2 + x, mp)
    to_out = (jnp.clip(z - 1 + 2 * side, 0, L - 1) * 2 + x, mp)
    zlo = jnp.maximum(z - 1, 0) * 2 + x
    zhi = jnp.minimum(z + 1, L - 1) * 2 + x

    barrier = pltpu.get_barrier_semaphore()
    for dev in (to_core, to_y, to_x):
        pl.semaphore_signal(barrier, 1, device_id=dev, device_id_type=MESH)
    when(z > 0, lambda: pl.semaphore_signal(barrier, 1, device_id=(zlo, mp), device_id_type=MESH))
    when(z < L - 1, lambda: pl.semaphore_signal(barrier, 1, device_id=(zhi, mp), device_id_type=MESH))
    greeted = 3 + jnp.minimum(z, 1) + jnp.minimum(L - 1 - z, 1)

    def sl(r, n=seq):
        return pl.ds(pl.multiple_of(r * n, n), n)

    def sub(r, i):
        return pl.ds(pl.multiple_of(r * seq + i * SUB, SUB), SUB)

    mine = pl.ds(pl.multiple_of(core * half, 128), half)
    other = pl.ds(pl.multiple_of((1 - core) * half, 128), half)

    def remote(src, dst, ssem, rsem, dev):
        return pltpu.make_async_remote_copy(
            src_ref=src, dst_ref=dst, send_sem=ssem, recv_sem=rsem, device_id=dev, device_id_type=MESH
        )

    def core_copy(p, r):
        return remote(part.at[sl(r), other], cr.at[sl(r)], R["cs"].at[r], R["crs"].at[r], to_core)

    def y_copy(p, r):
        return remote(ys.at[sl(r)], yr.at[p % 2, sl(r)], R["yss"].at[r], R["yrs"].at[p % 2, r], to_y)

    def ag_copy(p, r):
        return remote(tot.at[sl(r), mine], tot.at[sl(r), mine], R["gs"].at[r], R["grs"].at[r], to_core)

    def sum_b(p, r):
        core_copy(p, r).wait()
        ys[sl(r), :] = part[sl(r), mine] + cr[sl(r), :]
        y_copy(p, r).start()

    def sum_c(p, r):
        y_copy(p, r).wait()
        tot[sl(r), mine] = ys[sl(r), :] + yr[p % 2, sl(r), :]
        ag_copy(p, r).start()

    def sum_d(p, r):
        ag_copy(p, r).wait()

    def vec(ref):
        return ref[...]

    small = 2 * ff + 4 * loc

    def small_add(i, v):
        g[small + i : small + i + 1, :] += v

    lane = lax.broadcasted_iota(jnp.int32, (1, loc), 1)
    masks = [((lane >= h * HD) & (lane < (h + 1) * HD)).astype(F32) for h in range(heads)]

    def by_head(v):
        return jnp.concatenate([v * m.astype(BF16) for m in masks], 0)

    def from_heads(v):
        total = v[:seq] * masks[0]
        for h in range(1, heads):
            total = total + v[h * seq : (h + 1) * seq] * masks[h]
        return total

    def norm1(r):
        @pl.loop(0, seq // SUB)
        def _(i):
            s = sub(r, i)
            v = tok[s, :].astype(F32) + timf[pl.ds(r, 1), :]
            start[s, :] = v
            xhat, _ = normed(v)
            entry[s, :] = (xhat * n1g[...] + n1b[...]).astype(BF16)

    def project(r):
        e = entry[sl(r), :]
        q_s[sl(r), :] = (nt(e, wqkv[0]) + qvb[0:1, :]).astype(BF16)
        k_s[sl(r), :] = nt(e, wqkv[1]).astype(BF16)
        v_s[sl(r), :] = (nt(e, wqkv[2]) + qvb[1:2, :]).astype(BF16)

    def attend(r):
        labels = jnp.broadcast_to(seg[pl.ds(r, 1), :], (seq, seq))
        same = labels == labels.T
        same = jnp.concatenate([same.astype(F32)] * heads, 0) > 0.5
        scores = nt(by_head(q_s[sl(r), :]), k_s[sl(r), :]) * HD ** (-0.5)
        scores = jnp.where(same, scores, -1e30)
        w = jnp.exp(scores - jnp.max(scores, -1, keepdims=True))
        pr = w / jnp.sum(w, -1, keepdims=True)
        probs[sl(r, heads * seq), :] = pr
        mixed = from_heads(nn(pr.astype(BF16), v_s[sl(r), :])).astype(BF16)
        mixed_s[sl(r), :] = mixed
        part[sl(r), :] = nn(mixed, wout[...])

        @pl.when(r == 0)
        def _():
            pl.semaphore_wait(barrier, greeted)

        core_copy(0, r).start()
        lt[2 * ff : 2 * ff + loc, sl(r)] = mixed.T

    def grad_act(r):
        c = cot[sl(r), :]
        gact[sl(r), :] = nt(c, wdn[...])
        small_add(0, colsum(c.astype(F32)))

    def feed(r):
        @pl.loop(0, seq // SUB)
        def _(i):
            s = sub(r, i)
            v = start[s, :] + (tot[s, :] + outb[...])
            mid[s, :] = v
            xhat, _ = normed(v)
            e2[s, :] = (xhat * n2g[...] + n2b[...]).astype(BF16)

        hp[...] = nn(e2[sl(r), :], wup[...])

        @pl.loop(0, seq // SUB)
        def _(i):
            s = sub(r, i)
            u = hp[pl.ds(pl.multiple_of(i * SUB, SUB), SUB), :] + upb[...]
            cdf = 0.5 * (1.0 + lax.erf(u * 0.7071067811865476))
            act[s, :] = (u * cdf).astype(BF16)
            slope = cdf + u * (0.3989422804014327 * jnp.exp(-0.5 * u * u))
            pre = (gact[s, :] * slope).astype(BF16)
            gp[s, :] = pre
            small_add(1, colsum(pre.astype(F32)))

        part[sl(r), :] = nt(gp[sl(r), :], wup[...])
        core_copy(1, r).start()
        lt[0:ff, sl(r)] = act[sl(r), :].T
        lt[ff : 2 * ff, sl(r)] = e2[sl(r), :].T

    def back2(r):
        @pl.loop(0, seq // SUB)
        def _(i):
            s = sub(r, i)
            ge = tot[s, :]
            xhat, scale = normed(mid[s, :])
            small_add(2, colsum(ge * xhat))
            small_add(3, colsum(ge))
            gx = ge * n2g[...]
            gm = cot[s, :].astype(F32) + scale * (
                gx - jnp.mean(gx, -1, keepdims=True) - xhat * jnp.mean(gx * xhat, -1, keepdims=True)
            )
            gmid[s, :] = gm
            low = gm.astype(BF16)
            gbr[s, :] = low
            small_add(4, colsum(low.astype(F32)))

        g3 = by_head(nt(gbr[sl(r), :], wout[...]).astype(BF16))
        pr = probs[sl(r, heads * seq), :]
        grad_probs = nt(g3, v_s[sl(r), :])
        inner = jnp.sum(pr * grad_probs, -1, keepdims=True)
        ds = (pr * (grad_probs - inner)).astype(BF16)
        gq = (from_heads(nn(ds, k_s[sl(r), :])) * HD ** (-0.5)).astype(BF16)
        gk = (tn(ds, by_head(q_s[sl(r), :])) * HD ** (-0.5)).astype(BF16)
        gv = tn(pr.astype(BF16), g3).astype(BF16)
        part[sl(r), :] = nn(gq, wqkv[0]) + nn(gk, wqkv[1]) + nn(gv, wqkv[2])
        core_copy(2, r).start()
        late = 2 * ff + loc
        for i, v in enumerate((gq, gk, gv)):
            lt[late + i * loc : late + (i + 1) * loc, sl(r)] = v.T
        g[small + 7 : small + 8, 0:loc] += colsum(gq.astype(F32))
        g[small + 7 : small + 8, half : half + loc] += colsum(gv.astype(F32))

    def back1(r):
        tg[pl.ds(r, 1), :] = jnp.zeros((1, width), F32)

        @pl.loop(0, seq // SUB)
        def _(i):
            s = sub(r, i)
            ge = tot[s, :]
            xhat, scale = normed(start[s, :])
            small_add(5, colsum(ge * xhat))
            small_add(6, colsum(ge))
            gy = ge * n1g[...]
            gs = gmid[s, :] + scale * (
                gy - jnp.mean(gy, -1, keepdims=True) - xhat * jnp.mean(gy * xhat, -1, keepdims=True)
            )
            ig[s, :] = gs.astype(BF16)
            tg[pl.ds(r, 1), :] += colsum(gs)

    def down(r):
        part[sl(r), :] = nn(act[sl(r), :], wdn[...])
        core_copy(3, r).start()

    def finish(r):
        @pl.loop(0, seq // SUB)
        def _(i):
            s = sub(r, i)
            out[s, :] = (mid[s, :] + (tot[s, :] + dnb[...])).astype(BF16)

    blk = loc

    early = ff // blk

    def weight_grads(j):
        s = pl.ds(pl.multiple_of(j * blk, blk), blk)

        def by(right):
            def fn():
                g[s, :] = nn(lt[s, :], right[...])

            return fn

        when(j < early, by(cot))
        when((j >= early) & (j < 2 * early), by(gp))
        when(j == 2 * early, by(gbr))
        when(j > 2 * early, by(entry))

    def go(copy, u, depth):
        when(u >= depth, lambda: copy(u - depth).wait_send())
        copy(u).start()

    def end(copy, n, depth):
        for u in range(n - min(depth, n), n):
            copy(u).wait_send()

    PU = 2 * loc // (4 * CH) if PRE else 0
    PG = PU // EACH
    AF = LAG + (1 if PRE else 0)

    def base_of(u):
        return (PU + u) * 4 * CH

    def later(u):
        return base_of(2 * PG + div(u - PU, EACH) * (EACH + 2) + rem(u - PU, EACH))

    def b_base(u, i):
        rest = 2 * PG + (u - PG) * (EACH + 2) + EACH
        u = jnp.where(u < PG, u * 2, rest) if PG else rest
        return base_of(jnp.minimum(u + i, UA + UB + UC - PU - 1))

    def a_base(u, owner):
        rest = later(u) + owner * 2 * CH
        return jnp.where(u < PU, owner * loc + u * 2 * CH, rest) if PU else rest

    def x_slot(u):
        return pl.ds(pl.multiple_of(rem(u, R["xr"].shape[0]) * 2 * CH, CH), 2 * CH)

    def x_first(u):
        src = pl.ds(pl.multiple_of(later(u) + (1 - x) * 2 * CH, CH), 2 * CH)
        return remote(
            g.at[src], R["xrb"].at[x_slot(u)], R["xs"].at[rem(u, SENDS)], R["xr"].at[rem(u, R["xr"].shape[0])], to_x
        )

    def cot_x(i):
        s = core * 2 + i
        return remote(R["cotf"].at[i], R["cotr"].at[s], R["cxs"].at[i], R["cxr"].at[i], to_x)

    def cot_c(i):
        s = core * 2 + i
        return remote(R["cotr"].at[s], R["cotr"].at[s], R["ccs"].at[i], R["ccr"].at[i], to_core)

    def act_x(r):
        return remote(R["actf"].at[r], R["actr"].at[r], R["axs"].at[r], R["axr"].at[r], to_x)

    def cot_out():
        loads["cot"].wait()
        n = R["cotf"].shape[1]
        for i in range(2):
            s = pl.ds(pl.multiple_of((core * 2 + i) * n, n), n)
            R["cotf"][i] = cot[s, :].astype(F32)
            cot_x(i).start()

    def cot_on():
        for i in range(2):
            cot_x(i).wait()
            cot_c(i).start()

    def act_out(r):
        s = pl.ds(pl.multiple_of((1 - x) * loc, loc), loc)
        R["actf"][r] = lt[s, sl(r)].astype(F32)
        act_x(r).start()

    def pair_grads():
        for i in range(2):
            cot_c(i).wait()
        cotx, n = R["cotx"], R["cotf"].shape[1]
        for i in range(4):
            cotx[i * n : (i + 1) * n, :] = R["cotr"][i].astype(BF16)
        for r in range(rows_n):
            act_x(r).wait()
            R["ltx"][:, r * seq : (r + 1) * seq] = R["actr"][r].astype(BF16)
        s = pl.ds(pl.multiple_of(x * loc, loc), loc)
        g[s, :] = nn(lt[s, :], cot[...]) + nn(R["ltx"][...], cotx[...])

    def rows_at(base, n):
        return pl.ds(pl.multiple_of(base, CH), n)

    class Line:
        def __init__(self, kind, n, first, stride, depth):
            self.kind, self.n, self.first, self.stride, self.depth = kind, n, first, stride, depth

        def unit(self, t, offset):
            rel = t - self.first - offset
            if self.stride == 1:
                return rel, (rel >= 0) & (rel < self.n)
            return div(rel, self.stride), (rel >= 0) & (rel < self.n * self.stride) & (rem(rel, self.stride) == 0)

        def sem(self, name, i, u):
            ref = R[self.kind + "_" + name]
            return ref.at[i, rem(u, ref.shape[1])]

        def slot(self, u, rows):
            return rows_at(rem(u, R[self.kind + "_r"].shape[1]) * rows, rows)

        def go(self, copy, u):
            go(copy, u, self.depth)

        def end(self, copy):
            end(copy, self.n, self.depth)

    class A(Line):
        def own(self, u):
            return rows_at(a_base(u, x), 2 * CH)

        def inward(self, u):
            dst = R["abuf"].at[cross, self.slot(u, 2 * CH)]
            return remote(g.at[self.own(u)], dst, self.sem("s", 0, u), self.sem("r", cross, u), to_in)

        def arrived(self, u, i):
            buf = R["abuf"].at[i, self.slot(u, 2 * CH)]
            remote(buf, buf, self.sem("s", 0, u), self.sem("r", i, u), to_in).wait_recv()
            return buf

        def outward(self, u):
            own = self.own(u)
            return remote(f.at[own], f.at[own], self.sem("u", 0, u), self.sem("t", 0, u), to_out)

        def x_last(self, u):
            own = self.own(u)
            return remote(f.at[own], f.at[own], self.sem("xs", 0, u), self.sem("xr", 0, u), to_x)

        def tick(self, t):
            u, valid_u = self.unit(t, last * LAG)

            def reduce():
                def add():
                    g[self.own(u), :] += self.arrived(u, 0)[...]

                if H > 1:
                    when(last > 0, add)
                self.go(self.inward, u)

            when(valid_u, reduce)
            v, valid_v = self.unit(t, (2 * H - 1 - last) * LAG)

            def finish():
                def turn():
                    f[self.own(v), :] = g[self.own(v), :] + self.arrived(v, 1)[...]

                when(last == H - 1, turn)
                if H > 1:
                    when(last < H - 1, lambda: self.outward(v).wait_recv())
                    when(last > 0, lambda: self.go(self.outward, v))
                self.go(self.x_last, v)

            when(valid_v, finish)
            e, valid_e = self.unit(t, (2 * H - last) * LAG)
            when(valid_e, lambda: self.x_last(e).wait_recv())

        def drain(self):
            self.end(self.inward)
            self.end(self.x_last)
            if H > 1:
                when(last > 0, lambda: self.end(self.outward))

    class B(Line):
        def all(self, u):
            return rows_at(b_base(u, 0), 4 * CH)

        def half(self, u, i):
            return rows_at(b_base(u, 0) + i * 2 * CH, 2 * CH)

        def inward(self, u):
            dst = R["bbuf"].at[self.slot(u, 4 * CH)]
            return remote(g.at[self.all(u)], dst, self.sem("s", 0, u), self.sem("r", 0, u), to_in)

        def swap(self, u):
            dst = R["bsw"].at[self.slot(u, 2 * CH)]
            return remote(g.at[self.half(u, 1 - side)], dst, self.sem("s", 0, u), self.sem("r", 1, u), to_in)

        def x_copy(self, u):
            dst = R["bxb"].at[self.slot(u, 2 * CH)]
            return remote(g.at[self.half(u, side)], dst, self.sem("xs", 0, u), self.sem("xr", 0, u), to_x)

        def back(self, u):
            own = self.half(u, side)
            return remote(f.at[own], f.at[own], self.sem("d", 0, u), self.sem("r", 2, u), to_in)

        def outward(self, u):
            own = self.all(u)
            return remote(f.at[own], f.at[own], self.sem("u", 0, u), self.sem("t", 0, u), to_out)

        def tick(self, t):
            u, valid_u = self.unit(t, last * LAG)

            def reduce():
                def add():
                    self.inward(u).wait_recv()
                    g[self.all(u), :] += R["bbuf"][self.slot(u, 4 * CH), :]

                if H > 1:
                    when(last > 0, add)
                    when(last < H - 1, lambda: self.go(self.inward, u))
                when(last == H - 1, lambda: self.go(self.swap, u))

            when(valid_u, reduce)
            middle = last == H - 1
            i, valid_i = self.unit(t, H * LAG)

            def over():
                self.swap(i).wait_recv()
                g[self.half(i, side), :] += R["bsw"][self.slot(i, 2 * CH), :]
                self.go(self.x_copy, i)

            when(valid_i & middle, over)
            j, valid_j = self.unit(t, (H + 1) * LAG)

            def total():
                self.x_copy(j).wait_recv()
                own = self.half(j, side)
                f[own, :] = g[own, :] + R["bxb"][self.slot(j, 2 * CH), :]
                self.go(self.back, j)

            when(valid_j & middle, total)
            v, valid_v = self.unit(t, (2 * H + 1 - last) * LAG)

            def finish():
                when(middle, lambda: self.back(v).wait_recv())
                if H > 1:
                    when(last < H - 1, lambda: self.outward(v).wait_recv())
                    when(last > 0, lambda: self.go(self.outward, v))

            when(valid_v, finish)

        def drain(self):
            def ends():
                for copy in (self.swap, self.x_copy, self.back):
                    self.end(copy)

            when(last == H - 1, ends)
            if H > 1:
                when(last < H - 1, lambda: self.end(self.inward))
                when(last > 0, lambda: self.end(self.outward))

    class C(Line):
        def own(self, u, d):
            return rows_at(b_base(u, 1) + d * 2 * CH, 2 * CH)

        def place(self, d):
            w = z if d == 0 else L - 1 - z
            return w, (zhi if d == 0 else zlo, mp), (zlo if d == 0 else zhi, mp)

        def copies(self, d):
            w, up, dn = self.place(d)
            own = lambda u: self.own(u, d)
            slot = lambda u: self.slot(u, 2 * CH)

            def send(u):
                return remote(g.at[own(u)], R["cbuf"].at[d, slot(u)], self.sem("s", d, u), self.sem("r", d, u), dn)

            def x_copy(u):
                return remote(g.at[own(u)], R["cxb"].at[d, slot(u)], self.sem("xs", d, u), self.sem("xr", d, u), to_x)

            def spread(u):
                return remote(f.at[own(u)], f.at[own(u)], self.sem("u", d, u), self.sem("t", d, u), up)

            return w, send, x_copy, spread

        def tick(self, t):
            for d in (0, 1):
                w, send, x_copy, spread = self.copies(d)
                u, valid_u = self.unit(t, (L - 1 - w) * LAG)

                def reduce():
                    def add():
                        send(u).wait_recv()
                        g[self.own(u, d), :] += R["cbuf"][d, self.slot(u, 2 * CH), :]

                    when(w < L - 1, add)
                    when(w > 0, lambda: self.go(send, u))
                    when(w == 0, lambda: self.go(x_copy, u))

                when(valid_u, reduce)
                v, valid_v = self.unit(t, (L + w) * LAG)

                def finish():
                    def turn():
                        x_copy(v).wait_recv()
                        own = self.own(v, d)
                        f[own, :] = g[own, :] + R["cxb"][d, self.slot(v, 2 * CH), :]

                    when(w == 0, turn)
                    when(w > 0, lambda: spread(v).wait_recv())
                    when(w < L - 1, lambda: self.go(spread, v))

                when(valid_v, finish)

        def drain(self):
            for d in (0, 1):
                w, send, x_copy, spread = self.copies(d)
                when(w > 0, lambda: self.end(send))
                when(w == 0, lambda: self.end(x_copy))
                when(w < L - 1, lambda: self.end(spread))

    lines = [C("c", UC, 0, EACH, 2), B("b", UB, 1, EACH, 2), A("a", UA, AF, 1, SENDS)]

    def dp_tick(t):
        u = t - (AF - LAG)

        def x_send():
            when(u >= PU + SENDS, lambda: x_first(u - SENDS).wait_send())
            x_first(u).start()

        when((u >= PU) & (u < UA), x_send)
        v = t - AF

        def x_add():
            x_first(v).wait_recv()
            s = rows_at(a_base(v, x), 2 * CH)
            g[s, :] += R["xrb"][x_slot(v), :]

        when((v >= PU) & (v < UA), x_add)
        for line in lines:
            line.tick(t)

    def dp_drain():
        end(x_first, UA, SENDS)
        for line in lines:
            line.drain()

    for copy in loads.values():
        copy.start()

    def vector(i, name):
        loads[name].wait()
        R["vecs"][i : i + 1, :] = R[name][...][None, :]

    g[small : small + 4 * CH, :] = jnp.zeros((4 * CH, width), F32)
    for name in ("tok", "tim"):
        loads[name].wait()
    timf[...] = tim[...].astype(F32)
    vector(0, "n1g")
    vector(1, "n1b")

    @pl.loop(0, rows_n)
    def _(r):
        norm1(r)

        @pl.when(r == 0)
        def _():
            for name in ("wqkv", "qvb", "seg", "wout"):
                loads[name].wait()

        project(r)
        attend(r)
        sum_b(0, r)
        if PRE:
            when(r == 0, cot_out)

    for name in ("wdn", "wup") if PRE else ("cot", "wdn", "wup"):
        loads[name].wait()
    for i, name in enumerate(("outb", "n2g", "n2b", "upb", "dnb")):
        vector(2 + i, name)

    @pl.loop(0, rows_n)
    def _(r):
        grad_act(r)
        when(r > 0, lambda: sum_b(1, r - 1))
        sum_c(0, r)
        sum_d(0, r)
        feed(r)
        if PRE:
            act_out(r)

    if PRE:
        cot_on()
    weight_grads(jnp.int32(2 if PRE else 0))

    blocks = (2 * ff + 4 * loc) // blk
    a_last = AF + LAG * 2 * H
    b_last, c_last = 1 + LAG * (2 * H + 1), LAG * (2 * L - 1)
    ticks = max(UA - 1 + a_last, EACH * (UB - 1) + b_last, EACH * (UC - 1) + c_last) + 1

    def done(j):
        if PRE:
            start = PU - 1 if j <= 2 else EACH * (j + 1) - 1
        else:
            start = (6 * j + 5) // (EACH + 2) * EACH + EACH - 1
        return start + max(a_last, b_last, c_last)

    def out_copy(j):
        s = pl.ds(j * blk, blk if j < blocks else 4 * CH)
        return pltpu.make_async_copy(f.at[s], f_out.at[s], R["fin"].at[j])

    done_copies = [
        pltpu.make_async_copy(a, b, R["fin"].at[blocks + 1 + i])
        for i, (a, b) in enumerate(((ig, ig_o), (tg, tg_o), (out, out_o)))
    ]

    @pl.loop(0, ticks)
    def _(t):
        dp_tick(t)

        def at(first, step, fn):
            r = (t - first) // step
            when((t >= first) & ((t - first) % step == 0) & (r < rows_n), lambda: fn(r))

        when(t == 0, lambda: sum_b(1, rows_n - 1))
        at(2, 3, lambda r: sum_c(1, r))

        def second(r):
            sum_d(1, r)
            back2(r)

        at(3, 3, second)
        at(4, 3, lambda r: sum_b(2, r))
        at(12, 3, lambda r: sum_c(2, r))

        def third(r):
            sum_d(2, r)
            back1(r)

        at(13, 3, third)
        at(14, 3, down)
        at(15, 3, lambda r: sum_b(3, r))
        at(21, 3, lambda r: sum_c(3, r))

        def fourth(r):
            sum_d(3, r)
            finish(r)

        at(22, 3, fourth)

        @pl.when(t == 22 + 3 * rows_n)
        def _():
            for copy in done_copies:
                copy.start()

        if PRE:
            when(t == AF - 1, pair_grads)
            when((rem(t, 4) == 2) & (t >= 6) & (t < 4 * blocks - 6), lambda: weight_grads(div(t + 6, 4)))
        else:
            when((rem(t, 3) == 1) & (t < 3 * blocks - 2), lambda: weight_grads(div(t + 2, 3)))
        for j in range(blocks):
            if done(j) < ticks:
                when(t == done(j), lambda: out_copy(j).start())

    dp_drain()
    for j in range(blocks + 1):
        if j == blocks or done(j) >= ticks:
            out_copy(j).start()
    for copy in done_copies + [out_copy(j) for j in range(blocks + 1)]:
        copy.wait()


def shards(n_dp, *args):
    (tok, tim, seg, n1g, n1b, wqkv, qvb, wout, outb, n2g, n2b, wup, upb, wdn, dnb, cot) = args
    tokens, width = tok.shape
    rows_n, seq = seg.shape
    loc, ff = wout.shape[0], wup.shape[1]
    heads = loc // HD
    half = width // 2
    big = 2 * ff + 4 * loc
    count = big // (4 * CH) + 1
    PU = 2 * loc // (4 * CH) if PRE else 0
    rest = count - PU - 2 * (PU // EACH)
    UC = PU // EACH + rest // (EACH + 2)
    UB = UC + rest % (EACH + 2) // EACH
    UA = count - UB - UC
    L = n_dp // 2
    LAG = hop_ticks(L)
    vm = pltpu.VMEM
    dma = pltpu.SemaphoreType.DMA
    W = two_power(max(LAG * (L - 1) + 1, 2 * LAG + 2))
    WB = two_power(LAG * (L + 1) // EACH + 1)
    WC = two_power(LAG * (2 * L - 1) // EACH + 1)
    total = count * 4 * CH
    flat = lambda n: vm((n,), F32)
    scratch = dict(
        tok=vm((tokens, width), BF16),
        cot=vm((tokens, width), BF16),
        wqkv=vm((3, loc, width), BF16),
        wout=vm((loc, width), BF16),
        wup=vm((width, ff), BF16),
        wdn=vm((ff, width), BF16),
        ins=dma((16,)),
        tim=vm((rows_n, width), BF16),
        seg=vm((rows_n, seq), jnp.int32),
        qvb=vm((2, loc), F32),
        **{s: flat(width) for s in ("n1g", "n1b", "outb", "n2g", "n2b", "dnb")},
        upb=flat(ff),
        vecs=vm((8, width), F32),
        timf=vm((rows_n, width), F32),
        start=vm((tokens, width), F32),
        entry=vm((tokens, width), BF16),
        q=vm((tokens, loc), BF16),
        k=vm((tokens, loc), BF16),
        v=vm((tokens, loc), BF16),
        probs=vm((heads * tokens, seq), F32),
        mixed=vm((tokens, loc), BF16),
        part=vm((tokens, width), F32),
        cr=vm((tokens, half), F32),
        ys=vm((tokens, half), F32),
        yr=vm((2, tokens, half), F32),
        tot=vm((tokens, width), F32),
        mid=vm((tokens, width), F32),
        e2=vm((tokens, width), BF16),
        hp=vm((seq, ff), F32),
        act=vm((tokens, ff), BF16),
        gp=vm((tokens, ff), BF16),
        gact=vm((tokens, ff), F32),
        gmid=vm((tokens, width), F32),
        gbr=vm((tokens, width), BF16),
        out=vm((tokens, width), BF16),
        ig=vm((tokens, width), BF16),
        tg=vm((rows_n, width), F32),
        lt=vm((big, tokens), BF16),
        g=vm((total, width), F32),
        f=vm((total, width), F32),
        xrb=vm((W * 2 * CH, width), F32),
        abuf=vm((2, W * 2 * CH, width), F32),
        bbuf=vm((WB * 4 * CH, width), F32),
        bsw=vm((WB * 2 * CH, width), F32),
        bxb=vm((WB * 2 * CH, width), F32),
        cbuf=vm((2, WC * 2 * CH, width), F32),
        cxb=vm((2, WC * 2 * CH, width), F32),
        **{s: dma((rows_n,)) for s in ("cs", "crs", "yss", "gs", "grs")},
        yrs=dma((2, rows_n)),
        fin=dma((big // loc + 4,)),
        xs=dma((SENDS,)),
        xr=dma((W,)),
        **{"a_" + s: dma((1, SENDS)) for s in ("s", "u", "xs")},
        a_r=dma((2, W)),
        **{"a_" + s: dma((1, W)) for s in ("t", "xr")},
        **{"b_" + s: dma((1, 2)) for s in ("s", "u", "d", "xs")},
        b_r=dma((3, WB)),
        **{"b_" + s: dma((1, WB)) for s in ("t", "xr")},
        **{"c_" + s: dma((2, 2)) for s in ("s", "u", "xs")},
        **{"c_" + s: dma((2, WC)) for s in ("r", "t", "xr")},
    )
    if PRE:
        scratch.update(
            cotf=vm((2, tokens // 4, width), F32),
            cotr=vm((4, tokens // 4, width), F32),
            cotx=vm((tokens, width), BF16),
            actf=vm((rows_n, loc, seq), F32),
            actr=vm((rows_n, loc, seq), F32),
            ltx=vm((loc, tokens), BF16),
            **{s: dma((2,)) for s in ("cxs", "cxr", "ccs", "ccr")},
            **{s: dma((rows_n,)) for s in ("axs", "axr")},
        )
    any_spec = pl.BlockSpec(memory_space=pl.ANY)
    vm_spec = pl.BlockSpec(memory_space=pltpu.VMEM)
    out, ig, tg, f = pl.pallas_call(
        functools.partial(kernel, n_dp, (UA, UB, UC), tuple(scratch)),
        out_shape=(
            jax.ShapeDtypeStruct((tokens, width), BF16),
            jax.ShapeDtypeStruct((tokens, width), BF16),
            jax.ShapeDtypeStruct((rows_n, width), F32),
            jax.ShapeDtypeStruct((total, width), F32),
        ),
        in_specs=[any_spec] * 16,
        out_specs=(any_spec,) * 4,
        scratch_shapes=list(scratch.values()),
        compiler_params=pltpu.CompilerParams(
            collective_id=0, has_side_effects=True, vmem_limit_bytes=63 * 2**20
        ),
        cost_estimate=pl.CostEstimate(flops=6 * 10**9, bytes_accessed=20 * 10**6, transcendentals=0),
    )(
        tok, tim, seg, n1g, n1b, wqkv.transpose(0, 2, 1), qvb, wout, outb, n2g, n2b, wup, upb, wdn, dnb, cot
    )
    f32 = lambda *shape: jax.ShapeDtypeStruct(shape, F32)
    moved = (
        jax.ShapeDtypeStruct((tokens, width), BF16),
        jax.ShapeDtypeStruct((tokens, width), BF16),
        f32(rows_n, width),
        f32(3, loc, width),
        f32(loc, width),
        f32(width, ff),
        f32(ff, width),
    )
    results = pl.pallas_call(
        functools.partial(place, big),
        out_shape=moved + (f32(2, loc), f32(ff)) + (f32(width),) * 6,
        in_specs=[any_spec] * 4,
        out_specs=(any_spec,) * 7 + (vm_spec,) * 8,
        scratch_shapes=[
            vm((8, width), F32),
            vm((big, width), F32),
            vm((tokens, width), BF16),
            vm((tokens, width), BF16),
            vm((rows_n, width), F32),
            dma((10,)),
            dma((10,)),
        ],
        compiler_params=pltpu.CompilerParams(vmem_limit_bytes=63 * 2**20),
    )(out, ig, tg, f)
    out, ig, tg, qkv, outw, up, down, qvb, upb, downb, n2g, n2b, outb, n1g, n1b = results
    return out, ig, tg, n1g, n1b, qkv.transpose(0, 2, 1), qvb, outw, outb, n2g, n2b, up, upb, down, downb


def place(big, *refs):
    out, ig, tg, f, out_o, ig_o, tg_o, qkv, outw, up, down, qvb, upb, downb = refs[:14]
    n2g, n2b, outb, n1g, n1b, sm, buf, vo, vi, vt, sem, sem_o = refs[14:]
    loc, ff = outw.shape[0], down.shape[0]
    half = f.shape[1] // 2
    moves = []
    row = 0
    for n, ref in ((ff, down), (ff, up), (loc, outw), (loc, qkv.at[0]), (loc, qkv.at[1]), (loc, qkv.at[2])):
        s = pl.ds(row, n)
        moves.append((f.at[s], buf.at[s], ref))
        row += n
    moves += [(out, vo, out_o), (ig, vi, ig_o), (tg, vt, tg_o)]
    first = pltpu.make_async_copy(f.at[pl.ds(big, 8)], sm, sem.at[9])
    first.start()
    loads = [pltpu.make_async_copy(a, v, sem.at[i]) for i, (a, v, b) in enumerate(moves)]
    stores = [pltpu.make_async_copy(v, b, sem_o.at[i]) for i, (a, v, b) in enumerate(moves)]
    for copy in loads:
        copy.start()
    for load, store in zip(loads, stores):
        load.wait()
        store.start()
    first.wait()
    for i, ref in enumerate((downb, upb, n2g, n2b, outb, n1g, n1b)):
        ref[...] = sm[i : i + 1, :].reshape(ref.shape)
    qvb[0:1, :] = sm[7:8, 0:loc]
    qvb[1:2, :] = sm[7:8, half : half + loc]
    for copy in stores:
        copy.wait()


def solution(mesh):
    placed = (
        P("dp", None),
        P("dp", None),
        P("dp", None),
        P(),
        P(),
        P(None, None, "mp"),
        P(None, "mp"),
        P("mp", None),
        P(),
        P(),
        P(),
        P(None, "mp"),
        P("mp"),
        P("mp", None),
        P(),
        P("dp", None),
    )
    return jax.shard_map(
        functools.partial(shards, mesh.shape["dp"]),
        mesh=mesh,
        in_specs=placed,
        out_specs=(
            P("dp", None),
            P("dp", None),
            P("dp", None),
            P(),
            P(),
            P(None, None, "mp"),
            P(None, "mp"),
            P("mp", None),
            P(),
            P(),
            P(),
            P(None, "mp"),
            P("mp"),
            P("mp", None),
            P(),
        ),
        check_vma=False,
    )
```

```python
import functools

import jax
import jax.numpy as jnp
from jax import lax
from jax.experimental import pallas as pl
from jax.experimental.pallas import tpu as pltpu
from jax.sharding import PartitionSpec as P

HD = 64
SUB = 128
CH = 8
W_PIECES = 3
EACH = 3
SENDS = 4
MESH = pl.DeviceIdType.MESH
F32 = jnp.float32
BF16 = jnp.bfloat16


ARGS = ("tok", "tim", "seg", "n1g", "n1b", "wqkv", "qvb", "wout", "outb", "n2g", "n2b")
ARGS += ("wup", "upb", "wdn", "dnb", "cot")


def hop_ticks(line):
    return 2 if line <= 8 else 1


def when(cond, fn):
    pl.when(cond)(fn)


def rem(a, n):
    return lax.rem(a, jnp.int32(n))


def div(a, n):
    return lax.div(a, jnp.int32(n))


def two_power(n):
    return 1 << (n - 1).bit_length()


def nt(a, b):
    return lax.dot_general(a, b, (((1,), (1,)), ((), ())), preferred_element_type=F32)


def tn(a, b):
    return lax.dot_general(a, b, (((0,), (0,)), ((), ())), preferred_element_type=F32)


def nn(a, b):
    return jnp.dot(a, b, preferred_element_type=F32)


def normed(v):
    centred = v - jnp.mean(v, -1, keepdims=True)
    spread = jnp.mean(centred * centred, -1, keepdims=True)
    scale = lax.rsqrt(spread + 1e-05)
    return centred * scale, scale


def colsum(v):
    return jnp.sum(v, 0, keepdims=True)


def kernel(n_dp, units, names, *refs):
    out_o, ig_o, tg_o, f_out = refs[16:20]
    R = dict(zip(names, refs[20:]))
    order = ("tok", "tim", "n1g", "n1b", "wqkv", "qvb", "seg", "wout", "outb", "cot", "wdn")
    order += ("n2g", "n2b", "wup", "upb", "dnb")
    tok, tim, wqkv, qvb, seg, wout, cot, wdn, wup = (
        R[s] for s in ("tok", "tim", "wqkv", "qvb", "seg", "wout", "cot", "wdn", "wup")
    )
    loads = {
        name: pltpu.make_async_copy(refs[ARGS.index(name)], R[name], R["ins"].at[i]) for i, name in enumerate(order)
    }
    n1g, n1b, outb, n2g, n2b, upb, dnb = (R["vecs"].at[pl.ds(i, 1)] for i in range(7))
    timf, start, entry, q_s, k_s, v_s = (R[s] for s in ("timf", "start", "entry", "q", "k", "v"))
    probs, mixed_s, part, cr, ys, yr = (R[s] for s in ("probs", "mixed", "part", "cr", "ys", "yr"))
    tot, mid, e2, hp, act, gp = (R[s] for s in ("tot", "mid", "e2", "hp", "act", "gp"))
    out, ig, tg = (R[s] for s in ("out", "ig", "tg"))
    gact, gmid, gbr, lt, g, f = (R[s] for s in ("gact", "gmid", "gbr", "lt", "g", "f"))

    rows_n, seq = seg.shape
    width = tok.shape[1]
    half = width // 2
    loc = wout.shape[0]
    heads = loc // HD
    ff = wup.shape[1]
    UA, UB, UC = units
    L = n_dp // 2
    LAG = hop_ticks(L)
    H = L // 2
    dp = lax.axis_index("dp")
    mp = lax.axis_index("mp")
    core = mp % 2
    x = dp % 2
    z = dp // 2
    to_core = (dp, mp + 1 - 2 * core)
    to_y = (dp, (mp + 2) % 4)
    to_x = (dp + 1 - 2 * x, mp)
    last = jnp.minimum(z, L - 1 - z)
    side = div(z, H)
    cross = jnp.where(last == H - 1, 1, 0)
    to_in = ((z + 1 - 2 * side) * 2 + x, mp)
    to_out = (jnp.clip(z - 1 + 2 * side, 0, L - 1) * 2 + x, mp)
    zlo = jnp.maximum(z - 1, 0) * 2 + x
    zhi = jnp.minimum(z + 1, L - 1) * 2 + x

    barrier = pltpu.get_barrier_semaphore()
    for dev in (to_core, to_y, to_x):
        pl.semaphore_signal(barrier, 1, device_id=dev, device_id_type=MESH)
    when(z > 0, lambda: pl.semaphore_signal(barrier, 1, device_id=(zlo, mp), device_id_type=MESH))
    when(z < L - 1, lambda: pl.semaphore_signal(barrier, 1, device_id=(zhi, mp), device_id_type=MESH))
    greeted = 3 + jnp.minimum(z, 1) + jnp.minimum(L - 1 - z, 1)

    def sl(r, n=seq):
        return pl.ds(pl.multiple_of(r * n, n), n)

    def sub(r, i):
        return pl.ds(pl.multiple_of(r * seq + i * SUB, SUB), SUB)

    mine = pl.ds(pl.multiple_of(core * half, 128), half)
    other = pl.ds(pl.multiple_of((1 - core) * half, 128), half)

    def remote(src, dst, ssem, rsem, dev):
        return pltpu.make_async_remote_copy(
            src_ref=src, dst_ref=dst, send_sem=ssem, recv_sem=rsem, device_id=dev, device_id_type=MESH
        )

    def core_copy(p, r):
        return remote(part.at[sl(r), other], cr.at[sl(r)], R["cs"].at[r], R["crs"].at[r], to_core)

    def y_copy(p, r):
        return remote(ys.at[sl(r)], yr.at[p % 2, sl(r)], R["yss"].at[r], R["yrs"].at[p % 2, r], to_y)

    def ag_copy(p, r):
        return remote(tot.at[sl(r), mine], tot.at[sl(r), mine], R["gs"].at[r], R["grs"].at[r], to_core)

    def sum_b(p, r):
        core_copy(p, r).wait()
        ys[sl(r), :] = part[sl(r), mine] + cr[sl(r), :]
        y_copy(p, r).start()

    def sum_c(p, r):
        y_copy(p, r).wait()
        tot[sl(r), mine] = ys[sl(r), :] + yr[p % 2, sl(r), :]
        ag_copy(p, r).start()

    def sum_d(p, r):
        ag_copy(p, r).wait()

    def vec(ref):
        return ref[...]

    small = 2 * ff + 4 * loc

    def small_add(i, v):
        g[small + i : small + i + 1, :] += v

    lane = lax.broadcasted_iota(jnp.int32, (1, loc), 1)
    masks = [((lane >= h * HD) & (lane < (h + 1) * HD)).astype(F32) for h in range(heads)]

    def by_head(v):
        return jnp.concatenate([v * m.astype(BF16) for m in masks], 0)

    def from_heads(v):
        total = v[:seq] * masks[0]
        for h in range(1, heads):
            total = total + v[h * seq : (h + 1) * seq] * masks[h]
        return total

    def norm1(r):
        @pl.loop(0, seq // SUB)
        def _(i):
            s = sub(r, i)
            v = tok[s, :].astype(F32) + timf[pl.ds(r, 1), :]
            start[s, :] = v
            xhat, _ = normed(v)
            entry[s, :] = (xhat * n1g[...] + n1b[...]).astype(BF16)

    def project(r):
        e = entry[sl(r), :]
        q_s[sl(r), :] = (nt(e, wqkv[0]) + qvb[0:1, :]).astype(BF16)
        k_s[sl(r), :] = nt(e, wqkv[1]).astype(BF16)
        v_s[sl(r), :] = (nt(e, wqkv[2]) + qvb[1:2, :]).astype(BF16)

    def attend(r):
        labels = jnp.broadcast_to(seg[pl.ds(r, 1), :], (seq, seq))
        same = labels == labels.T
        same = jnp.concatenate([same.astype(F32)] * heads, 0) > 0.5
        scores = nt(by_head(q_s[sl(r), :]), k_s[sl(r), :]) * HD ** (-0.5)
        scores = jnp.where(same, scores, -1e30)
        w = jnp.exp(scores - jnp.max(scores, -1, keepdims=True))
        pr = w / jnp.sum(w, -1, keepdims=True)
        probs[sl(r, heads * seq), :] = pr
        mixed = from_heads(nn(pr.astype(BF16), v_s[sl(r), :])).astype(BF16)
        mixed_s[sl(r), :] = mixed
        turned = mixed.T
        lt[2 * ff : 2 * ff + loc, sl(r)] = turned
        mixa[mp, r] = turned.astype(F32)
        m_core(r).start()
        m_y(r).start()

    wf, wall, mixa = R["wf"], R["wall"], R["mixa"]
    mp_y, mp_c = rem(mp + 2, 4), mp + 1 - 2 * core
    mine_0, other_0 = mp - core, mp_y - core
    hl = loc // 2
    pr_n = hl // W_PIECES

    def w_core():
        return remote(wf.at[mp], wf.at[mp], R["wcs"], R["wcr"], to_core)

    def w_rows(start, n):
        return pl.ds(pl.multiple_of(start, CH), n)

    def w_y(i):
        s = w_rows(x * hl + i * pr_n, pr_n)
        return remote(wf.at[mp, s], wf.at[mp, s], R["wys"].at[i], R["wyr"].at[i], to_y)

    def w_x(i):
        s = w_rows(x * hl + i * pr_n, pr_n)
        return remote(wf.at[mp_y, s], wf.at[mp_y, s], R["wxs"].at[i], R["wxr"].at[i], to_x)

    def w_share(h):
        s = w_rows((x + h - 2 * x * h) * hl, hl)
        return remote(wf.at[mp_y, s], wf.at[mp_y, s], R["whs"].at[h], R["whr"].at[h], to_core)

    def m_core(r):
        return remote(mixa.at[mp, r], mixa.at[mp, r], R["cs"].at[r], R["crs"].at[r], to_core)

    def m_y(r):
        return remote(mixa.at[mp, r], mixa.at[mp, r], R["yss"].at[r], R["yrs"].at[0, r], to_y)

    def m_share(r):
        return remote(mixa.at[mp_y, r], mixa.at[mp_y, r], R["gs"].at[r], R["grs"].at[r], to_core)

    def weights_out():
        loads["wout"].wait()
        wf[mp] = wout[...].astype(F32)
        pl.semaphore_wait(barrier, greeted)
        for i in range(W_PIECES):
            w_y(i).start()
        w_core().start()

    def weights_on(i):
        w_y(i).wait()
        w_x(i).start()

    def pair_sum(m, r):
        return tn(mixa[m, r].astype(BF16), wall[m]) + tn(mixa[m + 1, r].astype(BF16), wall[m + 1])

    def near_part(r):
        m_core(r).wait()
        part[sl(r), :] = pair_sum(mine_0, r)

    def across(r):
        m_y(r).wait()
        m_share(r).start()

    def far_part(r):
        m_share(r).wait()
        tot[sl(r), :] = part[sl(r), :] + pair_sum(other_0, r)

    def grad_act(r):
        c = cot[sl(r), :]
        gact[sl(r), :] = nt(c, wdn[...])
        small_add(0, colsum(c.astype(F32)))

    def feed(r):
        @pl.loop(0, seq // SUB)
        def _(i):
            s = sub(r, i)
            v = start[s, :] + (tot[s, :] + outb[...])
            mid[s, :] = v
            xhat, _ = normed(v)
            e2[s, :] = (xhat * n2g[...] + n2b[...]).astype(BF16)

        hp[...] = nn(e2[sl(r), :], wup[...])

        @pl.loop(0, seq // SUB)
        def _(i):
            s = sub(r, i)
            u = hp[pl.ds(pl.multiple_of(i * SUB, SUB), SUB), :] + upb[...]
            cdf = 0.5 * (1.0 + lax.erf(u * 0.7071067811865476))
            act[s, :] = (u * cdf).astype(BF16)
            slope = cdf + u * (0.3989422804014327 * jnp.exp(-0.5 * u * u))
            pre = (gact[s, :] * slope).astype(BF16)
            gp[s, :] = pre
            small_add(1, colsum(pre.astype(F32)))

        part[sl(r), :] = nt(gp[sl(r), :], wup[...])
        core_copy(1, r).start()
        lt[0:ff, sl(r)] = act[sl(r), :].T
        lt[ff : 2 * ff, sl(r)] = e2[sl(r), :].T

    def back2(r):
        @pl.loop(0, seq // SUB)
        def _(i):
            s = sub(r, i)
            ge = tot[s, :]
            xhat, scale = normed(mid[s, :])
            small_add(2, colsum(ge * xhat))
            small_add(3, colsum(ge))
            gx = ge * n2g[...]
            gm = cot[s, :].astype(F32) + scale * (
                gx - jnp.mean(gx, -1, keepdims=True) - xhat * jnp.mean(gx * xhat, -1, keepdims=True)
            )
            gmid[s, :] = gm
            low = gm.astype(BF16)
            gbr[s, :] = low
            small_add(4, colsum(low.astype(F32)))

        g3 = by_head(nt(gbr[sl(r), :], wout[...]).astype(BF16))
        pr = probs[sl(r, heads * seq), :]
        grad_probs = nt(g3, v_s[sl(r), :])
        inner = jnp.sum(pr * grad_probs, -1, keepdims=True)
        ds = (pr * (grad_probs - inner)).astype(BF16)
        gq = (from_heads(nn(ds, k_s[sl(r), :])) * HD ** (-0.5)).astype(BF16)
        gk = (tn(ds, by_head(q_s[sl(r), :])) * HD ** (-0.5)).astype(BF16)
        gv = tn(pr.astype(BF16), g3).astype(BF16)
        part[sl(r), :] = nn(gq, wqkv[0]) + nn(gk, wqkv[1]) + nn(gv, wqkv[2])
        core_copy(2, r).start()
        late = 2 * ff + loc
        for i, v in enumerate((gq, gk, gv)):
            lt[late + i * loc : late + (i + 1) * loc, sl(r)] = v.T
        g[small + 7 : small + 8, 0:loc] += colsum(gq.astype(F32))
        g[small + 7 : small + 8, half : half + loc] += colsum(gv.astype(F32))

    def back1(r):
        tg[pl.ds(r, 1), :] = jnp.zeros((1, width), F32)

        @pl.loop(0, seq // SUB)
        def _(i):
            s = sub(r, i)
            ge = tot[s, :]
            xhat, scale = normed(start[s, :])
            small_add(5, colsum(ge * xhat))
            small_add(6, colsum(ge))
            gy = ge * n1g[...]
            gs = gmid[s, :] + scale * (
                gy - jnp.mean(gy, -1, keepdims=True) - xhat * jnp.mean(gy * xhat, -1, keepdims=True)
            )
            ig[s, :] = gs.astype(BF16)
            tg[pl.ds(r, 1), :] += colsum(gs)

    def down(r):
        part[sl(r), :] = nn(act[sl(r), :], wdn[...])
        core_copy(3, r).start()

    def finish(r):
        @pl.loop(0, seq // SUB)
        def _(i):
            s = sub(r, i)
            out[s, :] = (mid[s, :] + (tot[s, :] + dnb[...])).astype(BF16)

    blk = loc

    early = ff // blk

    def weight_grads(j):
        s = pl.ds(pl.multiple_of(j * blk, blk), blk)

        def by(right):
            def fn():
                g[s, :] = nn(lt[s, :], right[...])

            return fn

        when(j < early, by(cot))
        when((j >= early) & (j < 2 * early), by(gp))
        when(j == 2 * early, by(gbr))
        when(j > 2 * early, by(entry))

    def go(copy, u, depth):
        when(u >= depth, lambda: copy(u - depth).wait_send())
        copy(u).start()

    def end(copy, n, depth):
        for u in range(n - min(depth, n), n):
            copy(u).wait_send()

    AF = LAG

    def base_of(u):
        return u * 4 * CH

    def later(u):
        return base_of(div(u, EACH) * (EACH + 2) + rem(u, EACH))

    def b_base(u, i):
        return base_of(jnp.minimum(u * (EACH + 2) + EACH + i, UA + UB + UC - 1))

    def a_base(u, owner):
        return later(u) + owner * 2 * CH

    def x_slot(u):
        return pl.ds(pl.multiple_of(rem(u, R["xr"].shape[0]) * 2 * CH, CH), 2 * CH)

    def x_first(u):
        src = pl.ds(pl.multiple_of(later(u) + (1 - x) * 2 * CH, CH), 2 * CH)
        return remote(
            g.at[src], R["xrb"].at[x_slot(u)], R["xs"].at[rem(u, SENDS)], R["xr"].at[rem(u, R["xr"].shape[0])], to_x
        )

    def rows_at(base, n):
        return pl.ds(pl.multiple_of(base, CH), n)

    class Line:
        def __init__(self, kind, n, first, stride, depth):
            self.kind, self.n, self.first, self.stride, self.depth = kind, n, first, stride, depth

        def unit(self, t, offset):
            rel = t - self.first - offset
            if self.stride == 1:
                return rel, (rel >= 0) & (rel < self.n)
            return div(rel, self.stride), (rel >= 0) & (rel < self.n * self.stride) & (rem(rel, self.stride) == 0)

        def sem(self, name, i, u):
            ref = R[self.kind + "_" + name]
            return ref.at[i, rem(u, ref.shape[1])]

        def slot(self, u, rows):
            return rows_at(rem(u, R[self.kind + "_r"].shape[1]) * rows, rows)

        def go(self, copy, u):
            go(copy, u, self.depth)

        def end(self, copy):
            end(copy, self.n, self.depth)

    class A(Line):
        def own(self, u):
            return rows_at(a_base(u, x), 2 * CH)

        def inward(self, u):
            dst = R["abuf"].at[cross, self.slot(u, 2 * CH)]
            return remote(g.at[self.own(u)], dst, self.sem("s", 0, u), self.sem("r", cross, u), to_in)

        def arrived(self, u, i):
            buf = R["abuf"].at[i, self.slot(u, 2 * CH)]
            remote(buf, buf, self.sem("s", 0, u), self.sem("r", i, u), to_in).wait_recv()
            return buf

        def outward(self, u):
            own = self.own(u)
            return remote(f.at[own], f.at[own], self.sem("u", 0, u), self.sem("t", 0, u), to_out)

        def x_last(self, u):
            own = self.own(u)
            return remote(f.at[own], f.at[own], self.sem("xs", 0, u), self.sem("xr", 0, u), to_x)

        def tick(self, t):
            u, valid_u = self.unit(t, last * LAG)

            def reduce():
                def add():
                    g[self.own(u), :] += self.arrived(u, 0)[...]

                if H > 1:
                    when(last > 0, add)
                self.go(self.inward, u)

            when(valid_u, reduce)
            v, valid_v = self.unit(t, (2 * H - 1 - last) * LAG)

            def finish():
                def turn():
                    f[self.own(v), :] = g[self.own(v), :] + self.arrived(v, 1)[...]

                when(last == H - 1, turn)
                if H > 1:
                    when(last < H - 1, lambda: self.outward(v).wait_recv())
                    when(last > 0, lambda: self.go(self.outward, v))
                self.go(self.x_last, v)

            when(valid_v, finish)
            e, valid_e = self.unit(t, (2 * H - last) * LAG)
            when(valid_e, lambda: self.x_last(e).wait_recv())

        def drain(self):
            self.end(self.inward)
            self.end(self.x_last)
            if H > 1:
                when(last > 0, lambda: self.end(self.outward))

    class B(Line):
        def all(self, u):
            return rows_at(b_base(u, 0), 4 * CH)

        def half(self, u, i):
            return rows_at(b_base(u, 0) + i * 2 * CH, 2 * CH)

        def inward(self, u):
            dst = R["bbuf"].at[self.slot(u, 4 * CH)]
            return remote(g.at[self.all(u)], dst, self.sem("s", 0, u), self.sem("r", 0, u), to_in)

        def swap(self, u):
            dst = R["bsw"].at[self.slot(u, 2 * CH)]
            return remote(g.at[self.half(u, 1 - side)], dst, self.sem("s", 0, u), self.sem("r", 1, u), to_in)

        def x_copy(self, u):
            dst = R["bxb"].at[self.slot(u, 2 * CH)]
            return remote(g.at[self.half(u, side)], dst, self.sem("xs", 0, u), self.sem("xr", 0, u), to_x)

        def back(self, u):
            own = self.half(u, side)
            return remote(f.at[own], f.at[own], self.sem("d", 0, u), self.sem("r", 2, u), to_in)

        def outward(self, u):
            own = self.all(u)
            return remote(f.at[own], f.at[own], self.sem("u", 0, u), self.sem("t", 0, u), to_out)

        def tick(self, t):
            u, valid_u = self.unit(t, last * LAG)

            def reduce():
                def add():
                    self.inward(u).wait_recv()
                    g[self.all(u), :] += R["bbuf"][self.slot(u, 4 * CH), :]

                if H > 1:
                    when(last > 0, add)
                    when(last < H - 1, lambda: self.go(self.inward, u))
                when(last == H - 1, lambda: self.go(self.swap, u))

            when(valid_u, reduce)
            middle = last == H - 1
            i, valid_i = self.unit(t, H * LAG)

            def over():
                self.swap(i).wait_recv()
                g[self.half(i, side), :] += R["bsw"][self.slot(i, 2 * CH), :]
                self.go(self.x_copy, i)

            when(valid_i & middle, over)
            j, valid_j = self.unit(t, (H + 1) * LAG)

            def total():
                self.x_copy(j).wait_recv()
                own = self.half(j, side)
                f[own, :] = g[own, :] + R["bxb"][self.slot(j, 2 * CH), :]
                self.go(self.back, j)

            when(valid_j & middle, total)
            v, valid_v = self.unit(t, (2 * H + 1 - last) * LAG)

            def finish():
                when(middle, lambda: self.back(v).wait_recv())
                if H > 1:
                    when(last < H - 1, lambda: self.outward(v).wait_recv())
                    when(last > 0, lambda: self.go(self.outward, v))

            when(valid_v, finish)

        def drain(self):
            def ends():
                for copy in (self.swap, self.x_copy, self.back):
                    self.end(copy)

            when(last == H - 1, ends)
            if H > 1:
                when(last < H - 1, lambda: self.end(self.inward))
                when(last > 0, lambda: self.end(self.outward))

    class C(Line):
        def own(self, u, d):
            return rows_at(b_base(u, 1) + d * 2 * CH, 2 * CH)

        def place(self, d):
            w = z if d == 0 else L - 1 - z
            return w, (zhi if d == 0 else zlo, mp), (zlo if d == 0 else zhi, mp)

        def copies(self, d):
            w, up, dn = self.place(d)
            own = lambda u: self.own(u, d)
            slot = lambda u: self.slot(u, 2 * CH)

            def send(u):
                return remote(g.at[own(u)], R["cbuf"].at[d, slot(u)], self.sem("s", d, u), self.sem("r", d, u), dn)

            def x_copy(u):
                return remote(g.at[own(u)], R["cxb"].at[d, slot(u)], self.sem("xs", d, u), self.sem("xr", d, u), to_x)

            def spread(u):
                return remote(f.at[own(u)], f.at[own(u)], self.sem("u", d, u), self.sem("t", d, u), up)

            return w, send, x_copy, spread

        def tick(self, t):
            for d in (0, 1):
                w, send, x_copy, spread = self.copies(d)
                u, valid_u = self.unit(t, (L - 1 - w) * LAG)

                def reduce():
                    def add():
                        send(u).wait_recv()
                        g[self.own(u, d), :] += R["cbuf"][d, self.slot(u, 2 * CH), :]

                    when(w < L - 1, add)
                    when(w > 0, lambda: self.go(send, u))
                    when(w == 0, lambda: self.go(x_copy, u))

                when(valid_u, reduce)
                v, valid_v = self.unit(t, (L + w) * LAG)

                def finish():
                    def turn():
                        x_copy(v).wait_recv()
                        own = self.own(v, d)
                        f[own, :] = g[own, :] + R["cxb"][d, self.slot(v, 2 * CH), :]

                    when(w == 0, turn)
                    when(w > 0, lambda: spread(v).wait_recv())
                    when(w < L - 1, lambda: self.go(spread, v))

                when(valid_v, finish)

        def drain(self):
            for d in (0, 1):
                w, send, x_copy, spread = self.copies(d)
                when(w > 0, lambda: self.end(send))
                when(w == 0, lambda: self.end(x_copy))
                when(w < L - 1, lambda: self.end(spread))

    lines = [C("c", UC, 0, EACH, 2), B("b", UB, 1, EACH, 2), A("a", UA, AF, 1, SENDS)]

    def dp_tick(t):
        when(t < UA, lambda: go(x_first, t, SENDS))
        v = t - AF

        def x_add():
            x_first(v).wait_recv()
            s = rows_at(a_base(v, x), 2 * CH)
            g[s, :] += R["xrb"][x_slot(v), :]

        when((v >= 0) & (v < UA), x_add)
        for line in lines:
            line.tick(t)

    def dp_drain():
        end(x_first, UA, SENDS)
        for line in lines:
            line.drain()

    for copy in loads.values():
        copy.start()

    def vector(i, name):
        loads[name].wait()
        R["vecs"][i : i + 1, :] = R[name][...][None, :]

    g[small : small + 4 * CH, :] = jnp.zeros((4 * CH, width), F32)
    for name in ("tok", "tim"):
        loads[name].wait()
    timf[...] = tim[...].astype(F32)
    vector(0, "n1g")
    vector(1, "n1b")

    @pl.loop(0, rows_n)
    def _(r):
        norm1(r)

        @pl.when(r == 0)
        def _():
            for name in ("wqkv", "qvb", "seg"):
                loads[name].wait()

        project(r)
        when(r == 0, weights_out)
        attend(r)
        for i in range(W_PIECES - 1):
            when(r == rows_n - W_PIECES + 1 + i, lambda: weights_on(i))

    for name in ("cot", "wdn", "wup"):
        loads[name].wait()
    for i, name in enumerate(("outb", "n2g", "n2b", "upb", "dnb")):
        vector(2 + i, name)
    pl.loop(0, rows_n)(grad_act)
    weights_on(W_PIECES - 1)
    w_share(0).start()
    w_core().wait()
    for i in range(2):
        wall[mine_0 + i] = wf[mine_0 + i].astype(BF16)
    pl.loop(0, rows_n)(near_part)
    ahead = min(2, rows_n)
    for r in range(ahead):
        across(r)
    for i in range(W_PIECES):
        w_x(i).wait()
    w_share(1).start()
    for h in range(2):
        w_share(h).wait()
    for i in range(2):
        wall[other_0 + i] = wf[other_0 + i].astype(BF16)

    @pl.loop(0, rows_n)
    def _(r):
        far_part(r)
        feed(r)
        when(r + ahead < rows_n, lambda: across(r + ahead))
        when(r > 0, lambda: sum_b(1, r - 1))

    weight_grads(jnp.int32(0))

    blocks = (2 * ff + 4 * loc) // blk
    a_last = AF + LAG * 2 * H
    b_last, c_last = 1 + LAG * (2 * H + 1), LAG * (2 * L - 1)
    ticks = max(UA - 1 + a_last, EACH * (UB - 1) + b_last, EACH * (UC - 1) + c_last) + 1

    def done(j):
        start = (6 * j + 5) // (EACH + 2) * EACH + EACH - 1
        return start + max(a_last, b_last, c_last)

    def out_copy(j):
        s = pl.ds(j * blk, blk if j < blocks else 4 * CH)
        return pltpu.make_async_copy(f.at[s], f_out.at[s], R["fin"].at[j])

    done_copies = [
        pltpu.make_async_copy(a, b, R["fin"].at[blocks + 1 + i])
        for i, (a, b) in enumerate(((ig, ig_o), (tg, tg_o), (out, out_o)))
    ]

    @pl.loop(0, ticks)
    def _(t):
        dp_tick(t)

        def at(first, step, fn):
            r = (t - first) // step
            when((t >= first) & ((t - first) % step == 0) & (r < rows_n), lambda: fn(r))

        when(t == 0, lambda: sum_b(1, rows_n - 1))
        at(2, 3, lambda r: sum_c(1, r))

        def second(r):
            sum_d(1, r)
            back2(r)

        at(3, 3, second)
        at(4, 3, lambda r: sum_b(2, r))
        at(12, 3, lambda r: sum_c(2, r))

        def third(r):
            sum_d(2, r)
            back1(r)

        at(13, 3, third)
        at(14, 3, down)
        at(15, 3, lambda r: sum_b(3, r))
        at(21, 3, lambda r: sum_c(3, r))

        def fourth(r):
            sum_d(3, r)
            finish(r)

        at(22, 3, fourth)

        @pl.when(t == 22 + 3 * rows_n)
        def _():
            for copy in done_copies:
                copy.start()

        when((rem(t, 3) == 1) & (t < 3 * blocks - 2), lambda: weight_grads(div(t + 2, 3)))
        for j in range(blocks):
            if done(j) < ticks:
                when(t == done(j), lambda: out_copy(j).start())

    dp_drain()
    for j in range(blocks + 1):
        if j == blocks or done(j) >= ticks:
            out_copy(j).start()
    for copy in done_copies + [out_copy(j) for j in range(blocks + 1)]:
        copy.wait()


def shards(n_dp, *args):
    (tok, tim, seg, n1g, n1b, wqkv, qvb, wout, outb, n2g, n2b, wup, upb, wdn, dnb, cot) = args
    tokens, width = tok.shape
    rows_n, seq = seg.shape
    loc, ff = wout.shape[0], wup.shape[1]
    heads = loc // HD
    half = width // 2
    big = 2 * ff + 4 * loc
    count = big // (4 * CH) + 1
    UC = count // (EACH + 2)
    UB = UC + count % (EACH + 2) // EACH
    UA = count - UB - UC
    L = n_dp // 2
    LAG = hop_ticks(L)
    vm = pltpu.VMEM
    dma = pltpu.SemaphoreType.DMA
    W = two_power(max(LAG * (L - 1) + 1, 2 * LAG + 2))
    WB = two_power(LAG * (L + 1) // EACH + 1)
    WC = two_power(LAG * (2 * L - 1) // EACH + 1)
    total = count * 4 * CH
    flat = lambda n: vm((n,), F32)
    scratch = dict(
        tok=vm((tokens, width), BF16),
        cot=vm((tokens, width), BF16),
        wqkv=vm((3, loc, width), BF16),
        wout=vm((loc, width), BF16),
        wup=vm((width, ff), BF16),
        wdn=vm((ff, width), BF16),
        ins=dma((16,)),
        tim=vm((rows_n, width), BF16),
        seg=vm((rows_n, seq), jnp.int32),
        qvb=vm((2, loc), F32),
        **{s: flat(width) for s in ("n1g", "n1b", "outb", "n2g", "n2b", "dnb")},
        upb=flat(ff),
        vecs=vm((8, width), F32),
        timf=vm((rows_n, width), F32),
        start=vm((tokens, width), F32),
        entry=vm((tokens, width), BF16),
        q=vm((tokens, loc), BF16),
        k=vm((tokens, loc), BF16),
        v=vm((tokens, loc), BF16),
        probs=vm((heads * tokens, seq), F32),
        mixed=vm((tokens, loc), BF16),
        part=vm((tokens, width), F32),
        cr=vm((tokens, half), F32),
        ys=vm((tokens, half), F32),
        yr=vm((2, tokens, half), F32),
        tot=vm((tokens, width), F32),
        mid=vm((tokens, width), F32),
        e2=vm((tokens, width), BF16),
        hp=vm((seq, ff), F32),
        act=vm((tokens, ff), BF16),
        gp=vm((tokens, ff), BF16),
        gact=vm((tokens, ff), F32),
        gmid=vm((tokens, width), F32),
        gbr=vm((tokens, width), BF16),
        out=vm((tokens, width), BF16),
        ig=vm((tokens, width), BF16),
        tg=vm((rows_n, width), F32),
        lt=vm((big, tokens), BF16),
        g=vm((total, width), F32),
        f=vm((total, width), F32),
        xrb=vm((W * 2 * CH, width), F32),
        abuf=vm((2, W * 2 * CH, width), F32),
        bbuf=vm((WB * 4 * CH, width), F32),
        bsw=vm((WB * 2 * CH, width), F32),
        bxb=vm((WB * 2 * CH, width), F32),
        cbuf=vm((2, WC * 2 * CH, width), F32),
        cxb=vm((2, WC * 2 * CH, width), F32),
        wf=vm((4, loc, width), F32),
        wall=vm((4, loc, width), BF16),
        mixa=vm((4, rows_n, loc, seq), F32),
        wcs=dma,
        wcr=dma,
        **{s: dma((W_PIECES,)) for s in ("wys", "wyr", "wxs", "wxr")},
        **{s: dma((2,)) for s in ("whs", "whr")},
        **{s: dma((rows_n,)) for s in ("cs", "crs", "yss", "gs", "grs")},
        yrs=dma((2, rows_n)),
        fin=dma((big // loc + 4,)),
        xs=dma((SENDS,)),
        xr=dma((W,)),
        **{"a_" + s: dma((1, SENDS)) for s in ("s", "u", "xs")},
        a_r=dma((2, W)),
        **{"a_" + s: dma((1, W)) for s in ("t", "xr")},
        **{"b_" + s: dma((1, 2)) for s in ("s", "u", "d", "xs")},
        b_r=dma((3, WB)),
        **{"b_" + s: dma((1, WB)) for s in ("t", "xr")},
        **{"c_" + s: dma((2, 2)) for s in ("s", "u", "xs")},
        **{"c_" + s: dma((2, WC)) for s in ("r", "t", "xr")},
    )
    any_spec = pl.BlockSpec(memory_space=pl.ANY)
    vm_spec = pl.BlockSpec(memory_space=pltpu.VMEM)
    out, ig, tg, f = pl.pallas_call(
        functools.partial(kernel, n_dp, (UA, UB, UC), tuple(scratch)),
        out_shape=(
            jax.ShapeDtypeStruct((tokens, width), BF16),
            jax.ShapeDtypeStruct((tokens, width), BF16),
            jax.ShapeDtypeStruct((rows_n, width), F32),
            jax.ShapeDtypeStruct((total, width), F32),
        ),
        in_specs=[any_spec] * 16,
        out_specs=(any_spec,) * 4,
        scratch_shapes=list(scratch.values()),
        compiler_params=pltpu.CompilerParams(
            collective_id=0, has_side_effects=True, vmem_limit_bytes=63 * 2**20
        ),
        cost_estimate=pl.CostEstimate(flops=6 * 10**9, bytes_accessed=20 * 10**6, transcendentals=0),
    )(
        tok, tim, seg, n1g, n1b, wqkv.transpose(0, 2, 1), qvb, wout, outb, n2g, n2b, wup, upb, wdn, dnb, cot
    )
    f32 = lambda *shape: jax.ShapeDtypeStruct(shape, F32)
    moved = (
        jax.ShapeDtypeStruct((tokens, width), BF16),
        jax.ShapeDtypeStruct((tokens, width), BF16),
        f32(rows_n, width),
        f32(3, loc, width),
        f32(loc, width),
        f32(width, ff),
        f32(ff, width),
    )
    results = pl.pallas_call(
        functools.partial(place, big),
        out_shape=moved + (f32(2, loc), f32(ff)) + (f32(width),) * 6,
        in_specs=[any_spec] * 4,
        out_specs=(any_spec,) * 15,
        scratch_shapes=[
            vm((8, width), F32),
            vm((big, width), F32),
            vm((tokens, width), BF16),
            vm((tokens, width), BF16),
            vm((rows_n, width), F32),
            vm((2, loc), F32),
            *[vm((width,), F32)] * 7,
            dma((18,)),
            dma((26,)),
        ],
        compiler_params=pltpu.CompilerParams(vmem_limit_bytes=63 * 2**20),
    )(out, ig, tg, f)
    out, ig, tg, qkv, outw, up, down, qvb, upb, downb, n2g, n2b, outb, n1g, n1b = results
    return out, ig, tg, n1g, n1b, qkv.transpose(0, 2, 1), qvb, outw, outb, n2g, n2b, up, upb, down, downb


def place(big, *refs):
    out, ig, tg, f, out_o, ig_o, tg_o, qkv, outw, up, down, qvb, upb, downb = refs[:14]
    n2g, n2b, outb, n1g, n1b, sm, buf, vo, vi, vt, vq = refs[14:25]
    flat = refs[25:32]
    sem, sem_o = refs[32:]
    loc, ff = outw.shape[0], down.shape[0]
    half = f.shape[1] // 2
    moves = [(tg, vt, tg_o)]
    row = 0
    for n, ref in ((ff, down), (ff, up), (loc, outw), (loc, qkv.at[0]), (loc, qkv.at[1]), (loc, qkv.at[2])):
        step = max(n * 12 // (2 * ff + 4 * loc), 1)
        for i in range(step):
            s = pl.ds(row, n // step)
            moves.append((f.at[s], buf.at[s], ref.at[pl.ds(i * (n // step), n // step)]))
            row += n // step
    moves += [(out, vo, out_o), (ig, vi, ig_o)]
    first = pltpu.make_async_copy(f.at[pl.ds(big, 8)], sm, sem.at[len(moves)])
    first.start()
    loads = [pltpu.make_async_copy(a, v, sem.at[i]) for i, (a, v, b) in enumerate(moves)]
    stores = [pltpu.make_async_copy(v, b, sem_o.at[i]) for i, (a, v, b) in enumerate(moves)]
    for copy in loads[:20]:
        copy.start()
    first.wait()
    small = (downb, upb, n2g, n2b, outb, n1g, n1b)
    for i, ref in enumerate(flat):
        ref[...] = sm[i : i + 1, :].reshape(ref.shape)
    vq[0:1, :] = sm[7:8, 0:loc]
    vq[1:2, :] = sm[7:8, half : half + loc]
    for ref, o in zip(flat + (vq,), small + (qvb,)):
        stores.append(pltpu.make_async_copy(ref, o, sem_o.at[len(stores)]))
        stores[-1].start()
    for i, load in enumerate(loads):
        load.wait()
        if i + 20 < len(loads):
            loads[i + 20].start()
        stores[i].start()
    for copy in stores:
        copy.wait()


def solution(mesh):
    placed = (
        P("dp", None),
        P("dp", None),
        P("dp", None),
        P(),
        P(),
        P(None, None, "mp"),
        P(None, "mp"),
        P("mp", None),
        P(),
        P(),
        P(),
        P(None, "mp"),
        P("mp"),
        P("mp", None),
        P(),
        P("dp", None),
    )
    return jax.shard_map(
        functools.partial(shards, mesh.shape["dp"]),
        mesh=mesh,
        in_specs=placed,
        out_specs=(
            P("dp", None),
            P("dp", None),
            P("dp", None),
            P(),
            P(),
            P(None, None, "mp"),
            P(None, "mp"),
            P("mp", None),
            P(),
            P(),
            P(),
            P(None, "mp"),
            P("mp"),
            P("mp", None),
            P(),
        ),
        check_vma=False,
    )
```

```python
import functools

import jax
import jax.numpy as jnp
from jax import lax
from jax.experimental import pallas as pl
from jax.experimental.pallas import tpu as pltpu
from jax.sharding import PartitionSpec as P

HD = 64
SUB = 128
CH = 8
W_PIECES = 3
EACH = 3
SENDS = 4
MESH = pl.DeviceIdType.MESH
F32 = jnp.float32
BF16 = jnp.bfloat16


ARGS = ("tok", "tim", "seg", "n1g", "n1b", "wqkv", "qvb", "wout", "outb", "n2g", "n2b")
ARGS += ("wup", "upb", "wdn", "dnb", "cot")


def hop_ticks(line):
    return 2 if line <= 8 else 1


def when(cond, fn):
    pl.when(cond)(fn)


def rem(a, n):
    return lax.rem(a, jnp.int32(n))


def div(a, n):
    return lax.div(a, jnp.int32(n))


def two_power(n):
    return 1 << (n - 1).bit_length()


def nt(a, b):
    return lax.dot_general(a, b, (((1,), (1,)), ((), ())), preferred_element_type=F32)


def tn(a, b):
    return lax.dot_general(a, b, (((0,), (0,)), ((), ())), preferred_element_type=F32)


def nn(a, b):
    return jnp.dot(a, b, preferred_element_type=F32)


def normed(v):
    centred = v - jnp.mean(v, -1, keepdims=True)
    spread = jnp.mean(centred * centred, -1, keepdims=True)
    scale = lax.rsqrt(spread + 1e-05)
    return centred * scale, scale


def colsum(v):
    return jnp.sum(v, 0, keepdims=True)


def kernel(n_dp, units, names, *refs):
    out_o, ig_o, tg_o, f_out = refs[16:20]
    R = dict(zip(names, refs[20:]))
    order = ("tok", "tim", "n1g", "n1b", "wqkv", "qvb", "seg", "wout", "outb", "cot", "wdn")
    order += ("n2g", "n2b", "wup", "upb", "dnb")
    tok, tim, wqkv, qvb, seg, wout, cot, wdn, wup = (
        R[s] for s in ("tok", "tim", "wqkv", "qvb", "seg", "wout", "cot", "wdn", "wup")
    )
    loads = {
        name: pltpu.make_async_copy(refs[ARGS.index(name)], R[name], R["ins"].at[i]) for i, name in enumerate(order)
    }
    n1g, n1b, outb, n2g, n2b, upb, dnb = (R["vecs"].at[pl.ds(i, 1)] for i in range(7))
    timf, start, entry, q_s, k_s, v_s = (R[s] for s in ("timf", "start", "entry", "q", "k", "v"))
    probs, mixed_s, part, cr, ys, yr = (R[s] for s in ("probs", "mixed", "part", "cr", "ys", "yr"))
    tot, mid, e2, hp, act, gp = (R[s] for s in ("tot", "mid", "e2", "hp", "act", "gp"))
    out, ig, tg = (R[s] for s in ("out", "ig", "tg"))
    gact, gmid, gbr, lt, g, f = (R[s] for s in ("gact", "gmid", "gbr", "lt", "g", "f"))

    rows_n, seq = seg.shape
    width = tok.shape[1]
    half = width // 2
    loc = wout.shape[0]
    heads = loc // HD
    ff = wup.shape[1]
    UA, UB, UC = units
    L = n_dp // 2
    LAG = hop_ticks(L)
    H = L // 2
    dp = lax.axis_index("dp")
    mp = lax.axis_index("mp")
    core = mp % 2
    x = dp % 2
    z = dp // 2
    to_core = (dp, mp + 1 - 2 * core)
    to_y = (dp, (mp + 2) % 4)
    to_x = (dp + 1 - 2 * x, mp)
    last = jnp.minimum(z, L - 1 - z)
    side = div(z, H)
    cross = jnp.where(last == H - 1, 1, 0)
    to_in = ((z + 1 - 2 * side) * 2 + x, mp)
    to_out = (jnp.clip(z - 1 + 2 * side, 0, L - 1) * 2 + x, mp)
    zlo = jnp.maximum(z - 1, 0) * 2 + x
    zhi = jnp.minimum(z + 1, L - 1) * 2 + x

    barrier = pltpu.get_barrier_semaphore()
    for dev in (to_core, to_y, to_x):
        pl.semaphore_signal(barrier, 1, device_id=dev, device_id_type=MESH)
    when(z > 0, lambda: pl.semaphore_signal(barrier, 1, device_id=(zlo, mp), device_id_type=MESH))
    when(z < L - 1, lambda: pl.semaphore_signal(barrier, 1, device_id=(zhi, mp), device_id_type=MESH))
    greeted = 3 + jnp.minimum(z, 1) + jnp.minimum(L - 1 - z, 1)

    def sl(r, n=seq):
        return pl.ds(pl.multiple_of(r * n, n), n)

    def sub(r, i):
        return pl.ds(pl.multiple_of(r * seq + i * SUB, SUB), SUB)

    mine = pl.ds(pl.multiple_of(core * half, 128), half)
    other = pl.ds(pl.multiple_of((1 - core) * half, 128), half)

    def remote(src, dst, ssem, rsem, dev):
        return pltpu.make_async_remote_copy(
            src_ref=src, dst_ref=dst, send_sem=ssem, recv_sem=rsem, device_id=dev, device_id_type=MESH
        )

    def core_copy(p, r):
        return remote(part.at[sl(r), other], cr.at[sl(r)], R["cs"].at[r], R["crs"].at[r], to_core)

    def y_copy(p, r):
        return remote(ys.at[sl(r)], yr.at[p % 2, sl(r)], R["yss"].at[r], R["yrs"].at[p % 2, r], to_y)

    def ag_copy(p, r):
        return remote(tot.at[sl(r), mine], tot.at[sl(r), mine], R["gs"].at[r], R["grs"].at[r], to_core)

    def sum_b(p, r):
        core_copy(p, r).wait()
        ys[sl(r), :] = part[sl(r), mine] + cr[sl(r), :]
        y_copy(p, r).start()

    def sum_c(p, r):
        y_copy(p, r).wait()
        tot[sl(r), mine] = ys[sl(r), :] + yr[p % 2, sl(r), :]
        ag_copy(p, r).start()

    def sum_d(p, r):
        ag_copy(p, r).wait()

    def vec(ref):
        return ref[...]

    small = 2 * ff + 4 * loc

    def small_add(i, v):
        g[small + i : small + i + 1, :] += v

    lane = lax.broadcasted_iota(jnp.int32, (1, loc), 1)
    masks = [((lane >= h * HD) & (lane < (h + 1) * HD)).astype(F32) for h in range(heads)]

    def by_head(v):
        return jnp.concatenate([v * m.astype(BF16) for m in masks], 0)

    def from_heads(v):
        total = v[:seq] * masks[0]
        for h in range(1, heads):
            total = total + v[h * seq : (h + 1) * seq] * masks[h]
        return total

    def norm1(r):
        @pl.loop(0, seq // SUB)
        def _(i):
            s = sub(r, i)
            v = tok[s, :].astype(F32) + timf[pl.ds(r, 1), :]
            start[s, :] = v
            xhat, _ = normed(v)
            entry[s, :] = (xhat * n1g[...] + n1b[...]).astype(BF16)

    def project(r):
        e = entry[sl(r), :]
        q_s[sl(r), :] = (nt(e, wqkv[0]) + qvb[0:1, :]).astype(BF16)
        k_s[sl(r), :] = nt(e, wqkv[1]).astype(BF16)
        v_s[sl(r), :] = (nt(e, wqkv[2]) + qvb[1:2, :]).astype(BF16)

    def attend(r):
        labels = jnp.broadcast_to(seg[pl.ds(r, 1), :], (seq, seq))
        same = labels == labels.T
        same = jnp.concatenate([same.astype(F32)] * heads, 0) > 0.5
        scores = nt(by_head(q_s[sl(r), :]), k_s[sl(r), :]) * HD ** (-0.5)
        scores = jnp.where(same, scores, -1e30)
        w = jnp.exp(scores - jnp.max(scores, -1, keepdims=True))
        pr = w / jnp.sum(w, -1, keepdims=True)
        probs[sl(r, heads * seq), :] = pr
        mixed = from_heads(nn(pr.astype(BF16), v_s[sl(r), :])).astype(BF16)
        mixed_s[sl(r), :] = mixed
        turned = mixed.T
        lt[2 * ff : 2 * ff + loc, sl(r)] = turned
        mixa[mp, r] = turned.astype(F32)
        m_core(r).start()
        m_y(r).start()

    wf, wall, mixa = R["wf"], R["wall"], R["mixa"]
    mp_y, mp_c = rem(mp + 2, 4), mp + 1 - 2 * core
    mine_0, other_0 = mp - core, mp_y - core
    hl = loc // 2
    pr_n = hl // W_PIECES

    def w_core():
        return remote(wf.at[mp], wf.at[mp], R["wcs"], R["wcr"], to_core)

    def w_rows(start, n):
        return pl.ds(pl.multiple_of(start, CH), n)

    def w_y(i):
        s = w_rows(x * hl + i * pr_n, pr_n)
        return remote(wf.at[mp, s], wf.at[mp, s], R["wys"].at[i], R["wyr"].at[i], to_y)

    def w_x(i):
        s = w_rows(x * hl + i * pr_n, pr_n)
        return remote(wf.at[mp_y, s], wf.at[mp_y, s], R["wxs"].at[i], R["wxr"].at[i], to_x)

    def w_share(h):
        s = w_rows((x + h - 2 * x * h) * hl, hl)
        return remote(wf.at[mp_y, s], wf.at[mp_y, s], R["whs"].at[h], R["whr"].at[h], to_core)

    def m_core(r):
        return remote(mixa.at[mp, r], mixa.at[mp, r], R["cs"].at[r], R["crs"].at[r], to_core)

    def m_y(r):
        return remote(mixa.at[mp, r], mixa.at[mp, r], R["yss"].at[r], R["yrs"].at[0, r], to_y)

    def m_share(r):
        return remote(mixa.at[mp_y, r], mixa.at[mp_y, r], R["gs"].at[r], R["grs"].at[r], to_core)

    def weights_out():
        loads["wout"].wait()
        wf[mp] = wout[...].astype(F32)
        pl.semaphore_wait(barrier, greeted)
        for i in range(W_PIECES):
            w_y(i).start()
        w_core().start()

    def weights_on(i):
        w_y(i).wait()
        w_x(i).start()

    def pair_sum(m, r):
        return tn(mixa[m, r].astype(BF16), wall[m]) + tn(mixa[m + 1, r].astype(BF16), wall[m + 1])

    def near_part(r):
        m_core(r).wait()
        part[sl(r), :] = pair_sum(mine_0, r)

    def across(r):
        m_y(r).wait()
        m_share(r).start()

    def far_part(r):
        m_share(r).wait()
        tot[sl(r), :] = part[sl(r), :] + pair_sum(other_0, r)

    def grad_act(r):
        c = cot[sl(r), :]
        gact[sl(r), :] = nt(c, wdn[...])
        small_add(0, colsum(c.astype(F32)))

    def feed(r):
        @pl.loop(0, seq // SUB)
        def _(i):
            s = sub(r, i)
            v = start[s, :] + (tot[s, :] + outb[...])
            mid[s, :] = v
            xhat, _ = normed(v)
            e2[s, :] = (xhat * n2g[...] + n2b[...]).astype(BF16)

        hp[...] = nn(e2[sl(r), :], wup[...])

        @pl.loop(0, seq // SUB)
        def _(i):
            s = sub(r, i)
            u = hp[pl.ds(pl.multiple_of(i * SUB, SUB), SUB), :] + upb[...]
            cdf = 0.5 * (1.0 + lax.erf(u * 0.7071067811865476))
            act[s, :] = (u * cdf).astype(BF16)
            slope = cdf + u * (0.3989422804014327 * jnp.exp(-0.5 * u * u))
            pre = (gact[s, :] * slope).astype(BF16)
            gp[s, :] = pre
            small_add(1, colsum(pre.astype(F32)))

        lt[0:ff, sl(r)] = act[sl(r), :].T

    def feed_on(r):
        part[sl(r), :] = nt(gp[sl(r), :], wup[...])
        core_copy(1, r).start()
        lt[ff : 2 * ff, sl(r)] = e2[sl(r), :].T

    def back2(r):
        @pl.loop(0, seq // SUB)
        def _(i):
            s = sub(r, i)
            ge = tot[s, :]
            xhat, scale = normed(mid[s, :])
            small_add(2, colsum(ge * xhat))
            small_add(3, colsum(ge))
            gx = ge * n2g[...]
            gm = cot[s, :].astype(F32) + scale * (
                gx - jnp.mean(gx, -1, keepdims=True) - xhat * jnp.mean(gx * xhat, -1, keepdims=True)
            )
            gmid[s, :] = gm
            low = gm.astype(BF16)
            gbr[s, :] = low
            small_add(4, colsum(low.astype(F32)))

        g3 = by_head(nt(gbr[sl(r), :], wout[...]).astype(BF16))
        pr = probs[sl(r, heads * seq), :]
        grad_probs = nt(g3, v_s[sl(r), :])
        inner = jnp.sum(pr * grad_probs, -1, keepdims=True)
        ds = (pr * (grad_probs - inner)).astype(BF16)
        gq = (from_heads(nn(ds, k_s[sl(r), :])) * HD ** (-0.5)).astype(BF16)
        gk = (tn(ds, by_head(q_s[sl(r), :])) * HD ** (-0.5)).astype(BF16)
        gv = tn(pr.astype(BF16), g3).astype(BF16)
        part[sl(r), :] = nn(gq, wqkv[0]) + nn(gk, wqkv[1]) + nn(gv, wqkv[2])
        core_copy(2, r).start()
        late = 2 * ff + loc
        for i, v in enumerate((gq, gk, gv)):
            lt[late + i * loc : late + (i + 1) * loc, sl(r)] = v.T
        g[small + 7 : small + 8, 0:loc] += colsum(gq.astype(F32))
        g[small + 7 : small + 8, half : half + loc] += colsum(gv.astype(F32))

    def back1(r):
        tg[pl.ds(r, 1), :] = jnp.zeros((1, width), F32)

        @pl.loop(0, seq // SUB)
        def _(i):
            s = sub(r, i)
            ge = tot[s, :]
            xhat, scale = normed(start[s, :])
            small_add(5, colsum(ge * xhat))
            small_add(6, colsum(ge))
            gy = ge * n1g[...]
            gs = gmid[s, :] + scale * (
                gy - jnp.mean(gy, -1, keepdims=True) - xhat * jnp.mean(gy * xhat, -1, keepdims=True)
            )
            ig[s, :] = gs.astype(BF16)
            tg[pl.ds(r, 1), :] += colsum(gs)

    def down(r):
        part[sl(r), :] = nn(act[sl(r), :], wdn[...])
        core_copy(3, r).start()

    def finish(r):
        @pl.loop(0, seq // SUB)
        def _(i):
            s = sub(r, i)
            out[s, :] = (mid[s, :] + (tot[s, :] + dnb[...])).astype(BF16)

    blk = loc

    early = ff // blk

    def weight_grads(j):
        s = pl.ds(pl.multiple_of(j * blk, blk), blk)

        def by(right):
            def fn():
                g[s, :] = nn(lt[s, :], right[...])

            return fn

        when(j < early, by(cot))
        when((j >= early) & (j < 2 * early), by(gp))
        when(j == 2 * early, by(gbr))
        when(j > 2 * early, by(entry))

    def go(copy, u, depth):
        when(u >= depth, lambda: copy(u - depth).wait_send())
        copy(u).start()

    def end(copy, n, depth):
        for u in range(n - min(depth, n), n):
            copy(u).wait_send()

    AF = LAG

    def base_of(u):
        return u * 4 * CH

    def later(u):
        return base_of(div(u, EACH) * (EACH + 2) + rem(u, EACH))

    def b_base(u, i):
        return base_of(jnp.minimum(u * (EACH + 2) + EACH + i, UA + UB + UC - 1))

    def a_base(u, owner):
        return later(u) + owner * 2 * CH

    def x_slot(u):
        return pl.ds(pl.multiple_of(rem(u, R["xr"].shape[0]) * 2 * CH, CH), 2 * CH)

    def x_first(u):
        src = pl.ds(pl.multiple_of(later(u) + (1 - x) * 2 * CH, CH), 2 * CH)
        return remote(
            g.at[src], R["xrb"].at[x_slot(u)], R["xs"].at[rem(u, SENDS)], R["xr"].at[rem(u, R["xr"].shape[0])], to_x
        )

    def rows_at(base, n):
        return pl.ds(pl.multiple_of(base, CH), n)

    class Line:
        def __init__(self, kind, n, first, stride, depth):
            self.kind, self.n, self.first, self.stride, self.depth = kind, n, first, stride, depth

        def unit(self, t, offset):
            rel = t - self.first - offset
            if self.stride == 1:
                return rel, (rel >= 0) & (rel < self.n)
            return div(rel, self.stride), (rel >= 0) & (rel < self.n * self.stride) & (rem(rel, self.stride) == 0)

        def sem(self, name, i, u):
            ref = R[self.kind + "_" + name]
            return ref.at[i, rem(u, ref.shape[1])]

        def slot(self, u, rows):
            return rows_at(rem(u, R[self.kind + "_r"].shape[1]) * rows, rows)

        def go(self, copy, u):
            go(copy, u, self.depth)

        def end(self, copy):
            end(copy, self.n, self.depth)

    class A(Line):
        def own(self, u):
            return rows_at(a_base(u, x), 2 * CH)

        def inward(self, u):
            dst = R["abuf"].at[cross, self.slot(u, 2 * CH)]
            return remote(g.at[self.own(u)], dst, self.sem("s", 0, u), self.sem("r", cross, u), to_in)

        def arrived(self, u, i):
            buf = R["abuf"].at[i, self.slot(u, 2 * CH)]
            remote(buf, buf, self.sem("s", 0, u), self.sem("r", i, u), to_in).wait_recv()
            return buf

        def outward(self, u):
            own = self.own(u)
            return remote(f.at[own], f.at[own], self.sem("u", 0, u), self.sem("t", 0, u), to_out)

        def x_last(self, u):
            own = self.own(u)
            return remote(f.at[own], f.at[own], self.sem("xs", 0, u), self.sem("xr", 0, u), to_x)

        def tick(self, t):
            u, valid_u = self.unit(t, last * LAG)

            def reduce():
                def add():
                    g[self.own(u), :] += self.arrived(u, 0)[...]

                if H > 1:
                    when(last > 0, add)
                self.go(self.inward, u)

            when(valid_u, reduce)
            v, valid_v = self.unit(t, (2 * H - 1 - last) * LAG)

            def finish():
                def turn():
                    f[self.own(v), :] = g[self.own(v), :] + self.arrived(v, 1)[...]

                when(last == H - 1, turn)
                if H > 1:
                    when(last < H - 1, lambda: self.outward(v).wait_recv())
                    when(last > 0, lambda: self.go(self.outward, v))
                self.go(self.x_last, v)

            when(valid_v, finish)
            e, valid_e = self.unit(t, (2 * H - last) * LAG)
            when(valid_e, lambda: self.x_last(e).wait_recv())

        def drain(self):
            self.end(self.inward)
            self.end(self.x_last)
            if H > 1:
                when(last > 0, lambda: self.end(self.outward))

    class B(Line):
        def all(self, u):
            return rows_at(b_base(u, 0), 4 * CH)

        def half(self, u, i):
            return rows_at(b_base(u, 0) + i * 2 * CH, 2 * CH)

        def inward(self, u):
            dst = R["bbuf"].at[self.slot(u, 4 * CH)]
            return remote(g.at[self.all(u)], dst, self.sem("s", 0, u), self.sem("r", 0, u), to_in)

        def swap(self, u):
            dst = R["bsw"].at[self.slot(u, 2 * CH)]
            return remote(g.at[self.half(u, 1 - side)], dst, self.sem("s", 0, u), self.sem("r", 1, u), to_in)

        def x_copy(self, u):
            dst = R["bxb"].at[self.slot(u, 2 * CH)]
            return remote(g.at[self.half(u, side)], dst, self.sem("xs", 0, u), self.sem("xr", 0, u), to_x)

        def back(self, u):
            own = self.half(u, side)
            return remote(f.at[own], f.at[own], self.sem("d", 0, u), self.sem("r", 2, u), to_in)

        def outward(self, u):
            own = self.all(u)
            return remote(f.at[own], f.at[own], self.sem("u", 0, u), self.sem("t", 0, u), to_out)

        def tick(self, t):
            u, valid_u = self.unit(t, last * LAG)

            def reduce():
                def add():
                    self.inward(u).wait_recv()
                    g[self.all(u), :] += R["bbuf"][self.slot(u, 4 * CH), :]

                if H > 1:
                    when(last > 0, add)
                    when(last < H - 1, lambda: self.go(self.inward, u))
                when(last == H - 1, lambda: self.go(self.swap, u))

            when(valid_u, reduce)
            middle = last == H - 1
            i, valid_i = self.unit(t, H * LAG)

            def over():
                self.swap(i).wait_recv()
                g[self.half(i, side), :] += R["bsw"][self.slot(i, 2 * CH), :]
                self.go(self.x_copy, i)

            when(valid_i & middle, over)
            j, valid_j = self.unit(t, (H + 1) * LAG)

            def total():
                self.x_copy(j).wait_recv()
                own = self.half(j, side)
                f[own, :] = g[own, :] + R["bxb"][self.slot(j, 2 * CH), :]
                self.go(self.back, j)

            when(valid_j & middle, total)
            v, valid_v = self.unit(t, (2 * H + 1 - last) * LAG)

            def finish():
                when(middle, lambda: self.back(v).wait_recv())
                if H > 1:
                    when(last < H - 1, lambda: self.outward(v).wait_recv())
                    when(last > 0, lambda: self.go(self.outward, v))

            when(valid_v, finish)

        def drain(self):
            def ends():
                for copy in (self.swap, self.x_copy, self.back):
                    self.end(copy)

            when(last == H - 1, ends)
            if H > 1:
                when(last < H - 1, lambda: self.end(self.inward))
                when(last > 0, lambda: self.end(self.outward))

    class C(Line):
        def own(self, u, d):
            return rows_at(b_base(u, 1) + d * 2 * CH, 2 * CH)

        def place(self, d):
            w = z if d == 0 else L - 1 - z
            return w, (zhi if d == 0 else zlo, mp), (zlo if d == 0 else zhi, mp)

        def copies(self, d):
            w, up, dn = self.place(d)
            own = lambda u: self.own(u, d)
            slot = lambda u: self.slot(u, 2 * CH)

            def send(u):
                return remote(g.at[own(u)], R["cbuf"].at[d, slot(u)], self.sem("s", d, u), self.sem("r", d, u), dn)

            def x_copy(u):
                return remote(g.at[own(u)], R["cxb"].at[d, slot(u)], self.sem("xs", d, u), self.sem("xr", d, u), to_x)

            def spread(u):
                return remote(f.at[own(u)], f.at[own(u)], self.sem("u", d, u), self.sem("t", d, u), up)

            return w, send, x_copy, spread

        def tick(self, t):
            for d in (0, 1):
                w, send, x_copy, spread = self.copies(d)
                u, valid_u = self.unit(t, (L - 1 - w) * LAG)

                def reduce():
                    def add():
                        send(u).wait_recv()
                        g[self.own(u, d), :] += R["cbuf"][d, self.slot(u, 2 * CH), :]

                    when(w < L - 1, add)
                    when(w > 0, lambda: self.go(send, u))
                    when(w == 0, lambda: self.go(x_copy, u))

                when(valid_u, reduce)
                v, valid_v = self.unit(t, (L + w) * LAG)

                def finish():
                    def turn():
                        x_copy(v).wait_recv()
                        own = self.own(v, d)
                        f[own, :] = g[own, :] + R["cxb"][d, self.slot(v, 2 * CH), :]

                    when(w == 0, turn)
                    when(w > 0, lambda: spread(v).wait_recv())
                    when(w < L - 1, lambda: self.go(spread, v))

                when(valid_v, finish)

        def drain(self):
            for d in (0, 1):
                w, send, x_copy, spread = self.copies(d)
                when(w > 0, lambda: self.end(send))
                when(w == 0, lambda: self.end(x_copy))
                when(w < L - 1, lambda: self.end(spread))

    lines = [C("c", UC, 0, EACH, 2), B("b", UB, 1, EACH, 2), A("a", UA, AF, 1, SENDS)]

    def dp_tick(t):
        when(t < UA, lambda: go(x_first, t, SENDS))
        v = t - AF

        def x_add():
            x_first(v).wait_recv()
            s = rows_at(a_base(v, x), 2 * CH)
            g[s, :] += R["xrb"][x_slot(v), :]

        when((v >= 0) & (v < UA), x_add)
        for line in lines:
            line.tick(t)

    def dp_drain():
        end(x_first, UA, SENDS)
        for line in lines:
            line.drain()

    for copy in loads.values():
        copy.start()

    def vector(i, name):
        loads[name].wait()
        R["vecs"][i : i + 1, :] = R[name][...][None, :]

    g[small : small + 4 * CH, :] = jnp.zeros((4 * CH, width), F32)
    for name in ("tok", "tim"):
        loads[name].wait()
    timf[...] = tim[...].astype(F32)
    vector(0, "n1g")
    vector(1, "n1b")

    @pl.loop(0, rows_n)
    def _(r):
        norm1(r)

        @pl.when(r == 0)
        def _():
            for name in ("wqkv", "qvb", "seg"):
                loads[name].wait()

        project(r)
        when(r == 0, weights_out)
        attend(r)
        for i in range(W_PIECES - 1):
            when(r == rows_n - W_PIECES + 1 + i, lambda: weights_on(i))

    for name in ("cot", "wdn", "wup"):
        loads[name].wait()
    for i, name in enumerate(("outb", "n2g", "n2b", "upb", "dnb")):
        vector(2 + i, name)
    pl.loop(0, rows_n)(grad_act)
    weights_on(W_PIECES - 1)
    w_share(0).start()
    w_core().wait()
    for i in range(2):
        wall[mine_0 + i] = wf[mine_0 + i].astype(BF16)
    pl.loop(0, rows_n)(near_part)
    ahead = min(2, rows_n)
    for r in range(ahead):
        across(r)
    for i in range(W_PIECES):
        w_x(i).wait()
    w_share(1).start()
    for h in range(2):
        w_share(h).wait()
    for i in range(2):
        wall[other_0 + i] = wf[other_0 + i].astype(BF16)

    @pl.loop(0, rows_n)
    def _(r):
        far_part(r)
        feed(r)
        when(r + ahead < rows_n, lambda: across(r + ahead))

    weight_grads(jnp.int32(0))

    blocks = (2 * ff + 4 * loc) // blk
    a_last = AF + LAG * 2 * H
    b_last, c_last = 1 + LAG * (2 * H + 1), LAG * (2 * L - 1)
    ticks = max(UA - 1 + a_last, EACH * (UB - 1) + b_last, EACH * (UC - 1) + c_last) + 1

    def done(j):
        start = (6 * j + 5) // (EACH + 2) * EACH + EACH - 1
        return start + max(a_last, b_last, c_last)

    def out_copy(j):
        s = pl.ds(j * blk, blk if j < blocks else 4 * CH)
        return pltpu.make_async_copy(f.at[s], f_out.at[s], R["fin"].at[j])

    done_copies = [
        pltpu.make_async_copy(a, b, R["fin"].at[blocks + 1 + i])
        for i, (a, b) in enumerate(((ig, ig_o), (tg, tg_o), (out, out_o)))
    ]

    @pl.loop(0, ticks)
    def _(t):
        dp_tick(t)

        def at(first, step, fn):
            r = (t - first) // step
            when((t >= first) & ((t - first) % step == 0) & (r < rows_n), lambda: fn(r))

        at(1, 1, lambda r: sum_b(1, r))
        at(0, 1, feed_on)
        at(5, 3, lambda r: sum_c(1, r))

        def second(r):
            sum_d(1, r)
            back2(r)

        at(6, 3, second)
        at(7, 3, lambda r: sum_b(2, r))
        at(13, 3, lambda r: sum_c(2, r))

        def third(r):
            sum_d(2, r)
            back1(r)

        at(14, 3, third)
        at(15, 3, down)
        at(16, 3, lambda r: sum_b(3, r))
        at(22, 3, lambda r: sum_c(3, r))

        def fourth(r):
            sum_d(3, r)
            finish(r)

        at(23, 3, fourth)

        @pl.when(t == 23 + 3 * rows_n)
        def _():
            for copy in done_copies:
                copy.start()

        when((rem(t, 3) == 1) & (t < 3 * blocks - 2), lambda: weight_grads(div(t + 2, 3)))
        for j in range(blocks):
            if done(j) < ticks:
                when(t == done(j), lambda: out_copy(j).start())

    dp_drain()
    for j in range(blocks + 1):
        if j == blocks or done(j) >= ticks:
            out_copy(j).start()
    for copy in done_copies + [out_copy(j) for j in range(blocks + 1)]:
        copy.wait()


def shards(n_dp, *args):
    (tok, tim, seg, n1g, n1b, wqkv, qvb, wout, outb, n2g, n2b, wup, upb, wdn, dnb, cot) = args
    tokens, width = tok.shape
    rows_n, seq = seg.shape
    loc, ff = wout.shape[0], wup.shape[1]
    heads = loc // HD
    half = width // 2
    big = 2 * ff + 4 * loc
    count = big // (4 * CH) + 1
    UC = count // (EACH + 2)
    UB = UC + count % (EACH + 2) // EACH
    UA = count - UB - UC
    L = n_dp // 2
    LAG = hop_ticks(L)
    vm = pltpu.VMEM
    dma = pltpu.SemaphoreType.DMA
    W = two_power(max(LAG * (L - 1) + 1, 2 * LAG + 2))
    WB = two_power(LAG * (L + 1) // EACH + 1)
    WC = two_power(LAG * (2 * L - 1) // EACH + 1)
    total = count * 4 * CH
    flat = lambda n: vm((n,), F32)
    scratch = dict(
        tok=vm((tokens, width), BF16),
        cot=vm((tokens, width), BF16),
        wqkv=vm((3, loc, width), BF16),
        wout=vm((loc, width), BF16),
        wup=vm((width, ff), BF16),
        wdn=vm((ff, width), BF16),
        ins=dma((16,)),
        tim=vm((rows_n, width), BF16),
        seg=vm((rows_n, seq), jnp.int32),
        qvb=vm((2, loc), F32),
        **{s: flat(width) for s in ("n1g", "n1b", "outb", "n2g", "n2b", "dnb")},
        upb=flat(ff),
        vecs=vm((8, width), F32),
        timf=vm((rows_n, width), F32),
        start=vm((tokens, width), F32),
        entry=vm((tokens, width), BF16),
        q=vm((tokens, loc), BF16),
        k=vm((tokens, loc), BF16),
        v=vm((tokens, loc), BF16),
        probs=vm((heads * tokens, seq), F32),
        mixed=vm((tokens, loc), BF16),
        part=vm((tokens, width), F32),
        cr=vm((tokens, half), F32),
        ys=vm((tokens, half), F32),
        yr=vm((2, tokens, half), F32),
        tot=vm((tokens, width), F32),
        mid=vm((tokens, width), F32),
        e2=vm((tokens, width), BF16),
        hp=vm((seq, ff), F32),
        act=vm((tokens, ff), BF16),
        gp=vm((tokens, ff), BF16),
        gact=vm((tokens, ff), F32),
        gmid=vm((tokens, width), F32),
        gbr=vm((tokens, width), BF16),
        out=vm((tokens, width), BF16),
        ig=vm((tokens, width), BF16),
        tg=vm((rows_n, width), F32),
        lt=vm((big, tokens), BF16),
        g=vm((total, width), F32),
        f=vm((total, width), F32),
        xrb=vm((W * 2 * CH, width), F32),
        abuf=vm((2, W * 2 * CH, width), F32),
        bbuf=vm((WB * 4 * CH, width), F32),
        bsw=vm((WB * 2 * CH, width), F32),
        bxb=vm((WB * 2 * CH, width), F32),
        cbuf=vm((2, WC * 2 * CH, width), F32),
        cxb=vm((2, WC * 2 * CH, width), F32),
        wf=vm((4, loc, width), F32),
        wall=vm((4, loc, width), BF16),
        mixa=vm((4, rows_n, loc, seq), F32),
        wcs=dma,
        wcr=dma,
        **{s: dma((W_PIECES,)) for s in ("wys", "wyr", "wxs", "wxr")},
        **{s: dma((2,)) for s in ("whs", "whr")},
        **{s: dma((rows_n,)) for s in ("cs", "crs", "yss", "gs", "grs")},
        yrs=dma((2, rows_n)),
        fin=dma((big // loc + 4,)),
        xs=dma((SENDS,)),
        xr=dma((W,)),
        **{"a_" + s: dma((1, SENDS)) for s in ("s", "u", "xs")},
        a_r=dma((2, W)),
        **{"a_" + s: dma((1, W)) for s in ("t", "xr")},
        **{"b_" + s: dma((1, 2)) for s in ("s", "u", "d", "xs")},
        b_r=dma((3, WB)),
        **{"b_" + s: dma((1, WB)) for s in ("t", "xr")},
        **{"c_" + s: dma((2, 2)) for s in ("s", "u", "xs")},
        **{"c_" + s: dma((2, WC)) for s in ("r", "t", "xr")},
    )
    any_spec = pl.BlockSpec(memory_space=pl.ANY)
    vm_spec = pl.BlockSpec(memory_space=pltpu.VMEM)
    out, ig, tg, f = pl.pallas_call(
        functools.partial(kernel, n_dp, (UA, UB, UC), tuple(scratch)),
        out_shape=(
            jax.ShapeDtypeStruct((tokens, width), BF16),
            jax.ShapeDtypeStruct((tokens, width), BF16),
            jax.ShapeDtypeStruct((rows_n, width), F32),
            jax.ShapeDtypeStruct((total, width), F32),
        ),
        in_specs=[any_spec] * 16,
        out_specs=(any_spec,) * 4,
        scratch_shapes=list(scratch.values()),
        compiler_params=pltpu.CompilerParams(
            collective_id=0, has_side_effects=True, vmem_limit_bytes=63 * 2**20
        ),
        cost_estimate=pl.CostEstimate(flops=6 * 10**9, bytes_accessed=20 * 10**6, transcendentals=0),
    )(
        tok, tim, seg, n1g, n1b, wqkv.transpose(0, 2, 1), qvb, wout, outb, n2g, n2b, wup, upb, wdn, dnb, cot
    )
    f32 = lambda *shape: jax.ShapeDtypeStruct(shape, F32)
    moved = (
        jax.ShapeDtypeStruct((tokens, width), BF16),
        jax.ShapeDtypeStruct((tokens, width), BF16),
        f32(rows_n, width),
        f32(3, loc, width),
        f32(loc, width),
        f32(width, ff),
        f32(ff, width),
    )
    results = pl.pallas_call(
        functools.partial(place, big),
        out_shape=moved + (f32(2, loc), f32(ff)) + (f32(width),) * 6,
        in_specs=[any_spec] * 4,
        out_specs=(any_spec,) * 15,
        scratch_shapes=[
            vm((8, width), F32),
            vm((big, width), F32),
            vm((tokens, width), BF16),
            vm((tokens, width), BF16),
            vm((rows_n, width), F32),
            vm((2, loc), F32),
            *[vm((width,), F32)] * 7,
            dma((18,)),
            dma((26,)),
        ],
        compiler_params=pltpu.CompilerParams(vmem_limit_bytes=63 * 2**20),
    )(out, ig, tg, f)
    out, ig, tg, qkv, outw, up, down, qvb, upb, downb, n2g, n2b, outb, n1g, n1b = results
    return out, ig, tg, n1g, n1b, qkv.transpose(0, 2, 1), qvb, outw, outb, n2g, n2b, up, upb, down, downb


def place(big, *refs):
    out, ig, tg, f, out_o, ig_o, tg_o, qkv, outw, up, down, qvb, upb, downb = refs[:14]
    n2g, n2b, outb, n1g, n1b, sm, buf, vo, vi, vt, vq = refs[14:25]
    flat = refs[25:32]
    sem, sem_o = refs[32:]
    loc, ff = outw.shape[0], down.shape[0]
    half = f.shape[1] // 2
    moves = [(tg, vt, tg_o)]
    row = 0
    for n, ref in ((ff, down), (ff, up), (loc, outw), (loc, qkv.at[0]), (loc, qkv.at[1]), (loc, qkv.at[2])):
        step = max(n * 12 // (2 * ff + 4 * loc), 1)
        for i in range(step):
            s = pl.ds(row, n // step)
            moves.append((f.at[s], buf.at[s], ref.at[pl.ds(i * (n // step), n // step)]))
            row += n // step
    moves += [(out, vo, out_o), (ig, vi, ig_o)]
    first = pltpu.make_async_copy(f.at[pl.ds(big, 8)], sm, sem.at[len(moves)])
    first.start()
    loads = [pltpu.make_async_copy(a, v, sem.at[i]) for i, (a, v, b) in enumerate(moves)]
    stores = [pltpu.make_async_copy(v, b, sem_o.at[i]) for i, (a, v, b) in enumerate(moves)]
    for copy in loads[:20]:
        copy.start()
    first.wait()
    small = (downb, upb, n2g, n2b, outb, n1g, n1b)
    for i, ref in enumerate(flat):
        ref[...] = sm[i : i + 1, :].reshape(ref.shape)
    vq[0:1, :] = sm[7:8, 0:loc]
    vq[1:2, :] = sm[7:8, half : half + loc]
    for ref, o in zip(flat + (vq,), small + (qvb,)):
        stores.append(pltpu.make_async_copy(ref, o, sem_o.at[len(stores)]))
        stores[-1].start()
    for i, load in enumerate(loads):
        load.wait()
        if i + 20 < len(loads):
            loads[i + 20].start()
        stores[i].start()
    for copy in stores:
        copy.wait()


def solution(mesh):
    placed = (
        P("dp", None),
        P("dp", None),
        P("dp", None),
        P(),
        P(),
        P(None, None, "mp"),
        P(None, "mp"),
        P("mp", None),
        P(),
        P(),
        P(),
        P(None, "mp"),
        P("mp"),
        P("mp", None),
        P(),
        P("dp", None),
    )
    return jax.shard_map(
        functools.partial(shards, mesh.shape["dp"]),
        mesh=mesh,
        in_specs=placed,
        out_specs=(
            P("dp", None),
            P("dp", None),
            P("dp", None),
            P(),
            P(),
            P(None, None, "mp"),
            P(None, "mp"),
            P("mp", None),
            P(),
            P(),
            P(),
            P(None, "mp"),
            P("mp"),
            P("mp", None),
            P(),
        ),
        check_vma=False,
    )
```

```python
import functools

import jax
import jax.numpy as jnp
from jax import lax
from jax.experimental import pallas as pl
from jax.experimental.pallas import tpu as pltpu
from jax.sharding import PartitionSpec as P

HD = 64
SUB = 128
CH = 8
W_PIECES = 3
EACH = 3
S_FIRST = 30
SENDS = 4
MESH = pl.DeviceIdType.MESH
F32 = jnp.float32
BF16 = jnp.bfloat16


ARGS = ("tok", "tim", "seg", "n1g", "n1b", "wqkv", "qvb", "wout", "outb", "n2g", "n2b")
ARGS += ("wup", "upb", "wdn", "dnb", "cot")


def hop_ticks(line):
    return 2 if line <= 8 else 1


def when(cond, fn):
    pl.when(cond)(fn)


def rem(a, n):
    return lax.rem(a, jnp.int32(n))


def div(a, n):
    return lax.div(a, jnp.int32(n))


def two_power(n):
    return 1 << (n - 1).bit_length()


def nt(a, b):
    return lax.dot_general(a, b, (((1,), (1,)), ((), ())), preferred_element_type=F32)


def tn(a, b):
    return lax.dot_general(a, b, (((0,), (0,)), ((), ())), preferred_element_type=F32)


def nn(a, b):
    return jnp.dot(a, b, preferred_element_type=F32)


def normed(v):
    centred = v - jnp.mean(v, -1, keepdims=True)
    spread = jnp.mean(centred * centred, -1, keepdims=True)
    scale = lax.rsqrt(spread + 1e-05)
    return centred * scale, scale


def colsum(v):
    return jnp.sum(v, 0, keepdims=True)


def kernel(n_dp, units, names, *refs):
    out_o, ig_o, tg_o, f_out = refs[16:20]
    R = dict(zip(names, refs[20:]))
    order = ("tok", "tim", "n1g", "n1b", "wqkv", "qvb", "seg", "wout", "outb", "cot", "wdn")
    order += ("n2g", "n2b", "wup", "upb", "dnb")
    tok, tim, wqkv, qvb, seg, wout, cot, wdn, wup = (
        R[s] for s in ("tok", "tim", "wqkv", "qvb", "seg", "wout", "cot", "wdn", "wup")
    )
    loads = {
        name: pltpu.make_async_copy(refs[ARGS.index(name)], R[name], R["ins"].at[i]) for i, name in enumerate(order)
    }
    n1g, n1b, outb, n2g, n2b, upb, dnb = (R["vecs"].at[pl.ds(i, 1)] for i in range(7))
    timf, start, entry, q_s, k_s, v_s = (R[s] for s in ("timf", "start", "entry", "q", "k", "v"))
    probs, mixed_s, part, cr, ys, yr = (R[s] for s in ("probs", "mixed", "part", "cr", "ys", "yr"))
    tot, mid, e2, hp, act, gp = (R[s] for s in ("tot", "mid", "e2", "hp", "act", "gp"))
    out, ig, tg = (R[s] for s in ("out", "ig", "tg"))
    gact, gmid, gbr, lt, g, f = (R[s] for s in ("gact", "gmid", "gbr", "lt", "g", "f"))

    rows_n, seq = seg.shape
    width = tok.shape[1]
    half = width // 2
    loc = wout.shape[0]
    heads = loc // HD
    ff = wup.shape[1]
    UA, UB, UC = units
    L = n_dp // 2
    LAG = hop_ticks(L)
    H = L // 2
    dp = lax.axis_index("dp")
    mp = lax.axis_index("mp")
    core = mp % 2
    x = dp % 2
    z = dp // 2
    to_core = (dp, mp + 1 - 2 * core)
    to_y = (dp, (mp + 2) % 4)
    to_x = (dp + 1 - 2 * x, mp)
    last = jnp.minimum(z, L - 1 - z)
    side = div(z, H)
    cross = jnp.where(last == H - 1, 1, 0)
    to_in = ((z + 1 - 2 * side) * 2 + x, mp)
    to_out = (jnp.clip(z - 1 + 2 * side, 0, L - 1) * 2 + x, mp)
    zlo = jnp.maximum(z - 1, 0) * 2 + x
    zhi = jnp.minimum(z + 1, L - 1) * 2 + x

    barrier = pltpu.get_barrier_semaphore()
    for dev in (to_core, to_y, to_x):
        pl.semaphore_signal(barrier, 1, device_id=dev, device_id_type=MESH)
    when(z > 0, lambda: pl.semaphore_signal(barrier, 1, device_id=(zlo, mp), device_id_type=MESH))
    when(z < L - 1, lambda: pl.semaphore_signal(barrier, 1, device_id=(zhi, mp), device_id_type=MESH))
    greeted = 3 + jnp.minimum(z, 1) + jnp.minimum(L - 1 - z, 1)

    def sl(r, n=seq):
        return pl.ds(pl.multiple_of(r * n, n), n)

    def sub(r, i):
        return pl.ds(pl.multiple_of(r * seq + i * SUB, SUB), SUB)

    mine = pl.ds(pl.multiple_of(core * half, 128), half)
    other = pl.ds(pl.multiple_of((1 - core) * half, 128), half)

    def remote(src, dst, ssem, rsem, dev):
        return pltpu.make_async_remote_copy(
            src_ref=src, dst_ref=dst, send_sem=ssem, recv_sem=rsem, device_id=dev, device_id_type=MESH
        )

    def core_copy(p, r):
        return remote(part.at[sl(r), other], cr.at[sl(r)], R["cs"].at[r], R["crs"].at[r], to_core)

    def y_copy(p, r):
        return remote(ys.at[sl(r)], yr.at[p % 2, sl(r)], R["yss"].at[r], R["yrs"].at[p % 2, r], to_y)

    def ag_copy(p, r):
        return remote(tot.at[sl(r), mine], tot.at[sl(r), mine], R["gs"].at[r], R["grs"].at[r], to_core)

    def sum_b(p, r):
        core_copy(p, r).wait()
        ys[sl(r), :] = part[sl(r), mine] + cr[sl(r), :]
        y_copy(p, r).start()

    def sum_c(p, r):
        y_copy(p, r).wait()
        tot[sl(r), mine] = ys[sl(r), :] + yr[p % 2, sl(r), :]
        ag_copy(p, r).start()

    def sum_d(p, r):
        ag_copy(p, r).wait()

    def vec(ref):
        return ref[...]

    small = 2 * ff + 4 * loc

    def small_add(i, v):
        g[small + i : small + i + 1, :] += v

    lane = lax.broadcasted_iota(jnp.int32, (1, loc), 1)
    masks = [((lane >= h * HD) & (lane < (h + 1) * HD)).astype(F32) for h in range(heads)]

    def by_head(v):
        return jnp.concatenate([v * m.astype(BF16) for m in masks], 0)

    def from_heads(v):
        total = v[:seq] * masks[0]
        for h in range(1, heads):
            total = total + v[h * seq : (h + 1) * seq] * masks[h]
        return total

    def norm1(r):
        @pl.loop(0, seq // SUB)
        def _(i):
            s = sub(r, i)
            v = tok[s, :].astype(F32) + timf[pl.ds(r, 1), :]
            start[s, :] = v
            xhat, _ = normed(v)
            entry[s, :] = (xhat * n1g[...] + n1b[...]).astype(BF16)

    def project(r):
        e = entry[sl(r), :]
        q_s[sl(r), :] = (nt(e, wqkv[0]) + qvb[0:1, :]).astype(BF16)
        k_s[sl(r), :] = nt(e, wqkv[1]).astype(BF16)
        v_s[sl(r), :] = (nt(e, wqkv[2]) + qvb[1:2, :]).astype(BF16)

    def attend(r):
        labels = jnp.broadcast_to(seg[pl.ds(r, 1), :], (seq, seq))
        same = labels == labels.T
        same = jnp.concatenate([same.astype(F32)] * heads, 0) > 0.5
        scores = nt(by_head(q_s[sl(r), :]), k_s[sl(r), :]) * HD ** (-0.5)
        scores = jnp.where(same, scores, -1e30)
        w = jnp.exp(scores - jnp.max(scores, -1, keepdims=True))
        pr = w / jnp.sum(w, -1, keepdims=True)
        probs[sl(r, heads * seq), :] = pr
        mixed = from_heads(nn(pr.astype(BF16), v_s[sl(r), :])).astype(BF16)
        mixed_s[sl(r), :] = mixed
        turned = mixed.T
        lt[2 * ff : 2 * ff + loc, sl(r)] = turned
        mixa[mp, r] = turned.astype(F32)
        m_core(r).start()
        m_y(r).start()

    wf, wall, mixa = R["wf"], R["wall"], R["mixa"]
    mp_y, mp_c = rem(mp + 2, 4), mp + 1 - 2 * core
    mine_0, other_0 = mp - core, mp_y - core
    hl = loc // 2
    pr_n = hl // W_PIECES

    def w_core():
        return remote(wf.at[mp], wf.at[mp], R["wcs"], R["wcr"], to_core)

    def w_rows(start, n):
        return pl.ds(pl.multiple_of(start, CH), n)

    def w_y(i):
        s = w_rows(x * hl + i * pr_n, pr_n)
        return remote(wf.at[mp, s], wf.at[mp, s], R["wys"].at[i], R["wyr"].at[i], to_y)

    def w_x(i):
        s = w_rows(x * hl + i * pr_n, pr_n)
        return remote(wf.at[mp_y, s], wf.at[mp_y, s], R["wxs"].at[i], R["wxr"].at[i], to_x)

    def w_share(h):
        s = w_rows((x + h - 2 * x * h) * hl, hl)
        return remote(wf.at[mp_y, s], wf.at[mp_y, s], R["whs"].at[h], R["whr"].at[h], to_core)

    def m_core(r):
        return remote(mixa.at[mp, r], mixa.at[mp, r], R["cs"].at[r], R["crs"].at[r], to_core)

    def m_y(r):
        return remote(mixa.at[mp, r], mixa.at[mp, r], R["yss"].at[r], R["yrs"].at[0, r], to_y)

    def m_share(r):
        return remote(mixa.at[mp_y, r], mixa.at[mp_y, r], R["gs"].at[r], R["grs"].at[r], to_core)

    def weights_out():
        loads["wout"].wait()
        wf[mp] = wout[...].astype(F32)
        pl.semaphore_wait(barrier, greeted)
        for i in range(W_PIECES):
            w_y(i).start()
        w_core().start()

    def weights_on(i):
        w_y(i).wait()
        w_x(i).start()

    def pair_sum(m, r):
        return tn(mixa[m, r].astype(BF16), wall[m]) + tn(mixa[m + 1, r].astype(BF16), wall[m + 1])

    def near_part(r):
        m_core(r).wait()
        part[sl(r), :] = pair_sum(mine_0, r)

    def across(r):
        m_y(r).wait()
        m_share(r).start()

    def far_part(r):
        m_share(r).wait()
        tot[sl(r), :] = part[sl(r), :] + pair_sum(other_0, r)

    def grad_act(r):
        c = cot[sl(r), :]
        gact[sl(r), :] = nt(c, wdn[...])
        small_add(0, colsum(c.astype(F32)))

    def feed(r):
        @pl.loop(0, seq // SUB)
        def _(i):
            s = sub(r, i)
            v = start[s, :] + (tot[s, :] + outb[...])
            mid[s, :] = v
            xhat, _ = normed(v)
            e2[s, :] = (xhat * n2g[...] + n2b[...]).astype(BF16)

        hp[...] = nn(e2[sl(r), :], wup[...])

        @pl.loop(0, seq // SUB)
        def _(i):
            s = sub(r, i)
            u = hp[pl.ds(pl.multiple_of(i * SUB, SUB), SUB), :] + upb[...]
            cdf = 0.5 * (1.0 + lax.erf(u * 0.7071067811865476))
            act[s, :] = (u * cdf).astype(BF16)
            slope = cdf + u * (0.3989422804014327 * jnp.exp(-0.5 * u * u))
            pre = (gact[s, :] * slope).astype(BF16)
            gp[s, :] = pre
            small_add(1, colsum(pre.astype(F32)))

        lt[0:ff, sl(r)] = act[sl(r), :].T

    def feed_on(r):
        part[sl(r), :] = nt(gp[sl(r), :], wup[...])
        core_copy(1, r).start()
        lt[ff : 2 * ff, sl(r)] = e2[sl(r), :].T

    def back2(r):
        @pl.loop(0, seq // SUB)
        def _(i):
            s = sub(r, i)
            ge = tot[s, :]
            xhat, scale = normed(mid[s, :])
            small_add(2, colsum(ge * xhat))
            small_add(3, colsum(ge))
            gx = ge * n2g[...]
            gm = cot[s, :].astype(F32) + scale * (
                gx - jnp.mean(gx, -1, keepdims=True) - xhat * jnp.mean(gx * xhat, -1, keepdims=True)
            )
            gmid[s, :] = gm
            low = gm.astype(BF16)
            gbr[s, :] = low
            small_add(4, colsum(low.astype(F32)))

        g3 = by_head(nt(gbr[sl(r), :], wout[...]).astype(BF16))
        pr = probs[sl(r, heads * seq), :]
        grad_probs = nt(g3, v_s[sl(r), :])
        inner = jnp.sum(pr * grad_probs, -1, keepdims=True)
        ds = (pr * (grad_probs - inner)).astype(BF16)
        gq = (from_heads(nn(ds, k_s[sl(r), :])) * HD ** (-0.5)).astype(BF16)
        gk = (tn(ds, by_head(q_s[sl(r), :])) * HD ** (-0.5)).astype(BF16)
        gv = tn(pr.astype(BF16), g3).astype(BF16)
        part[sl(r), :] = nn(gq, wqkv[0]) + nn(gk, wqkv[1]) + nn(gv, wqkv[2])
        core_copy(2, r).start()
        late = 2 * ff + loc
        for i, v in enumerate((gq, gk, gv)):
            lt[late + i * loc : late + (i + 1) * loc, sl(r)] = v.T
        g[small + 7 : small + 8, 0:loc] += colsum(gq.astype(F32))
        g[small + 7 : small + 8, half : half + loc] += colsum(gv.astype(F32))

    def back1(r):
        tg[pl.ds(r, 1), :] = jnp.zeros((1, width), F32)

        @pl.loop(0, seq // SUB)
        def _(i):
            s = sub(r, i)
            ge = tot[s, :]
            xhat, scale = normed(start[s, :])
            small_add(5, colsum(ge * xhat))
            small_add(6, colsum(ge))
            gy = ge * n1g[...]
            gs = gmid[s, :] + scale * (
                gy - jnp.mean(gy, -1, keepdims=True) - xhat * jnp.mean(gy * xhat, -1, keepdims=True)
            )
            ig[s, :] = gs.astype(BF16)
            tg[pl.ds(r, 1), :] += colsum(gs)

    def down(r):
        part[sl(r), :] = nn(act[sl(r), :], wdn[...])
        core_copy(3, r).start()

    def finish(r):
        @pl.loop(0, seq // SUB)
        def _(i):
            s = sub(r, i)
            out[s, :] = (mid[s, :] + (tot[s, :] + dnb[...])).astype(BF16)

    blk = loc

    early = ff // blk

    def weight_grads(j):
        s = pl.ds(pl.multiple_of(j * blk, blk), blk)

        def by(right):
            def fn():
                g[s, :] = nn(lt[s, :], right[...])

            return fn

        when(j < early, by(cot))
        when((j >= early) & (j < 2 * early), by(gp))
        when(j == 2 * early, by(gbr))
        when(j > 2 * early, by(entry))

    def go(copy, u, depth):
        when(u >= depth, lambda: copy(u - depth).wait_send())
        copy(u).start()

    def end(copy, n, depth):
        for u in range(n - min(depth, n), n):
            copy(u).wait_send()

    AF = LAG

    def base_of(u):
        return u * 4 * CH

    def later(u):
        return base_of(div(u, EACH) * (EACH + 2) + rem(u, EACH))

    def b_base(u, i):
        return base_of(jnp.minimum(u * (EACH + 2) + EACH + i, UA + UB + UC - 1))

    def a_base(u, owner):
        return later(u) + owner * 2 * CH

    def x_slot(u):
        return pl.ds(pl.multiple_of(rem(u, R["xr"].shape[0]) * 2 * CH, CH), 2 * CH)

    def x_first(u):
        src = pl.ds(pl.multiple_of(later(u) + (1 - x) * 2 * CH, CH), 2 * CH)
        return remote(
            g.at[src], R["xrb"].at[x_slot(u)], R["xs"].at[rem(u, SENDS)], R["xr"].at[rem(u, R["xr"].shape[0])], to_x
        )

    def rows_at(base, n):
        return pl.ds(pl.multiple_of(base, CH), n)

    class Line:
        def __init__(self, kind, n, first, stride, depth):
            self.kind, self.n, self.first, self.stride, self.depth = kind, n, first, stride, depth

        def unit(self, t, offset):
            rel = t - self.first - offset
            if self.stride == 1:
                return rel, (rel >= 0) & (rel < self.n)
            return div(rel, self.stride), (rel >= 0) & (rel < self.n * self.stride) & (rem(rel, self.stride) == 0)

        def sem(self, name, i, u):
            ref = R[self.kind + "_" + name]
            return ref.at[i, rem(u, ref.shape[1])]

        def slot(self, u, rows):
            return rows_at(rem(u, R[self.kind + "_r"].shape[1]) * rows, rows)

        def go(self, copy, u):
            go(copy, u, self.depth)

        def end(self, copy):
            end(copy, self.n, self.depth)

    class A(Line):
        def own(self, u):
            return rows_at(a_base(u, x), 2 * CH)

        def inward(self, u):
            dst = R["abuf"].at[cross, self.slot(u, 2 * CH)]
            return remote(g.at[self.own(u)], dst, self.sem("s", 0, u), self.sem("r", cross, u), to_in)

        def arrived(self, u, i):
            buf = R["abuf"].at[i, self.slot(u, 2 * CH)]
            remote(buf, buf, self.sem("s", 0, u), self.sem("r", i, u), to_in).wait_recv()
            return buf

        def outward(self, u):
            own = self.own(u)
            return remote(f.at[own], f.at[own], self.sem("u", 0, u), self.sem("t", 0, u), to_out)

        def x_last(self, u):
            own = self.own(u)
            return remote(f.at[own], f.at[own], self.sem("xs", 0, u), self.sem("xr", 0, u), to_x)

        def tick(self, t):
            u, valid_u = self.unit(t, last * LAG)

            def reduce():
                def add():
                    g[self.own(u), :] += self.arrived(u, 0)[...]

                if H > 1:
                    when(last > 0, add)
                self.go(self.inward, u)

            when(valid_u, reduce)
            v, valid_v = self.unit(t, (2 * H - 1 - last) * LAG)

            def finish():
                def turn():
                    f[self.own(v), :] = g[self.own(v), :] + self.arrived(v, 1)[...]

                when(last == H - 1, turn)
                if H > 1:
                    when(last < H - 1, lambda: self.outward(v).wait_recv())
                    when(last > 0, lambda: self.go(self.outward, v))
                self.go(self.x_last, v)

            when(valid_v, finish)
            e, valid_e = self.unit(t, (2 * H - last) * LAG)
            when(valid_e, lambda: self.x_last(e).wait_recv())

        def drain(self):
            self.end(self.inward)
            self.end(self.x_last)
            if H > 1:
                when(last > 0, lambda: self.end(self.outward))

    class B(Line):
        def all(self, u):
            return rows_at(b_base(u, 0), 4 * CH)

        def half(self, u, i):
            return rows_at(b_base(u, 0) + i * 2 * CH, 2 * CH)

        def inward(self, u):
            dst = R["bbuf"].at[self.slot(u, 4 * CH)]
            return remote(g.at[self.all(u)], dst, self.sem("s", 0, u), self.sem("r", 0, u), to_in)

        def swap(self, u):
            dst = R["bsw"].at[self.slot(u, 2 * CH)]
            return remote(g.at[self.half(u, 1 - side)], dst, self.sem("s", 0, u), self.sem("r", 1, u), to_in)

        def x_copy(self, u):
            dst = R["bxb"].at[self.slot(u, 2 * CH)]
            return remote(g.at[self.half(u, side)], dst, self.sem("xs", 0, u), self.sem("xr", 0, u), to_x)

        def back(self, u):
            own = self.half(u, side)
            return remote(f.at[own], f.at[own], self.sem("d", 0, u), self.sem("r", 2, u), to_in)

        def outward(self, u):
            own = self.all(u)
            return remote(f.at[own], f.at[own], self.sem("u", 0, u), self.sem("t", 0, u), to_out)

        def tick(self, t):
            u, valid_u = self.unit(t, last * LAG)

            def reduce():
                def add():
                    self.inward(u).wait_recv()
                    g[self.all(u), :] += R["bbuf"][self.slot(u, 4 * CH), :]

                if H > 1:
                    when(last > 0, add)
                    when(last < H - 1, lambda: self.go(self.inward, u))
                when(last == H - 1, lambda: self.go(self.swap, u))

            when(valid_u, reduce)
            middle = last == H - 1
            i, valid_i = self.unit(t, H * LAG)

            def over():
                self.swap(i).wait_recv()
                g[self.half(i, side), :] += R["bsw"][self.slot(i, 2 * CH), :]
                self.go(self.x_copy, i)

            when(valid_i & middle, over)
            j, valid_j = self.unit(t, (H + 1) * LAG)

            def total():
                self.x_copy(j).wait_recv()
                own = self.half(j, side)
                f[own, :] = g[own, :] + R["bxb"][self.slot(j, 2 * CH), :]
                self.go(self.back, j)

            when(valid_j & middle, total)
            v, valid_v = self.unit(t, (2 * H + 1 - last) * LAG)

            def finish():
                when(middle, lambda: self.back(v).wait_recv())
                if H > 1:
                    when(last < H - 1, lambda: self.outward(v).wait_recv())
                    when(last > 0, lambda: self.go(self.outward, v))

            when(valid_v, finish)

        def drain(self):
            def ends():
                for copy in (self.swap, self.x_copy, self.back):
                    self.end(copy)

            when(last == H - 1, ends)
            if H > 1:
                when(last < H - 1, lambda: self.end(self.inward))
                when(last > 0, lambda: self.end(self.outward))

    class C(Line):
        dirs, rows = (0, 1), 2 * CH

        def own(self, u, d):
            return rows_at(b_base(u, 1) + d * 2 * CH, 2 * CH)

        def place(self, d):
            w = z if d == 0 else L - 1 - z
            return w, (zhi if d == 0 else zlo, mp), (zlo if d == 0 else zhi, mp)

        def copies(self, d):
            w, up, dn = self.place(d)
            own = lambda u: self.own(u, d)
            slot = lambda u: self.slot(u, self.rows)

            def send(u):
                return remote(g.at[own(u)], R[self.kind + "buf"].at[d, slot(u)], self.sem("s", d, u), self.sem("r", d, u), dn)

            def x_copy(u):
                return remote(g.at[own(u)], R[self.kind + "xb"].at[d, slot(u)], self.sem("xs", d, u), self.sem("xr", d, u), to_x)

            def spread(u):
                return remote(f.at[own(u)], f.at[own(u)], self.sem("u", d, u), self.sem("t", d, u), up)

            return w, send, x_copy, spread

        def tick(self, t):
            for d in self.dirs:
                w, send, x_copy, spread = self.copies(d)
                u, valid_u = self.unit(t, (L - 1 - w) * LAG)

                def reduce():
                    def add():
                        send(u).wait_recv()
                        g[self.own(u, d), :] += R[self.kind + "buf"][d, self.slot(u, self.rows), :]

                    when(w < L - 1, add)
                    when(w > 0, lambda: self.go(send, u))
                    when(w == 0, lambda: self.go(x_copy, u))

                when(valid_u, reduce)
                v, valid_v = self.unit(t, (L + w) * LAG)

                def finish():
                    def turn():
                        x_copy(v).wait_recv()
                        own = self.own(v, d)
                        f[own, :] = g[own, :] + R[self.kind + "xb"][d, self.slot(v, self.rows), :]

                    when(w == 0, turn)
                    when(w > 0, lambda: spread(v).wait_recv())
                    when(w < L - 1, lambda: self.go(spread, v))

                when(valid_v, finish)

        def drain(self):
            for d in self.dirs:
                w, send, x_copy, spread = self.copies(d)
                when(w > 0, lambda: self.end(send))
                when(w == 0, lambda: self.end(x_copy))
                when(w < L - 1, lambda: self.end(spread))

    class S(C):
        dirs, rows = (0,), CH

        def own(self, u, d):
            return pl.ds(small, CH)

    lines = [C("c", UC, 0, EACH, 2), A("a", UA, AF, 1, SENDS), B("b", UB, 1, EACH, 2), S("e", 1, S_FIRST, 1, 1)]

    def dp_tick(t):
        when(t < UA, lambda: go(x_first, t, SENDS))
        v = t - AF

        def x_add():
            x_first(v).wait_recv()
            s = rows_at(a_base(v, x), 2 * CH)
            g[s, :] += R["xrb"][x_slot(v), :]

        when((v >= 0) & (v < UA), x_add)
        for line in lines:
            line.tick(t)

    def dp_drain():
        end(x_first, UA, SENDS)
        for line in lines:
            line.drain()

    for copy in loads.values():
        copy.start()

    def vector(i, name):
        loads[name].wait()
        R["vecs"][i : i + 1, :] = R[name][...][None, :]

    g[small : small + CH, :] = jnp.zeros((CH, width), F32)
    for name in ("tok", "tim"):
        loads[name].wait()
    timf[...] = tim[...].astype(F32)
    vector(0, "n1g")
    vector(1, "n1b")

    @pl.loop(0, rows_n)
    def _(r):
        norm1(r)

        @pl.when(r == 0)
        def _():
            for name in ("wqkv", "qvb", "seg"):
                loads[name].wait()

        project(r)
        when(r == 0, weights_out)
        attend(r)
        for i in range(W_PIECES - 1):
            when(r == rows_n - W_PIECES + 1 + i, lambda: weights_on(i))

    for name in ("cot", "wdn", "wup"):
        loads[name].wait()
    for i, name in enumerate(("outb", "n2g", "n2b", "upb", "dnb")):
        vector(2 + i, name)
    pl.loop(0, rows_n)(grad_act)
    weights_on(W_PIECES - 1)
    w_share(0).start()
    w_core().wait()
    for i in range(2):
        wall[mine_0 + i] = wf[mine_0 + i].astype(BF16)
    pl.loop(0, rows_n)(near_part)
    ahead = min(2, rows_n)
    for r in range(ahead):
        across(r)
    for i in range(W_PIECES):
        w_x(i).wait()
    w_share(1).start()
    for h in range(2):
        w_share(h).wait()
    for i in range(2):
        wall[other_0 + i] = wf[other_0 + i].astype(BF16)

    @pl.loop(0, rows_n)
    def _(r):
        far_part(r)
        feed(r)
        when(r + ahead < rows_n, lambda: across(r + ahead))

    weight_grads(jnp.int32(0))

    blocks = (2 * ff + 4 * loc) // blk
    a_last = AF + LAG * 2 * H
    b_last, c_last = 1 + LAG * (2 * H + 1), LAG * (2 * L - 1)
    ends = [S_FIRST + c_last]
    for u in range(UA + UB + UC):
        i, k = u // (EACH + 2), u % (EACH + 2)
        if k < EACH and u < UA + UB + UC - (UB > UC):
            ends.append(i * EACH + k + a_last)
        else:
            ends.append(i * EACH + c_last if k > EACH else (UB - 1 if k < EACH else i) * EACH + b_last)
    ticks = max(ends) + 1
    per = blk // (4 * CH)

    def done(j):
        return ends[0] if j == blocks else max(ends[1 + j * per : 1 + (j + 1) * per])

    def out_copy(j):
        s = pl.ds(j * blk, blk if j < blocks else CH)
        return pltpu.make_async_copy(f.at[s], f_out.at[s], R["fin"].at[j])

    done_copies = [
        pltpu.make_async_copy(a, b, R["fin"].at[blocks + 1 + i])
        for i, (a, b) in enumerate(((ig, ig_o), (tg, tg_o), (out, out_o)))
    ]

    @pl.loop(0, ticks)
    def _(t):
        dp_tick(t)

        def at(first, step, fn):
            r = (t - first) // step
            when((t >= first) & ((t - first) % step == 0) & (r < rows_n), lambda: fn(r))

        at(2, 2, lambda r: sum_b(1, r))
        at(1, 2, feed_on)
        at(5, 3, lambda r: sum_c(1, r))

        def second(r):
            sum_d(1, r)
            back2(r)

        at(7, 3, second)
        at(9, 3, lambda r: sum_b(2, r))
        at(15, 3, lambda r: sum_c(2, r))

        def third(r):
            sum_d(2, r)
            back1(r)

        at(17, 3, third)
        at(18, 3, down)
        at(20, 3, lambda r: sum_b(3, r))
        at(26, 3, lambda r: sum_c(3, r))

        def fourth(r):
            sum_d(3, r)
            finish(r)

        at(28, 3, fourth)

        @pl.when(t == 28 + 3 * rows_n)
        def _():
            for copy in done_copies:
                copy.start()

        when((rem(t, 3) == 1) & (t < 3 * blocks - 2), lambda: weight_grads(div(t + 2, 3)))
        for j in range(blocks + 1):
            if done(j) < ticks - 1:
                when(t == done(j), lambda: out_copy(j).start())

    dp_drain()
    for j in range(blocks + 1):
        if done(j) >= ticks - 1:
            out_copy(j).start()
    for copy in done_copies + [out_copy(j) for j in range(blocks + 1)]:
        copy.wait()


def shards(n_dp, *args):
    (tok, tim, seg, n1g, n1b, wqkv, qvb, wout, outb, n2g, n2b, wup, upb, wdn, dnb, cot) = args
    tokens, width = tok.shape
    rows_n, seq = seg.shape
    loc, ff = wout.shape[0], wup.shape[1]
    heads = loc // HD
    half = width // 2
    big = 2 * ff + 4 * loc
    count = big // (4 * CH)
    UC = count // (EACH + 2)
    UB = UC + min(count % (EACH + 2) // 2, 1)
    UA = count - UB - UC
    L = n_dp // 2
    LAG = hop_ticks(L)
    vm = pltpu.VMEM
    dma = pltpu.SemaphoreType.DMA
    W = two_power(max(LAG * (L - 1) + 1, 2 * LAG + 2))
    WB = two_power(LAG * (L + 1) // EACH + 1)
    WC = two_power(LAG * (2 * L - 1) // EACH + 1)
    total = big + CH
    flat = lambda n: vm((n,), F32)
    scratch = dict(
        tok=vm((tokens, width), BF16),
        cot=vm((tokens, width), BF16),
        wqkv=vm((3, loc, width), BF16),
        wout=vm((loc, width), BF16),
        wup=vm((width, ff), BF16),
        wdn=vm((ff, width), BF16),
        ins=dma((16,)),
        tim=vm((rows_n, width), BF16),
        seg=vm((rows_n, seq), jnp.int32),
        qvb=vm((2, loc), F32),
        **{s: flat(width) for s in ("n1g", "n1b", "outb", "n2g", "n2b", "dnb")},
        upb=flat(ff),
        vecs=vm((8, width), F32),
        timf=vm((rows_n, width), F32),
        start=vm((tokens, width), F32),
        entry=vm((tokens, width), BF16),
        q=vm((tokens, loc), BF16),
        k=vm((tokens, loc), BF16),
        v=vm((tokens, loc), BF16),
        probs=vm((heads * tokens, seq), F32),
        mixed=vm((tokens, loc), BF16),
        part=vm((tokens, width), F32),
        cr=vm((tokens, half), F32),
        ys=vm((tokens, half), F32),
        yr=vm((2, tokens, half), F32),
        tot=vm((tokens, width), F32),
        mid=vm((tokens, width), F32),
        e2=vm((tokens, width), BF16),
        hp=vm((seq, ff), F32),
        act=vm((tokens, ff), BF16),
        gp=vm((tokens, ff), BF16),
        gact=vm((tokens, ff), F32),
        gmid=vm((tokens, width), F32),
        gbr=vm((tokens, width), BF16),
        out=vm((tokens, width), BF16),
        ig=vm((tokens, width), BF16),
        tg=vm((rows_n, width), F32),
        lt=vm((big, tokens), BF16),
        g=vm((total, width), F32),
        f=vm((total, width), F32),
        xrb=vm((W * 2 * CH, width), F32),
        abuf=vm((2, W * 2 * CH, width), F32),
        bbuf=vm((WB * 4 * CH, width), F32),
        bsw=vm((WB * 2 * CH, width), F32),
        bxb=vm((WB * 2 * CH, width), F32),
        cbuf=vm((2, WC * 2 * CH, width), F32),
        cxb=vm((2, WC * 2 * CH, width), F32),
        ebuf=vm((1, CH, width), F32),
        exb=vm((1, CH, width), F32),
        **{"e_" + s: dma((1, 1)) for s in ("s", "u", "xs", "r", "t", "xr")},
        wf=vm((4, loc, width), F32),
        wall=vm((4, loc, width), BF16),
        mixa=vm((4, rows_n, loc, seq), F32),
        wcs=dma,
        wcr=dma,
        **{s: dma((W_PIECES,)) for s in ("wys", "wyr", "wxs", "wxr")},
        **{s: dma((2,)) for s in ("whs", "whr")},
        **{s: dma((rows_n,)) for s in ("cs", "crs", "yss", "gs", "grs")},
        yrs=dma((2, rows_n)),
        fin=dma((big // loc + 4,)),
        xs=dma((SENDS,)),
        xr=dma((W,)),
        **{"a_" + s: dma((1, SENDS)) for s in ("s", "u", "xs")},
        a_r=dma((2, W)),
        **{"a_" + s: dma((1, W)) for s in ("t", "xr")},
        **{"b_" + s: dma((1, 2)) for s in ("s", "u", "d", "xs")},
        b_r=dma((3, WB)),
        **{"b_" + s: dma((1, WB)) for s in ("t", "xr")},
        **{"c_" + s: dma((2, 2)) for s in ("s", "u", "xs")},
        **{"c_" + s: dma((2, WC)) for s in ("r", "t", "xr")},
    )
    any_spec = pl.BlockSpec(memory_space=pl.ANY)
    vm_spec = pl.BlockSpec(memory_space=pltpu.VMEM)
    out, ig, tg, f = pl.pallas_call(
        functools.partial(kernel, n_dp, (UA, UB, UC), tuple(scratch)),
        out_shape=(
            jax.ShapeDtypeStruct((tokens, width), BF16),
            jax.ShapeDtypeStruct((tokens, width), BF16),
            jax.ShapeDtypeStruct((rows_n, width), F32),
            jax.ShapeDtypeStruct((total, width), F32),
        ),
        in_specs=[any_spec] * 16,
        out_specs=(any_spec,) * 4,
        scratch_shapes=list(scratch.values()),
        compiler_params=pltpu.CompilerParams(
            collective_id=0, has_side_effects=True, vmem_limit_bytes=63 * 2**20
        ),
        cost_estimate=pl.CostEstimate(flops=6 * 10**9, bytes_accessed=20 * 10**6, transcendentals=0),
    )(
        tok, tim, seg, n1g, n1b, wqkv.transpose(0, 2, 1), qvb, wout, outb, n2g, n2b, wup, upb, wdn, dnb, cot
    )
    f32 = lambda *shape: jax.ShapeDtypeStruct(shape, F32)
    moved = (
        jax.ShapeDtypeStruct((tokens, width), BF16),
        jax.ShapeDtypeStruct((tokens, width), BF16),
        f32(rows_n, width),
        f32(3, loc, width),
        f32(loc, width),
        f32(width, ff),
        f32(ff, width),
    )
    results = pl.pallas_call(
        functools.partial(place, big),
        out_shape=moved + (f32(2, loc), f32(ff)) + (f32(width),) * 6,
        in_specs=[any_spec] * 4,
        out_specs=(any_spec,) * 15,
        scratch_shapes=[
            vm((8, width), F32),
            vm((big, width), F32),
            vm((tokens, width), BF16),
            vm((tokens, width), BF16),
            vm((rows_n, width), F32),
            vm((2, loc), F32),
            *[vm((width,), F32)] * 7,
            dma((18,)),
            dma((26,)),
        ],
        compiler_params=pltpu.CompilerParams(vmem_limit_bytes=63 * 2**20),
    )(out, ig, tg, f)
    out, ig, tg, qkv, outw, up, down, qvb, upb, downb, n2g, n2b, outb, n1g, n1b = results
    return out, ig, tg, n1g, n1b, qkv.transpose(0, 2, 1), qvb, outw, outb, n2g, n2b, up, upb, down, downb


def place(big, *refs):
    out, ig, tg, f, out_o, ig_o, tg_o, qkv, outw, up, down, qvb, upb, downb = refs[:14]
    n2g, n2b, outb, n1g, n1b, sm, buf, vo, vi, vt, vq = refs[14:25]
    flat = refs[25:32]
    sem, sem_o = refs[32:]
    loc, ff = outw.shape[0], down.shape[0]
    half = f.shape[1] // 2
    moves = [(tg, vt, tg_o)]
    row = 0
    for n, ref in ((ff, down), (ff, up), (loc, outw), (loc, qkv.at[0]), (loc, qkv.at[1]), (loc, qkv.at[2])):
        step = max(n * 12 // (2 * ff + 4 * loc), 1)
        for i in range(step):
            s = pl.ds(row, n // step)
            moves.append((f.at[s], buf.at[s], ref.at[pl.ds(i * (n // step), n // step)]))
            row += n // step
    moves += [(out, vo, out_o), (ig, vi, ig_o)]
    first = pltpu.make_async_copy(f.at[pl.ds(big, 8)], sm, sem.at[len(moves)])
    first.start()
    loads = [pltpu.make_async_copy(a, v, sem.at[i]) for i, (a, v, b) in enumerate(moves)]
    stores = [pltpu.make_async_copy(v, b, sem_o.at[i]) for i, (a, v, b) in enumerate(moves)]
    for copy in loads[:20]:
        copy.start()
    first.wait()
    small = (downb, upb, n2g, n2b, outb, n1g, n1b)
    for i, ref in enumerate(flat):
        ref[...] = sm[i : i + 1, :].reshape(ref.shape)
    vq[0:1, :] = sm[7:8, 0:loc]
    vq[1:2, :] = sm[7:8, half : half + loc]
    for ref, o in zip(flat + (vq,), small + (qvb,)):
        stores.append(pltpu.make_async_copy(ref, o, sem_o.at[len(stores)]))
        stores[-1].start()
    for i, load in enumerate(loads):
        load.wait()
        if i + 20 < len(loads):
            loads[i + 20].start()
        stores[i].start()
    for copy in stores:
        copy.wait()


def solution(mesh):
    placed = (
        P("dp", None),
        P("dp", None),
        P("dp", None),
        P(),
        P(),
        P(None, None, "mp"),
        P(None, "mp"),
        P("mp", None),
        P(),
        P(),
        P(),
        P(None, "mp"),
        P("mp"),
        P("mp", None),
        P(),
        P("dp", None),
    )
    return jax.shard_map(
        functools.partial(shards, mesh.shape["dp"]),
        mesh=mesh,
        in_specs=placed,
        out_specs=(
            P("dp", None),
            P("dp", None),
            P("dp", None),
            P(),
            P(),
            P(None, None, "mp"),
            P(None, "mp"),
            P("mp", None),
            P(),
            P(),
            P(),
            P(None, "mp"),
            P("mp"),
            P("mp", None),
            P(),
        ),
        check_vma=False,
    )
```

```python
import functools

import jax
import jax.numpy as jnp
from jax import lax
from jax.experimental import pallas as pl
from jax.experimental.pallas import tpu as pltpu
from jax.sharding import PartitionSpec as P

HD = 64
SUB = 128
CH = 8
W_PIECES = 3
EACH = 3
S_FIRST = 30
SENDS = 4
MESH = pl.DeviceIdType.MESH
F32 = jnp.float32
BF16 = jnp.bfloat16


ARGS = ("tok", "tim", "seg", "n1g", "n1b", "wqkv", "qvb", "wout", "outb", "n2g", "n2b")
ARGS += ("wup", "upb", "wdn", "dnb", "cot")


def hop_ticks(line):
    return 2 if line <= 8 else 1


def when(cond, fn):
    pl.when(cond)(fn)


def rem(a, n):
    return lax.rem(a, jnp.int32(n))


def div(a, n):
    return lax.div(a, jnp.int32(n))


def two_power(n):
    return 1 << (n - 1).bit_length()


def nt(a, b):
    return lax.dot_general(a, b, (((1,), (1,)), ((), ())), preferred_element_type=F32)


def tn(a, b):
    return lax.dot_general(a, b, (((0,), (0,)), ((), ())), preferred_element_type=F32)


def nn(a, b):
    return jnp.dot(a, b, preferred_element_type=F32)


def normed(v):
    centred = v - jnp.mean(v, -1, keepdims=True)
    spread = jnp.mean(centred * centred, -1, keepdims=True)
    scale = lax.rsqrt(spread + 1e-05)
    return centred * scale, scale


def colsum(v):
    return jnp.sum(v, 0, keepdims=True)


def kernel(n_dp, units, names, *refs):
    out_o, ig_o, tg_o, f_out = refs[16:20]
    R = dict(zip(names, refs[20:]))
    order = ("tok", "tim", "n1g", "n1b", "wqkv", "qvb", "seg", "wout", "outb", "cot", "wdn")
    order += ("n2g", "n2b", "wup", "upb", "dnb")
    tok, tim, wqkv, qvb, seg, wout, cot, wdn, wup = (
        R[s] for s in ("tok", "tim", "wqkv", "qvb", "seg", "wout", "cot", "wdn", "wup")
    )
    loads = {
        name: pltpu.make_async_copy(refs[ARGS.index(name)], R[name], R["ins"].at[i]) for i, name in enumerate(order)
    }
    n1g, n1b, outb, n2g, n2b, upb, dnb = (R["vecs"].at[pl.ds(i, 1)] for i in range(7))
    timf, start, entry, q_s, k_s, v_s = (R[s] for s in ("timf", "start", "entry", "q", "k", "v"))
    probs, mixed_s, part, cr, ys, yr = (R[s] for s in ("probs", "mixed", "part", "cr", "ys", "yr"))
    tot, mid, e2, hp, act, gp = (R[s] for s in ("tot", "mid", "e2", "hp", "act", "gp"))
    out, ig, tg = (R[s] for s in ("out", "ig", "tg"))
    gact, gmid, gbr, lt, g, f = (R[s] for s in ("gact", "gmid", "gbr", "lt", "g", "f"))

    rows_n, seq = seg.shape
    width = tok.shape[1]
    half = width // 2
    loc = wout.shape[0]
    heads = loc // HD
    ff = wup.shape[1]
    UA, UB, UC = units
    L = n_dp // 2
    LAG = hop_ticks(L)
    H = L // 2
    dp = lax.axis_index("dp")
    mp = lax.axis_index("mp")
    core = mp % 2
    x = dp % 2
    z = dp // 2
    to_core = (dp, mp + 1 - 2 * core)
    to_y = (dp, (mp + 2) % 4)
    to_x = (dp + 1 - 2 * x, mp)
    last = jnp.minimum(z, L - 1 - z)
    side = div(z, H)
    cross = jnp.where(last == H - 1, 1, 0)
    to_in = ((z + 1 - 2 * side) * 2 + x, mp)
    to_out = (jnp.clip(z - 1 + 2 * side, 0, L - 1) * 2 + x, mp)
    zlo = jnp.maximum(z - 1, 0) * 2 + x
    zhi = jnp.minimum(z + 1, L - 1) * 2 + x

    barrier = pltpu.get_barrier_semaphore()
    for dev in (to_core, to_y, to_x):
        pl.semaphore_signal(barrier, 1, device_id=dev, device_id_type=MESH)
    when(z > 0, lambda: pl.semaphore_signal(barrier, 1, device_id=(zlo, mp), device_id_type=MESH))
    when(z < L - 1, lambda: pl.semaphore_signal(barrier, 1, device_id=(zhi, mp), device_id_type=MESH))
    greeted = 3 + jnp.minimum(z, 1) + jnp.minimum(L - 1 - z, 1)

    def sl(r, n=seq):
        return pl.ds(pl.multiple_of(r * n, n), n)

    def sub(r, i):
        return pl.ds(pl.multiple_of(r * seq + i * SUB, SUB), SUB)

    mine = pl.ds(pl.multiple_of(core * half, 128), half)
    other = pl.ds(pl.multiple_of((1 - core) * half, 128), half)

    def remote(src, dst, ssem, rsem, dev):
        return pltpu.make_async_remote_copy(
            src_ref=src, dst_ref=dst, send_sem=ssem, recv_sem=rsem, device_id=dev, device_id_type=MESH
        )

    def core_copy(p, r):
        return remote(part.at[sl(r), other], cr.at[sl(r)], R["cs"].at[r], R["crs"].at[r], to_core)

    def y_copy(p, r):
        return remote(ys.at[sl(r)], yr.at[p % 2, sl(r)], R["yss"].at[r], R["yrs"].at[p % 2, r], to_y)

    def ag_copy(p, r):
        return remote(tot.at[sl(r), mine], tot.at[sl(r), mine], R["gs"].at[r], R["grs"].at[r], to_core)

    def sum_b(p, r):
        core_copy(p, r).wait()
        ys[sl(r), :] = part[sl(r), mine] + cr[sl(r), :]
        y_copy(p, r).start()

    def sum_c(p, r):
        y_copy(p, r).wait()
        tot[sl(r), mine] = ys[sl(r), :] + yr[p % 2, sl(r), :]
        ag_copy(p, r).start()

    def sum_d(p, r):
        ag_copy(p, r).wait()

    def vec(ref):
        return ref[...]

    small = 2 * ff + 4 * loc

    def small_add(i, v):
        g[small + i : small + i + 1, :] += v

    lane = lax.broadcasted_iota(jnp.int32, (1, loc), 1)
    masks = [((lane >= h * HD) & (lane < (h + 1) * HD)).astype(F32) for h in range(heads)]

    def by_head(v):
        return jnp.concatenate([v * m.astype(BF16) for m in masks], 0)

    def from_heads(v):
        total = v[:seq] * masks[0]
        for h in range(1, heads):
            total = total + v[h * seq : (h + 1) * seq] * masks[h]
        return total

    def norm1(r):
        @pl.loop(0, seq // SUB)
        def _(i):
            s = sub(r, i)
            v = tok[s, :].astype(F32) + timf[pl.ds(r, 1), :]
            start[s, :] = v
            xhat, _ = normed(v)
            entry[s, :] = (xhat * n1g[...] + n1b[...]).astype(BF16)

    def project(r):
        e = entry[sl(r), :]
        q_s[sl(r), :] = (nt(e, wqkv[0]) + qvb[0:1, :]).astype(BF16)
        k_s[sl(r), :] = nt(e, wqkv[1]).astype(BF16)
        v_s[sl(r), :] = (nt(e, wqkv[2]) + qvb[1:2, :]).astype(BF16)

    def attend(r):
        labels = jnp.broadcast_to(seg[pl.ds(r, 1), :], (seq, seq))
        same = labels == labels.T
        same = jnp.concatenate([same.astype(F32)] * heads, 0) > 0.5
        scores = nt(by_head(q_s[sl(r), :]), k_s[sl(r), :]) * HD ** (-0.5)
        scores = jnp.where(same, scores, -1e30)
        w = jnp.exp(scores - jnp.max(scores, -1, keepdims=True))
        pr = w / jnp.sum(w, -1, keepdims=True)
        probs[sl(r, heads * seq), :] = pr
        mixed = from_heads(nn(pr.astype(BF16), v_s[sl(r), :])).astype(BF16)
        mixed_s[sl(r), :] = mixed
        turned = mixed.T
        lt[2 * ff : 2 * ff + loc, sl(r)] = turned
        mixa[mp, r] = turned.astype(F32)
        m_core(r).start()
        m_y(r).start()

    wf, wall, mixa = R["wf"], R["wall"], R["mixa"]
    mp_y, mp_c = rem(mp + 2, 4), mp + 1 - 2 * core
    mine_0, other_0 = mp - core, mp_y - core
    hl = loc // 2
    pr_n = hl // W_PIECES

    def w_core():
        return remote(wf.at[mp], wf.at[mp], R["wcs"], R["wcr"], to_core)

    def w_rows(start, n):
        return pl.ds(pl.multiple_of(start, CH), n)

    def w_y(i):
        s = w_rows(x * hl + i * pr_n, pr_n)
        return remote(wf.at[mp, s], wf.at[mp, s], R["wys"].at[i], R["wyr"].at[i], to_y)

    def w_x(i):
        s = w_rows(x * hl + i * pr_n, pr_n)
        return remote(wf.at[mp_y, s], wf.at[mp_y, s], R["wxs"].at[i], R["wxr"].at[i], to_x)

    def w_share(h):
        s = w_rows((x + h - 2 * x * h) * hl, hl)
        return remote(wf.at[mp_y, s], wf.at[mp_y, s], R["whs"].at[h], R["whr"].at[h], to_core)

    def m_core(r):
        return remote(mixa.at[mp, r], mixa.at[mp, r], R["cs"].at[r], R["crs"].at[r], to_core)

    def m_y(r):
        return remote(mixa.at[mp, r], mixa.at[mp, r], R["yss"].at[r], R["yrs"].at[0, r], to_y)

    def m_share(r):
        return remote(mixa.at[mp_y, r], mixa.at[mp_y, r], R["gs"].at[r], R["grs"].at[r], to_core)

    def weights_out():
        loads["wout"].wait()
        wf[mp] = wout[...].astype(F32)
        pl.semaphore_wait(barrier, greeted)
        for i in range(W_PIECES):
            w_y(i).start()
        w_core().start()

    def weights_on(i):
        w_y(i).wait()
        w_x(i).start()

    def pair_sum(m, r):
        return tn(mixa[m, r].astype(BF16), wall[m]) + tn(mixa[m + 1, r].astype(BF16), wall[m + 1])

    def near_part(r):
        m_core(r).wait()
        part[sl(r), :] = pair_sum(mine_0, r)

    def across(r):
        m_y(r).wait()
        m_share(r).start()

    def far_part(r):
        m_share(r).wait()
        tot[sl(r), :] = part[sl(r), :] + pair_sum(other_0, r)

    def grad_act(r):
        c = cot[sl(r), :]
        gact[sl(r), :] = nt(c, wdn[...])
        small_add(0, colsum(c.astype(F32)))

    def feed(r):
        @pl.loop(0, seq // SUB)
        def _(i):
            s = sub(r, i)
            v = start[s, :] + (tot[s, :] + outb[...])
            mid[s, :] = v
            xhat, _ = normed(v)
            e2[s, :] = (xhat * n2g[...] + n2b[...]).astype(BF16)

        hp[...] = nn(e2[sl(r), :], wup[...])

        @pl.loop(0, seq // SUB)
        def _(i):
            s = sub(r, i)
            u = hp[pl.ds(pl.multiple_of(i * SUB, SUB), SUB), :] + upb[...]
            cdf = 0.5 * (1.0 + lax.erf(u * 0.7071067811865476))
            act[s, :] = (u * cdf).astype(BF16)
            slope = cdf + u * (0.3989422804014327 * jnp.exp(-0.5 * u * u))
            pre = (gact[s, :] * slope).astype(BF16)
            gp[s, :] = pre
            small_add(1, colsum(pre.astype(F32)))

        lt[0:ff, sl(r)] = act[sl(r), :].T

    def feed_on(r):
        part[sl(r), :] = nt(gp[sl(r), :], wup[...])
        core_copy(1, r).start()
        lt[ff : 2 * ff, sl(r)] = e2[sl(r), :].T

    def back2(r):
        @pl.loop(0, seq // SUB)
        def _(i):
            s = sub(r, i)
            ge = tot[s, :]
            xhat, scale = normed(mid[s, :])
            small_add(2, colsum(ge * xhat))
            small_add(3, colsum(ge))
            gx = ge * n2g[...]
            gm = cot[s, :].astype(F32) + scale * (
                gx - jnp.mean(gx, -1, keepdims=True) - xhat * jnp.mean(gx * xhat, -1, keepdims=True)
            )
            gmid[s, :] = gm
            low = gm.astype(BF16)
            gbr[s, :] = low
            small_add(4, colsum(low.astype(F32)))

        g3 = by_head(nt(gbr[sl(r), :], wout[...]).astype(BF16))
        pr = probs[sl(r, heads * seq), :]
        grad_probs = nt(g3, v_s[sl(r), :])
        inner = jnp.sum(pr * grad_probs, -1, keepdims=True)
        ds = (pr * (grad_probs - inner)).astype(BF16)
        gq = (from_heads(nn(ds, k_s[sl(r), :])) * HD ** (-0.5)).astype(BF16)
        gk = (tn(ds, by_head(q_s[sl(r), :])) * HD ** (-0.5)).astype(BF16)
        gv = tn(pr.astype(BF16), g3).astype(BF16)
        part[sl(r), :] = nn(gq, wqkv[0]) + nn(gk, wqkv[1]) + nn(gv, wqkv[2])
        core_copy(2, r).start()
        late = 2 * ff + loc
        for i, v in enumerate((gq, gk, gv)):
            lt[late + i * loc : late + (i + 1) * loc, sl(r)] = v.T
        g[small + 7 : small + 8, 0:loc] += colsum(gq.astype(F32))
        g[small + 7 : small + 8, half : half + loc] += colsum(gv.astype(F32))

    def back1(r):
        tg[pl.ds(r, 1), :] = jnp.zeros((1, width), F32)

        @pl.loop(0, seq // SUB)
        def _(i):
            s = sub(r, i)
            ge = tot[s, :]
            xhat, scale = normed(start[s, :])
            small_add(5, colsum(ge * xhat))
            small_add(6, colsum(ge))
            gy = ge * n1g[...]
            gs = gmid[s, :] + scale * (
                gy - jnp.mean(gy, -1, keepdims=True) - xhat * jnp.mean(gy * xhat, -1, keepdims=True)
            )
            ig[s, :] = gs.astype(BF16)
            tg[pl.ds(r, 1), :] += colsum(gs)

    def down(r):
        part[sl(r), :] = nn(act[sl(r), :], wdn[...])
        core_copy(3, r).start()

    def finish(r):
        @pl.loop(0, seq // SUB)
        def _(i):
            s = sub(r, i)
            out[s, :] = (mid[s, :] + (tot[s, :] + dnb[...])).astype(BF16)

    blk = loc

    early = ff // blk

    def weight_grads(j):
        s = pl.ds(pl.multiple_of(j * blk, blk), blk)

        def by(right):
            def fn():
                g[s, :] = nn(lt[s, :], right[...])

            return fn

        when(j < early, by(cot))
        when((j >= early) & (j < 2 * early), by(gp))
        when(j == 2 * early, by(gbr))
        when(j > 2 * early, by(entry))

    def go(copy, u, depth):
        when(u >= depth, lambda: copy(u - depth).wait_send())
        copy(u).start()

    def end(copy, n, depth):
        for u in range(n - min(depth, n), n):
            copy(u).wait_send()

    AF = LAG

    def base_of(u):
        return u * 4 * CH

    def later(u):
        return base_of(div(u, EACH) * (EACH + 2) + rem(u, EACH))

    def b_base(u, i):
        return base_of(jnp.minimum(u * (EACH + 2) + EACH + i, UA + UB + UC - 1))

    def a_base(u, owner):
        return later(u) + owner * 2 * CH

    def x_slot(u):
        return pl.ds(pl.multiple_of(rem(u, R["xr"].shape[0]) * 2 * CH, CH), 2 * CH)

    def x_first(u):
        src = pl.ds(pl.multiple_of(later(u) + (1 - x) * 2 * CH, CH), 2 * CH)
        return remote(
            g.at[src], R["xrb"].at[x_slot(u)], R["xs"].at[rem(u, SENDS)], R["xr"].at[rem(u, R["xr"].shape[0])], to_x
        )

    def rows_at(base, n):
        return pl.ds(pl.multiple_of(base, CH), n)

    class Line:
        def __init__(self, kind, n, first, stride, depth):
            self.kind, self.n, self.first, self.stride, self.depth = kind, n, first, stride, depth

        def unit(self, t, offset):
            rel = t - self.first - offset
            if self.stride == 1:
                return rel, (rel >= 0) & (rel < self.n)
            return div(rel, self.stride), (rel >= 0) & (rel < self.n * self.stride) & (rem(rel, self.stride) == 0)

        def sem(self, name, i, u):
            ref = R[self.kind + "_" + name]
            return ref.at[i, rem(u, ref.shape[1])]

        def slot(self, u, rows):
            return rows_at(rem(u, R[self.kind + "_r"].shape[1]) * rows, rows)

        def go(self, copy, u):
            go(copy, u, self.depth)

        def end(self, copy):
            end(copy, self.n, self.depth)

    class A(Line):
        def own(self, u):
            return rows_at(a_base(u, x), 2 * CH)

        def inward(self, u):
            dst = R["abuf"].at[cross, self.slot(u, 2 * CH)]
            return remote(g.at[self.own(u)], dst, self.sem("s", 0, u), self.sem("r", cross, u), to_in)

        def arrived(self, u, i):
            buf = R["abuf"].at[i, self.slot(u, 2 * CH)]
            remote(buf, buf, self.sem("s", 0, u), self.sem("r", i, u), to_in).wait_recv()
            return buf

        def outward(self, u):
            own = self.own(u)
            return remote(f.at[own], f.at[own], self.sem("u", 0, u), self.sem("t", 0, u), to_out)

        def x_last(self, u):
            own = self.own(u)
            return remote(f.at[own], f.at[own], self.sem("xs", 0, u), self.sem("xr", 0, u), to_x)

        def tick(self, t):
            u, valid_u = self.unit(t, last * LAG)

            def reduce():
                def add():
                    g[self.own(u), :] += self.arrived(u, 0)[...]

                if H > 1:
                    when(last > 0, add)
                self.go(self.inward, u)

            when(valid_u, reduce)
            v, valid_v = self.unit(t, (2 * H - 1 - last) * LAG)

            def finish():
                def turn():
                    f[self.own(v), :] = g[self.own(v), :] + self.arrived(v, 1)[...]

                when(last == H - 1, turn)
                if H > 1:
                    when(last < H - 1, lambda: self.outward(v).wait_recv())
                    when(last > 0, lambda: self.go(self.outward, v))
                self.go(self.x_last, v)

            when(valid_v, finish)
            e, valid_e = self.unit(t, (2 * H - last) * LAG)
            when(valid_e, lambda: self.x_last(e).wait_recv())

        def drain(self):
            self.end(self.inward)
            self.end(self.x_last)
            if H > 1:
                when(last > 0, lambda: self.end(self.outward))

    class B(Line):
        def all(self, u):
            return rows_at(b_base(u, 0), 4 * CH)

        def half(self, u, i):
            return rows_at(b_base(u, 0) + i * 2 * CH, 2 * CH)

        def inward(self, u):
            dst = R["bbuf"].at[self.slot(u, 4 * CH)]
            return remote(g.at[self.all(u)], dst, self.sem("s", 0, u), self.sem("r", 0, u), to_in)

        def swap(self, u):
            dst = R["bsw"].at[self.slot(u, 2 * CH)]
            return remote(g.at[self.half(u, 1 - side)], dst, self.sem("s", 0, u), self.sem("r", 1, u), to_in)

        def x_copy(self, u):
            dst = R["bxb"].at[self.slot(u, 2 * CH)]
            return remote(g.at[self.half(u, side)], dst, self.sem("xs", 0, u), self.sem("xr", 0, u), to_x)

        def back(self, u):
            own = self.half(u, side)
            return remote(f.at[own], f.at[own], self.sem("d", 0, u), self.sem("r", 2, u), to_in)

        def outward(self, u):
            own = self.all(u)
            return remote(f.at[own], f.at[own], self.sem("u", 0, u), self.sem("t", 0, u), to_out)

        def tick(self, t):
            u, valid_u = self.unit(t, last * LAG)

            def reduce():
                def add():
                    self.inward(u).wait_recv()
                    g[self.all(u), :] += R["bbuf"][self.slot(u, 4 * CH), :]

                if H > 1:
                    when(last > 0, add)
                    when(last < H - 1, lambda: self.go(self.inward, u))
                when(last == H - 1, lambda: self.go(self.swap, u))

            when(valid_u, reduce)
            middle = last == H - 1
            i, valid_i = self.unit(t, H * LAG)

            def over():
                self.swap(i).wait_recv()
                g[self.half(i, side), :] += R["bsw"][self.slot(i, 2 * CH), :]
                self.go(self.x_copy, i)

            when(valid_i & middle, over)
            j, valid_j = self.unit(t, (H + 1) * LAG)

            def total():
                self.x_copy(j).wait_recv()
                own = self.half(j, side)
                f[own, :] = g[own, :] + R["bxb"][self.slot(j, 2 * CH), :]
                self.go(self.back, j)

            when(valid_j & middle, total)
            v, valid_v = self.unit(t, (2 * H + 1 - last) * LAG)

            def finish():
                when(middle, lambda: self.back(v).wait_recv())
                if H > 1:
                    when(last < H - 1, lambda: self.outward(v).wait_recv())
                    when(last > 0, lambda: self.go(self.outward, v))

            when(valid_v, finish)

        def drain(self):
            def ends():
                for copy in (self.swap, self.x_copy, self.back):
                    self.end(copy)

            when(last == H - 1, ends)
            if H > 1:
                when(last < H - 1, lambda: self.end(self.inward))
                when(last > 0, lambda: self.end(self.outward))

    class C(Line):
        dirs, rows = (0, 1), 2 * CH

        def own(self, u, d):
            return rows_at(b_base(u, 1) + d * 2 * CH, 2 * CH)

        def place(self, d):
            w = z if d == 0 else L - 1 - z
            return w, (zhi if d == 0 else zlo, mp), (zlo if d == 0 else zhi, mp)

        def copies(self, d):
            w, up, dn = self.place(d)
            own = lambda u: self.own(u, d)
            slot = lambda u: self.slot(u, self.rows)

            def send(u):
                return remote(g.at[own(u)], R[self.kind + "buf"].at[d, slot(u)], self.sem("s", d, u), self.sem("r", d, u), dn)

            def x_copy(u):
                return remote(g.at[own(u)], R[self.kind + "xb"].at[d, slot(u)], self.sem("xs", d, u), self.sem("xr", d, u), to_x)

            def spread(u):
                return remote(f.at[own(u)], f.at[own(u)], self.sem("u", d, u), self.sem("t", d, u), up)

            return w, send, x_copy, spread

        def tick(self, t):
            for d in self.dirs:
                w, send, x_copy, spread = self.copies(d)
                u, valid_u = self.unit(t, (L - 1 - w) * LAG)

                def reduce():
                    def add():
                        send(u).wait_recv()
                        g[self.own(u, d), :] += R[self.kind + "buf"][d, self.slot(u, self.rows), :]

                    when(w < L - 1, add)
                    when(w > 0, lambda: self.go(send, u))
                    when(w == 0, lambda: self.go(x_copy, u))

                when(valid_u, reduce)
                v, valid_v = self.unit(t, (L + w) * LAG)

                def finish():
                    def turn():
                        x_copy(v).wait_recv()
                        own = self.own(v, d)
                        f[own, :] = g[own, :] + R[self.kind + "xb"][d, self.slot(v, self.rows), :]

                    when(w == 0, turn)
                    when(w > 0, lambda: spread(v).wait_recv())
                    when(w < L - 1, lambda: self.go(spread, v))

                when(valid_v, finish)

        def drain(self):
            for d in self.dirs:
                w, send, x_copy, spread = self.copies(d)
                when(w > 0, lambda: self.end(send))
                when(w == 0, lambda: self.end(x_copy))
                when(w < L - 1, lambda: self.end(spread))

    class S(C):
        dirs, rows = (0,), CH

        def own(self, u, d):
            return pl.ds(small, CH)

    lines = [C("c", UC, 0, EACH, 2), A("a", UA, AF, 1, SENDS), B("b", UB, 1, EACH, 2), S("e", 1, S_FIRST, 1, 1)]

    def dp_tick(t):
        when(t < UA, lambda: go(x_first, t, SENDS))
        v = t - AF

        def x_add():
            x_first(v).wait_recv()
            s = rows_at(a_base(v, x), 2 * CH)
            g[s, :] += R["xrb"][x_slot(v), :]

        when((v >= 0) & (v < UA), x_add)
        for line in lines:
            line.tick(t)

    def dp_drain():
        end(x_first, UA, SENDS)
        for line in lines:
            line.drain()

    for copy in loads.values():
        copy.start()

    def vector(i, name):
        loads[name].wait()
        R["vecs"][i : i + 1, :] = R[name][...][None, :]

    g[small : small + CH, :] = jnp.zeros((CH, width), F32)
    for name in ("tok", "tim"):
        loads[name].wait()
    timf[...] = tim[...].astype(F32)
    vector(0, "n1g")
    vector(1, "n1b")

    @pl.loop(0, rows_n)
    def _(r):
        norm1(r)

        @pl.when(r == 0)
        def _():
            for name in ("wqkv", "qvb", "seg"):
                loads[name].wait()

        project(r)
        when(r == 0, weights_out)
        attend(r)
        for i in range(W_PIECES - 1):
            when(r == rows_n - W_PIECES + 1 + i, lambda: weights_on(i))

    for name in ("cot", "wdn", "wup"):
        loads[name].wait()
    for i, name in enumerate(("outb", "n2g", "n2b", "upb", "dnb")):
        vector(2 + i, name)
    pl.loop(0, rows_n)(grad_act)
    weights_on(W_PIECES - 1)
    w_share(0).start()
    w_core().wait()
    for i in range(2):
        wall[mine_0 + i] = wf[mine_0 + i].astype(BF16)
    pl.loop(0, rows_n)(near_part)
    ahead = min(2, rows_n)
    for r in range(ahead):
        across(r)
    for i in range(W_PIECES):
        w_x(i).wait()
    w_share(1).start()
    for h in range(2):
        w_share(h).wait()
    for i in range(2):
        wall[other_0 + i] = wf[other_0 + i].astype(BF16)

    @pl.loop(0, rows_n)
    def _(r):
        far_part(r)
        feed(r)
        when(r + ahead < rows_n, lambda: across(r + ahead))

    weight_grads(jnp.int32(0))

    blocks = (2 * ff + 4 * loc) // blk
    a_last = AF + LAG * 2 * H
    b_last, c_last = 1 + LAG * (2 * H + 1), LAG * (2 * L - 1)
    ends = [S_FIRST + c_last]
    for u in range(UA + UB + UC):
        i, k = u // (EACH + 2), u % (EACH + 2)
        if k < EACH and u < UA + UB + UC - (UB > UC):
            ends.append(i * EACH + k + a_last)
        else:
            ends.append(i * EACH + c_last if k > EACH else (UB - 1 if k < EACH else i) * EACH + b_last)
    ticks = max(ends) + 1
    per = blk // (4 * CH)

    def done(j):
        return ends[0] if j == blocks else max(ends[1 + j * per : 1 + (j + 1) * per])

    def out_copy(j):
        s = pl.ds(j * blk, blk if j < blocks else CH)
        return pltpu.make_async_copy(f.at[s], f_out.at[s], R["fin"].at[j])

    done_copies = [
        pltpu.make_async_copy(a, b, R["fin"].at[blocks + 1 + i])
        for i, (a, b) in enumerate(((ig, ig_o), (tg, tg_o), (out, out_o)))
    ]

    @pl.loop(0, ticks)
    def _(t):
        dp_tick(t)

        def at(first, step, fn):
            r = (t - first) // step
            when((t >= first) & ((t - first) % step == 0) & (r < rows_n), lambda: fn(r))

        at(2, 2, lambda r: sum_b(1, r))
        at(1, 2, feed_on)
        at(5, 3, lambda r: sum_c(1, r))

        def second(r):
            sum_d(1, r)
            back2(r)

        at(7, 3, second)
        at(9, 3, lambda r: sum_b(2, r))
        at(15, 3, lambda r: sum_c(2, r))

        def third(r):
            sum_d(2, r)
            back1(r)

        at(17, 3, third)
        at(18, 3, down)
        at(20, 3, lambda r: sum_b(3, r))
        at(26, 3, lambda r: sum_c(3, r))

        def fourth(r):
            sum_d(3, r)
            finish(r)

        at(28, 3, fourth)

        @pl.when(t == 28 + 3 * rows_n)
        def _():
            for copy in done_copies:
                copy.start()

        when((rem(t, 3) == 1) & (t < 3 * blocks - 2), lambda: weight_grads(div(t + 2, 3)))
        for j in range(blocks + 1):
            if done(j) < ticks - 1:
                when(t == done(j), lambda: out_copy(j).start())

    dp_drain()
    for j in range(blocks + 1):
        if done(j) >= ticks - 1:
            out_copy(j).start()
    for copy in done_copies + [out_copy(j) for j in range(blocks + 1)]:
        copy.wait()


def shards(n_dp, *args):
    (tok, tim, seg, n1g, n1b, wqkv, qvb, wout, outb, n2g, n2b, wup, upb, wdn, dnb, cot) = args
    tokens, width = tok.shape
    rows_n, seq = seg.shape
    loc, ff = wout.shape[0], wup.shape[1]
    heads = loc // HD
    half = width // 2
    big = 2 * ff + 4 * loc
    count = big // (4 * CH)
    UC = count // (EACH + 2)
    UB = UC + min(count % (EACH + 2) // 2, 1)
    UA = count - UB - UC
    L = n_dp // 2
    LAG = hop_ticks(L)
    vm = pltpu.VMEM
    dma = pltpu.SemaphoreType.DMA
    W = two_power(max(LAG * (L - 1) + 1, 2 * LAG + 2))
    WB = two_power(LAG * (L + 1) // EACH + 1)
    WC = two_power(LAG * (2 * L - 1) // EACH + 1)
    total = big + CH
    flat = lambda n: vm((n,), F32)
    scratch = dict(
        tok=vm((tokens, width), BF16),
        cot=vm((tokens, width), BF16),
        wqkv=vm((3, loc, width), BF16),
        wout=vm((loc, width), BF16),
        wup=vm((width, ff), BF16),
        wdn=vm((ff, width), BF16),
        ins=dma((16,)),
        tim=vm((rows_n, width), BF16),
        seg=vm((rows_n, seq), jnp.int32),
        qvb=vm((2, loc), F32),
        **{s: flat(width) for s in ("n1g", "n1b", "outb", "n2g", "n2b", "dnb")},
        upb=flat(ff),
        vecs=vm((8, width), F32),
        timf=vm((rows_n, width), F32),
        start=vm((tokens, width), F32),
        entry=vm((tokens, width), BF16),
        q=vm((tokens, loc), BF16),
        k=vm((tokens, loc), BF16),
        v=vm((tokens, loc), BF16),
        probs=vm((heads * tokens, seq), F32),
        mixed=vm((tokens, loc), BF16),
        part=vm((tokens, width), F32),
        cr=vm((tokens, half), F32),
        ys=vm((tokens, half), F32),
        yr=vm((2, tokens, half), F32),
        tot=vm((tokens, width), F32),
        mid=vm((tokens, width), F32),
        e2=vm((tokens, width), BF16),
        hp=vm((seq, ff), F32),
        act=vm((tokens, ff), BF16),
        gp=vm((tokens, ff), BF16),
        gact=vm((tokens, ff), F32),
        gmid=vm((tokens, width), F32),
        gbr=vm((tokens, width), BF16),
        out=vm((tokens, width), BF16),
        ig=vm((tokens, width), BF16),
        tg=vm((rows_n, width), F32),
        lt=vm((big, tokens), BF16),
        g=vm((total, width), F32),
        f=vm((total, width), F32),
        xrb=vm((W * 2 * CH, width), F32),
        abuf=vm((2, W * 2 * CH, width), F32),
        bbuf=vm((WB * 4 * CH, width), F32),
        bsw=vm((WB * 2 * CH, width), F32),
        bxb=vm((WB * 2 * CH, width), F32),
        cbuf=vm((2, WC * 2 * CH, width), F32),
        cxb=vm((2, WC * 2 * CH, width), F32),
        ebuf=vm((1, CH, width), F32),
        exb=vm((1, CH, width), F32),
        **{"e_" + s: dma((1, 1)) for s in ("s", "u", "xs", "r", "t", "xr")},
        wf=vm((4, loc, width), F32),
        wall=vm((4, loc, width), BF16),
        mixa=vm((4, rows_n, loc, seq), F32),
        wcs=dma,
        wcr=dma,
        **{s: dma((W_PIECES,)) for s in ("wys", "wyr", "wxs", "wxr")},
        **{s: dma((2,)) for s in ("whs", "whr")},
        **{s: dma((rows_n,)) for s in ("cs", "crs", "yss", "gs", "grs")},
        yrs=dma((2, rows_n)),
        fin=dma((big // loc + 4,)),
        xs=dma((SENDS,)),
        xr=dma((W,)),
        **{"a_" + s: dma((1, SENDS)) for s in ("s", "u", "xs")},
        a_r=dma((2, W)),
        **{"a_" + s: dma((1, W)) for s in ("t", "xr")},
        **{"b_" + s: dma((1, 2)) for s in ("s", "u", "d", "xs")},
        b_r=dma((3, WB)),
        **{"b_" + s: dma((1, WB)) for s in ("t", "xr")},
        **{"c_" + s: dma((2, 2)) for s in ("s", "u", "xs")},
        **{"c_" + s: dma((2, WC)) for s in ("r", "t", "xr")},
    )
    any_spec = pl.BlockSpec(memory_space=pl.ANY)
    vm_spec = pl.BlockSpec(memory_space=pltpu.VMEM)
    operands = (tok, tim, seg, n1g, n1b, wqkv.transpose(0, 2, 1), qvb, wout, outb, n2g, n2b)
    operands += (wup, upb, wdn, dnb, cot)
    near = L <= 8
    result = pltpu.VMEM if near else jax.ShapeDtypeStruct
    out, ig, tg, f = pl.pallas_call(
        functools.partial(kernel, n_dp, (UA, UB, UC), tuple(scratch)),
        out_shape=(
            result((tokens, width), BF16),
            result((tokens, width), BF16),
            result((rows_n, width), F32),
            result((total, width), F32),
        ),
        in_specs=[any_spec] * 16,
        out_specs=(vm_spec if near else any_spec,) * 4,
        scratch_shapes=list(scratch.values()),
        compiler_params=pltpu.CompilerParams(
            collective_id=0, has_side_effects=True, vmem_limit_bytes=(52 if near else 63) * 2**20
        ),
        cost_estimate=pl.CostEstimate(flops=6 * 10**9, bytes_accessed=20 * 10**6, transcendentals=0),
    )(
        *[pltpu.with_memory_space_constraint(v, pltpu.HBM) for v in operands]
    )
    f32 = lambda *shape: jax.ShapeDtypeStruct(shape, F32)
    moved = (
        jax.ShapeDtypeStruct((tokens, width), BF16),
        jax.ShapeDtypeStruct((tokens, width), BF16),
        f32(rows_n, width),
        f32(3, loc, width),
        f32(loc, width),
        f32(width, ff),
        f32(ff, width),
    )
    results = pl.pallas_call(
        functools.partial(place, big, near),
        out_shape=moved + (f32(2, loc), f32(ff)) + (f32(width),) * 6,
        in_specs=[vm_spec if near else any_spec] * 4,
        out_specs=(any_spec,) * 15,
        scratch_shapes=[
            *([] if near else [vm((tokens, width), BF16), vm((tokens, width), BF16)]),
            *([] if near else [vm((rows_n, width), F32), vm((total, width), F32)]),
            vm((2, loc), F32),
            *[vm((width,), F32)] * 7,
            dma((4,)),
            dma((17,)),
        ],
        compiler_params=pltpu.CompilerParams(vmem_limit_bytes=(4 if near else 63) * 2**20),
    )(out, ig, tg, f)
    out, ig, tg, qkv, outw, up, down, qvb, upb, downb, n2g, n2b, outb, n1g, n1b = results
    return out, ig, tg, n1g, n1b, qkv.transpose(0, 2, 1), qvb, outw, outb, n2g, n2b, up, upb, down, downb


def place(big, near, *refs):
    results, outs = refs[:4], refs[4:19]
    held = results if near else refs[19:23]
    vq, *flat, sem, sem_o = refs[19 if near else 23 :]
    out_o, ig_o, tg_o, qkv, outw, up, down, qvb, upb, downb, n2g, n2b, outb, n1g, n1b = outs
    loc, ff = outw.shape[0], down.shape[0]
    half = down.shape[1] // 2
    if not near:
        loads = [pltpu.make_async_copy(a, b, sem.at[i]) for i, (a, b) in enumerate(zip(results, held))]
        for copy in loads:
            copy.start()
        for copy in loads:
            copy.wait()
    out, ig, tg, f = held
    moves = []
    row = 0
    for n, ref in ((ff, down), (ff, up), (loc, outw), (loc, qkv.at[0]), (loc, qkv.at[1]), (loc, qkv.at[2])):
        moves.append((f.at[pl.ds(row, n)], ref))
        row += n
    moves += [(out, out_o), (ig, ig_o), (tg, tg_o)]
    small = (downb, upb, n2g, n2b, outb, n1g, n1b)
    moves += [*zip(flat, small), (vq, qvb)]
    stores = [pltpu.make_async_copy(a, b, sem_o.at[i]) for i, (a, b) in enumerate(moves)]
    for copy in stores[:9]:
        copy.start()
    for i, ref in enumerate(flat):
        ref[...] = f[big + i : big + i + 1, :].reshape(ref.shape)
    vq[0:1, :] = f[big + 7 : big + 8, 0:loc]
    vq[1:2, :] = f[big + 7 : big + 8, half : half + loc]
    for copy in stores[9:]:
        copy.start()
    for copy in stores:
        copy.wait()


def solution(mesh):
    placed = (
        P("dp", None),
        P("dp", None),
        P("dp", None),
        P(),
        P(),
        P(None, None, "mp"),
        P(None, "mp"),
        P("mp", None),
        P(),
        P(),
        P(),
        P(None, "mp"),
        P("mp"),
        P("mp", None),
        P(),
        P("dp", None),
    )
    return jax.shard_map(
        functools.partial(shards, mesh.shape["dp"]),
        mesh=mesh,
        in_specs=placed,
        out_specs=(
            P("dp", None),
            P("dp", None),
            P("dp", None),
            P(),
            P(),
            P(None, None, "mp"),
            P(None, "mp"),
            P("mp", None),
            P(),
            P(),
            P(),
            P(None, "mp"),
            P("mp"),
            P("mp", None),
            P(),
        ),
        check_vma=False,
    )
```

```python
import functools

import jax
import jax.numpy as jnp
from jax import lax
from jax.experimental import pallas as pl
from jax.experimental.pallas import tpu as pltpu
from jax.sharding import PartitionSpec as P

HD = 64
SUB = 128
CH = 8
W_PIECES = 3
EACH = 3
S_FIRST = 30
SENDS = 4
MESH = pl.DeviceIdType.MESH
F32 = jnp.float32
BF16 = jnp.bfloat16


ARGS = ("tok", "tim", "seg", "n1g", "n1b", "wqkv", "qvb", "wout", "outb", "n2g", "n2b")
ARGS += ("wup", "upb", "wdn", "dnb", "cot")


def hop_ticks(line):
    return 2 if line <= 8 else 1


def when(cond, fn):
    pl.when(cond)(fn)


def rem(a, n):
    return lax.rem(a, jnp.int32(n))


def div(a, n):
    return lax.div(a, jnp.int32(n))


def two_power(n):
    return 1 << (n - 1).bit_length()


def nt(a, b):
    return lax.dot_general(a, b, (((1,), (1,)), ((), ())), preferred_element_type=F32)


def tn(a, b):
    return lax.dot_general(a, b, (((0,), (0,)), ((), ())), preferred_element_type=F32)


def nn(a, b):
    return jnp.dot(a, b, preferred_element_type=F32)


def normed(v):
    centred = v - jnp.mean(v, -1, keepdims=True)
    spread = jnp.mean(centred * centred, -1, keepdims=True)
    scale = lax.rsqrt(spread + 1e-05)
    return centred * scale, scale


def colsum(v):
    return jnp.sum(v, 0, keepdims=True)


def kernel(n_dp, near, units, names, *refs):
    out_o, ig_o, tg_o, f_out = refs[16:20]
    R = dict(zip(names, refs[20:]))
    order = ("tok", "tim", "n1g", "n1b", "wqkv", "qvb", "seg", "wout", "outb", "cot", "wdn")
    order += ("n2g", "n2b", "wup", "upb", "dnb")
    tok, tim, wqkv, qvb, seg, wout, cot, wdn, wup = (
        R[s] for s in ("tok", "tim", "wqkv", "qvb", "seg", "wout", "cot", "wdn", "wup")
    )
    loads = {
        name: pltpu.make_async_copy(refs[ARGS.index(name)], R[name], R["ins"].at[i]) for i, name in enumerate(order)
    }
    n1g, n1b, outb, n2g, n2b, upb, dnb = (R["vecs"].at[pl.ds(i, 1)] for i in range(7))
    timf, start, entry, q_s, k_s, v_s = (R[s] for s in ("timf", "start", "entry", "q", "k", "v"))
    probs, mixed_s, part, cr, ys, yr = (R[s] for s in ("probs", "mixed", "part", "cr", "ys", "yr"))
    tot, mid, e2, hp, act, gp = (R[s] for s in ("tot", "mid", "e2", "hp", "act", "gp"))
    out, ig, tg = (out_o, ig_o, tg_o) if near else (R[s] for s in ("out", "ig", "tg"))
    gact, gmid, gbr, lt, g = (R[s] for s in ("gact", "gmid", "gbr", "lt", "g"))
    f = f_out if near else R["f"]

    rows_n, seq = seg.shape
    width = tok.shape[1]
    half = width // 2
    loc = wout.shape[0]
    heads = loc // HD
    ff = wup.shape[1]
    UA, UB, UC = units
    L = n_dp // 2
    LAG = hop_ticks(L)
    H = L // 2
    dp = lax.axis_index("dp")
    mp = lax.axis_index("mp")
    core = mp % 2
    x = dp % 2
    z = dp // 2
    to_core = (dp, mp + 1 - 2 * core)
    to_y = (dp, (mp + 2) % 4)
    to_x = (dp + 1 - 2 * x, mp)
    last = jnp.minimum(z, L - 1 - z)
    side = div(z, H)
    cross = jnp.where(last == H - 1, 1, 0)
    to_in = ((z + 1 - 2 * side) * 2 + x, mp)
    to_out = (jnp.clip(z - 1 + 2 * side, 0, L - 1) * 2 + x, mp)
    zlo = jnp.maximum(z - 1, 0) * 2 + x
    zhi = jnp.minimum(z + 1, L - 1) * 2 + x

    barrier = pltpu.get_barrier_semaphore()
    for dev in (to_core, to_y, to_x):
        pl.semaphore_signal(barrier, 1, device_id=dev, device_id_type=MESH)
    when(z > 0, lambda: pl.semaphore_signal(barrier, 1, device_id=(zlo, mp), device_id_type=MESH))
    when(z < L - 1, lambda: pl.semaphore_signal(barrier, 1, device_id=(zhi, mp), device_id_type=MESH))
    greeted = 3 + jnp.minimum(z, 1) + jnp.minimum(L - 1 - z, 1)

    def sl(r, n=seq):
        return pl.ds(pl.multiple_of(r * n, n), n)

    def sub(r, i):
        return pl.ds(pl.multiple_of(r * seq + i * SUB, SUB), SUB)

    mine = pl.ds(pl.multiple_of(core * half, 128), half)
    other = pl.ds(pl.multiple_of((1 - core) * half, 128), half)

    def remote(src, dst, ssem, rsem, dev):
        return pltpu.make_async_remote_copy(
            src_ref=src, dst_ref=dst, send_sem=ssem, recv_sem=rsem, device_id=dev, device_id_type=MESH
        )

    def core_copy(p, r):
        return remote(part.at[sl(r), other], cr.at[sl(r)], R["cs"].at[r], R["crs"].at[r], to_core)

    def y_copy(p, r):
        return remote(ys.at[sl(r)], yr.at[p % 2, sl(r)], R["yss"].at[r], R["yrs"].at[p % 2, r], to_y)

    def ag_copy(p, r):
        return remote(tot.at[sl(r), mine], tot.at[sl(r), mine], R["gs"].at[r], R["grs"].at[r], to_core)

    def sum_b(p, r):
        core_copy(p, r).wait()
        ys[sl(r), :] = part[sl(r), mine] + cr[sl(r), :]
        y_copy(p, r).start()

    def sum_c(p, r):
        y_copy(p, r).wait()
        tot[sl(r), mine] = ys[sl(r), :] + yr[p % 2, sl(r), :]
        ag_copy(p, r).start()

    def sum_d(p, r):
        ag_copy(p, r).wait()

    def vec(ref):
        return ref[...]

    small = 2 * ff + 4 * loc

    def small_add(i, v):
        g[small + i : small + i + 1, :] += v

    lane = lax.broadcasted_iota(jnp.int32, (1, loc), 1)
    masks = [((lane >= h * HD) & (lane < (h + 1) * HD)).astype(F32) for h in range(heads)]

    def by_head(v):
        return jnp.concatenate([v * m.astype(BF16) for m in masks], 0)

    def from_heads(v):
        total = v[:seq] * masks[0]
        for h in range(1, heads):
            total = total + v[h * seq : (h + 1) * seq] * masks[h]
        return total

    def norm1(r):
        @pl.loop(0, seq // SUB)
        def _(i):
            s = sub(r, i)
            v = tok[s, :].astype(F32) + timf[pl.ds(r, 1), :]
            start[s, :] = v
            xhat, _ = normed(v)
            entry[s, :] = (xhat * n1g[...] + n1b[...]).astype(BF16)

    def project(r):
        e = entry[sl(r), :]
        q_s[sl(r), :] = (nt(e, wqkv[0]) + qvb[0:1, :]).astype(BF16)
        k_s[sl(r), :] = nt(e, wqkv[1]).astype(BF16)
        v_s[sl(r), :] = (nt(e, wqkv[2]) + qvb[1:2, :]).astype(BF16)

    def attend(r):
        labels = jnp.broadcast_to(seg[pl.ds(r, 1), :], (seq, seq))
        same = labels == labels.T
        same = jnp.concatenate([same.astype(F32)] * heads, 0) > 0.5
        scores = nt(by_head(q_s[sl(r), :]), k_s[sl(r), :]) * HD ** (-0.5)
        scores = jnp.where(same, scores, -1e30)
        w = jnp.exp(scores - jnp.max(scores, -1, keepdims=True))
        pr = w / jnp.sum(w, -1, keepdims=True)
        probs[sl(r, heads * seq), :] = pr
        mixed = from_heads(nn(pr.astype(BF16), v_s[sl(r), :])).astype(BF16)
        mixed_s[sl(r), :] = mixed
        turned = mixed.T
        lt[2 * ff : 2 * ff + loc, sl(r)] = turned
        mixa[mp, r] = turned.astype(F32)
        m_core(r).start()
        m_y(r).start()

    wf, wall, mixa = R["wf"], R["wall"], R["mixa"]
    mp_y, mp_c = rem(mp + 2, 4), mp + 1 - 2 * core
    mine_0, other_0 = mp - core, mp_y - core
    hl = loc // 2
    pr_n = hl // W_PIECES

    def w_core():
        return remote(wf.at[mp], wf.at[mp], R["wcs"], R["wcr"], to_core)

    def w_rows(start, n):
        return pl.ds(pl.multiple_of(start, CH), n)

    def w_y(i):
        s = w_rows(x * hl + i * pr_n, pr_n)
        return remote(wf.at[mp, s], wf.at[mp, s], R["wys"].at[i], R["wyr"].at[i], to_y)

    def w_x(i):
        s = w_rows(x * hl + i * pr_n, pr_n)
        return remote(wf.at[mp_y, s], wf.at[mp_y, s], R["wxs"].at[i], R["wxr"].at[i], to_x)

    def w_share(h):
        s = w_rows((x + h - 2 * x * h) * hl, hl)
        return remote(wf.at[mp_y, s], wf.at[mp_y, s], R["whs"].at[h], R["whr"].at[h], to_core)

    def m_core(r):
        return remote(mixa.at[mp, r], mixa.at[mp, r], R["cs"].at[r], R["crs"].at[r], to_core)

    def m_y(r):
        return remote(mixa.at[mp, r], mixa.at[mp, r], R["yss"].at[r], R["yrs"].at[0, r], to_y)

    def m_share(r):
        return remote(mixa.at[mp_y, r], mixa.at[mp_y, r], R["gs"].at[r], R["grs"].at[r], to_core)

    def weights_out():
        loads["wout"].wait()
        wf[mp] = wout[...].astype(F32)
        pl.semaphore_wait(barrier, greeted)
        for i in range(W_PIECES):
            w_y(i).start()
        w_core().start()

    def weights_on(i):
        w_y(i).wait()
        w_x(i).start()

    def pair_sum(m, r):
        return tn(mixa[m, r].astype(BF16), wall[m]) + tn(mixa[m + 1, r].astype(BF16), wall[m + 1])

    def near_part(r):
        m_core(r).wait()
        part[sl(r), :] = pair_sum(mine_0, r)

    def across(r):
        m_y(r).wait()
        m_share(r).start()

    def far_part(r):
        m_share(r).wait()
        tot[sl(r), :] = part[sl(r), :] + pair_sum(other_0, r)

    def grad_act(r):
        c = cot[sl(r), :]
        gact[sl(r), :] = nt(c, wdn[...])
        small_add(0, colsum(c.astype(F32)))

    def feed(r):
        @pl.loop(0, seq // SUB)
        def _(i):
            s = sub(r, i)
            v = start[s, :] + (tot[s, :] + outb[...])
            mid[s, :] = v
            xhat, _ = normed(v)
            e2[s, :] = (xhat * n2g[...] + n2b[...]).astype(BF16)

        hp[...] = nn(e2[sl(r), :], wup[...])

        @pl.loop(0, seq // SUB)
        def _(i):
            s = sub(r, i)
            u = hp[pl.ds(pl.multiple_of(i * SUB, SUB), SUB), :] + upb[...]
            cdf = 0.5 * (1.0 + lax.erf(u * 0.7071067811865476))
            act[s, :] = (u * cdf).astype(BF16)
            slope = cdf + u * (0.3989422804014327 * jnp.exp(-0.5 * u * u))
            pre = (gact[s, :] * slope).astype(BF16)
            gp[s, :] = pre
            small_add(1, colsum(pre.astype(F32)))

        lt[0:ff, sl(r)] = act[sl(r), :].T

    def feed_on(r):
        part[sl(r), :] = nt(gp[sl(r), :], wup[...])
        core_copy(1, r).start()
        lt[ff : 2 * ff, sl(r)] = e2[sl(r), :].T

    def back2(r):
        @pl.loop(0, seq // SUB)
        def _(i):
            s = sub(r, i)
            ge = tot[s, :]
            xhat, scale = normed(mid[s, :])
            small_add(2, colsum(ge * xhat))
            small_add(3, colsum(ge))
            gx = ge * n2g[...]
            gm = cot[s, :].astype(F32) + scale * (
                gx - jnp.mean(gx, -1, keepdims=True) - xhat * jnp.mean(gx * xhat, -1, keepdims=True)
            )
            gmid[s, :] = gm
            low = gm.astype(BF16)
            gbr[s, :] = low
            small_add(4, colsum(low.astype(F32)))

        g3 = by_head(nt(gbr[sl(r), :], wout[...]).astype(BF16))
        pr = probs[sl(r, heads * seq), :]
        grad_probs = nt(g3, v_s[sl(r), :])
        inner = jnp.sum(pr * grad_probs, -1, keepdims=True)
        ds = (pr * (grad_probs - inner)).astype(BF16)
        gq = (from_heads(nn(ds, k_s[sl(r), :])) * HD ** (-0.5)).astype(BF16)
        gk = (tn(ds, by_head(q_s[sl(r), :])) * HD ** (-0.5)).astype(BF16)
        gv = tn(pr.astype(BF16), g3).astype(BF16)
        part[sl(r), :] = nn(gq, wqkv[0]) + nn(gk, wqkv[1]) + nn(gv, wqkv[2])
        core_copy(2, r).start()
        late = 2 * ff + loc
        for i, v in enumerate((gq, gk, gv)):
            lt[late + i * loc : late + (i + 1) * loc, sl(r)] = v.T
        g[small + 7 : small + 8, 0:loc] += colsum(gq.astype(F32))
        g[small + 7 : small + 8, half : half + loc] += colsum(gv.astype(F32))

    def back1(r):
        tg[pl.ds(r, 1), :] = jnp.zeros((1, width), F32)

        @pl.loop(0, seq // SUB)
        def _(i):
            s = sub(r, i)
            ge = tot[s, :]
            xhat, scale = normed(start[s, :])
            small_add(5, colsum(ge * xhat))
            small_add(6, colsum(ge))
            gy = ge * n1g[...]
            gs = gmid[s, :] + scale * (
                gy - jnp.mean(gy, -1, keepdims=True) - xhat * jnp.mean(gy * xhat, -1, keepdims=True)
            )
            ig[s, :] = gs.astype(BF16)
            tg[pl.ds(r, 1), :] += colsum(gs)

    def down(r):
        part[sl(r), :] = nn(act[sl(r), :], wdn[...])
        core_copy(3, r).start()

    def finish(r):
        @pl.loop(0, seq // SUB)
        def _(i):
            s = sub(r, i)
            out[s, :] = (mid[s, :] + (tot[s, :] + dnb[...])).astype(BF16)

    blk = loc

    early = ff // blk

    def weight_grads(j):
        s = pl.ds(pl.multiple_of(j * blk, blk), blk)

        def by(right):
            def fn():
                g[s, :] = nn(lt[s, :], right[...])

            return fn

        when(j < early, by(cot))
        when((j >= early) & (j < 2 * early), by(gp))
        when(j == 2 * early, by(gbr))
        when(j > 2 * early, by(entry))

    def go(copy, u, depth):
        when(u >= depth, lambda: copy(u - depth).wait_send())
        copy(u).start()

    def end(copy, n, depth):
        for u in range(n - min(depth, n), n):
            copy(u).wait_send()

    AF = LAG

    def base_of(u):
        return u * 4 * CH

    def later(u):
        return base_of(div(u, EACH) * (EACH + 2) + rem(u, EACH))

    def b_base(u, i):
        return base_of(jnp.minimum(u * (EACH + 2) + EACH + i, UA + UB + UC - 1))

    def a_base(u, owner):
        return later(u) + owner * 2 * CH

    def x_slot(u):
        return pl.ds(pl.multiple_of(rem(u, R["xr"].shape[0]) * 2 * CH, CH), 2 * CH)

    def x_first(u):
        src = pl.ds(pl.multiple_of(later(u) + (1 - x) * 2 * CH, CH), 2 * CH)
        return remote(
            g.at[src], R["xrb"].at[x_slot(u)], R["xs"].at[rem(u, SENDS)], R["xr"].at[rem(u, R["xr"].shape[0])], to_x
        )

    def rows_at(base, n):
        return pl.ds(pl.multiple_of(base, CH), n)

    class Line:
        def __init__(self, kind, n, first, stride, depth):
            self.kind, self.n, self.first, self.stride, self.depth = kind, n, first, stride, depth

        def unit(self, t, offset):
            rel = t - self.first - offset
            if self.stride == 1:
                return rel, (rel >= 0) & (rel < self.n)
            return div(rel, self.stride), (rel >= 0) & (rel < self.n * self.stride) & (rem(rel, self.stride) == 0)

        def sem(self, name, i, u):
            ref = R[self.kind + "_" + name]
            return ref.at[i, rem(u, ref.shape[1])]

        def slot(self, u, rows):
            return rows_at(rem(u, R[self.kind + "_r"].shape[1]) * rows, rows)

        def go(self, copy, u):
            go(copy, u, self.depth)

        def end(self, copy):
            end(copy, self.n, self.depth)

    class A(Line):
        def own(self, u):
            return rows_at(a_base(u, x), 2 * CH)

        def inward(self, u):
            dst = R["abuf"].at[cross, self.slot(u, 2 * CH)]
            return remote(g.at[self.own(u)], dst, self.sem("s", 0, u), self.sem("r", cross, u), to_in)

        def arrived(self, u, i):
            buf = R["abuf"].at[i, self.slot(u, 2 * CH)]
            remote(buf, buf, self.sem("s", 0, u), self.sem("r", i, u), to_in).wait_recv()
            return buf

        def outward(self, u):
            own = self.own(u)
            return remote(f.at[own], f.at[own], self.sem("u", 0, u), self.sem("r", 1, u), to_out)

        def x_last(self, u):
            own = self.own(u)
            return remote(f.at[own], f.at[own], self.sem("xs", 0, u), self.sem("xr", 0, u), to_x)

        def tick(self, t):
            u, valid_u = self.unit(t, last * LAG)

            def reduce():
                def add():
                    g[self.own(u), :] += self.arrived(u, 0)[...]

                if H > 1:
                    when(last > 0, add)
                self.go(self.inward, u)

            when(valid_u, reduce)
            v, valid_v = self.unit(t, (2 * H - 1 - last) * LAG)

            def finish():
                def turn():
                    f[self.own(v), :] = g[self.own(v), :] + self.arrived(v, 1)[...]

                when(last == H - 1, turn)
                if H > 1:
                    when(last < H - 1, lambda: self.outward(v).wait_recv())
                    when(last > 0, lambda: self.go(self.outward, v))
                self.go(self.x_last, v)

            when(valid_v, finish)
            e, valid_e = self.unit(t, (2 * H - last) * LAG)
            when(valid_e, lambda: self.x_last(e).wait_recv())

        def drain(self):
            self.end(self.inward)
            self.end(self.x_last)
            if H > 1:
                when(last > 0, lambda: self.end(self.outward))

    class B(Line):
        def all(self, u):
            return rows_at(b_base(u, 0), 4 * CH)

        def half(self, u, i):
            return rows_at(b_base(u, 0) + i * 2 * CH, 2 * CH)

        def inward(self, u):
            dst = R["bbuf"].at[self.slot(u, 4 * CH)]
            return remote(g.at[self.all(u)], dst, self.sem("s", 0, u), self.sem("r", 0, u), to_in)

        def swap(self, u):
            dst = R["bsw"].at[self.slot(u, 2 * CH)]
            return remote(g.at[self.half(u, 1 - side)], dst, self.sem("s", 0, u), self.sem("r", 1, u), to_in)

        def x_copy(self, u):
            dst = R["bxb"].at[self.slot(u, 2 * CH)]
            return remote(g.at[self.half(u, side)], dst, self.sem("xs", 0, u), self.sem("xr", 0, u), to_x)

        def back(self, u):
            own = self.half(u, side)
            return remote(f.at[own], f.at[own], self.sem("d", 0, u), self.sem("r", 2, u), to_in)

        def outward(self, u):
            own = self.all(u)
            return remote(f.at[own], f.at[own], self.sem("u", 0, u), self.sem("r", 1, u), to_out)

        def tick(self, t):
            u, valid_u = self.unit(t, last * LAG)

            def reduce():
                def add():
                    self.inward(u).wait_recv()
                    g[self.all(u), :] += R["bbuf"][self.slot(u, 4 * CH), :]

                if H > 1:
                    when(last > 0, add)
                    when(last < H - 1, lambda: self.go(self.inward, u))
                when(last == H - 1, lambda: self.go(self.swap, u))

            when(valid_u, reduce)
            middle = last == H - 1
            i, valid_i = self.unit(t, H * LAG)

            def over():
                self.swap(i).wait_recv()
                g[self.half(i, side), :] += R["bsw"][self.slot(i, 2 * CH), :]
                self.go(self.x_copy, i)

            when(valid_i & middle, over)
            j, valid_j = self.unit(t, (H + 1) * LAG)

            def total():
                self.x_copy(j).wait_recv()
                own = self.half(j, side)
                f[own, :] = g[own, :] + R["bxb"][self.slot(j, 2 * CH), :]
                self.go(self.back, j)

            when(valid_j & middle, total)
            v, valid_v = self.unit(t, (2 * H + 1 - last) * LAG)

            def finish():
                when(middle, lambda: self.back(v).wait_recv())
                if H > 1:
                    when(last < H - 1, lambda: self.outward(v).wait_recv())
                    when(last > 0, lambda: self.go(self.outward, v))

            when(valid_v, finish)

        def drain(self):
            def ends():
                for copy in (self.swap, self.x_copy, self.back):
                    self.end(copy)

            when(last == H - 1, ends)
            if H > 1:
                when(last < H - 1, lambda: self.end(self.inward))
                when(last > 0, lambda: self.end(self.outward))

    class C(Line):
        dirs, rows = (0, 1), 2 * CH

        def own(self, u, d):
            return rows_at(b_base(u, 1) + d * 2 * CH, 2 * CH)

        def place(self, d):
            w = z if d == 0 else L - 1 - z
            return w, (zhi if d == 0 else zlo, mp), (zlo if d == 0 else zhi, mp)

        def copies(self, d):
            w, up, dn = self.place(d)
            own = lambda u: self.own(u, d)
            slot = lambda u: self.slot(u, self.rows)

            def send(u):
                return remote(g.at[own(u)], R[self.kind + "buf"].at[d, slot(u)], self.sem("s", d, u), self.sem("r", d, u), dn)

            def x_copy(u):
                return remote(g.at[own(u)], R[self.kind + "xb"].at[d, slot(u)], self.sem("s", d, u), self.sem("t", d, u), to_x)

            def spread(u):
                return remote(f.at[own(u)], f.at[own(u)], self.sem("u", d, u), self.sem("t", d, u), up)

            return w, send, x_copy, spread

        def tick(self, t):
            for d in self.dirs:
                w, send, x_copy, spread = self.copies(d)
                u, valid_u = self.unit(t, (L - 1 - w) * LAG)

                def reduce():
                    def add():
                        send(u).wait_recv()
                        g[self.own(u, d), :] += R[self.kind + "buf"][d, self.slot(u, self.rows), :]

                    when(w < L - 1, add)
                    when(w > 0, lambda: self.go(send, u))
                    when(w == 0, lambda: self.go(x_copy, u))

                when(valid_u, reduce)
                v, valid_v = self.unit(t, (L + w) * LAG)

                def finish():
                    def turn():
                        x_copy(v).wait_recv()
                        own = self.own(v, d)
                        f[own, :] = g[own, :] + R[self.kind + "xb"][d, self.slot(v, self.rows), :]

                    when(w == 0, turn)
                    when(w > 0, lambda: spread(v).wait_recv())
                    when(w < L - 1, lambda: self.go(spread, v))

                when(valid_v, finish)

        def drain(self):
            for d in self.dirs:
                w, send, x_copy, spread = self.copies(d)
                when(w > 0, lambda: self.end(send))
                when(w == 0, lambda: self.end(x_copy))
                when(w < L - 1, lambda: self.end(spread))

    class S(C):
        dirs, rows = (0,), CH

        def own(self, u, d):
            return pl.ds(small, CH)

    lines = [C("c", UC, 0, EACH, 2), A("a", UA, AF, 1, SENDS), B("b", UB, 1, EACH, 2), S("e", 1, S_FIRST, 1, 1)]

    def dp_tick(t):
        when(t < UA, lambda: go(x_first, t, SENDS))
        v = t - AF

        def x_add():
            x_first(v).wait_recv()
            s = rows_at(a_base(v, x), 2 * CH)
            g[s, :] += R["xrb"][x_slot(v), :]

        when((v >= 0) & (v < UA), x_add)
        for line in lines:
            line.tick(t)

    def dp_drain():
        end(x_first, UA, SENDS)
        for line in lines:
            line.drain()

    for copy in loads.values():
        copy.start()

    def vector(i, name):
        loads[name].wait()
        R["vecs"][i : i + 1, :] = R[name][...][None, :]

    g[small : small + CH, :] = jnp.zeros((CH, width), F32)
    for name in ("tok", "tim"):
        loads[name].wait()
    timf[...] = tim[...].astype(F32)
    vector(0, "n1g")
    vector(1, "n1b")

    @pl.loop(0, rows_n)
    def _(r):
        norm1(r)

        @pl.when(r == 0)
        def _():
            for name in ("wqkv", "qvb", "seg"):
                loads[name].wait()

        project(r)
        when(r == 0, weights_out)
        attend(r)
        for i in range(W_PIECES - 1):
            when(r == rows_n - W_PIECES + 1 + i, lambda: weights_on(i))

    for name in ("cot", "wdn", "wup"):
        loads[name].wait()
    for i, name in enumerate(("outb", "n2g", "n2b", "upb", "dnb")):
        vector(2 + i, name)
    pl.loop(0, rows_n)(grad_act)
    weights_on(W_PIECES - 1)
    w_share(0).start()
    w_core().wait()
    for i in range(2):
        wall[mine_0 + i] = wf[mine_0 + i].astype(BF16)
    pl.loop(0, rows_n)(near_part)
    ahead = min(2, rows_n)
    for r in range(ahead):
        across(r)
    for i in range(W_PIECES):
        w_x(i).wait()
    w_share(1).start()
    for h in range(2):
        w_share(h).wait()
    for i in range(2):
        wall[other_0 + i] = wf[other_0 + i].astype(BF16)

    @pl.loop(0, rows_n)
    def _(r):
        far_part(r)
        feed(r)
        when(r + ahead < rows_n, lambda: across(r + ahead))

    weight_grads(jnp.int32(0))

    blocks = (2 * ff + 4 * loc) // blk
    a_last = AF + LAG * 2 * H
    b_last, c_last = 1 + LAG * (2 * H + 1), LAG * (2 * L - 1)
    ends = [S_FIRST + c_last]
    for u in range(UA + UB + UC):
        i, k = u // (EACH + 2), u % (EACH + 2)
        if k < EACH and u < UA + UB + UC - (UB > UC):
            ends.append(i * EACH + k + a_last)
        else:
            ends.append(i * EACH + c_last if k > EACH else (UB - 1 if k < EACH else i) * EACH + b_last)
    ticks = max(ends) + 1
    per = blk // (4 * CH)

    def done(j):
        return ends[0] if j == blocks else max(ends[1 + j * per : 1 + (j + 1) * per])

    def out_copy(j):
        s = pl.ds(j * blk, blk if j < blocks else CH)
        return pltpu.make_async_copy(f.at[s], f_out.at[s], R["fin"].at[j])

    done_copies = [] if near else [
        pltpu.make_async_copy(a, b, R["fin"].at[blocks + 1 + i])
        for i, (a, b) in enumerate(((ig, ig_o), (tg, tg_o), (out, out_o)))
    ]

    @pl.loop(0, ticks)
    def _(t):
        dp_tick(t)

        def at(first, step, fn):
            r = (t - first) // step
            when((t >= first) & ((t - first) % step == 0) & (r < rows_n), lambda: fn(r))

        at(2, 2, lambda r: sum_b(1, r))
        at(1, 2, feed_on)
        at(5, 3, lambda r: sum_c(1, r))

        def second(r):
            sum_d(1, r)
            back2(r)

        at(7, 3, second)
        at(9, 3, lambda r: sum_b(2, r))
        at(15, 3, lambda r: sum_c(2, r))

        def third(r):
            sum_d(2, r)
            back1(r)

        at(17, 3, third)
        at(18, 3, down)
        at(20, 3, lambda r: sum_b(3, r))
        at(26, 3, lambda r: sum_c(3, r))

        def fourth(r):
            sum_d(3, r)
            finish(r)

        at(28, 3, fourth)

        @pl.when(t == 28 + 3 * rows_n)
        def _():
            for copy in done_copies:
                copy.start()

        when((rem(t, 3) == 1) & (t < 3 * blocks - 2), lambda: weight_grads(div(t + 2, 3)))
        for j in range(0 if near else blocks + 1):
            if done(j) < ticks - 1:
                when(t == done(j), lambda: out_copy(j).start())

    dp_drain()
    left = 0 if near else blocks + 1
    for j in range(left):
        if done(j) >= ticks - 1:
            out_copy(j).start()
    for copy in done_copies + [out_copy(j) for j in range(left)]:
        copy.wait()


def shards(n_dp, *args):
    (tok, tim, seg, n1g, n1b, wqkv, qvb, wout, outb, n2g, n2b, wup, upb, wdn, dnb, cot) = args
    tokens, width = tok.shape
    rows_n, seq = seg.shape
    loc, ff = wout.shape[0], wup.shape[1]
    heads = loc // HD
    half = width // 2
    big = 2 * ff + 4 * loc
    count = big // (4 * CH)
    UC = count // (EACH + 2)
    UB = UC + min(count % (EACH + 2) // 2, 1)
    UA = count - UB - UC
    L = n_dp // 2
    LAG = hop_ticks(L)
    near = L <= 8
    vm = pltpu.VMEM
    dma = pltpu.SemaphoreType.DMA
    W = two_power(max(LAG * (L - 1) + 1, 2 * LAG + 2))
    WB = two_power(LAG * (L + 1) // EACH + 1)
    WC = two_power(LAG * (2 * L - 1) // EACH + 1)
    total = big + CH
    flat = lambda n: vm((n,), F32)
    scratch = dict(
        tok=vm((tokens, width), BF16),
        cot=vm((tokens, width), BF16),
        wqkv=vm((3, loc, width), BF16),
        wout=vm((loc, width), BF16),
        wup=vm((width, ff), BF16),
        wdn=vm((ff, width), BF16),
        ins=dma((16,)),
        tim=vm((rows_n, width), BF16),
        seg=vm((rows_n, seq), jnp.int32),
        qvb=vm((2, loc), F32),
        **{s: flat(width) for s in ("n1g", "n1b", "outb", "n2g", "n2b", "dnb")},
        upb=flat(ff),
        vecs=vm((8, width), F32),
        timf=vm((rows_n, width), F32),
        start=vm((tokens, width), F32),
        entry=vm((tokens, width), BF16),
        q=vm((tokens, loc), BF16),
        k=vm((tokens, loc), BF16),
        v=vm((tokens, loc), BF16),
        probs=vm((heads * tokens, seq), F32),
        mixed=vm((tokens, loc), BF16),
        part=vm((tokens, width), F32),
        cr=vm((tokens, half), F32),
        ys=vm((tokens, half), F32),
        yr=vm((2, tokens, half), F32),
        tot=vm((tokens, width), F32),
        mid=vm((tokens, width), F32),
        e2=vm((tokens, width), BF16),
        hp=vm((seq, ff), F32),
        act=vm((tokens, ff), BF16),
        gp=vm((tokens, ff), BF16),
        gact=vm((tokens, ff), F32),
        gmid=vm((tokens, width), F32),
        gbr=vm((tokens, width), BF16),
        **{n: vm((tokens, width), BF16) for n in (() if near else ("out", "ig"))},
        **({} if near else dict(tg=vm((rows_n, width), F32))),
        lt=vm((big, tokens), BF16),
        g=vm((total, width), F32),
        **({} if near else dict(f=vm((total, width), F32))),
        xrb=vm((W * 2 * CH, width), F32),
        abuf=vm((2, W * 2 * CH, width), F32),
        bbuf=vm((WB * 4 * CH, width), F32),
        bsw=vm((WB * 2 * CH, width), F32),
        bxb=vm((WB * 2 * CH, width), F32),
        cbuf=vm((2, WC * 2 * CH, width), F32),
        cxb=vm((2, WC * 2 * CH, width), F32),
        ebuf=vm((1, CH, width), F32),
        exb=vm((1, CH, width), F32),
        **{"e_" + s: dma((1, 1)) for s in ("s", "u", "r", "t")},
        wf=vm((4, loc, width), F32),
        wall=vm((4, loc, width), BF16),
        mixa=vm((4, rows_n, loc, seq), F32),
        wcs=dma,
        wcr=dma,
        **{s: dma((W_PIECES,)) for s in ("wys", "wyr", "wxs", "wxr")},
        **{s: dma((2,)) for s in ("whs", "whr")},
        **{s: dma((rows_n,)) for s in ("cs", "crs", "yss", "gs", "grs")},
        yrs=dma((2, rows_n)),
        **({} if near else dict(fin=dma((big // loc + 4,)))),
        xs=dma((SENDS,)),
        xr=dma((W,)),
        **{"a_" + s: dma((1, SENDS)) for s in ("s", "u", "xs")},
        a_r=dma((2, W)),
        a_xr=dma((1, W)),
        **{"b_" + s: dma((1, 2)) for s in ("s", "u", "d", "xs")},
        b_r=dma((3, WB)),
        b_xr=dma((1, WB)),
        **{"c_" + s: dma((2, 2)) for s in ("s", "u")},
        **{"c_" + s: dma((2, WC)) for s in ("r", "t")},
    )
    any_spec = pl.BlockSpec(memory_space=pl.ANY)
    vm_spec = pl.BlockSpec(memory_space=pltpu.VMEM)
    operands = (tok, tim, seg, n1g, n1b, wqkv.transpose(0, 2, 1), qvb, wout, outb, n2g, n2b)
    operands += (wup, upb, wdn, dnb, cot)
    result = pltpu.VMEM if near else jax.ShapeDtypeStruct
    out, ig, tg, f = pl.pallas_call(
        functools.partial(kernel, n_dp, near, (UA, UB, UC), tuple(scratch)),
        out_shape=(
            result((tokens, width), BF16),
            result((tokens, width), BF16),
            result((rows_n, width), F32),
            result((total, width), F32),
        ),
        in_specs=[any_spec] * 16,
        out_specs=(vm_spec if near else any_spec,) * 4,
        scratch_shapes=list(scratch.values()),
        compiler_params=pltpu.CompilerParams(
            collective_id=0, has_side_effects=True, vmem_limit_bytes=(52 if near else 63) * 2**20
        ),
        cost_estimate=pl.CostEstimate(flops=6 * 10**9, bytes_accessed=20 * 10**6, transcendentals=0),
    )(
        *[pltpu.with_memory_space_constraint(v, pltpu.HBM) for v in operands]
    )
    f32 = lambda *shape: jax.ShapeDtypeStruct(shape, F32)
    moved = (
        jax.ShapeDtypeStruct((tokens, width), BF16),
        jax.ShapeDtypeStruct((tokens, width), BF16),
        f32(rows_n, width),
        f32(3, loc, width),
        f32(loc, width),
        f32(width, ff),
        f32(ff, width),
    )
    results = pl.pallas_call(
        functools.partial(place, big, near),
        out_shape=moved + (f32(2, loc), f32(ff)) + (f32(width),) * 6,
        in_specs=[vm_spec if near else any_spec] * 4,
        out_specs=(any_spec,) * 15,
        scratch_shapes=[
            *([] if near else [vm((tokens, width), BF16), vm((tokens, width), BF16)]),
            *([] if near else [vm((rows_n, width), F32), vm((total, width), F32)]),
            vm((2, loc), F32),
            *[vm((width,), F32)] * 7,
            dma((4,)),
            dma((17,)),
        ],
        compiler_params=pltpu.CompilerParams(vmem_limit_bytes=(4 if near else 63) * 2**20),
    )(out, ig, tg, f)
    out, ig, tg, qkv, outw, up, down, qvb, upb, downb, n2g, n2b, outb, n1g, n1b = results
    return out, ig, tg, n1g, n1b, qkv.transpose(0, 2, 1), qvb, outw, outb, n2g, n2b, up, upb, down, downb


def place(big, near, *refs):
    results, outs = refs[:4], refs[4:19]
    held = results if near else refs[19:23]
    vq, *flat, sem, sem_o = refs[19 if near else 23 :]
    out_o, ig_o, tg_o, qkv, outw, up, down, qvb, upb, downb, n2g, n2b, outb, n1g, n1b = outs
    loc, ff = outw.shape[0], down.shape[0]
    half = down.shape[1] // 2
    if not near:
        loads = [pltpu.make_async_copy(a, b, sem.at[i]) for i, (a, b) in enumerate(zip(results, held))]
        for copy in loads:
            copy.start()
        for copy in loads:
            copy.wait()
    out, ig, tg, f = held
    moves = []
    row = 0
    for n, ref in ((ff, down), (ff, up), (loc, outw), (loc, qkv.at[0]), (loc, qkv.at[1]), (loc, qkv.at[2])):
        moves.append((f.at[pl.ds(row, n)], ref))
        row += n
    moves += [(out, out_o), (ig, ig_o), (tg, tg_o)]
    small = (downb, upb, n2g, n2b, outb, n1g, n1b)
    moves += [*zip(flat, small), (vq, qvb)]
    stores = [pltpu.make_async_copy(a, b, sem_o.at[i]) for i, (a, b) in enumerate(moves)]
    for copy in stores[:9]:
        copy.start()
    for i, ref in enumerate(flat):
        ref[...] = f[big + i : big + i + 1, :].reshape(ref.shape)
    vq[0:1, :] = f[big + 7 : big + 8, 0:loc]
    vq[1:2, :] = f[big + 7 : big + 8, half : half + loc]
    for copy in stores[9:]:
        copy.start()
    for copy in stores:
        copy.wait()


def solution(mesh):
    placed = (
        P("dp", None),
        P("dp", None),
        P("dp", None),
        P(),
        P(),
        P(None, None, "mp"),
        P(None, "mp"),
        P("mp", None),
        P(),
        P(),
        P(),
        P(None, "mp"),
        P("mp"),
        P("mp", None),
        P(),
        P("dp", None),
    )
    return jax.shard_map(
        functools.partial(shards, mesh.shape["dp"]),
        mesh=mesh,
        in_specs=placed,
        out_specs=(
            P("dp", None),
            P("dp", None),
            P("dp", None),
            P(),
            P(),
            P(None, None, "mp"),
            P(None, "mp"),
            P("mp", None),
            P(),
            P(),
            P(),
            P(None, "mp"),
            P("mp"),
            P("mp", None),
            P(),
        ),
        check_vma=False,
    )
```

```python
import functools

import jax
import jax.numpy as jnp
from jax import lax
from jax.experimental import pallas as pl
from jax.experimental.pallas import tpu as pltpu
from jax.sharding import PartitionSpec as P

HD = 64
SUB = 128
CH = 8
W_PIECES = 2
EACH = 3
S_FIRST = 30
SENDS = 4
MESH = pl.DeviceIdType.MESH
F32 = jnp.float32
BF16 = jnp.bfloat16


ARGS = ("tok", "tim", "seg", "n1g", "n1b", "wqkv", "qvb", "wout", "outb", "n2g", "n2b")
ARGS += ("wup", "upb", "wdn", "dnb", "cot")


def hop_ticks(line):
    return 2 if line <= 8 else 1


def when(cond, fn):
    pl.when(cond)(fn)


def rem(a, n):
    return lax.rem(a, jnp.int32(n))


def div(a, n):
    return lax.div(a, jnp.int32(n))


def two_power(n):
    return 1 << (n - 1).bit_length()


def nt(a, b):
    return lax.dot_general(a, b, (((1,), (1,)), ((), ())), preferred_element_type=F32)


def tn(a, b):
    return lax.dot_general(a, b, (((0,), (0,)), ((), ())), preferred_element_type=F32)


def nn(a, b):
    return jnp.dot(a, b, preferred_element_type=F32)


def normed(v):
    centred = v - jnp.mean(v, -1, keepdims=True)
    spread = jnp.mean(centred * centred, -1, keepdims=True)
    scale = lax.rsqrt(spread + 1e-05)
    return centred * scale, scale


def colsum(v):
    return jnp.sum(v, 0, keepdims=True)


def kernel(n_dp, near, units, names, *refs):
    out_o, ig_o, tg_o, f_out = refs[16:20]
    R = dict(zip(names, refs[20:]))
    order = ("tok", "tim", "n1g", "n1b", "wqkv", "qvb", "seg", "wout", "outb", "cot", "wdn")
    order += ("n2g", "n2b", "wup", "upb", "dnb")
    tok, tim, wqkv, qvb, seg, wout, cot, wdn, wup = (
        R[s] for s in ("tok", "tim", "wqkv", "qvb", "seg", "wout", "cot", "wdn", "wup")
    )
    loads = {
        name: pltpu.make_async_copy(refs[ARGS.index(name)], R[name], R["ins"].at[i]) for i, name in enumerate(order)
    }
    n1g, n1b, outb, n2g, n2b, upb, dnb = (R["vecs"].at[pl.ds(i, 1)] for i in range(7))
    timf, start, entry, q_s, k_s, v_s = (R[s] for s in ("timf", "start", "entry", "q", "k", "v"))
    probs, mixed_s, part, cr, ys, yr = (R[s] for s in ("probs", "mixed", "part", "cr", "ys", "yr"))
    tot, mid, e2, hp, act, gp = (R[s] for s in ("tot", "mid", "e2", "hp", "act", "gp"))
    out, ig, tg = (out_o, ig_o, tg_o) if near else (R[s] for s in ("out", "ig", "tg"))
    gact, gmid, gbr, lt, g = (R[s] for s in ("gact", "gmid", "gbr", "lt", "g"))
    f = f_out if near else R["f"]

    rows_n, seq = seg.shape
    width = tok.shape[1]
    half = width // 2
    loc = wout.shape[0]
    heads = loc // HD
    ff = wup.shape[1]
    UA, UB, UC = units
    L = n_dp // 2
    LAG = hop_ticks(L)
    H = L // 2
    dp = lax.axis_index("dp")
    mp = lax.axis_index("mp")
    core = mp % 2
    x = dp % 2
    z = dp // 2
    to_core = (dp, mp + 1 - 2 * core)
    to_y = (dp, (mp + 2) % 4)
    to_x = (dp + 1 - 2 * x, mp)
    last = jnp.minimum(z, L - 1 - z)
    side = div(z, H)
    cross = jnp.where(last == H - 1, 1, 0)
    to_in = ((z + 1 - 2 * side) * 2 + x, mp)
    to_out = (jnp.clip(z - 1 + 2 * side, 0, L - 1) * 2 + x, mp)
    zlo = jnp.maximum(z - 1, 0) * 2 + x
    zhi = jnp.minimum(z + 1, L - 1) * 2 + x

    barrier = pltpu.get_barrier_semaphore()
    for dev in (to_core, to_y, to_x):
        pl.semaphore_signal(barrier, 1, device_id=dev, device_id_type=MESH)
    when(z > 0, lambda: pl.semaphore_signal(barrier, 1, device_id=(zlo, mp), device_id_type=MESH))
    when(z < L - 1, lambda: pl.semaphore_signal(barrier, 1, device_id=(zhi, mp), device_id_type=MESH))
    greeted = 3 + jnp.minimum(z, 1) + jnp.minimum(L - 1 - z, 1)

    def sl(r, n=seq):
        return pl.ds(pl.multiple_of(r * n, n), n)

    def sub(r, i):
        return pl.ds(pl.multiple_of(r * seq + i * SUB, SUB), SUB)

    mine = pl.ds(pl.multiple_of(core * half, 128), half)
    other = pl.ds(pl.multiple_of((1 - core) * half, 128), half)

    def remote(src, dst, ssem, rsem, dev):
        return pltpu.make_async_remote_copy(
            src_ref=src, dst_ref=dst, send_sem=ssem, recv_sem=rsem, device_id=dev, device_id_type=MESH
        )

    def core_copy(p, r):
        return remote(part.at[sl(r), other], cr.at[sl(r)], R["cs"].at[r], R["crs"].at[r], to_core)

    def y_copy(p, r):
        return remote(ys.at[sl(r)], yr.at[p % 2, sl(r)], R["yss"].at[r], R["yrs"].at[p % 2, r], to_y)

    def ag_copy(p, r):
        return remote(tot.at[sl(r), mine], tot.at[sl(r), mine], R["gs"].at[r], R["grs"].at[r], to_core)

    def sum_b(p, r):
        core_copy(p, r).wait()
        ys[sl(r), :] = part[sl(r), mine] + cr[sl(r), :]
        y_copy(p, r).start()

    def sum_c(p, r):
        y_copy(p, r).wait()
        tot[sl(r), mine] = ys[sl(r), :] + yr[p % 2, sl(r), :]
        ag_copy(p, r).start()

    def sum_d(p, r):
        ag_copy(p, r).wait()

    def vec(ref):
        return ref[...]

    small = 2 * ff + 4 * loc

    def small_add(i, v):
        g[small + i : small + i + 1, :] += v

    lane = lax.broadcasted_iota(jnp.int32, (1, loc), 1)
    masks = [((lane >= h * HD) & (lane < (h + 1) * HD)).astype(F32) for h in range(heads)]

    def by_head(v):
        return jnp.concatenate([v * m.astype(BF16) for m in masks], 0)

    def from_heads(v):
        total = v[:seq] * masks[0]
        for h in range(1, heads):
            total = total + v[h * seq : (h + 1) * seq] * masks[h]
        return total

    def norm1(r):
        @pl.loop(0, seq // SUB)
        def _(i):
            s = sub(r, i)
            v = tok[s, :].astype(F32) + timf[pl.ds(r, 1), :]
            start[s, :] = v
            xhat, _ = normed(v)
            entry[s, :] = (xhat * n1g[...] + n1b[...]).astype(BF16)

    def project(r):
        e = entry[sl(r), :]
        q_s[sl(r), :] = (nt(e, wqkv[0]) + qvb[0:1, :]).astype(BF16)
        k_s[sl(r), :] = nt(e, wqkv[1]).astype(BF16)
        v_s[sl(r), :] = (nt(e, wqkv[2]) + qvb[1:2, :]).astype(BF16)

    def attend(r):
        labels = jnp.broadcast_to(seg[pl.ds(r, 1), :], (seq, seq))
        same = labels == labels.T
        same = jnp.concatenate([same.astype(F32)] * heads, 0) > 0.5
        scores = nt(by_head(q_s[sl(r), :]), k_s[sl(r), :]) * HD ** (-0.5)
        scores = jnp.where(same, scores, -1e30)
        w = jnp.exp(scores - jnp.max(scores, -1, keepdims=True))
        pr = w / jnp.sum(w, -1, keepdims=True)
        probs[sl(r, heads * seq), :] = pr
        mixed = from_heads(nn(pr.astype(BF16), v_s[sl(r), :])).astype(BF16)
        mixed_s[sl(r), :] = mixed
        turned = mixed.T
        lt[2 * ff : 2 * ff + loc, sl(r)] = turned
        mixa[mp, r] = turned.astype(F32)
        m_core(r).start()
        m_y(r).start()

    wf, wall, mixa = R["wf"], R["wall"], R["mixa"]
    mp_y, mp_c = rem(mp + 2, 4), mp + 1 - 2 * core
    mine_0, other_0 = mp - core, mp_y - core
    hl = loc // 4
    pr_n = hl // W_PIECES
    zz = rem(z, 2)
    quarter = zz * 2 + x
    to_zz = ((z + 1 - 2 * zz) * 2 + x, mp)

    def w_core():
        return remote(wf.at[mp], wf.at[mp], R["wcs"], R["wcr"], to_core)

    def w_rows(start, n):
        return pl.ds(pl.multiple_of(start, CH), n)

    def w_y(i):
        s = w_rows(quarter * hl + i * pr_n, pr_n)
        return remote(wf.at[mp, s], wf.at[mp, s], R["wys"].at[i], R["wyr"].at[i], to_y)

    def w_x(i):
        s = w_rows(quarter * hl + i * pr_n, pr_n)
        return remote(wf.at[mp_y, s], wf.at[mp_y, s], R["wxs"].at[i], R["wxr"].at[i], to_x)

    def w_z(k, i):
        s = w_rows((zz * 2 + (x + k - 2 * x * k)) * hl + i * pr_n, pr_n)
        j = k * W_PIECES + i
        return remote(wf.at[mp_y, s], wf.at[mp_y, s], R["wzs"].at[j], R["wzr"].at[j], to_zz)

    def w_share(h):
        s = w_rows((zz + h - 2 * zz * h) * 2 * hl, 2 * hl)
        return remote(wf.at[mp_y, s], wf.at[mp_y, s], R["whs"].at[h], R["whr"].at[h], to_core)

    def m_core(r):
        return remote(mixa.at[mp, r], mixa.at[mp, r], R["cs"].at[r], R["crs"].at[r], to_core)

    def m_y(r):
        return remote(mixa.at[mp, r], mixa.at[mp, r], R["yss"].at[r], R["yrs"].at[0, r], to_y)

    def m_share(r):
        return remote(mixa.at[mp_y, r], mixa.at[mp_y, r], R["gs"].at[r], R["grs"].at[r], to_core)

    def weights_out():
        loads["wout"].wait()
        wf[mp] = wout[...].astype(F32)
        pl.semaphore_wait(barrier, greeted)
        for i in range(W_PIECES):
            w_y(i).start()
        w_core().start()

    def weights_on(i):
        w_y(i).wait()
        w_x(i).start()
        w_z(0, i).start()

    def pair_sum(m, r):
        return tn(mixa[m, r].astype(BF16), wall[m]) + tn(mixa[m + 1, r].astype(BF16), wall[m + 1])

    def near_part(r):
        m_core(r).wait()
        part[sl(r), :] = pair_sum(mine_0, r)

    def across(r):
        m_y(r).wait()
        m_share(r).start()

    def far_part(r):
        m_share(r).wait()
        tot[sl(r), :] = part[sl(r), :] + pair_sum(other_0, r)

    def grad_act(r):
        c = cot[sl(r), :]
        gact[sl(r), :] = nt(c, wdn[...])
        small_add(0, colsum(c.astype(F32)))

    def feed(k):
        both = sl(k, 2 * seq)
        for i in range(2):
            s = sl(k * 2 + i)
            v = start[s, :] + (tot[s, :] + outb[...])
            mid[s, :] = v
            xhat, _ = normed(v)
            e2[s, :] = (xhat * n2g[...] + n2b[...]).astype(BF16)

        hp[...] = nn(e2[both, :], wup[...])

        for i in range(2):
            s = sl(k * 2 + i)
            u = hp[i * seq : (i + 1) * seq, :] + upb[...]
            cdf = 0.5 * (1.0 + lax.erf(u * 0.7071067811865476))
            act[s, :] = (u * cdf).astype(BF16)
            slope = cdf + u * (0.3989422804014327 * jnp.exp(-0.5 * u * u))
            pre = (gact[s, :] * slope).astype(BF16)
            gp[s, :] = pre
            small_add(1, colsum(pre.astype(F32)))

        lt[0:ff, both] = act[both, :].T

    def feed_on(r):
        part[sl(r), :] = nt(gp[sl(r), :], wup[...])
        core_copy(1, r).start()
        lt[ff : 2 * ff, sl(r)] = e2[sl(r), :].T

    def back2(r):
        @pl.loop(0, seq // SUB)
        def _(i):
            s = sub(r, i)
            ge = tot[s, :]
            xhat, scale = normed(mid[s, :])
            small_add(2, colsum(ge * xhat))
            small_add(3, colsum(ge))
            gx = ge * n2g[...]
            gm = cot[s, :].astype(F32) + scale * (
                gx - jnp.mean(gx, -1, keepdims=True) - xhat * jnp.mean(gx * xhat, -1, keepdims=True)
            )
            gmid[s, :] = gm
            low = gm.astype(BF16)
            gbr[s, :] = low
            small_add(4, colsum(low.astype(F32)))

        g3 = by_head(nt(gbr[sl(r), :], wout[...]).astype(BF16))
        pr = probs[sl(r, heads * seq), :]
        grad_probs = nt(g3, v_s[sl(r), :])
        inner = jnp.sum(pr * grad_probs, -1, keepdims=True)
        ds = (pr * (grad_probs - inner)).astype(BF16)
        gq = (from_heads(nn(ds, k_s[sl(r), :])) * HD ** (-0.5)).astype(BF16)
        gk = (tn(ds, by_head(q_s[sl(r), :])) * HD ** (-0.5)).astype(BF16)
        gv = tn(pr.astype(BF16), g3).astype(BF16)
        part[sl(r), :] = nn(gq, wqkv[0]) + nn(gk, wqkv[1]) + nn(gv, wqkv[2])
        core_copy(2, r).start()
        late = 2 * ff + loc
        for i, v in enumerate((gq, gk, gv)):
            lt[late + i * loc : late + (i + 1) * loc, sl(r)] = v.T
        g[small + 7 : small + 8, 0:loc] += colsum(gq.astype(F32))
        g[small + 7 : small + 8, half : half + loc] += colsum(gv.astype(F32))

    def back1(r):
        tg[pl.ds(r, 1), :] = jnp.zeros((1, width), F32)

        @pl.loop(0, seq // SUB)
        def _(i):
            s = sub(r, i)
            ge = tot[s, :]
            xhat, scale = normed(start[s, :])
            small_add(5, colsum(ge * xhat))
            small_add(6, colsum(ge))
            gy = ge * n1g[...]
            gs = gmid[s, :] + scale * (
                gy - jnp.mean(gy, -1, keepdims=True) - xhat * jnp.mean(gy * xhat, -1, keepdims=True)
            )
            ig[s, :] = gs.astype(BF16)
            tg[pl.ds(r, 1), :] += colsum(gs)

    def down(r):
        part[sl(r), :] = nn(act[sl(r), :], wdn[...])
        core_copy(3, r).start()

    def finish(r):
        @pl.loop(0, seq // SUB)
        def _(i):
            s = sub(r, i)
            out[s, :] = (mid[s, :] + (tot[s, :] + dnb[...])).astype(BF16)

    blk = loc

    early = ff // blk

    def weight_grads(j):
        s = pl.ds(pl.multiple_of(j * blk, blk), blk)

        def by(right):
            def fn():
                g[s, :] = nn(lt[s, :], right[...])

            return fn

        when(j < early, by(cot))
        when((j >= early) & (j < 2 * early), by(gp))
        when(j == 2 * early, by(gbr))
        when(j > 2 * early, by(entry))

    def go(copy, u, depth):
        when(u >= depth, lambda: copy(u - depth).wait_send())
        copy(u).start()

    def end(copy, n, depth):
        for u in range(n - min(depth, n), n):
            copy(u).wait_send()

    AF = LAG

    def base_of(u):
        return u * 4 * CH

    def later(u):
        return base_of(div(u, EACH) * (EACH + 2) + rem(u, EACH))

    def b_base(u, i):
        return base_of(jnp.minimum(u * (EACH + 2) + EACH + i, UA + UB + UC - 1))

    def a_base(u, owner):
        return later(u) + owner * 2 * CH

    def x_slot(u):
        return pl.ds(pl.multiple_of(rem(u, R["xr"].shape[0]) * 2 * CH, CH), 2 * CH)

    def x_first(u):
        src = pl.ds(pl.multiple_of(later(u) + (1 - x) * 2 * CH, CH), 2 * CH)
        return remote(
            g.at[src], R["xrb"].at[x_slot(u)], R["xs"].at[rem(u, SENDS)], R["xr"].at[rem(u, R["xr"].shape[0])], to_x
        )

    def rows_at(base, n):
        return pl.ds(pl.multiple_of(base, CH), n)

    class Line:
        def __init__(self, kind, n, first, stride, depth):
            self.kind, self.n, self.first, self.stride, self.depth = kind, n, first, stride, depth

        def unit(self, t, offset):
            rel = t - self.first - offset
            if self.stride == 1:
                return rel, (rel >= 0) & (rel < self.n)
            return div(rel, self.stride), (rel >= 0) & (rel < self.n * self.stride) & (rem(rel, self.stride) == 0)

        def sem(self, name, i, u):
            ref = R[self.kind + "_" + name]
            return ref.at[i, rem(u, ref.shape[1])]

        def slot(self, u, rows):
            return rows_at(rem(u, R[self.kind + "_r"].shape[1]) * rows, rows)

        def go(self, copy, u):
            go(copy, u, self.depth)

        def end(self, copy):
            end(copy, self.n, self.depth)

    class A(Line):
        def own(self, u):
            return rows_at(a_base(u, x), 2 * CH)

        def inward(self, u):
            dst = R["abuf"].at[cross, self.slot(u, 2 * CH)]
            return remote(g.at[self.own(u)], dst, self.sem("s", 0, u), self.sem("r", cross, u), to_in)

        def arrived(self, u, i):
            buf = R["abuf"].at[i, self.slot(u, 2 * CH)]
            remote(buf, buf, self.sem("s", 0, u), self.sem("r", i, u), to_in).wait_recv()
            return buf

        def outward(self, u):
            own = self.own(u)
            return remote(f.at[own], f.at[own], self.sem("u", 0, u), self.sem("r", 1, u), to_out)

        def x_last(self, u):
            own = self.own(u)
            return remote(f.at[own], f.at[own], self.sem("xs", 0, u), self.sem("xr", 0, u), to_x)

        def tick(self, t):
            u, valid_u = self.unit(t, last * LAG)

            def reduce():
                def add():
                    g[self.own(u), :] += self.arrived(u, 0)[...]

                if H > 1:
                    when(last > 0, add)
                self.go(self.inward, u)

            when(valid_u, reduce)
            v, valid_v = self.unit(t, (2 * H - 1 - last) * LAG)

            def finish():
                def turn():
                    f[self.own(v), :] = g[self.own(v), :] + self.arrived(v, 1)[...]

                when(last == H - 1, turn)
                if H > 1:
                    when(last < H - 1, lambda: self.outward(v).wait_recv())
                    when(last > 0, lambda: self.go(self.outward, v))
                self.go(self.x_last, v)

            when(valid_v, finish)
            e, valid_e = self.unit(t, (2 * H - last) * LAG)
            when(valid_e, lambda: self.x_last(e).wait_recv())

        def drain(self):
            self.end(self.inward)
            self.end(self.x_last)
            if H > 1:
                when(last > 0, lambda: self.end(self.outward))

    class B(Line):
        def all(self, u):
            return rows_at(b_base(u, 0), 4 * CH)

        def half(self, u, i):
            return rows_at(b_base(u, 0) + i * 2 * CH, 2 * CH)

        def inward(self, u):
            dst = R["bbuf"].at[self.slot(u, 4 * CH)]
            return remote(g.at[self.all(u)], dst, self.sem("s", 0, u), self.sem("r", 0, u), to_in)

        def swap(self, u):
            dst = R["bsw"].at[self.slot(u, 2 * CH)]
            return remote(g.at[self.half(u, 1 - side)], dst, self.sem("s", 0, u), self.sem("r", 1, u), to_in)

        def x_copy(self, u):
            dst = R["bxb"].at[self.slot(u, 2 * CH)]
            return remote(g.at[self.half(u, side)], dst, self.sem("xs", 0, u), self.sem("xr", 0, u), to_x)

        def back(self, u):
            own = self.half(u, side)
            return remote(f.at[own], f.at[own], self.sem("d", 0, u), self.sem("r", 2, u), to_in)

        def outward(self, u):
            own = self.all(u)
            return remote(f.at[own], f.at[own], self.sem("u", 0, u), self.sem("r", 1, u), to_out)

        def tick(self, t):
            u, valid_u = self.unit(t, last * LAG)

            def reduce():
                def add():
                    self.inward(u).wait_recv()
                    g[self.all(u), :] += R["bbuf"][self.slot(u, 4 * CH), :]

                if H > 1:
                    when(last > 0, add)
                    when(last < H - 1, lambda: self.go(self.inward, u))
                when(last == H - 1, lambda: self.go(self.swap, u))

            when(valid_u, reduce)
            middle = last == H - 1
            i, valid_i = self.unit(t, H * LAG)

            def over():
                self.swap(i).wait_recv()
                g[self.half(i, side), :] += R["bsw"][self.slot(i, 2 * CH), :]
                self.go(self.x_copy, i)

            when(valid_i & middle, over)
            j, valid_j = self.unit(t, (H + 1) * LAG)

            def total():
                self.x_copy(j).wait_recv()
                own = self.half(j, side)
                f[own, :] = g[own, :] + R["bxb"][self.slot(j, 2 * CH), :]
                self.go(self.back, j)

            when(valid_j & middle, total)
            v, valid_v = self.unit(t, (2 * H + 1 - last) * LAG)

            def finish():
                when(middle, lambda: self.back(v).wait_recv())
                if H > 1:
                    when(last < H - 1, lambda: self.outward(v).wait_recv())
                    when(last > 0, lambda: self.go(self.outward, v))

            when(valid_v, finish)

        def drain(self):
            def ends():
                for copy in (self.swap, self.x_copy, self.back):
                    self.end(copy)

            when(last == H - 1, ends)
            if H > 1:
                when(last < H - 1, lambda: self.end(self.inward))
                when(last > 0, lambda: self.end(self.outward))

    class C(Line):
        dirs, rows = (0, 1), 2 * CH

        def own(self, u, d):
            return rows_at(b_base(u, 1) + d * 2 * CH, 2 * CH)

        def place(self, d):
            w = z if d == 0 else L - 1 - z
            return w, (zhi if d == 0 else zlo, mp), (zlo if d == 0 else zhi, mp)

        def copies(self, d):
            w, up, dn = self.place(d)
            own = lambda u: self.own(u, d)
            slot = lambda u: self.slot(u, self.rows)

            def send(u):
                return remote(g.at[own(u)], R[self.kind + "buf"].at[d, slot(u)], self.sem("s", d, u), self.sem("r", d, u), dn)

            def x_copy(u):
                return remote(g.at[own(u)], R[self.kind + "xb"].at[d, slot(u)], self.sem("s", d, u), self.sem("t", d, u), to_x)

            def spread(u):
                return remote(f.at[own(u)], f.at[own(u)], self.sem("u", d, u), self.sem("t", d, u), up)

            return w, send, x_copy, spread

        def tick(self, t):
            for d in self.dirs:
                w, send, x_copy, spread = self.copies(d)
                u, valid_u = self.unit(t, (L - 1 - w) * LAG)

                def reduce():
                    def add():
                        send(u).wait_recv()
                        g[self.own(u, d), :] += R[self.kind + "buf"][d, self.slot(u, self.rows), :]

                    when(w < L - 1, add)
                    when(w > 0, lambda: self.go(send, u))
                    when(w == 0, lambda: self.go(x_copy, u))

                when(valid_u, reduce)
                v, valid_v = self.unit(t, (L + w) * LAG)

                def finish():
                    def turn():
                        x_copy(v).wait_recv()
                        own = self.own(v, d)
                        f[own, :] = g[own, :] + R[self.kind + "xb"][d, self.slot(v, self.rows), :]

                    when(w == 0, turn)
                    when(w > 0, lambda: spread(v).wait_recv())
                    when(w < L - 1, lambda: self.go(spread, v))

                when(valid_v, finish)

        def drain(self):
            for d in self.dirs:
                w, send, x_copy, spread = self.copies(d)
                when(w > 0, lambda: self.end(send))
                when(w == 0, lambda: self.end(x_copy))
                when(w < L - 1, lambda: self.end(spread))

    class S(C):
        dirs, rows = (0,), CH

        def own(self, u, d):
            return pl.ds(small, CH)

    lines = [C("c", UC, 0, EACH, 2), A("a", UA, AF, 1, SENDS), B("b", UB, 1, EACH, 2), S("e", 1, S_FIRST, 1, 1)]

    def dp_tick(t):
        when(t < UA, lambda: go(x_first, t, SENDS))
        v = t - AF

        def x_add():
            x_first(v).wait_recv()
            s = rows_at(a_base(v, x), 2 * CH)
            g[s, :] += R["xrb"][x_slot(v), :]

        when((v >= 0) & (v < UA), x_add)
        for line in lines:
            line.tick(t)

    def dp_drain():
        end(x_first, UA, SENDS)
        for line in lines:
            line.drain()

    for copy in loads.values():
        copy.start()

    def vector(i, name):
        loads[name].wait()
        R["vecs"][i : i + 1, :] = R[name][...][None, :]

    g[small : small + CH, :] = jnp.zeros((CH, width), F32)
    for name in ("tok", "tim"):
        loads[name].wait()
    timf[...] = tim[...].astype(F32)
    vector(0, "n1g")
    vector(1, "n1b")

    @pl.loop(0, rows_n)
    def _(r):
        norm1(r)

        @pl.when(r == 0)
        def _():
            for name in ("wqkv", "qvb", "seg"):
                loads[name].wait()

        project(r)
        when(r == 0, weights_out)
        attend(r)
        for i in range(W_PIECES):
            when(r == rows_n - W_PIECES - 1 + i, lambda: weights_on(i))

    for name in ("cot", "wdn", "wup"):
        loads[name].wait()
    for i, name in enumerate(("outb", "n2g", "n2b", "upb", "dnb")):
        vector(2 + i, name)
    w_x(0).wait()
    w_z(1, 0).start()
    w_core().wait()
    for i in range(2):
        wall[mine_0 + i] = wf[mine_0 + i].astype(BF16)
    pl.loop(0, rows_n // 2)(near_part)
    for i in range(1, W_PIECES):
        w_x(i).wait()
        w_z(1, i).start()
    w_share(0).start()
    pl.loop(0, rows_n)(grad_act)
    pl.loop(rows_n // 2, rows_n)(near_part)
    pl.loop(0, rows_n - 1)(across)
    for k in range(2):
        for i in range(W_PIECES):
            w_z(k, i).wait()
    w_share(1).start()
    across(rows_n - 1)
    for h in range(2):
        w_share(h).wait()
    for i in range(2):
        wall[other_0 + i] = wf[other_0 + i].astype(BF16)

    @pl.loop(0, rows_n // 2)
    def _(k):
        for i in range(2):
            far_part(k * 2 + i)
        feed(k)

    weight_grads(jnp.int32(0))

    blocks = (2 * ff + 4 * loc) // blk
    a_last = AF + LAG * 2 * H
    b_last, c_last = 1 + LAG * (2 * H + 1), LAG * (2 * L - 1)
    ends = [S_FIRST + c_last]
    for u in range(UA + UB + UC):
        i, k = u // (EACH + 2), u % (EACH + 2)
        if k < EACH and u < UA + UB + UC - (UB > UC):
            ends.append(i * EACH + k + a_last)
        else:
            ends.append(i * EACH + c_last if k > EACH else (UB - 1 if k < EACH else i) * EACH + b_last)
    ticks = max(ends) + 1
    per = blk // (4 * CH)

    def done(j):
        return ends[0] if j == blocks else max(ends[1 + j * per : 1 + (j + 1) * per])

    def out_copy(j):
        s = pl.ds(j * blk, blk if j < blocks else CH)
        return pltpu.make_async_copy(f.at[s], f_out.at[s], R["fin"].at[j])

    done_copies = [] if near else [
        pltpu.make_async_copy(a, b, R["fin"].at[blocks + 1 + i])
        for i, (a, b) in enumerate(((ig, ig_o), (tg, tg_o), (out, out_o)))
    ]

    @pl.loop(0, ticks)
    def _(t):
        dp_tick(t)

        def at(first, step, fn):
            r = (t - first) // step
            when((t >= first) & ((t - first) % step == 0) & (r < rows_n), lambda: fn(r))

        at(2, 2, lambda r: sum_b(1, r))
        at(1, 2, feed_on)
        at(5, 3, lambda r: sum_c(1, r))

        def second(r):
            sum_d(1, r)
            back2(r)

        at(7, 3, second)
        at(9, 3, lambda r: sum_b(2, r))
        at(15, 3, lambda r: sum_c(2, r))

        def third(r):
            sum_d(2, r)
            back1(r)

        at(17, 3, third)
        at(18, 3, down)
        at(20, 3, lambda r: sum_b(3, r))
        at(26, 3, lambda r: sum_c(3, r))

        def fourth(r):
            sum_d(3, r)
            finish(r)

        at(28, 3, fourth)

        @pl.when(t == 28 + 3 * rows_n)
        def _():
            for copy in done_copies:
                copy.start()

        when((rem(t, 3) == 1) & (t < 3 * blocks - 2), lambda: weight_grads(div(t + 2, 3)))
        for j in range(0 if near else blocks + 1):
            if done(j) < ticks - 1:
                when(t == done(j), lambda: out_copy(j).start())

    dp_drain()
    left = 0 if near else blocks + 1
    for j in range(left):
        if done(j) >= ticks - 1:
            out_copy(j).start()
    for copy in done_copies + [out_copy(j) for j in range(left)]:
        copy.wait()


def shards(n_dp, *args):
    (tok, tim, seg, n1g, n1b, wqkv, qvb, wout, outb, n2g, n2b, wup, upb, wdn, dnb, cot) = args
    tokens, width = tok.shape
    rows_n, seq = seg.shape
    loc, ff = wout.shape[0], wup.shape[1]
    heads = loc // HD
    half = width // 2
    big = 2 * ff + 4 * loc
    count = big // (4 * CH)
    UC = count // (EACH + 2)
    UB = UC + min(count % (EACH + 2) // 2, 1)
    UA = count - UB - UC
    L = n_dp // 2
    LAG = hop_ticks(L)
    near = L <= 8
    vm = pltpu.VMEM
    dma = pltpu.SemaphoreType.DMA
    W = two_power(max(LAG * (L - 1) + 1, 2 * LAG + 2))
    WB = two_power(LAG * (L + 1) // EACH + 1)
    WC = two_power(LAG * (2 * L - 1) // EACH + 1)
    total = big + CH
    flat = lambda n: vm((n,), F32)
    scratch = dict(
        tok=vm((tokens, width), BF16),
        cot=vm((tokens, width), BF16),
        wqkv=vm((3, loc, width), BF16),
        wout=vm((loc, width), BF16),
        wup=vm((width, ff), BF16),
        wdn=vm((ff, width), BF16),
        ins=dma((16,)),
        tim=vm((rows_n, width), BF16),
        seg=vm((rows_n, seq), jnp.int32),
        qvb=vm((2, loc), F32),
        **{s: flat(width) for s in ("n1g", "n1b", "outb", "n2g", "n2b", "dnb")},
        upb=flat(ff),
        vecs=vm((8, width), F32),
        timf=vm((rows_n, width), F32),
        start=vm((tokens, width), F32),
        entry=vm((tokens, width), BF16),
        q=vm((tokens, loc), BF16),
        k=vm((tokens, loc), BF16),
        v=vm((tokens, loc), BF16),
        probs=vm((heads * tokens, seq), F32),
        mixed=vm((tokens, loc), BF16),
        part=vm((tokens, width), F32),
        cr=vm((tokens, half), F32),
        ys=vm((tokens, half), F32),
        yr=vm((2, tokens, half), F32),
        tot=vm((tokens, width), F32),
        mid=vm((tokens, width), F32),
        e2=vm((tokens, width), BF16),
        hp=vm((2 * seq, ff), F32),
        act=vm((tokens, ff), BF16),
        gp=vm((tokens, ff), BF16),
        gact=vm((tokens, ff), F32),
        gmid=vm((tokens, width), F32),
        gbr=vm((tokens, width), BF16),
        **{n: vm((tokens, width), BF16) for n in (() if near else ("out", "ig"))},
        **({} if near else dict(tg=vm((rows_n, width), F32))),
        lt=vm((big, tokens), BF16),
        g=vm((total, width), F32),
        **({} if near else dict(f=vm((total, width), F32))),
        xrb=vm((W * 2 * CH, width), F32),
        abuf=vm((2, W * 2 * CH, width), F32),
        bbuf=vm((WB * 4 * CH, width), F32),
        bsw=vm((WB * 2 * CH, width), F32),
        bxb=vm((WB * 2 * CH, width), F32),
        cbuf=vm((2, WC * 2 * CH, width), F32),
        cxb=vm((2, WC * 2 * CH, width), F32),
        ebuf=vm((1, CH, width), F32),
        exb=vm((1, CH, width), F32),
        **{"e_" + s: dma((1, 1)) for s in ("s", "u", "r", "t")},
        wf=vm((4, loc, width), F32),
        wall=vm((4, loc, width), BF16),
        mixa=vm((4, rows_n, loc, seq), F32),
        wcs=dma,
        wcr=dma,
        **{s: dma((W_PIECES,)) for s in ("wys", "wyr", "wxs", "wxr")},
        **{s: dma((2 * W_PIECES,)) for s in ("wzs", "wzr")},
        **{s: dma((2,)) for s in ("whs", "whr")},
        **{s: dma((rows_n,)) for s in ("cs", "crs", "yss", "gs", "grs")},
        yrs=dma((2, rows_n)),
        **({} if near else dict(fin=dma((big // loc + 4,)))),
        xs=dma((SENDS,)),
        xr=dma((W,)),
        **{"a_" + s: dma((1, SENDS)) for s in ("s", "u", "xs")},
        a_r=dma((2, W)),
        a_xr=dma((1, W)),
        **{"b_" + s: dma((1, 2)) for s in ("s", "u", "d", "xs")},
        b_r=dma((3, WB)),
        b_xr=dma((1, WB)),
        **{"c_" + s: dma((2, 2)) for s in ("s", "u")},
        **{"c_" + s: dma((2, WC)) for s in ("r", "t")},
    )
    any_spec = pl.BlockSpec(memory_space=pl.ANY)
    vm_spec = pl.BlockSpec(memory_space=pltpu.VMEM)
    operands = (tok, tim, seg, n1g, n1b, wqkv.transpose(0, 2, 1), qvb, wout, outb, n2g, n2b)
    operands += (wup, upb, wdn, dnb, cot)
    result = pltpu.VMEM if near else jax.ShapeDtypeStruct
    out, ig, tg, f = pl.pallas_call(
        functools.partial(kernel, n_dp, near, (UA, UB, UC), tuple(scratch)),
        out_shape=(
            result((tokens, width), BF16),
            result((tokens, width), BF16),
            result((rows_n, width), F32),
            result((total, width), F32),
        ),
        in_specs=[any_spec] * 16,
        out_specs=(vm_spec if near else any_spec,) * 4,
        scratch_shapes=list(scratch.values()),
        compiler_params=pltpu.CompilerParams(
            collective_id=0, has_side_effects=True, vmem_limit_bytes=(52 if near else 63) * 2**20
        ),
        cost_estimate=pl.CostEstimate(flops=6 * 10**9, bytes_accessed=20 * 10**6, transcendentals=0),
    )(
        *[pltpu.with_memory_space_constraint(v, pltpu.HBM) for v in operands]
    )
    f32 = lambda *shape: jax.ShapeDtypeStruct(shape, F32)
    moved = (
        jax.ShapeDtypeStruct((tokens, width), BF16),
        jax.ShapeDtypeStruct((tokens, width), BF16),
        f32(rows_n, width),
        f32(3, loc, width),
        f32(loc, width),
        f32(width, ff),
        f32(ff, width),
    )
    results = pl.pallas_call(
        functools.partial(place, big, near),
        out_shape=moved + (f32(2, loc), f32(ff)) + (f32(width),) * 6,
        in_specs=[vm_spec if near else any_spec] * 4,
        out_specs=(any_spec,) * 15,
        scratch_shapes=[
            *([] if near else [vm((tokens, width), BF16), vm((tokens, width), BF16)]),
            *([] if near else [vm((rows_n, width), F32), vm((total, width), F32)]),
            vm((2, loc), F32),
            *[vm((width,), F32)] * 7,
            dma((4,)),
            dma((17,)),
        ],
        compiler_params=pltpu.CompilerParams(vmem_limit_bytes=(4 if near else 63) * 2**20),
    )(out, ig, tg, f)
    out, ig, tg, qkv, outw, up, down, qvb, upb, downb, n2g, n2b, outb, n1g, n1b = results
    return out, ig, tg, n1g, n1b, qkv.transpose(0, 2, 1), qvb, outw, outb, n2g, n2b, up, upb, down, downb


def place(big, near, *refs):
    results, outs = refs[:4], refs[4:19]
    held = results if near else refs[19:23]
    vq, *flat, sem, sem_o = refs[19 if near else 23 :]
    out_o, ig_o, tg_o, qkv, outw, up, down, qvb, upb, downb, n2g, n2b, outb, n1g, n1b = outs
    loc, ff = outw.shape[0], down.shape[0]
    half = down.shape[1] // 2
    if not near:
        loads = [pltpu.make_async_copy(a, b, sem.at[i]) for i, (a, b) in enumerate(zip(results, held))]
        for copy in loads:
            copy.start()
        for copy in loads:
            copy.wait()
    out, ig, tg, f = held
    moves = []
    row = 0
    for n, ref in ((ff, down), (ff, up), (loc, outw), (loc, qkv.at[0]), (loc, qkv.at[1]), (loc, qkv.at[2])):
        moves.append((f.at[pl.ds(row, n)], ref))
        row += n
    moves += [(out, out_o), (ig, ig_o), (tg, tg_o)]
    small = (downb, upb, n2g, n2b, outb, n1g, n1b)
    moves += [*zip(flat, small), (vq, qvb)]
    stores = [pltpu.make_async_copy(a, b, sem_o.at[i]) for i, (a, b) in enumerate(moves)]
    for copy in stores[:9]:
        copy.start()
    for i, ref in enumerate(flat):
        ref[...] = f[big + i : big + i + 1, :].reshape(ref.shape)
    vq[0:1, :] = f[big + 7 : big + 8, 0:loc]
    vq[1:2, :] = f[big + 7 : big + 8, half : half + loc]
    for copy in stores[9:]:
        copy.start()
    for copy in stores:
        copy.wait()


def solution(mesh):
    placed = (
        P("dp", None),
        P("dp", None),
        P("dp", None),
        P(),
        P(),
        P(None, None, "mp"),
        P(None, "mp"),
        P("mp", None),
        P(),
        P(),
        P(),
        P(None, "mp"),
        P("mp"),
        P("mp", None),
        P(),
        P("dp", None),
    )
    return jax.shard_map(
        functools.partial(shards, mesh.shape["dp"]),
        mesh=mesh,
        in_specs=placed,
        out_specs=(
            P("dp", None),
            P("dp", None),
            P("dp", None),
            P(),
            P(),
            P(None, None, "mp"),
            P(None, "mp"),
            P("mp", None),
            P(),
            P(),
            P(),
            P(None, "mp"),
            P("mp"),
            P("mp", None),
            P(),
        ),
        check_vma=False,
    )
```

```python
import functools

import jax
import jax.numpy as jnp
from jax import lax
from jax.experimental import pallas as pl
from jax.experimental.pallas import tpu as pltpu
from jax.sharding import PartitionSpec as P

HD = 64
SUB = 128
CH = 8
W_PIECES = 2
EACH = 3
S_FIRST = 30
SENDS = 4
MESH = pl.DeviceIdType.MESH
F32 = jnp.float32
BF16 = jnp.bfloat16


ARGS = ("tok", "tim", "seg", "n1g", "n1b", "wqkv", "qvb", "wout", "outb", "n2g", "n2b")
ARGS += ("wup", "upb", "wdn", "dnb", "cot")


def hop_ticks(line):
    return 2 if line <= 8 else 1


def when(cond, fn):
    pl.when(cond)(fn)


def rem(a, n):
    return lax.rem(a, jnp.int32(n))


def div(a, n):
    return lax.div(a, jnp.int32(n))


def two_power(n):
    return 1 << (n - 1).bit_length()


def nt(a, b):
    return lax.dot_general(a, b, (((1,), (1,)), ((), ())), preferred_element_type=F32)


def tn(a, b):
    return lax.dot_general(a, b, (((0,), (0,)), ((), ())), preferred_element_type=F32)


def nn(a, b):
    return jnp.dot(a, b, preferred_element_type=F32)


def normed(v):
    centred = v - jnp.mean(v, -1, keepdims=True)
    spread = jnp.mean(centred * centred, -1, keepdims=True)
    scale = lax.rsqrt(spread + 1e-05)
    return centred * scale, scale


def colsum(v):
    return jnp.sum(v, 0, keepdims=True)


def kernel(n_dp, near, units, names, *refs):
    out_o, ig_o, tg_o, f_out = refs[16:20]
    R = dict(zip(names, refs[20:]))
    order = ("tok", "tim", "n1g", "n1b", "wqkv", "qvb", "seg", "wout", "outb", "cot", "wdn")
    order += ("n2g", "n2b", "wup", "upb", "dnb")
    tok, tim, wqkv, qvb, seg, wout, cot, wdn, wup = (
        R[s] for s in ("tok", "tim", "wqkv", "qvb", "seg", "wout", "cot", "wdn", "wup")
    )
    loads = {
        name: pltpu.make_async_copy(refs[ARGS.index(name)], R[name], R["ins"].at[i]) for i, name in enumerate(order)
    }
    n1g, n1b, outb, n2g, n2b, upb, dnb = (R["vecs"].at[pl.ds(i, 1)] for i in range(7))
    timf, start, entry, q_s, k_s, v_s = (R[s] for s in ("timf", "start", "entry", "q", "k", "v"))
    probs, mixed_s, part, cr, ys, yr = (R[s] for s in ("probs", "mixed", "part", "cr", "ys", "yr"))
    tot, mid, e2, hp, act, gp = (R[s] for s in ("tot", "mid", "e2", "hp", "act", "gp"))
    out, ig, tg = (out_o, ig_o, tg_o) if near else (R[s] for s in ("out", "ig", "tg"))
    gact, gmid, gbr, lt, g = (R[s] for s in ("gact", "gmid", "gbr", "lt", "g"))
    f = f_out if near else R["f"]

    rows_n, seq = seg.shape
    width = tok.shape[1]
    half = width // 2
    loc = wout.shape[0]
    heads = loc // HD
    ff = wup.shape[1]
    UA, UB, UC = units
    L = n_dp // 2
    LAG = hop_ticks(L)
    H = L // 2
    dp = lax.axis_index("dp")
    mp = lax.axis_index("mp")
    core = mp % 2
    x = dp % 2
    z = dp // 2
    to_core = (dp, mp + 1 - 2 * core)
    to_y = (dp, (mp + 2) % 4)
    to_x = (dp + 1 - 2 * x, mp)
    last = jnp.minimum(z, L - 1 - z)
    side = div(z, H)
    cross = jnp.where(last == H - 1, 1, 0)
    to_in = ((z + 1 - 2 * side) * 2 + x, mp)
    to_out = (jnp.clip(z - 1 + 2 * side, 0, L - 1) * 2 + x, mp)
    zlo = jnp.maximum(z - 1, 0) * 2 + x
    zhi = jnp.minimum(z + 1, L - 1) * 2 + x

    barrier = pltpu.get_barrier_semaphore()
    for dev in (to_core, to_y, to_x):
        pl.semaphore_signal(barrier, 1, device_id=dev, device_id_type=MESH)
    when(z > 0, lambda: pl.semaphore_signal(barrier, 1, device_id=(zlo, mp), device_id_type=MESH))
    when(z < L - 1, lambda: pl.semaphore_signal(barrier, 1, device_id=(zhi, mp), device_id_type=MESH))
    greeted = 3 + jnp.minimum(z, 1) + jnp.minimum(L - 1 - z, 1)

    def sl(r, n=seq):
        return pl.ds(pl.multiple_of(r * n, n), n)

    def sub(r, i):
        return pl.ds(pl.multiple_of(r * seq + i * SUB, SUB), SUB)

    mine = pl.ds(pl.multiple_of(core * half, 128), half)
    other = pl.ds(pl.multiple_of((1 - core) * half, 128), half)

    def remote(src, dst, ssem, rsem, dev):
        return pltpu.make_async_remote_copy(
            src_ref=src, dst_ref=dst, send_sem=ssem, recv_sem=rsem, device_id=dev, device_id_type=MESH
        )

    def core_copy(p, r):
        return remote(part.at[sl(r), other], cr.at[sl(r)], R["cs"].at[r], R["crs"].at[r], to_core)

    def y_copy(p, r):
        return remote(ys.at[sl(r)], yr.at[p % 2, sl(r)], R["yss"].at[r], R["yrs"].at[p % 2, r], to_y)

    def ag_copy(p, r):
        return remote(tot.at[sl(r), mine], tot.at[sl(r), mine], R["gs"].at[r], R["grs"].at[r], to_core)

    def sum_b(p, r):
        core_copy(p, r).wait()
        ys[sl(r), :] = part[sl(r), mine] + cr[sl(r), :]
        y_copy(p, r).start()

    def sum_c(p, r):
        y_copy(p, r).wait()
        tot[sl(r), mine] = ys[sl(r), :] + yr[p % 2, sl(r), :]
        ag_copy(p, r).start()

    def sum_d(p, r):
        ag_copy(p, r).wait()

    def vec(ref):
        return ref[...]

    small = 2 * ff + 4 * loc

    def small_add(i, v):
        g[small + i : small + i + 1, :] += v

    lane = lax.broadcasted_iota(jnp.int32, (1, loc), 1)
    masks = [((lane >= h * HD) & (lane < (h + 1) * HD)).astype(F32) for h in range(heads)]

    def by_head(v):
        return jnp.concatenate([v * m.astype(BF16) for m in masks], 0)

    def from_heads(v):
        total = v[:seq] * masks[0]
        for h in range(1, heads):
            total = total + v[h * seq : (h + 1) * seq] * masks[h]
        return total

    def norm1(r):
        @pl.loop(0, seq // SUB)
        def _(i):
            s = sub(r, i)
            v = tok[s, :].astype(F32) + timf[pl.ds(r, 1), :]
            start[s, :] = v
            xhat, _ = normed(v)
            entry[s, :] = (xhat * n1g[...] + n1b[...]).astype(BF16)

    def project(r):
        e = entry[sl(r), :]
        q_s[sl(r), :] = (nt(e, wqkv[0]) + qvb[0:1, :]).astype(BF16)
        k_s[sl(r), :] = nt(e, wqkv[1]).astype(BF16)
        v_s[sl(r), :] = (nt(e, wqkv[2]) + qvb[1:2, :]).astype(BF16)

    def attend(r):
        labels = jnp.broadcast_to(seg[pl.ds(r, 1), :], (seq, seq))
        same = labels == labels.T
        same = jnp.concatenate([same.astype(F32)] * heads, 0) > 0.5
        scores = nt(by_head(q_s[sl(r), :]), k_s[sl(r), :]) * HD ** (-0.5)
        scores = jnp.where(same, scores, -1e30)
        w = jnp.exp(scores - jnp.max(scores, -1, keepdims=True))
        pr = w / jnp.sum(w, -1, keepdims=True)
        probs[sl(r, heads * seq), :] = pr
        mixed = from_heads(nn(pr.astype(BF16), v_s[sl(r), :])).astype(BF16)
        mixed_s[sl(r), :] = mixed
        turned = mixed.T
        lt[2 * ff : 2 * ff + loc, sl(r)] = turned
        mixa[mp, r] = turned.astype(F32)
        m_core(r).start()
        m_y(r).start()

    wf, wall, mixa = R["wf"], R["wall"], R["mixa"]
    mp_y, mp_c = rem(mp + 2, 4), mp + 1 - 2 * core
    mine_0, other_0 = mp - core, mp_y - core
    hl = loc // 4
    pr_n = hl // W_PIECES
    zz = rem(z, 2)
    quarter = zz * 2 + x
    to_zz = ((z + 1 - 2 * zz) * 2 + x, mp)

    def w_core():
        return remote(wf.at[mp], wf.at[mp], R["wcs"], R["wcr"], to_core)

    def w_rows(start, n):
        return pl.ds(pl.multiple_of(start, CH), n)

    def w_y(i):
        s = w_rows(quarter * hl + i * pr_n, pr_n)
        return remote(wf.at[mp, s], wf.at[mp, s], R["wys"].at[i], R["wyr"].at[i], to_y)

    def w_x(i):
        s = w_rows(quarter * hl + i * pr_n, pr_n)
        return remote(wf.at[mp_y, s], wf.at[mp_y, s], R["wxs"].at[i], R["wxr"].at[i], to_x)

    def w_z(k, i):
        s = w_rows((zz * 2 + (x + k - 2 * x * k)) * hl + i * pr_n, pr_n)
        j = k * W_PIECES + i
        return remote(wf.at[mp_y, s], wf.at[mp_y, s], R["wzs"].at[j], R["wzr"].at[j], to_zz)

    def w_share(h):
        s = w_rows((zz + h - 2 * zz * h) * 2 * hl, 2 * hl)
        return remote(wf.at[mp_y, s], wf.at[mp_y, s], R["whs"].at[h], R["whr"].at[h], to_core)

    def m_core(r):
        return remote(mixa.at[mp, r], mixa.at[mp, r], R["cs"].at[r], R["crs"].at[r], to_core)

    def m_y(r):
        return remote(mixa.at[mp, r], mixa.at[mp, r], R["yss"].at[r], R["yrs"].at[0, r], to_y)

    def m_share(r):
        return remote(mixa.at[mp_y, r], mixa.at[mp_y, r], R["gs"].at[r], R["grs"].at[r], to_core)

    def weights_out():
        loads["wout"].wait()
        wf[mp] = wout[...].astype(F32)
        pl.semaphore_wait(barrier, greeted)
        for i in range(W_PIECES):
            w_y(i).start()
        w_core().start()

    def weights_on(i):
        w_y(i).wait()
        w_x(i).start()
        w_z(0, i).start()

    def pair_sum(m, r):
        return tn(mixa[m, r].astype(BF16), wall[m]) + tn(mixa[m + 1, r].astype(BF16), wall[m + 1])

    def near_part(r):
        m_core(r).wait()
        part[sl(r), :] = pair_sum(mine_0, r)

    def across(r):
        m_y(r).wait()
        m_share(r).start()

    def far_part(r):
        m_share(r).wait()
        tot[sl(r), :] = part[sl(r), :] + pair_sum(other_0, r)

    def grad_act(r):
        c = cot[sl(r), :]
        gact[sl(r), :] = nt(c, wdn[...])
        small_add(0, colsum(c.astype(F32)))

    def feed(k):
        both = sl(k, 4 * seq)
        for i in range(4):
            s = sl(k * 4 + i)
            v = start[s, :] + (tot[s, :] + outb[...])
            mid[s, :] = v
            xhat, _ = normed(v)
            e2[s, :] = (xhat * n2g[...] + n2b[...]).astype(BF16)

        hp[...] = nn(e2[both, :], wup[...])

        for i in range(4):
            s = sl(k * 4 + i)
            u = hp[i * seq : (i + 1) * seq, :] + upb[...]
            cdf = 0.5 * (1.0 + lax.erf(u * 0.7071067811865476))
            act[s, :] = (u * cdf).astype(BF16)
            slope = cdf + u * (0.3989422804014327 * jnp.exp(-0.5 * u * u))
            pre = (gact[s, :] * slope).astype(BF16)
            gp[s, :] = pre
            small_add(1, colsum(pre.astype(F32)))

        lt[0:ff, both] = act[both, :].T

    def feed_on(r):
        part[sl(r), :] = nt(gp[sl(r), :], wup[...])
        core_copy(1, r).start()
        lt[ff : 2 * ff, sl(r)] = e2[sl(r), :].T

    def back2(r):
        @pl.loop(0, seq // SUB)
        def _(i):
            s = sub(r, i)
            ge = tot[s, :]
            xhat, scale = normed(mid[s, :])
            small_add(2, colsum(ge * xhat))
            small_add(3, colsum(ge))
            gx = ge * n2g[...]
            gm = cot[s, :].astype(F32) + scale * (
                gx - jnp.mean(gx, -1, keepdims=True) - xhat * jnp.mean(gx * xhat, -1, keepdims=True)
            )
            gmid[s, :] = gm
            low = gm.astype(BF16)
            gbr[s, :] = low
            small_add(4, colsum(low.astype(F32)))

        g3 = by_head(nt(gbr[sl(r), :], wout[...]).astype(BF16))
        pr = probs[sl(r, heads * seq), :]
        grad_probs = nt(g3, v_s[sl(r), :])
        inner = jnp.sum(pr * grad_probs, -1, keepdims=True)
        ds = (pr * (grad_probs - inner)).astype(BF16)
        gq = (from_heads(nn(ds, k_s[sl(r), :])) * HD ** (-0.5)).astype(BF16)
        gk = (tn(ds, by_head(q_s[sl(r), :])) * HD ** (-0.5)).astype(BF16)
        gv = tn(pr.astype(BF16), g3).astype(BF16)
        part[sl(r), :] = nn(gq, wqkv[0]) + nn(gk, wqkv[1]) + nn(gv, wqkv[2])
        core_copy(2, r).start()
        late = 2 * ff + loc
        for i, v in enumerate((gq, gk, gv)):
            lt[late + i * loc : late + (i + 1) * loc, sl(r)] = v.T
        g[small + 7 : small + 8, 0:loc] += colsum(gq.astype(F32))
        g[small + 7 : small + 8, half : half + loc] += colsum(gv.astype(F32))

    def back1(r):
        tg[pl.ds(r, 1), :] = jnp.zeros((1, width), F32)

        @pl.loop(0, seq // SUB)
        def _(i):
            s = sub(r, i)
            ge = tot[s, :]
            xhat, scale = normed(start[s, :])
            small_add(5, colsum(ge * xhat))
            small_add(6, colsum(ge))
            gy = ge * n1g[...]
            gs = gmid[s, :] + scale * (
                gy - jnp.mean(gy, -1, keepdims=True) - xhat * jnp.mean(gy * xhat, -1, keepdims=True)
            )
            ig[s, :] = gs.astype(BF16)
            tg[pl.ds(r, 1), :] += colsum(gs)

    def down(r):
        part[sl(r), :] = nn(act[sl(r), :], wdn[...])
        core_copy(3, r).start()

    def finish(r):
        @pl.loop(0, seq // SUB)
        def _(i):
            s = sub(r, i)
            out[s, :] = (mid[s, :] + (tot[s, :] + dnb[...])).astype(BF16)

    blk = loc

    early = ff // blk

    def weight_grads(j):
        s = pl.ds(pl.multiple_of(j * blk, blk), blk)

        def by(right):
            def fn():
                g[s, :] = nn(lt[s, :], right[...])

            return fn

        when(j < early, by(cot))
        when((j >= early) & (j < 2 * early), by(gp))
        when(j == 2 * early, by(gbr))
        when(j > 2 * early, by(entry))

    def go(copy, u, depth):
        when(u >= depth, lambda: copy(u - depth).wait_send())
        copy(u).start()

    def end(copy, n, depth):
        for u in range(n - min(depth, n), n):
            copy(u).wait_send()

    AF = LAG

    def base_of(u):
        return u * 4 * CH

    def later(u):
        return base_of(div(u, EACH) * (EACH + 2) + rem(u, EACH))

    def b_base(u, i):
        return base_of(jnp.minimum(u * (EACH + 2) + EACH + i, UA + UB + UC - 1))

    def a_base(u, owner):
        return later(u) + owner * 2 * CH

    def x_slot(u):
        return pl.ds(pl.multiple_of(rem(u, R["xr"].shape[0]) * 2 * CH, CH), 2 * CH)

    def x_first(u):
        src = pl.ds(pl.multiple_of(later(u) + (1 - x) * 2 * CH, CH), 2 * CH)
        return remote(
            g.at[src], R["xrb"].at[x_slot(u)], R["xs"].at[rem(u, SENDS)], R["xr"].at[rem(u, R["xr"].shape[0])], to_x
        )

    def rows_at(base, n):
        return pl.ds(pl.multiple_of(base, CH), n)

    class Line:
        def __init__(self, kind, n, first, stride, depth):
            self.kind, self.n, self.first, self.stride, self.depth = kind, n, first, stride, depth

        def unit(self, t, offset):
            rel = t - self.first - offset
            if self.stride == 1:
                return rel, (rel >= 0) & (rel < self.n)
            return div(rel, self.stride), (rel >= 0) & (rel < self.n * self.stride) & (rem(rel, self.stride) == 0)

        def sem(self, name, i, u):
            ref = R[self.kind + "_" + name]
            return ref.at[i, rem(u, ref.shape[1])]

        def slot(self, u, rows):
            return rows_at(rem(u, R[self.kind + "_r"].shape[1]) * rows, rows)

        def go(self, copy, u):
            go(copy, u, self.depth)

        def end(self, copy):
            end(copy, self.n, self.depth)

    class A(Line):
        def own(self, u):
            return rows_at(a_base(u, x), 2 * CH)

        def inward(self, u):
            dst = R["abuf"].at[cross, self.slot(u, 2 * CH)]
            return remote(g.at[self.own(u)], dst, self.sem("s", 0, u), self.sem("r", cross, u), to_in)

        def arrived(self, u, i):
            buf = R["abuf"].at[i, self.slot(u, 2 * CH)]
            remote(buf, buf, self.sem("s", 0, u), self.sem("r", i, u), to_in).wait_recv()
            return buf

        def outward(self, u):
            own = self.own(u)
            return remote(f.at[own], f.at[own], self.sem("u", 0, u), self.sem("r", 1, u), to_out)

        def x_last(self, u):
            own = self.own(u)
            return remote(f.at[own], f.at[own], self.sem("xs", 0, u), self.sem("xr", 0, u), to_x)

        def tick(self, t):
            u, valid_u = self.unit(t, last * LAG)

            def reduce():
                def add():
                    g[self.own(u), :] += self.arrived(u, 0)[...]

                if H > 1:
                    when(last > 0, add)
                self.go(self.inward, u)

            when(valid_u, reduce)
            v, valid_v = self.unit(t, (2 * H - 1 - last) * LAG)

            def finish():
                def turn():
                    f[self.own(v), :] = g[self.own(v), :] + self.arrived(v, 1)[...]

                when(last == H - 1, turn)
                if H > 1:
                    when(last < H - 1, lambda: self.outward(v).wait_recv())
                    when(last > 0, lambda: self.go(self.outward, v))
                self.go(self.x_last, v)

            when(valid_v, finish)
            e, valid_e = self.unit(t, (2 * H - last) * LAG)
            when(valid_e, lambda: self.x_last(e).wait_recv())

        def drain(self):
            self.end(self.inward)
            self.end(self.x_last)
            if H > 1:
                when(last > 0, lambda: self.end(self.outward))

    class B(Line):
        def all(self, u):
            return rows_at(b_base(u, 0), 4 * CH)

        def half(self, u, i):
            return rows_at(b_base(u, 0) + i * 2 * CH, 2 * CH)

        def inward(self, u):
            dst = R["bbuf"].at[self.slot(u, 4 * CH)]
            return remote(g.at[self.all(u)], dst, self.sem("s", 0, u), self.sem("r", 0, u), to_in)

        def swap(self, u):
            dst = R["bsw"].at[self.slot(u, 2 * CH)]
            return remote(g.at[self.half(u, 1 - side)], dst, self.sem("s", 0, u), self.sem("r", 1, u), to_in)

        def x_copy(self, u):
            dst = R["bxb"].at[self.slot(u, 2 * CH)]
            return remote(g.at[self.half(u, side)], dst, self.sem("xs", 0, u), self.sem("xr", 0, u), to_x)

        def back(self, u):
            own = self.half(u, side)
            return remote(f.at[own], f.at[own], self.sem("d", 0, u), self.sem("r", 2, u), to_in)

        def outward(self, u):
            own = self.all(u)
            return remote(f.at[own], f.at[own], self.sem("u", 0, u), self.sem("r", 1, u), to_out)

        def tick(self, t):
            u, valid_u = self.unit(t, last * LAG)

            def reduce():
                def add():
                    self.inward(u).wait_recv()
                    g[self.all(u), :] += R["bbuf"][self.slot(u, 4 * CH), :]

                if H > 1:
                    when(last > 0, add)
                    when(last < H - 1, lambda: self.go(self.inward, u))
                when(last == H - 1, lambda: self.go(self.swap, u))

            when(valid_u, reduce)
            middle = last == H - 1
            i, valid_i = self.unit(t, H * LAG)

            def over():
                self.swap(i).wait_recv()
                g[self.half(i, side), :] += R["bsw"][self.slot(i, 2 * CH), :]
                self.go(self.x_copy, i)

            when(valid_i & middle, over)
            j, valid_j = self.unit(t, (H + 1) * LAG)

            def total():
                self.x_copy(j).wait_recv()
                own = self.half(j, side)
                f[own, :] = g[own, :] + R["bxb"][self.slot(j, 2 * CH), :]
                self.go(self.back, j)

            when(valid_j & middle, total)
            v, valid_v = self.unit(t, (2 * H + 1 - last) * LAG)

            def finish():
                when(middle, lambda: self.back(v).wait_recv())
                if H > 1:
                    when(last < H - 1, lambda: self.outward(v).wait_recv())
                    when(last > 0, lambda: self.go(self.outward, v))

            when(valid_v, finish)

        def drain(self):
            def ends():
                for copy in (self.swap, self.x_copy, self.back):
                    self.end(copy)

            when(last == H - 1, ends)
            if H > 1:
                when(last < H - 1, lambda: self.end(self.inward))
                when(last > 0, lambda: self.end(self.outward))

    class C(Line):
        dirs, rows = (0, 1), 2 * CH

        def own(self, u, d):
            return rows_at(b_base(u, 1) + d * 2 * CH, 2 * CH)

        def place(self, d):
            w = z if d == 0 else L - 1 - z
            return w, (zhi if d == 0 else zlo, mp), (zlo if d == 0 else zhi, mp)

        def copies(self, d):
            w, up, dn = self.place(d)
            own = lambda u: self.own(u, d)
            slot = lambda u: self.slot(u, self.rows)

            def send(u):
                return remote(g.at[own(u)], R[self.kind + "buf"].at[d, slot(u)], self.sem("s", d, u), self.sem("r", d, u), dn)

            def x_copy(u):
                return remote(g.at[own(u)], R[self.kind + "xb"].at[d, slot(u)], self.sem("s", d, u), self.sem("t", d, u), to_x)

            def spread(u):
                return remote(f.at[own(u)], f.at[own(u)], self.sem("u", d, u), self.sem("t", d, u), up)

            return w, send, x_copy, spread

        def tick(self, t):
            for d in self.dirs:
                w, send, x_copy, spread = self.copies(d)
                u, valid_u = self.unit(t, (L - 1 - w) * LAG)

                def reduce():
                    def add():
                        send(u).wait_recv()
                        g[self.own(u, d), :] += R[self.kind + "buf"][d, self.slot(u, self.rows), :]

                    when(w < L - 1, add)
                    when(w > 0, lambda: self.go(send, u))
                    when(w == 0, lambda: self.go(x_copy, u))

                when(valid_u, reduce)
                v, valid_v = self.unit(t, (L + w) * LAG)

                def finish():
                    def turn():
                        x_copy(v).wait_recv()
                        own = self.own(v, d)
                        f[own, :] = g[own, :] + R[self.kind + "xb"][d, self.slot(v, self.rows), :]

                    when(w == 0, turn)
                    when(w > 0, lambda: spread(v).wait_recv())
                    when(w < L - 1, lambda: self.go(spread, v))

                when(valid_v, finish)

        def drain(self):
            for d in self.dirs:
                w, send, x_copy, spread = self.copies(d)
                when(w > 0, lambda: self.end(send))
                when(w == 0, lambda: self.end(x_copy))
                when(w < L - 1, lambda: self.end(spread))

    class S(C):
        dirs, rows = (0,), CH

        def own(self, u, d):
            return pl.ds(small, CH)

    lines = [C("c", UC, 0, EACH, 2), A("a", UA, AF, 1, SENDS), B("b", UB, 1, EACH, 2), S("e", 1, S_FIRST, 1, 1)]

    def dp_tick(t):
        when(t < UA, lambda: go(x_first, t, SENDS))
        v = t - AF

        def x_add():
            x_first(v).wait_recv()
            s = rows_at(a_base(v, x), 2 * CH)
            g[s, :] += R["xrb"][x_slot(v), :]

        when((v >= 0) & (v < UA), x_add)
        for line in lines:
            line.tick(t)

    def dp_drain():
        end(x_first, UA, SENDS)
        for line in lines:
            line.drain()

    for copy in loads.values():
        copy.start()

    def vector(i, name):
        loads[name].wait()
        R["vecs"][i : i + 1, :] = R[name][...][None, :]

    g[small : small + CH, :] = jnp.zeros((CH, width), F32)
    for name in ("tok", "tim"):
        loads[name].wait()
    timf[...] = tim[...].astype(F32)
    vector(0, "n1g")
    vector(1, "n1b")

    @pl.loop(0, rows_n)
    def _(r):
        norm1(r)

        @pl.when(r == 0)
        def _():
            for name in ("wqkv", "qvb", "seg"):
                loads[name].wait()

        project(r)
        when(r == 0, weights_out)
        attend(r)
        for i in range(W_PIECES):
            when(r == rows_n - W_PIECES - 1 + i, lambda: weights_on(i))

    for name in ("cot", "wdn", "wup"):
        loads[name].wait()
    for i, name in enumerate(("outb", "n2g", "n2b", "upb", "dnb")):
        vector(2 + i, name)
    w_x(0).wait()
    w_z(1, 0).start()
    w_core().wait()
    for i in range(2):
        wall[mine_0 + i] = wf[mine_0 + i].astype(BF16)
    pl.loop(0, rows_n // 2)(near_part)
    for i in range(1, W_PIECES):
        w_x(i).wait()
        w_z(1, i).start()
    w_share(0).start()
    pl.loop(0, rows_n)(grad_act)
    pl.loop(rows_n // 2, rows_n)(near_part)
    pl.loop(0, rows_n - 1)(across)
    for k in range(2):
        for i in range(W_PIECES):
            w_z(k, i).wait()
    w_share(1).start()
    across(rows_n - 1)
    for h in range(2):
        w_share(h).wait()
    for i in range(2):
        wall[other_0 + i] = wf[other_0 + i].astype(BF16)

    @pl.loop(0, rows_n // 4)
    def _(k):
        for i in range(4):
            far_part(k * 4 + i)
        feed(k)

    weight_grads(jnp.int32(0))

    blocks = (2 * ff + 4 * loc) // blk
    a_last = AF + LAG * 2 * H
    b_last, c_last = 1 + LAG * (2 * H + 1), LAG * (2 * L - 1)
    ends = [S_FIRST + c_last]
    for u in range(UA + UB + UC):
        i, k = u // (EACH + 2), u % (EACH + 2)
        if k < EACH and u < UA + UB + UC - (UB > UC):
            ends.append(i * EACH + k + a_last)
        else:
            ends.append(i * EACH + c_last if k > EACH else (UB - 1 if k < EACH else i) * EACH + b_last)
    ticks = max(ends) + 1
    per = blk // (4 * CH)

    def done(j):
        return ends[0] if j == blocks else max(ends[1 + j * per : 1 + (j + 1) * per])

    def out_copy(j):
        s = pl.ds(j * blk, blk if j < blocks else CH)
        return pltpu.make_async_copy(f.at[s], f_out.at[s], R["fin"].at[j])

    done_copies = [] if near else [
        pltpu.make_async_copy(a, b, R["fin"].at[blocks + 1 + i])
        for i, (a, b) in enumerate(((ig, ig_o), (tg, tg_o), (out, out_o)))
    ]

    @pl.loop(0, ticks)
    def _(t):
        dp_tick(t)

        def at(first, step, fn):
            r = (t - first) // step
            when((t >= first) & ((t - first) % step == 0) & (r < rows_n), lambda: fn(r))

        at(2, 2, lambda r: sum_b(1, r))
        at(1, 2, feed_on)
        at(5, 3, lambda r: sum_c(1, r))

        def second(r):
            sum_d(1, r)
            back2(r)

        at(7, 3, second)
        at(9, 3, lambda r: sum_b(2, r))
        at(15, 3, lambda r: sum_c(2, r))

        def third(r):
            sum_d(2, r)
            back1(r)

        at(17, 3, third)
        at(18, 3, down)
        at(20, 3, lambda r: sum_b(3, r))
        at(26, 3, lambda r: sum_c(3, r))

        def fourth(r):
            sum_d(3, r)
            finish(r)

        at(28, 3, fourth)

        @pl.when(t == 28 + 3 * rows_n)
        def _():
            for copy in done_copies:
                copy.start()

        when((rem(t, 3) == 1) & (t < 3 * blocks - 2), lambda: weight_grads(div(t + 2, 3)))
        for j in range(0 if near else blocks + 1):
            if done(j) < ticks - 1:
                when(t == done(j), lambda: out_copy(j).start())

    dp_drain()
    left = 0 if near else blocks + 1
    for j in range(left):
        if done(j) >= ticks - 1:
            out_copy(j).start()
    for copy in done_copies + [out_copy(j) for j in range(left)]:
        copy.wait()


def shards(n_dp, *args):
    (tok, tim, seg, n1g, n1b, wqkv, qvb, wout, outb, n2g, n2b, wup, upb, wdn, dnb, cot) = args
    tokens, width = tok.shape
    rows_n, seq = seg.shape
    loc, ff = wout.shape[0], wup.shape[1]
    heads = loc // HD
    half = width // 2
    big = 2 * ff + 4 * loc
    count = big // (4 * CH)
    UC = count // (EACH + 2)
    UB = UC + min(count % (EACH + 2) // 2, 1)
    UA = count - UB - UC
    L = n_dp // 2
    LAG = hop_ticks(L)
    near = L <= 8
    vm = pltpu.VMEM
    dma = pltpu.SemaphoreType.DMA
    W = two_power(max(LAG * (L - 1) + 1, 2 * LAG + 2))
    WB = two_power(LAG * (L + 1) // EACH + 1)
    WC = two_power(LAG * (2 * L - 1) // EACH + 1)
    total = big + CH
    flat = lambda n: vm((n,), F32)
    scratch = dict(
        tok=vm((tokens, width), BF16),
        cot=vm((tokens, width), BF16),
        wqkv=vm((3, loc, width), BF16),
        wout=vm((loc, width), BF16),
        wup=vm((width, ff), BF16),
        wdn=vm((ff, width), BF16),
        ins=dma((16,)),
        tim=vm((rows_n, width), BF16),
        seg=vm((rows_n, seq), jnp.int32),
        qvb=vm((2, loc), F32),
        **{s: flat(width) for s in ("n1g", "n1b", "outb", "n2g", "n2b", "dnb")},
        upb=flat(ff),
        vecs=vm((8, width), F32),
        timf=vm((rows_n, width), F32),
        start=vm((tokens, width), F32),
        entry=vm((tokens, width), BF16),
        q=vm((tokens, loc), BF16),
        k=vm((tokens, loc), BF16),
        v=vm((tokens, loc), BF16),
        probs=vm((heads * tokens, seq), F32),
        mixed=vm((tokens, loc), BF16),
        part=vm((tokens, width), F32),
        cr=vm((tokens, half), F32),
        ys=vm((tokens, half), F32),
        yr=vm((2, tokens, half), F32),
        tot=vm((tokens, width), F32),
        mid=vm((tokens, width), F32),
        e2=vm((tokens, width), BF16),
        hp=vm((4 * seq, ff), F32),
        act=vm((tokens, ff), BF16),
        gp=vm((tokens, ff), BF16),
        gact=vm((tokens, ff), F32),
        gmid=vm((tokens, width), F32),
        gbr=vm((tokens, width), BF16),
        **{n: vm((tokens, width), BF16) for n in (() if near else ("out", "ig"))},
        **({} if near else dict(tg=vm((rows_n, width), F32))),
        lt=vm((big, tokens), BF16),
        g=vm((total, width), F32),
        **({} if near else dict(f=vm((total, width), F32))),
        xrb=vm((W * 2 * CH, width), F32),
        abuf=vm((2, W * 2 * CH, width), F32),
        bbuf=vm((WB * 4 * CH, width), F32),
        bsw=vm((WB * 2 * CH, width), F32),
        bxb=vm((WB * 2 * CH, width), F32),
        cbuf=vm((2, WC * 2 * CH, width), F32),
        cxb=vm((2, WC * 2 * CH, width), F32),
        ebuf=vm((1, CH, width), F32),
        exb=vm((1, CH, width), F32),
        **{"e_" + s: dma((1, 1)) for s in ("s", "u", "r", "t")},
        wf=vm((4, loc, width), F32),
        wall=vm((4, loc, width), BF16),
        mixa=vm((4, rows_n, loc, seq), F32),
        wcs=dma,
        wcr=dma,
        **{s: dma((W_PIECES,)) for s in ("wys", "wyr", "wxs", "wxr")},
        **{s: dma((2 * W_PIECES,)) for s in ("wzs", "wzr")},
        **{s: dma((2,)) for s in ("whs", "whr")},
        **{s: dma((rows_n,)) for s in ("cs", "crs", "yss", "gs", "grs")},
        yrs=dma((2, rows_n)),
        **({} if near else dict(fin=dma((big // loc + 4,)))),
        xs=dma((SENDS,)),
        xr=dma((W,)),
        **{"a_" + s: dma((1, SENDS)) for s in ("s", "u", "xs")},
        a_r=dma((2, W)),
        a_xr=dma((1, W)),
        **{"b_" + s: dma((1, 2)) for s in ("s", "u", "d", "xs")},
        b_r=dma((3, WB)),
        b_xr=dma((1, WB)),
        **{"c_" + s: dma((2, 2)) for s in ("s", "u")},
        **{"c_" + s: dma((2, WC)) for s in ("r", "t")},
    )
    any_spec = pl.BlockSpec(memory_space=pl.ANY)
    vm_spec = pl.BlockSpec(memory_space=pltpu.VMEM)
    operands = (tok, tim, seg, n1g, n1b, wqkv.transpose(0, 2, 1), qvb, wout, outb, n2g, n2b)
    operands += (wup, upb, wdn, dnb, cot)
    result = pltpu.VMEM if near else jax.ShapeDtypeStruct
    out, ig, tg, f = pl.pallas_call(
        functools.partial(kernel, n_dp, near, (UA, UB, UC), tuple(scratch)),
        out_shape=(
            result((tokens, width), BF16),
            result((tokens, width), BF16),
            result((rows_n, width), F32),
            result((total, width), F32),
        ),
        in_specs=[any_spec] * 16,
        out_specs=(vm_spec if near else any_spec,) * 4,
        scratch_shapes=list(scratch.values()),
        compiler_params=pltpu.CompilerParams(
            collective_id=0, has_side_effects=True, vmem_limit_bytes=(52 if near else 63) * 2**20
        ),
        cost_estimate=pl.CostEstimate(flops=6 * 10**9, bytes_accessed=20 * 10**6, transcendentals=0),
    )(
        *[pltpu.with_memory_space_constraint(v, pltpu.HBM) for v in operands]
    )
    f32 = lambda *shape: jax.ShapeDtypeStruct(shape, F32)
    moved = (
        jax.ShapeDtypeStruct((tokens, width), BF16),
        jax.ShapeDtypeStruct((tokens, width), BF16),
        f32(rows_n, width),
        f32(3, loc, width),
        f32(loc, width),
        f32(width, ff),
        f32(ff, width),
    )
    results = pl.pallas_call(
        functools.partial(place, big, near),
        out_shape=moved + (f32(2, loc), f32(ff)) + (f32(width),) * 6,
        in_specs=[vm_spec if near else any_spec] * 4,
        out_specs=(any_spec,) * 15,
        scratch_shapes=[
            *([] if near else [vm((tokens, width), BF16), vm((tokens, width), BF16)]),
            *([] if near else [vm((rows_n, width), F32), vm((total, width), F32)]),
            vm((2, loc), F32),
            *[vm((width,), F32)] * 7,
            dma((4,)),
            dma((17,)),
        ],
        compiler_params=pltpu.CompilerParams(vmem_limit_bytes=(4 if near else 63) * 2**20),
    )(out, ig, tg, f)
    out, ig, tg, qkv, outw, up, down, qvb, upb, downb, n2g, n2b, outb, n1g, n1b = results
    return out, ig, tg, n1g, n1b, qkv.transpose(0, 2, 1), qvb, outw, outb, n2g, n2b, up, upb, down, downb


def place(big, near, *refs):
    results, outs = refs[:4], refs[4:19]
    held = results if near else refs[19:23]
    vq, *flat, sem, sem_o = refs[19 if near else 23 :]
    out_o, ig_o, tg_o, qkv, outw, up, down, qvb, upb, downb, n2g, n2b, outb, n1g, n1b = outs
    loc, ff = outw.shape[0], down.shape[0]
    half = down.shape[1] // 2
    if not near:
        loads = [pltpu.make_async_copy(a, b, sem.at[i]) for i, (a, b) in enumerate(zip(results, held))]
        for copy in loads:
            copy.start()
        for copy in loads:
            copy.wait()
    out, ig, tg, f = held
    moves = []
    row = 0
    for n, ref in ((ff, down), (ff, up), (loc, outw), (loc, qkv.at[0]), (loc, qkv.at[1]), (loc, qkv.at[2])):
        moves.append((f.at[pl.ds(row, n)], ref))
        row += n
    moves += [(out, out_o), (ig, ig_o), (tg, tg_o)]
    small = (downb, upb, n2g, n2b, outb, n1g, n1b)
    moves += [*zip(flat, small), (vq, qvb)]
    stores = [pltpu.make_async_copy(a, b, sem_o.at[i]) for i, (a, b) in enumerate(moves)]
    for copy in stores[:9]:
        copy.start()
    for i, ref in enumerate(flat):
        ref[...] = f[big + i : big + i + 1, :].reshape(ref.shape)
    vq[0:1, :] = f[big + 7 : big + 8, 0:loc]
    vq[1:2, :] = f[big + 7 : big + 8, half : half + loc]
    for copy in stores[9:]:
        copy.start()
    for copy in stores:
        copy.wait()


def solution(mesh):
    placed = (
        P("dp", None),
        P("dp", None),
        P("dp", None),
        P(),
        P(),
        P(None, None, "mp"),
        P(None, "mp"),
        P("mp", None),
        P(),
        P(),
        P(),
        P(None, "mp"),
        P("mp"),
        P("mp", None),
        P(),
        P("dp", None),
    )
    return jax.shard_map(
        functools.partial(shards, mesh.shape["dp"]),
        mesh=mesh,
        in_specs=placed,
        out_specs=(
            P("dp", None),
            P("dp", None),
            P("dp", None),
            P(),
            P(),
            P(None, None, "mp"),
            P(None, "mp"),
            P("mp", None),
            P(),
            P(),
            P(),
            P(None, "mp"),
            P("mp"),
            P("mp", None),
            P(),
        ),
        check_vma=False,
    )
```

```python
import functools

import jax
import jax.numpy as jnp
from jax import lax
from jax.experimental import pallas as pl
from jax.experimental.pallas import tpu as pltpu
from jax.sharding import PartitionSpec as P

HD = 64
SUB = 128
CH = 8
W_PIECES = 2
EACH = 3
S_FIRST = 30
SENDS = 4
MESH = pl.DeviceIdType.MESH
F32 = jnp.float32
BF16 = jnp.bfloat16


ARGS = ("tok", "tim", "seg", "n1g", "n1b", "wqkv", "qvb", "wout", "outb", "n2g", "n2b")
ARGS += ("wup", "upb", "wdn", "dnb", "cot")


def hop_ticks(line):
    return 2 if line <= 8 else 1


def when(cond, fn):
    pl.when(cond)(fn)


def rem(a, n):
    return lax.rem(a, jnp.int32(n))


def div(a, n):
    return lax.div(a, jnp.int32(n))


def two_power(n):
    return 1 << (n - 1).bit_length()


def nt(a, b):
    return lax.dot_general(a, b, (((1,), (1,)), ((), ())), preferred_element_type=F32)


def tn(a, b):
    return lax.dot_general(a, b, (((0,), (0,)), ((), ())), preferred_element_type=F32)


def nn(a, b):
    return jnp.dot(a, b, preferred_element_type=F32)


def normed(v):
    centred = v - jnp.mean(v, -1, keepdims=True)
    spread = jnp.mean(centred * centred, -1, keepdims=True)
    scale = lax.rsqrt(spread + 1e-05)
    return centred * scale, scale


def colsum(v):
    return jnp.sum(v, 0, keepdims=True)


def kernel(n_dp, near, units, names, *refs):
    out_o, ig_o, tg_o, f_out = refs[16:20]
    R = dict(zip(names, refs[20:]))
    order = ("tok", "wout", "tim", "n1g", "n1b", "wqkv", "qvb", "seg", "outb", "cot", "wdn")
    order += ("n2g", "n2b", "wup", "upb", "dnb")
    tok, tim, wqkv, qvb, seg, wout, cot, wdn, wup = (
        R[s] for s in ("tok", "tim", "wqkv", "qvb", "seg", "wout", "cot", "wdn", "wup")
    )
    loads = {
        name: pltpu.make_async_copy(refs[ARGS.index(name)], R[name], R["ins"].at[i]) for i, name in enumerate(order)
    }
    n1g, n1b, outb, n2g, n2b, upb, dnb = (R["vecs"].at[pl.ds(i, 1)] for i in range(7))
    timf, start, entry, q_s, k_s, v_s = (R[s] for s in ("timf", "start", "entry", "q", "k", "v"))
    probs, mixed_s, part, cr, ys, yr = (R[s] for s in ("probs", "mixed", "part", "cr", "ys", "yr"))
    tot, mid, e2, hp, act, gp = (R[s] for s in ("tot", "mid", "e2", "hp", "act", "gp"))
    out, ig, tg = (out_o, ig_o, tg_o) if near else (R[s] for s in ("out", "ig", "tg"))
    gact, gmid, gbr, lt, g = (R[s] for s in ("gact", "gmid", "gbr", "lt", "g"))
    f = f_out if near else R["f"]

    rows_n, seq = seg.shape
    width = tok.shape[1]
    half = width // 2
    loc = wout.shape[0]
    heads = loc // HD
    ff = wup.shape[1]
    UA, UB, UC = units
    L = n_dp // 2
    LAG = hop_ticks(L)
    H = L // 2
    dp = lax.axis_index("dp")
    mp = lax.axis_index("mp")
    core = mp % 2
    x = dp % 2
    z = dp // 2
    to_core = (dp, mp + 1 - 2 * core)
    to_y = (dp, (mp + 2) % 4)
    to_x = (dp + 1 - 2 * x, mp)
    last = jnp.minimum(z, L - 1 - z)
    side = div(z, H)
    cross = jnp.where(last == H - 1, 1, 0)
    to_in = ((z + 1 - 2 * side) * 2 + x, mp)
    to_out = (jnp.clip(z - 1 + 2 * side, 0, L - 1) * 2 + x, mp)
    zlo = jnp.maximum(z - 1, 0) * 2 + x
    zhi = jnp.minimum(z + 1, L - 1) * 2 + x

    barrier = pltpu.get_barrier_semaphore()
    for dev in (to_core, to_y, to_x):
        pl.semaphore_signal(barrier, 1, device_id=dev, device_id_type=MESH)
    when(z > 0, lambda: pl.semaphore_signal(barrier, 1, device_id=(zlo, mp), device_id_type=MESH))
    when(z < L - 1, lambda: pl.semaphore_signal(barrier, 1, device_id=(zhi, mp), device_id_type=MESH))
    greeted = 3 + jnp.minimum(z, 1) + jnp.minimum(L - 1 - z, 1)

    def sl(r, n=seq):
        return pl.ds(pl.multiple_of(r * n, n), n)

    def sub(r, i):
        return pl.ds(pl.multiple_of(r * seq + i * SUB, SUB), SUB)

    mine = pl.ds(pl.multiple_of(core * half, 128), half)
    other = pl.ds(pl.multiple_of((1 - core) * half, 128), half)

    def remote(src, dst, ssem, rsem, dev):
        return pltpu.make_async_remote_copy(
            src_ref=src, dst_ref=dst, send_sem=ssem, recv_sem=rsem, device_id=dev, device_id_type=MESH
        )

    def core_copy(p, r):
        return remote(part.at[sl(r), other], cr.at[sl(r)], R["cs"].at[r], R["crs"].at[r], to_core)

    def y_copy(p, r):
        return remote(ys.at[sl(r)], yr.at[p % 2, sl(r)], R["yss"].at[r], R["yrs"].at[p % 2, r], to_y)

    def ag_copy(p, r):
        return remote(tot.at[sl(r), mine], tot.at[sl(r), mine], R["gs"].at[r], R["grs"].at[r], to_core)

    def sum_b(p, r):
        core_copy(p, r).wait()
        ys[sl(r), :] = part[sl(r), mine] + cr[sl(r), :]
        y_copy(p, r).start()

    def sum_c(p, r):
        y_copy(p, r).wait()
        tot[sl(r), mine] = ys[sl(r), :] + yr[p % 2, sl(r), :]
        ag_copy(p, r).start()

    def sum_d(p, r):
        ag_copy(p, r).wait()

    def vec(ref):
        return ref[...]

    small = 2 * ff + 4 * loc

    def small_add(i, v):
        g[small + i : small + i + 1, :] += v

    lane = lax.broadcasted_iota(jnp.int32, (1, loc), 1)
    masks = [((lane >= h * HD) & (lane < (h + 1) * HD)).astype(F32) for h in range(heads)]

    def by_head(v):
        return jnp.concatenate([v * m.astype(BF16) for m in masks], 0)

    def from_heads(v):
        total = v[:seq] * masks[0]
        for h in range(1, heads):
            total = total + v[h * seq : (h + 1) * seq] * masks[h]
        return total

    def norm1(r):
        @pl.loop(0, seq // SUB)
        def _(i):
            s = sub(r, i)
            v = tok[s, :].astype(F32) + timf[pl.ds(r, 1), :]
            start[s, :] = v
            xhat, _ = normed(v)
            entry[s, :] = (xhat * n1g[...] + n1b[...]).astype(BF16)

    def project(r):
        e = entry[sl(r), :]
        q_s[sl(r), :] = (nt(e, wqkv[0]) + qvb[0:1, :]).astype(BF16)
        k_s[sl(r), :] = nt(e, wqkv[1]).astype(BF16)
        v_s[sl(r), :] = (nt(e, wqkv[2]) + qvb[1:2, :]).astype(BF16)

    def attend(r):
        labels = jnp.broadcast_to(seg[pl.ds(r, 1), :], (seq, seq))
        same = labels == labels.T
        same = jnp.concatenate([same.astype(F32)] * heads, 0) > 0.5
        scores = nt(by_head(q_s[sl(r), :]), k_s[sl(r), :]) * HD ** (-0.5)
        scores = jnp.where(same, scores, -1e30)
        w = jnp.exp(scores - jnp.max(scores, -1, keepdims=True))
        pr = w / jnp.sum(w, -1, keepdims=True)
        probs[sl(r, heads * seq), :] = pr
        mixed = from_heads(nn(pr.astype(BF16), v_s[sl(r), :])).astype(BF16)
        mixed_s[sl(r), :] = mixed
        turned = mixed.T
        lt[2 * ff : 2 * ff + loc, sl(r)] = turned
        mixa[mp, r] = turned.astype(F32)
        m_core(r).start()
        m_y(r).start()

    wf, wall, mixa = R["wf"], R["wall"], R["mixa"]
    mp_y, mp_c = rem(mp + 2, 4), mp + 1 - 2 * core
    mine_0, other_0 = mp - core, mp_y - core
    hl = loc // 4
    pr_n = hl // W_PIECES
    zz = rem(z, 2)
    quarter = zz * 2 + x
    to_zz = ((z + 1 - 2 * zz) * 2 + x, mp)

    def w_core():
        return remote(wf.at[mp], wf.at[mp], R["wcs"], R["wcr"], to_core)

    def w_rows(start, n):
        return pl.ds(pl.multiple_of(start, CH), n)

    def w_y(i):
        s = w_rows(quarter * hl + i * pr_n, pr_n)
        return remote(wf.at[mp, s], wf.at[mp, s], R["wys"].at[i], R["wyr"].at[i], to_y)

    def w_x(i):
        s = w_rows(quarter * hl + i * pr_n, pr_n)
        return remote(wf.at[mp_y, s], wf.at[mp_y, s], R["wxs"].at[i], R["wxr"].at[i], to_x)

    def w_z(k, i):
        s = w_rows((zz * 2 + (x + k - 2 * x * k)) * hl + i * pr_n, pr_n)
        j = k * W_PIECES + i
        return remote(wf.at[mp_y, s], wf.at[mp_y, s], R["wzs"].at[j], R["wzr"].at[j], to_zz)

    def w_share(h):
        s = w_rows((zz + h - 2 * zz * h) * 2 * hl, 2 * hl)
        return remote(wf.at[mp_y, s], wf.at[mp_y, s], R["whs"].at[h], R["whr"].at[h], to_core)

    def m_core(r):
        return remote(mixa.at[mp, r], mixa.at[mp, r], R["cs"].at[r], R["crs"].at[r], to_core)

    def m_y(r):
        return remote(mixa.at[mp, r], mixa.at[mp, r], R["yss"].at[r], R["yrs"].at[0, r], to_y)

    def m_share(r):
        return remote(mixa.at[mp_y, r], mixa.at[mp_y, r], R["gs"].at[r], R["grs"].at[r], to_core)

    def weights_out():
        loads["wout"].wait()
        wf[mp] = wout[...].astype(F32)
        pl.semaphore_wait(barrier, greeted)
        for i in range(W_PIECES):
            w_y(i).start()
        w_core().start()

    def weights_on(i):
        w_y(i).wait()
        w_x(i).start()
        w_z(0, i).start()

    def pair_sum(m, r):
        return tn(mixa[m, r].astype(BF16), wall[m]) + tn(mixa[m + 1, r].astype(BF16), wall[m + 1])

    def near_part(r):
        m_core(r).wait()
        part[sl(r), :] = pair_sum(mine_0, r)

    def across(r):
        m_y(r).wait()
        m_share(r).start()

    def far_part(r):
        m_share(r).wait()
        tot[sl(r), :] = part[sl(r), :] + pair_sum(other_0, r)

    def grad_act(r):
        c = cot[sl(r), :]
        gact[sl(r), :] = nt(c, wdn[...])
        small_add(0, colsum(c.astype(F32)))

    def feed(k):
        both = sl(k, 4 * seq)
        for i in range(4):
            s = sl(k * 4 + i)
            v = start[s, :] + (tot[s, :] + outb[...])
            mid[s, :] = v
            xhat, _ = normed(v)
            e2[s, :] = (xhat * n2g[...] + n2b[...]).astype(BF16)

        hp[...] = nn(e2[both, :], wup[...])

        for i in range(4):
            s = sl(k * 4 + i)
            u = hp[i * seq : (i + 1) * seq, :] + upb[...]
            cdf = 0.5 * (1.0 + lax.erf(u * 0.7071067811865476))
            act[s, :] = (u * cdf).astype(BF16)
            slope = cdf + u * (0.3989422804014327 * jnp.exp(-0.5 * u * u))
            pre = (gact[s, :] * slope).astype(BF16)
            gp[s, :] = pre
            small_add(1, colsum(pre.astype(F32)))

        lt[0:ff, both] = act[both, :].T

    def feed_on(r):
        part[sl(r), :] = nt(gp[sl(r), :], wup[...])
        core_copy(1, r).start()
        lt[ff : 2 * ff, sl(r)] = e2[sl(r), :].T

    def back2(r):
        @pl.loop(0, seq // SUB)
        def _(i):
            s = sub(r, i)
            ge = tot[s, :]
            xhat, scale = normed(mid[s, :])
            small_add(2, colsum(ge * xhat))
            small_add(3, colsum(ge))
            gx = ge * n2g[...]
            gm = cot[s, :].astype(F32) + scale * (
                gx - jnp.mean(gx, -1, keepdims=True) - xhat * jnp.mean(gx * xhat, -1, keepdims=True)
            )
            gmid[s, :] = gm
            low = gm.astype(BF16)
            gbr[s, :] = low
            small_add(4, colsum(low.astype(F32)))

        g3 = by_head(nt(gbr[sl(r), :], wout[...]).astype(BF16))
        pr = probs[sl(r, heads * seq), :]
        grad_probs = nt(g3, v_s[sl(r), :])
        inner = jnp.sum(pr * grad_probs, -1, keepdims=True)
        ds = (pr * (grad_probs - inner)).astype(BF16)
        gq = (from_heads(nn(ds, k_s[sl(r), :])) * HD ** (-0.5)).astype(BF16)
        gk = (tn(ds, by_head(q_s[sl(r), :])) * HD ** (-0.5)).astype(BF16)
        gv = tn(pr.astype(BF16), g3).astype(BF16)
        part[sl(r), :] = nn(gq, wqkv[0]) + nn(gk, wqkv[1]) + nn(gv, wqkv[2])
        core_copy(2, r).start()
        late = 2 * ff + loc
        for i, v in enumerate((gq, gk, gv)):
            lt[late + i * loc : late + (i + 1) * loc, sl(r)] = v.T
        g[small + 7 : small + 8, 0:loc] += colsum(gq.astype(F32))
        g[small + 7 : small + 8, half : half + loc] += colsum(gv.astype(F32))

    def back1(r):
        tg[pl.ds(r, 1), :] = jnp.zeros((1, width), F32)

        @pl.loop(0, seq // SUB)
        def _(i):
            s = sub(r, i)
            ge = tot[s, :]
            xhat, scale = normed(start[s, :])
            small_add(5, colsum(ge * xhat))
            small_add(6, colsum(ge))
            gy = ge * n1g[...]
            gs = gmid[s, :] + scale * (
                gy - jnp.mean(gy, -1, keepdims=True) - xhat * jnp.mean(gy * xhat, -1, keepdims=True)
            )
            ig[s, :] = gs.astype(BF16)
            tg[pl.ds(r, 1), :] += colsum(gs)

    def down(r):
        part[sl(r), :] = nn(act[sl(r), :], wdn[...])
        core_copy(3, r).start()

    def finish(r):
        @pl.loop(0, seq // SUB)
        def _(i):
            s = sub(r, i)
            out[s, :] = (mid[s, :] + (tot[s, :] + dnb[...])).astype(BF16)

    blk = loc

    early = ff // blk

    def weight_grads(j):
        s = pl.ds(pl.multiple_of(j * blk, blk), blk)

        def by(right):
            def fn():
                g[s, :] = nn(lt[s, :], right[...])

            return fn

        when(j < early, by(cot))
        when((j >= early) & (j < 2 * early), by(gp))
        when(j == 2 * early, by(gbr))
        when(j > 2 * early, by(entry))

    def go(copy, u, depth):
        when(u >= depth, lambda: copy(u - depth).wait_send())
        copy(u).start()

    def end(copy, n, depth):
        for u in range(n - min(depth, n), n):
            copy(u).wait_send()

    AF = LAG

    def base_of(u):
        return u * 4 * CH

    def later(u):
        return base_of(div(u, EACH) * (EACH + 2) + rem(u, EACH))

    def b_base(u, i):
        return base_of(jnp.minimum(u * (EACH + 2) + EACH + i, UA + UB + UC - 1))

    def a_base(u, owner):
        return later(u) + owner * 2 * CH

    def x_slot(u):
        return pl.ds(pl.multiple_of(rem(u, R["xr"].shape[0]) * 2 * CH, CH), 2 * CH)

    def x_first(u):
        src = pl.ds(pl.multiple_of(later(u) + (1 - x) * 2 * CH, CH), 2 * CH)
        return remote(
            g.at[src], R["xrb"].at[x_slot(u)], R["xs"].at[rem(u, SENDS)], R["xr"].at[rem(u, R["xr"].shape[0])], to_x
        )

    def rows_at(base, n):
        return pl.ds(pl.multiple_of(base, CH), n)

    class Line:
        def __init__(self, kind, n, first, stride, depth):
            self.kind, self.n, self.first, self.stride, self.depth = kind, n, first, stride, depth

        def unit(self, t, offset):
            rel = t - self.first - offset
            if self.stride == 1:
                return rel, (rel >= 0) & (rel < self.n)
            return div(rel, self.stride), (rel >= 0) & (rel < self.n * self.stride) & (rem(rel, self.stride) == 0)

        def sem(self, name, i, u):
            ref = R[self.kind + "_" + name]
            return ref.at[i, rem(u, ref.shape[1])]

        def slot(self, u, rows):
            return rows_at(rem(u, R[self.kind + "_r"].shape[1]) * rows, rows)

        def go(self, copy, u):
            go(copy, u, self.depth)

        def end(self, copy):
            end(copy, self.n, self.depth)

    class A(Line):
        def own(self, u):
            return rows_at(a_base(u, x), 2 * CH)

        def inward(self, u):
            dst = R["abuf"].at[cross, self.slot(u, 2 * CH)]
            return remote(g.at[self.own(u)], dst, self.sem("s", 0, u), self.sem("r", cross, u), to_in)

        def arrived(self, u, i):
            buf = R["abuf"].at[i, self.slot(u, 2 * CH)]
            remote(buf, buf, self.sem("s", 0, u), self.sem("r", i, u), to_in).wait_recv()
            return buf

        def outward(self, u):
            own = self.own(u)
            return remote(f.at[own], f.at[own], self.sem("u", 0, u), self.sem("r", 1, u), to_out)

        def x_last(self, u):
            own = self.own(u)
            return remote(f.at[own], f.at[own], self.sem("xs", 0, u), self.sem("xr", 0, u), to_x)

        def tick(self, t):
            u, valid_u = self.unit(t, last * LAG)

            def reduce():
                def add():
                    g[self.own(u), :] += self.arrived(u, 0)[...]

                if H > 1:
                    when(last > 0, add)
                self.go(self.inward, u)

            when(valid_u, reduce)
            v, valid_v = self.unit(t, (2 * H - 1 - last) * LAG)

            def finish():
                def turn():
                    f[self.own(v), :] = g[self.own(v), :] + self.arrived(v, 1)[...]

                when(last == H - 1, turn)
                if H > 1:
                    when(last < H - 1, lambda: self.outward(v).wait_recv())
                    when(last > 0, lambda: self.go(self.outward, v))
                self.go(self.x_last, v)

            when(valid_v, finish)
            e, valid_e = self.unit(t, (2 * H - last) * LAG)
            when(valid_e, lambda: self.x_last(e).wait_recv())

        def drain(self):
            self.end(self.inward)
            self.end(self.x_last)
            if H > 1:
                when(last > 0, lambda: self.end(self.outward))

    class B(Line):
        def all(self, u):
            return rows_at(b_base(u, 0), 4 * CH)

        def half(self, u, i):
            return rows_at(b_base(u, 0) + i * 2 * CH, 2 * CH)

        def inward(self, u):
            dst = R["bbuf"].at[self.slot(u, 4 * CH)]
            return remote(g.at[self.all(u)], dst, self.sem("s", 0, u), self.sem("r", 0, u), to_in)

        def swap(self, u):
            dst = R["bsw"].at[self.slot(u, 2 * CH)]
            return remote(g.at[self.half(u, 1 - side)], dst, self.sem("s", 0, u), self.sem("r", 1, u), to_in)

        def x_copy(self, u):
            dst = R["bxb"].at[self.slot(u, 2 * CH)]
            return remote(g.at[self.half(u, side)], dst, self.sem("xs", 0, u), self.sem("xr", 0, u), to_x)

        def back(self, u):
            own = self.half(u, side)
            return remote(f.at[own], f.at[own], self.sem("d", 0, u), self.sem("r", 2, u), to_in)

        def outward(self, u):
            own = self.all(u)
            return remote(f.at[own], f.at[own], self.sem("u", 0, u), self.sem("r", 1, u), to_out)

        def tick(self, t):
            u, valid_u = self.unit(t, last * LAG)

            def reduce():
                def add():
                    self.inward(u).wait_recv()
                    g[self.all(u), :] += R["bbuf"][self.slot(u, 4 * CH), :]

                if H > 1:
                    when(last > 0, add)
                    when(last < H - 1, lambda: self.go(self.inward, u))
                when(last == H - 1, lambda: self.go(self.swap, u))

            when(valid_u, reduce)
            middle = last == H - 1
            i, valid_i = self.unit(t, H * LAG)

            def over():
                self.swap(i).wait_recv()
                g[self.half(i, side), :] += R["bsw"][self.slot(i, 2 * CH), :]
                self.go(self.x_copy, i)

            when(valid_i & middle, over)
            j, valid_j = self.unit(t, (H + 1) * LAG)

            def total():
                self.x_copy(j).wait_recv()
                own = self.half(j, side)
                f[own, :] = g[own, :] + R["bxb"][self.slot(j, 2 * CH), :]
                self.go(self.back, j)

            when(valid_j & middle, total)
            v, valid_v = self.unit(t, (2 * H + 1 - last) * LAG)

            def finish():
                when(middle, lambda: self.back(v).wait_recv())
                if H > 1:
                    when(last < H - 1, lambda: self.outward(v).wait_recv())
                    when(last > 0, lambda: self.go(self.outward, v))

            when(valid_v, finish)

        def drain(self):
            def ends():
                for copy in (self.swap, self.x_copy, self.back):
                    self.end(copy)

            when(last == H - 1, ends)
            if H > 1:
                when(last < H - 1, lambda: self.end(self.inward))
                when(last > 0, lambda: self.end(self.outward))

    class C(Line):
        dirs, rows = (0, 1), 2 * CH

        def own(self, u, d):
            return rows_at(b_base(u, 1) + d * 2 * CH, 2 * CH)

        def place(self, d):
            w = z if d == 0 else L - 1 - z
            return w, (zhi if d == 0 else zlo, mp), (zlo if d == 0 else zhi, mp)

        def copies(self, d):
            w, up, dn = self.place(d)
            own = lambda u: self.own(u, d)
            slot = lambda u: self.slot(u, self.rows)

            def send(u):
                return remote(g.at[own(u)], R[self.kind + "buf"].at[d, slot(u)], self.sem("s", d, u), self.sem("r", d, u), dn)

            def x_copy(u):
                return remote(g.at[own(u)], R[self.kind + "xb"].at[d, slot(u)], self.sem("s", d, u), self.sem("t", d, u), to_x)

            def spread(u):
                return remote(f.at[own(u)], f.at[own(u)], self.sem("u", d, u), self.sem("t", d, u), up)

            return w, send, x_copy, spread

        def tick(self, t):
            for d in self.dirs:
                w, send, x_copy, spread = self.copies(d)
                u, valid_u = self.unit(t, (L - 1 - w) * LAG)

                def reduce():
                    def add():
                        send(u).wait_recv()
                        g[self.own(u, d), :] += R[self.kind + "buf"][d, self.slot(u, self.rows), :]

                    when(w < L - 1, add)
                    when(w > 0, lambda: self.go(send, u))
                    when(w == 0, lambda: self.go(x_copy, u))

                when(valid_u, reduce)
                v, valid_v = self.unit(t, (L + w) * LAG)

                def finish():
                    def turn():
                        x_copy(v).wait_recv()
                        own = self.own(v, d)
                        f[own, :] = g[own, :] + R[self.kind + "xb"][d, self.slot(v, self.rows), :]

                    when(w == 0, turn)
                    when(w > 0, lambda: spread(v).wait_recv())
                    when(w < L - 1, lambda: self.go(spread, v))

                when(valid_v, finish)

        def drain(self):
            for d in self.dirs:
                w, send, x_copy, spread = self.copies(d)
                when(w > 0, lambda: self.end(send))
                when(w == 0, lambda: self.end(x_copy))
                when(w < L - 1, lambda: self.end(spread))

    class S(C):
        dirs, rows = (0,), CH

        def own(self, u, d):
            return pl.ds(small, CH)

    lines = [C("c", UC, 0, EACH, 2), A("a", UA, AF, 1, SENDS), B("b", UB, 1, EACH, 2), S("e", 1, S_FIRST, 1, 1)]

    def dp_tick(t):
        when(t < UA, lambda: go(x_first, t, SENDS))
        v = t - AF

        def x_add():
            x_first(v).wait_recv()
            s = rows_at(a_base(v, x), 2 * CH)
            g[s, :] += R["xrb"][x_slot(v), :]

        when((v >= 0) & (v < UA), x_add)
        for line in lines:
            line.tick(t)

    def dp_drain():
        end(x_first, UA, SENDS)
        for line in lines:
            line.drain()

    for copy in loads.values():
        copy.start()

    def vector(i, name):
        loads[name].wait()
        R["vecs"][i : i + 1, :] = R[name][...][None, :]

    g[small : small + CH, :] = jnp.zeros((CH, width), F32)
    for name in ("tok", "tim"):
        loads[name].wait()
    timf[...] = tim[...].astype(F32)
    vector(0, "n1g")
    vector(1, "n1b")

    @pl.loop(0, rows_n)
    def _(r):
        norm1(r)

        @pl.when(r == 0)
        def _():
            for name in ("wqkv", "qvb", "seg"):
                loads[name].wait()

        when(r == 0, weights_out)
        project(r)
        attend(r)
        for i in range(W_PIECES):
            when(r == rows_n - W_PIECES - 1 + i, lambda: weights_on(i))

    for name in ("cot", "wdn", "wup"):
        loads[name].wait()
    for i, name in enumerate(("outb", "n2g", "n2b", "upb", "dnb")):
        vector(2 + i, name)
    w_x(0).wait()
    w_z(1, 0).start()
    w_core().wait()
    for i in range(2):
        wall[mine_0 + i] = wf[mine_0 + i].astype(BF16)
    pl.loop(0, rows_n // 2)(near_part)
    for i in range(1, W_PIECES):
        w_x(i).wait()
        w_z(1, i).start()
    w_share(0).start()
    pl.loop(0, rows_n)(grad_act)
    pl.loop(rows_n // 2, rows_n)(near_part)
    pl.loop(0, rows_n - 1)(across)
    for k in range(2):
        for i in range(W_PIECES):
            w_z(k, i).wait()
    w_share(1).start()
    across(rows_n - 1)
    for h in range(2):
        w_share(h).wait()
    for i in range(2):
        wall[other_0 + i] = wf[other_0 + i].astype(BF16)

    @pl.loop(0, rows_n // 4)
    def _(k):
        for i in range(4):
            far_part(k * 4 + i)
        feed(k)

    weight_grads(jnp.int32(0))

    blocks = (2 * ff + 4 * loc) // blk
    a_last = AF + LAG * 2 * H
    b_last, c_last = 1 + LAG * (2 * H + 1), LAG * (2 * L - 1)
    ends = [S_FIRST + c_last]
    for u in range(UA + UB + UC):
        i, k = u // (EACH + 2), u % (EACH + 2)
        if k < EACH and u < UA + UB + UC - (UB > UC):
            ends.append(i * EACH + k + a_last)
        else:
            ends.append(i * EACH + c_last if k > EACH else (UB - 1 if k < EACH else i) * EACH + b_last)
    ticks = max(ends) + 1
    per = blk // (4 * CH)

    def done(j):
        return ends[0] if j == blocks else max(ends[1 + j * per : 1 + (j + 1) * per])

    def out_copy(j):
        s = pl.ds(j * blk, blk if j < blocks else CH)
        return pltpu.make_async_copy(f.at[s], f_out.at[s], R["fin"].at[j])

    done_copies = [] if near else [
        pltpu.make_async_copy(a, b, R["fin"].at[blocks + 1 + i])
        for i, (a, b) in enumerate(((ig, ig_o), (tg, tg_o), (out, out_o)))
    ]

    @pl.loop(0, ticks)
    def _(t):
        dp_tick(t)

        def at(first, step, fn):
            r = (t - first) // step
            when((t >= first) & ((t - first) % step == 0) & (r < rows_n), lambda: fn(r))

        at(2, 2, lambda r: sum_b(1, r))
        at(1, 2, feed_on)
        at(5, 3, lambda r: sum_c(1, r))

        def second(r):
            sum_d(1, r)
            back2(r)

        at(7, 3, second)
        at(9, 3, lambda r: sum_b(2, r))
        at(15, 3, lambda r: sum_c(2, r))

        def third(r):
            sum_d(2, r)
            back1(r)

        at(17, 3, third)
        at(18, 3, down)
        at(20, 3, lambda r: sum_b(3, r))
        at(26, 3, lambda r: sum_c(3, r))

        def fourth(r):
            sum_d(3, r)
            finish(r)

        at(28, 3, fourth)

        @pl.when(t == 28 + 3 * rows_n)
        def _():
            for copy in done_copies:
                copy.start()

        when((rem(t, 3) == 1) & (t < 3 * blocks - 2), lambda: weight_grads(div(t + 2, 3)))
        for j in range(0 if near else blocks + 1):
            if done(j) < ticks - 1:
                when(t == done(j), lambda: out_copy(j).start())

    dp_drain()
    left = 0 if near else blocks + 1
    for j in range(left):
        if done(j) >= ticks - 1:
            out_copy(j).start()
    for copy in done_copies + [out_copy(j) for j in range(left)]:
        copy.wait()


def shards(n_dp, *args):
    (tok, tim, seg, n1g, n1b, wqkv, qvb, wout, outb, n2g, n2b, wup, upb, wdn, dnb, cot) = args
    tokens, width = tok.shape
    rows_n, seq = seg.shape
    loc, ff = wout.shape[0], wup.shape[1]
    heads = loc // HD
    half = width // 2
    big = 2 * ff + 4 * loc
    count = big // (4 * CH)
    UC = count // (EACH + 2)
    UB = UC + min(count % (EACH + 2) // 2, 1)
    UA = count - UB - UC
    L = n_dp // 2
    LAG = hop_ticks(L)
    near = L <= 8
    vm = pltpu.VMEM
    dma = pltpu.SemaphoreType.DMA
    W = two_power(max(LAG * (L - 1) + 1, 2 * LAG + 2))
    WB = two_power(LAG * (L + 1) // EACH + 1)
    WC = two_power(LAG * (2 * L - 1) // EACH + 1)
    total = big + CH
    flat = lambda n: vm((n,), F32)
    scratch = dict(
        tok=vm((tokens, width), BF16),
        cot=vm((tokens, width), BF16),
        wqkv=vm((3, loc, width), BF16),
        wout=vm((loc, width), BF16),
        wup=vm((width, ff), BF16),
        wdn=vm((ff, width), BF16),
        ins=dma((16,)),
        tim=vm((rows_n, width), BF16),
        seg=vm((rows_n, seq), jnp.int32),
        qvb=vm((2, loc), F32),
        **{s: flat(width) for s in ("n1g", "n1b", "outb", "n2g", "n2b", "dnb")},
        upb=flat(ff),
        vecs=vm((8, width), F32),
        timf=vm((rows_n, width), F32),
        start=vm((tokens, width), F32),
        entry=vm((tokens, width), BF16),
        q=vm((tokens, loc), BF16),
        k=vm((tokens, loc), BF16),
        v=vm((tokens, loc), BF16),
        probs=vm((heads * tokens, seq), F32),
        mixed=vm((tokens, loc), BF16),
        part=vm((tokens, width), F32),
        cr=vm((tokens, half), F32),
        ys=vm((tokens, half), F32),
        yr=vm((2, tokens, half), F32),
        tot=vm((tokens, width), F32),
        mid=vm((tokens, width), F32),
        e2=vm((tokens, width), BF16),
        hp=vm((4 * seq, ff), F32),
        act=vm((tokens, ff), BF16),
        gp=vm((tokens, ff), BF16),
        gact=vm((tokens, ff), F32),
        gmid=vm((tokens, width), F32),
        gbr=vm((tokens, width), BF16),
        **{n: vm((tokens, width), BF16) for n in (() if near else ("out", "ig"))},
        **({} if near else dict(tg=vm((rows_n, width), F32))),
        lt=vm((big, tokens), BF16),
        g=vm((total, width), F32),
        **({} if near else dict(f=vm((total, width), F32))),
        xrb=vm((W * 2 * CH, width), F32),
        abuf=vm((2, W * 2 * CH, width), F32),
        bbuf=vm((WB * 4 * CH, width), F32),
        bsw=vm((WB * 2 * CH, width), F32),
        bxb=vm((WB * 2 * CH, width), F32),
        cbuf=vm((2, WC * 2 * CH, width), F32),
        cxb=vm((2, WC * 2 * CH, width), F32),
        ebuf=vm((1, CH, width), F32),
        exb=vm((1, CH, width), F32),
        **{"e_" + s: dma((1, 1)) for s in ("s", "u", "r", "t")},
        wf=vm((4, loc, width), F32),
        wall=vm((4, loc, width), BF16),
        mixa=vm((4, rows_n, loc, seq), F32),
        wcs=dma,
        wcr=dma,
        **{s: dma((W_PIECES,)) for s in ("wys", "wyr", "wxs", "wxr")},
        **{s: dma((2 * W_PIECES,)) for s in ("wzs", "wzr")},
        **{s: dma((2,)) for s in ("whs", "whr")},
        **{s: dma((rows_n,)) for s in ("cs", "crs", "yss", "gs", "grs")},
        yrs=dma((2, rows_n)),
        **({} if near else dict(fin=dma((big // loc + 4,)))),
        xs=dma((SENDS,)),
        xr=dma((W,)),
        **{"a_" + s: dma((1, SENDS)) for s in ("s", "u", "xs")},
        a_r=dma((2, W)),
        a_xr=dma((1, W)),
        **{"b_" + s: dma((1, 2)) for s in ("s", "u", "d", "xs")},
        b_r=dma((3, WB)),
        b_xr=dma((1, WB)),
        **{"c_" + s: dma((2, 2)) for s in ("s", "u")},
        **{"c_" + s: dma((2, WC)) for s in ("r", "t")},
    )
    any_spec = pl.BlockSpec(memory_space=pl.ANY)
    vm_spec = pl.BlockSpec(memory_space=pltpu.VMEM)
    operands = (tok, tim, seg, n1g, n1b, wqkv.transpose(0, 2, 1), qvb, wout, outb, n2g, n2b)
    operands += (wup, upb, wdn, dnb, cot)
    result = pltpu.VMEM if near else jax.ShapeDtypeStruct
    out, ig, tg, f = pl.pallas_call(
        functools.partial(kernel, n_dp, near, (UA, UB, UC), tuple(scratch)),
        out_shape=(
            result((tokens, width), BF16),
            result((tokens, width), BF16),
            result((rows_n, width), F32),
            result((total, width), F32),
        ),
        in_specs=[any_spec] * 16,
        out_specs=(vm_spec if near else any_spec,) * 4,
        scratch_shapes=list(scratch.values()),
        compiler_params=pltpu.CompilerParams(
            collective_id=0, has_side_effects=True, vmem_limit_bytes=(52 if near else 63) * 2**20
        ),
        cost_estimate=pl.CostEstimate(flops=6 * 10**9, bytes_accessed=20 * 10**6, transcendentals=0),
    )(
        *[pltpu.with_memory_space_constraint(v, pltpu.HBM) for v in operands]
    )
    f32 = lambda *shape: jax.ShapeDtypeStruct(shape, F32)
    moved = (
        jax.ShapeDtypeStruct((tokens, width), BF16),
        jax.ShapeDtypeStruct((tokens, width), BF16),
        f32(rows_n, width),
        f32(3, loc, width),
        f32(loc, width),
        f32(width, ff),
        f32(ff, width),
    )
    results = pl.pallas_call(
        functools.partial(place, big, near),
        out_shape=moved + (f32(2, loc), f32(ff)) + (f32(width),) * 6,
        in_specs=[vm_spec if near else any_spec] * 4,
        out_specs=(any_spec,) * 15,
        scratch_shapes=[
            *([] if near else [vm((tokens, width), BF16), vm((tokens, width), BF16)]),
            *([] if near else [vm((rows_n, width), F32), vm((total, width), F32)]),
            vm((2, loc), F32),
            *[vm((width,), F32)] * 7,
            dma((4,)),
            dma((17,)),
        ],
        compiler_params=pltpu.CompilerParams(vmem_limit_bytes=(4 if near else 63) * 2**20),
    )(out, ig, tg, f)
    out, ig, tg, qkv, outw, up, down, qvb, upb, downb, n2g, n2b, outb, n1g, n1b = results
    return out, ig, tg, n1g, n1b, qkv.transpose(0, 2, 1), qvb, outw, outb, n2g, n2b, up, upb, down, downb


def place(big, near, *refs):
    results, outs = refs[:4], refs[4:19]
    held = results if near else refs[19:23]
    vq, *flat, sem, sem_o = refs[19 if near else 23 :]
    out_o, ig_o, tg_o, qkv, outw, up, down, qvb, upb, downb, n2g, n2b, outb, n1g, n1b = outs
    loc, ff = outw.shape[0], down.shape[0]
    half = down.shape[1] // 2
    if not near:
        loads = [pltpu.make_async_copy(a, b, sem.at[i]) for i, (a, b) in enumerate(zip(results, held))]
        for copy in loads:
            copy.start()
        for copy in loads:
            copy.wait()
    out, ig, tg, f = held
    moves = []
    row = 0
    for n, ref in ((ff, down), (ff, up), (loc, outw), (loc, qkv.at[0]), (loc, qkv.at[1]), (loc, qkv.at[2])):
        moves.append((f.at[pl.ds(row, n)], ref))
        row += n
    moves += [(out, out_o), (ig, ig_o), (tg, tg_o)]
    small = (downb, upb, n2g, n2b, outb, n1g, n1b)
    moves += [*zip(flat, small), (vq, qvb)]
    stores = [pltpu.make_async_copy(a, b, sem_o.at[i]) for i, (a, b) in enumerate(moves)]
    for copy in stores[:9]:
        copy.start()
    for i, ref in enumerate(flat):
        ref[...] = f[big + i : big + i + 1, :].reshape(ref.shape)
    vq[0:1, :] = f[big + 7 : big + 8, 0:loc]
    vq[1:2, :] = f[big + 7 : big + 8, half : half + loc]
    for copy in stores[9:]:
        copy.start()
    for copy in stores:
        copy.wait()


def solution(mesh):
    placed = (
        P("dp", None),
        P("dp", None),
        P("dp", None),
        P(),
        P(),
        P(None, None, "mp"),
        P(None, "mp"),
        P("mp", None),
        P(),
        P(),
        P(),
        P(None, "mp"),
        P("mp"),
        P("mp", None),
        P(),
        P("dp", None),
    )
    return jax.shard_map(
        functools.partial(shards, mesh.shape["dp"]),
        mesh=mesh,
        in_specs=placed,
        out_specs=(
            P("dp", None),
            P("dp", None),
            P("dp", None),
            P(),
            P(),
            P(None, None, "mp"),
            P(None, "mp"),
            P("mp", None),
            P(),
            P(),
            P(),
            P(None, "mp"),
            P("mp"),
            P("mp", None),
            P(),
        ),
        check_vma=False,
    )
```
